32 devices in a mesh: seq: 8 (over z, y), head: 4 (over x, core).
Axes of the slice: x: 2, y: 2, z: 4, core: 2. Of those that a mesh axis runs over, the one named last changes fastest.
Arguments:
- hidden_in: float32 [2048, 1536], P(('seq', 'head')), may hold values from -6 to 6
- norm1_gain: float32 [1536], replicated, may hold values from 0.5 to 1.5
- w_zx: bfloat16 [1536, 2, 3072], P(None, None, 'head'), may hold values from -0.15625 to 0.15625
- w_bc: bfloat16 [1536, 256], replicated, may hold values from -0.15625 to 0.15625
- w_dt: bfloat16 [1536, 48], P(None, 'head'), may hold values from -0.045898438 to 0.045898438
- conv_x: float32 [4, 3072], P(None, 'head'), may hold values from -0.5 to 0.5
- conv_bc: float32 [4, 256], replicated, may hold values from -0.5 to 0.5
- dt_bias: float32 [48], P('head'), may hold values from -4.6 to -2.3
- a_log: float32 [48], P('head'), may hold values from -11 to 0
- d_skip: float32 [48], P('head'), may hold values from 0.5 to 1.5
- gate_gain: float32 [3072], P('head'), may hold values from 0.5 to 1.5
- w_out: bfloat16 [3072, 1536], P('head'), may hold values from -0.109375 to 0.109375
- norm2_gain: float32 [1536], replicated, may hold values from 0.5 to 1.5
- router: bfloat16 [1536, 16], replicated, may hold values from -0.076660156 to 0.076660156
- expert_up: bfloat16 [32, 1536, 2, 256], P(('seq', 'head')), may hold values from -0.15625 to 0.15625
- expert_down: bfloat16 [32, 256, 1536], P(('seq', 'head')), may hold values from -0.25 to 0.25
- shared_up: bfloat16 [1536, 2, 1024], replicated, may hold values from -0.15625 to 0.15625
- shared_down: bfloat16 [1024, 1536], replicated, may hold values from -0.1875 to 0.1875
- out_grad: float32 [2048, 1536], P(('seq', 'head')), may hold values from -6 to 6
- seq_lengths: int32 [4], replicated, may hold values from 16 to 1888, as said below
- routes: int32 [2048, 6], P(('seq', 'head')), may hold values from 0 to 15, all different within a row; in each aligned block of 64 rows (0 to 63, 64 to 127, ...) at most 48 rows name the same one
Outputs:
- output: float32 [2048, 1536], P(('seq', 'head'))
- grad_in: float32 [2048, 1536], P(('seq', 'head'))
- grad_norm1: float32 [1536], replicated
- grad_zx: float32 [1536, 2, 3072], P('seq', None, 'head')
- grad_bc: float32 [1536, 256], P(('seq', 'head'))
- grad_dt: float32 [1536, 48], P('seq', 'head')
- grad_conv_x: float32 [4, 3072], replicated
- grad_conv_bc: float32 [4, 256], replicated
- grad_dt_bias: float32 [48], replicated
- grad_a_log: float32 [48], replicated
- grad_d_skip: float32 [48], replicated
- grad_gate_gain: float32 [3072], replicated
- grad_w_out: float32 [3072, 1536], P('head', 'seq')
- grad_norm2: float32 [1536], replicated
- grad_router: float32 [1536, 16], P(('seq', 'head'))
- grad_expert_up: float32 [32, 1536, 2, 256], P(('seq', 'head'))
- grad_expert_down: float32 [32, 256, 1536], P(('seq', 'head'))
- grad_shared_up: float32 [1536, 2, 1024], P(('seq', 'head'))
- grad_shared_down: float32 [1024, 1536], P(None, ('seq', 'head'))
The draws below stay inside these ranges and needn't reach their ends.
Inputs may be any that keep to these rules, and one draw needn't show every extreme that they name: `seq_lengths`: the lengths sum to 2048; the longest is 1888 and the other three together 5 * 32. `routes`: within the rows of one device no expert is named more than 48 times; a row names 6 different experts.
All inputs are finite; a program needn't handle non-finite values.
Results may differ from the reference program's by a relative error of at most 0.015.
Values may be sent and summed in bfloat16 or wider, within the bound.
A program may use at most 192 MiB of HBM per device.

```python
import math
import jax
import jax.numpy as jnp
import numpy as np
from jax import lax

D = 1536
HEADS = 48
HEAD_DIM = 64
NSTATE = 128
FFE = 512
FFS = 1024
TOPK = 6
BLOCK = 256
NSEQ = 4
TOK_DEV = 256
DI = 3072
TOKENS = 2048
ROWS = 64
EXPERTS = 16
CAP = 48
DEVICES = 32


def draw_seq_lengths(key, part):
    first_key, second_key = jax.random.split(jax.random.fold_in(key, 17))
    chosen_two = jax.random.randint(first_key, (NSEQ - 2,), TOK_DEV // 16, TOK_DEV // 4 + 1).astype(jnp.int32)
    remaining = (5 * TOK_DEV // 8 - jnp.sum(chosen_two)).astype(jnp.int32)
    longest = jnp.array([TOKENS - 5 * TOK_DEV // 8], jnp.int32)
    ordered = jnp.concatenate([longest, chosen_two, remaining[None]]).astype(jnp.int32)
    placing = jax.random.permutation(second_key, NSEQ)
    return ordered[placing].astype(jnp.int32)


def shard_levels(stream_key, extent, cuts, low, largest):
    factor_of, own = 1.0, jax.random.fold_in(stream_key, 6)
    for dim, blocks in cuts:
        draws = jnp.exp(jax.random.uniform(jax.random.fold_in(own, dim), (blocks,), jnp.float32, low / len(cuts), largest / len(cuts)))
        factor_of = factor_of * jnp.repeat(draws, extent[dim] // blocks).reshape([-1 if axis == dim else 1 for axis in range(len(extent))])
    return factor_of


def routed_block(stream_key, own, number, rows, amount, top, bound, skew):
    order = jax.random.permutation(stream_key, amount)
    packed, usual = shares(amount, rows * top, bound, skew, True), shares(amount, rows * top, bound, skew, False)
    places = jnp.arange(amount)

    def named(lengths, turn):
        used = int((lengths > 0).sum())
        fixed = max(1, used // 4)
        shifted = fixed + (places - fixed + turn * (used - fixed)) % max(1, amount - fixed)
        return jnp.zeros((amount,), jnp.int32).at[order[jnp.where(places < fixed, places, shifted)]].set(jnp.asarray(lengths, jnp.int32))

    lengths = jnp.where(number % 4 == 0, named(packed, number // 4), named(usual, number - number // 4 - 1))
    mixed = jax.random.permutation(jax.random.fold_in(own, 3), amount)
    source_of, taker = mixed[0:amount // 2 * 2:2], mixed[1:amount // 2 * 2:2]
    margin = jnp.minimum(lengths[source_of] - 1, bound - lengths[taker]) // 2
    margin = jnp.where((source_of == order[0]) | (taker == order[0]) | (lengths[taker] == 0), 0, jnp.maximum(margin, 0))
    shifted = jax.random.randint(jax.random.fold_in(own, 4), (amount // 2,), 0, 1 << 20) % (margin + 1)
    lengths = lengths.at[source_of].add(-shifted).at[taker].add(shifted)
    items = jnp.searchsorted(jnp.cumsum(lengths), jnp.arange(rows * top), side="right").astype(jnp.int32)
    grid = items.reshape(top, rows).T
    grid = grid[jax.random.permutation(jax.random.fold_in(own, 1), rows)]
    turn = jax.random.randint(jax.random.fold_in(own, 2), (rows, 1), 0, top)
    return jnp.take_along_axis(grid, (jnp.arange(top)[None, :] + turn) % top, axis=1)


def shares(amount, total, reach, lean, full):
    loads = [(1 << 20) // math.isqrt(standing ** lean) + 1 for standing in range(1, amount + 1)]
    largest = reach if full else min(reach, max(-(-total // amount), total * loads[0] // sum(loads)))
    least = 1 if total - largest >= amount - 1 else 0
    given, surplus = [largest] + [least] * (amount - 1), total - largest - least * (amount - 1)
    while surplus > 0:
        candidates = [i for i in range(1, amount) if given[i] < largest] or [i for i in range(1, amount) if given[i] < reach]
        whole, left = sum([loads[i] for i in candidates]), surplus
        for i in candidates:
            extra = min(reach - given[i], max(1, left * loads[i] // whole), surplus)
            given[i] = given[i] + extra
            surplus = surplus - extra
    return np.array(given)


def normal_values(stream_key, dims, width, most, cuts=(), kind=jnp.bfloat16):
    values = jax.random.normal(stream_key, dims, jnp.float32) * width
    if len(cuts) > 0:
        values = shard_levels(stream_key, dims, cuts, -0.22, 0.18) * values
    return jnp.clip(values, min=-most, max=most).astype(kind)


def setup_inputs(seed: int = 0) -> dict:
    key_of = jax.random.split(jax.random.key(seed), 22)
    hidden_in = normal_values(key_of[0], (TOKENS, D), 1.0, 6.0, ((0, 32),), jnp.float32)
    norm1_gain = jnp.clip(1.0 + 0.1 * jax.random.normal(key_of[1], (D,), jnp.float32), 0.5, 1.5)
    w_zx = normal_values(key_of[2], (D, 2, DI), D ** -0.5, 0.15625, ((2, 4),))
    w_bc = normal_values(key_of[3], (D, 2 * NSTATE), D ** -0.5, 0.15625)
    w_dt = normal_values(key_of[4], (D, HEADS), 0.0077, 0.045898438, ((1, 4),))
    conv_x = jnp.clip(jax.random.uniform(key_of[5], (4, DI), jnp.float32, -0.5, 0.5) * shard_levels(key_of[5], (4, DI), ((1, 4),), -0.4, 0.0), -0.5, 0.5)
    conv_bc = jnp.clip(jax.random.uniform(key_of[6], (4, 2 * NSTATE), jnp.float32, -0.5, 0.5), -0.5, 0.5)
    dt_bias = jnp.clip(-4.6 + 2.3 * jax.random.uniform(key_of[7], (HEADS,), jnp.float32) ** shard_levels(key_of[7], (HEADS,), ((0, 4),), -0.2, 0.2), -4.6, -2.3)
    a_log = jnp.clip(-11.0 + 11.0 * jax.random.uniform(key_of[8], (HEADS,), jnp.float32) ** shard_levels(key_of[8], (HEADS,), ((0, 4),), -0.2, 0.2), -11.0, 0.0)
    d_skip = jnp.clip(0.5 + 1.0 * jax.random.uniform(key_of[9], (HEADS,), jnp.float32) ** shard_levels(key_of[9], (HEADS,), ((0, 4),), -0.2, 0.2), 0.5, 1.5)
    gate_gain = jnp.clip(1.0 + 0.1 * jax.random.normal(key_of[10], (DI,), jnp.float32), 0.5, 1.5)
    w_out = normal_values(key_of[11], (DI, D), DI ** -0.5, 0.109375, ((0, 4),))
    norm2_gain = jnp.clip(1.0 + 0.1 * jax.random.normal(key_of[12], (D,), jnp.float32), 0.5, 1.5)
    router = normal_values(key_of[13], (D, EXPERTS), 0.0128, 0.076660156)
    expert_up = normal_values(key_of[14], (EXPERTS * 2, D, 2, FFE // 2), D ** -0.5, 0.15625, ((0, 32),))
    expert_down = normal_values(key_of[15], (EXPERTS * 2, FFE // 2, D), FFE ** -0.5, 0.25, ((0, 32),))
    shared_up = normal_values(key_of[16], (D, 2, FFS), D ** -0.5, 0.15625)
    shared_down = normal_values(key_of[17], (FFS, D), FFS ** -0.5, 0.1875)
    out_grad = normal_values(key_of[18], (TOKENS, D), 1.0, 6.0, ((0, 32),), jnp.float32)
    seq_lengths = draw_seq_lengths(jax.random.fold_in(key_of[21], 71), 0)
    routes_keys = jax.random.split(jax.random.fold_in(key_of[20], 1), TOKENS // ROWS)
    routes_turns = jax.random.permutation(jax.random.fold_in(key_of[20], 3), TOKENS // ROWS)
    routes = jax.vmap(lambda own, number: routed_block(jax.random.fold_in(key_of[20], 2), own, number, ROWS, EXPERTS, TOPK, CAP, 2))(routes_keys, routes_turns).reshape((TOKENS, TOPK))
    return dict(hidden_in=hidden_in, norm1_gain=norm1_gain, w_zx=w_zx, w_bc=w_bc, w_dt=w_dt, conv_x=conv_x, conv_bc=conv_bc, dt_bias=dt_bias, a_log=a_log, d_skip=d_skip, gate_gain=gate_gain, w_out=w_out, norm2_gain=norm2_gain, router=router, expert_up=expert_up, expert_down=expert_down, shared_up=shared_up, shared_down=shared_down, out_grad=out_grad, seq_lengths=seq_lengths, routes=routes)


highest = lax.Precision.HIGHEST
epsilon = 1e-05

@jax.custom_vjp
def low(v):
    return lax.optimization_barrier(v.astype(jnp.bfloat16)).astype(jnp.float32)

@jax.custom_vjp
def low_back(v):
    return v

def low_keep(v):
    return (low(v), None)

def low_pass(kept, grad):
    return (grad,)

def back_keep(v):
    return (v, None)

def back_low(kept, grad):
    return (low(grad),)
low.defvjp(low_keep, low_pass)
low_back.defvjp(back_keep, back_low)

def matmul(left, right):
    return jnp.dot(left, right, precision=highest, preferred_element_type=jnp.float32)

def rms_scale(values, gain_vec):
    return values * lax.rsqrt(lax.optimization_barrier(jnp.mean(values * values, axis=-1, keepdims=True)) + epsilon) * gain_vec

def segment_of(positions, seq_lengths):
    seq_ends = jnp.cumsum(seq_lengths).astype(jnp.int32)
    located = lax.optimization_barrier(jnp.sum((positions[:, None] >= seq_ends[None, :]).astype(jnp.int32), axis=1))
    return jnp.where(positions < 0, -1, located).astype(jnp.int32)

def start_flags(positions, seq_lengths):
    begins = (jnp.cumsum(seq_lengths) - seq_lengths).astype(jnp.int32)
    return lax.optimization_barrier(jnp.sum((positions[:, None] == begins[None, :]).astype(jnp.float32), axis=1))

def causal_conv(extended, weights, segment_ext):
    length = extended.shape[0] - 3
    current = segment_ext[3:]
    summed = weights[3] * extended[3:]
    for offset in (1, 2, 3):
        joined = (segment_ext[3 - offset:3 - offset + length] == current).astype(jnp.float32)
        summed = summed + weights[3 - offset] * extended[3 - offset:3 - offset + length] * joined[:, None]
    return summed

def block_step(carry_state, block_in):
    x_vals, b_vals, c_vals, log_rates, dt_vals, starts = block_in
    logdec = jnp.cumsum(log_rates, axis=0)
    run_ids = jnp.cumsum(starts)
    order_ids = jnp.arange(x_vals.shape[0])
    linked = ((run_ids[:, None] == run_ids[None, :]) & (order_ids[:, None] >= order_ids[None, :]))[:, :, None]
    log_gap = jnp.where(linked, logdec[:, None, :] - logdec[None, :, :], 0.0)
    decays = jnp.where(linked, jnp.exp(log_gap), 0.0)
    scores = jnp.dot(c_vals, b_vals.T, precision=highest)
    inner_out = jnp.einsum('tsh,shp->thp', decays * scores[:, :, None], dt_vals[:, :, None] * x_vals, precision=highest)
    unreset = (run_ids == 0.0).astype(jnp.float32)
    carried = (unreset[:, None] * jnp.exp(logdec))[:, :, None] * jnp.einsum('tn,hpn->thp', c_vals, carry_state, precision=highest)
    log_last = logdec[-1]
    tail_weight = jnp.exp(log_last[None, :] - logdec) * (run_ids == run_ids[-1]).astype(jnp.float32)[:, None]
    fresh_state = jnp.einsum('sh,shp,sn->hpn', tail_weight * dt_vals, x_vals, b_vals, precision=highest)
    keep_gain = jnp.exp(log_last) * (run_ids[-1] == 0.0).astype(jnp.float32)
    return (keep_gain[:, None, None] * carry_state + fresh_state, inner_out + carried)

def reference(hidden_in, norm1_gain, w_zx, w_bc, w_dt, conv_x, conv_bc, dt_bias, a_log, d_skip, gate_gain, w_out, norm2_gain, router, expert_up, expert_down, shared_up, shared_down, out_grad, seq_lengths, routes):
    positions = jnp.arange(TOKENS, dtype=jnp.int32)
    segment_ext = segment_of(jnp.arange(TOKENS + 3, dtype=jnp.int32) - 3, seq_lengths)
    starts = start_flags(positions, seq_lengths)
    flat_routes = routes.reshape(-1).astype(jnp.int32)
    onehot = (flat_routes[:, None] == jnp.arange(EXPERTS, dtype=jnp.int32)[None, :]).astype(jnp.int32)
    ranks = jnp.cumsum(onehot.reshape(DEVICES, ROWS * TOPK, EXPERTS), axis=1).reshape(-1, EXPERTS)
    slot_pos = lax.optimization_barrier(jnp.sum(ranks * onehot, axis=1)) - 1
    slot_ids = (jnp.arange(TOKENS * TOPK, dtype=jnp.int32) // (ROWS * TOPK) * CAP + slot_pos).astype(jnp.int32)
    row_of_slot = (jnp.arange(TOKENS * TOPK, dtype=jnp.int32) // TOPK).astype(jnp.int32)
    choose = (routes[:, :, None] == jnp.arange(EXPERTS, dtype=jnp.int32)[None, None, :]).astype(jnp.float32)

    def expert_sum(normed_two, gate_probs, expert_up, expert_down):
        rows_in = normed_two[row_of_slot]
        weights_flat = gate_probs.reshape(-1)

        def per_expert(running, expert_id):
            matched = flat_routes == expert_id
            target = jnp.where(matched, slot_ids, DEVICES * CAP)
            buffer = jnp.zeros((DEVICES * CAP, D), jnp.float32).at[target].set(rows_in, mode='drop')
            halves = []
            for half_index in range(2):
                inputs = low_back(buffer)
                upper = lax.dynamic_index_in_dim(expert_up, 2 * expert_id + half_index, 0, keepdims=False)
                lower = lax.dynamic_index_in_dim(expert_down, 2 * expert_id + half_index, 0, keepdims=False)
                middle = low_back(matmul(inputs, upper.reshape(D, FFE)))
                acting = low(jax.nn.silu(middle[:, :FFE // 2]) * middle[:, FFE // 2:])
                halves.append(low(matmul(acting, lower)))
            merged = low_back(halves[0] + halves[1])
            picked = merged[jnp.minimum(target, DEVICES * CAP - 1)] * (matched.astype(jnp.float32) * weights_flat)[:, None]
            return (running + lax.optimization_barrier(jnp.sum(picked.reshape(TOKENS, TOPK, D), axis=1)), None)
        start_sum = jnp.zeros((TOKENS, D), jnp.float32)
        summed, unused = lax.scan(jax.checkpoint(per_expert), start_sum, jnp.arange(EXPERTS, dtype=jnp.int32))
        return summed

    def forward(hidden_in, norm1_gain, w_zx, w_bc, w_dt, conv_x, conv_bc, dt_bias, a_log, d_skip, gate_gain, w_out, norm2_gain, router, expert_up, expert_down, shared_up, shared_down):
        normed_one = low(rms_scale(hidden_in, norm1_gain))
        zx_vals = low_back(matmul(normed_one, w_zx.reshape(D, 2 * DI)))
        bc_vals = matmul(normed_one, w_bc)
        dt_raw = matmul(normed_one, w_dt)
        pre_conv = jnp.concatenate([zx_vals[:, DI:], bc_vals], axis=1)
        extended = jnp.pad(pre_conv, ((3, 0), (0, 0)))
        conv_w = jnp.concatenate([conv_x, conv_bc], axis=1)
        activated = jax.nn.silu(causal_conv(extended, conv_w, segment_ext))
        x_heads = activated[:, :DI].reshape(TOKENS, HEADS, HEAD_DIM)
        b_vals = activated[:, DI:DI + NSTATE]
        c_vals = activated[:, DI + NSTATE:]
        dt_vals = jax.nn.softplus(dt_raw + dt_bias)
        log_rates = -dt_vals * jnp.exp(a_log)
        block_count = TOKENS // BLOCK
        blocks = (x_heads.reshape(block_count, BLOCK, HEADS, HEAD_DIM), b_vals.reshape(block_count, BLOCK, NSTATE), c_vals.reshape(block_count, BLOCK, NSTATE), log_rates.reshape(block_count, BLOCK, HEADS), dt_vals.reshape(block_count, BLOCK, HEADS), starts.reshape(block_count, BLOCK))
        initial = jnp.zeros((HEADS, HEAD_DIM, NSTATE), jnp.float32)
        final_state, mixed_out = lax.scan(jax.checkpoint(block_step), initial, blocks)
        ssd_out = mixed_out.reshape(TOKENS, HEADS, HEAD_DIM) + d_skip[None, :, None] * x_heads
        gated_vals = ssd_out.reshape(TOKENS, DI) * jax.nn.silu(zx_vals[:, :DI])
        normed_gate = low(rms_scale(gated_vals, gate_gain))
        mixer_out = low_back(matmul(normed_gate, w_out))
        residual = hidden_in + mixer_out
        normed_two = low(rms_scale(residual, norm2_gain))
        logits = low_back(matmul(normed_two, router))
        chosen = jnp.einsum('tke,te->tk', choose, logits, precision=highest)
        gate_probs = jax.nn.softmax(chosen, axis=-1)
        shared_mid = low_back(matmul(normed_two, shared_up.reshape(D, 2 * FFS)))
        shared_act = low(jax.nn.silu(shared_mid[:, :FFS]) * shared_mid[:, FFS:])
        shared_out = low_back(matmul(shared_act, shared_down))
        routed = expert_sum(normed_two, gate_probs, expert_up, expert_down)
        return residual + routed + shared_out
    primal_in = (hidden_in, norm1_gain, w_zx.astype(jnp.float32), w_bc.astype(jnp.float32), w_dt.astype(jnp.float32), conv_x, conv_bc, dt_bias, a_log, d_skip, gate_gain, w_out.astype(jnp.float32), norm2_gain, router.astype(jnp.float32), expert_up.astype(jnp.float32), expert_down.astype(jnp.float32), shared_up.astype(jnp.float32), shared_down.astype(jnp.float32))
    output, pullback = jax.vjp(forward, *primal_in)
    grads = pullback(out_grad)
    return (output, grads[0], grads[1], grads[2], grads[3], grads[4], grads[5], grads[6], grads[7], grads[8], grads[9], grads[10], grads[11], grads[12], grads[13], grads[14], grads[15], grads[16], grads[17])
```

```python
import functools
import jax
import jax.numpy as jnp
from jax import lax
from jax.experimental import pallas as pl
from jax.experimental.pallas import tpu as pltpu
from jax.sharding import PartitionSpec as P

MESH = pl.DeviceIdType.MESH
BLOCK = 256
EPS = 1e-05
LANES = 128
B16 = jnp.bfloat16
F32 = jnp.float32


def mm(left, right, dims=(((1,), (0,)), ((), ()))):
    return lax.dot_general(left, right, dims, preferred_element_type=F32)


NT = (((1,), (1,)), ((), ()))
TN = (((0,), (0,)), ((), ()))


def inverse_rms(values):
    return lax.rsqrt(jnp.mean(values * values, axis=-1, keepdims=True) + EPS)


def rms_back(values, inverse, gain, grad):
    weighted = grad * gain
    inner = jnp.mean(weighted * values, axis=-1, keepdims=True)
    return inverse * weighted - values * inverse**3 * inner


def silu_grad(values):
    sig = jax.nn.sigmoid(values)
    return sig * (1.0 + values * (1.0 - sig))


def pad_lanes(values, width):
    return jnp.pad(values, [(0, 0)] * (values.ndim - 1) + [(0, width - values.shape[-1])])


def hi_lo(values):
    high = values.astype(B16)
    return high, (values - high.astype(F32)).astype(B16)


def sizes(seq_size, head_size):
    return head_size // 2, head_size // 2, seq_size // (head_size // 2)


class Place:
    def __init__(self, seq_size, head_size):
        self.H = head_size
        self.X, self.Y, self.Z = sizes(seq_size, head_size)
        seq, head = lax.axis_index("seq"), lax.axis_index("head")
        self.z, self.y = seq // self.Y, seq % self.Y
        self.x, self.c = head // 2, head % 2

    def dev(self, dz=0, dy=0, dx=0, dc=0):
        z, y, x, c = self.at(dz, dy, dx, dc)
        return (z * self.Y + y, x * 2 + c)

    def at(self, dz=0, dy=0, dx=0, dc=0):
        return (
            (self.z + dz) % self.Z if dz else self.z,
            (self.y + dy) % self.Y if dy else self.y,
            (self.x + dx) % self.X if dx else self.x,
            (self.c + dc) % 2 if dc else self.c,
        )

    def slot(self, dz=0, dy=0, dx=0, dc=0):
        z, y, x, c = self.at(dz, dy, dx, dc)
        return (z * self.Y + y) * self.H + x * 2 + c

    def peers(self):
        out = [self.dev(dz=k) for k in range(1, self.Z)]
        out += [self.dev(dy=k) for k in range(1, self.Y)]
        out += [self.dev(dx=k) for k in range(1, self.X)]
        return out + [self.dev(dc=1)]


    def order(self):
        return list(range(1, self.Z)) + [0]


def greet(peers):
    barrier = pltpu.get_barrier_semaphore()
    for peer in peers:
        pl.semaphore_signal(barrier, inc=1, device_id=peer, device_id_type=MESH)
    pl.semaphore_wait(barrier, len(peers))


class Mail:
    def __init__(self, send, recv):
        self.send, self.recv, self.sent = send, recv, []

    def start(self, src, dst, dev):
        i = len(self.sent)
        copy = pltpu.make_async_remote_copy(
            src_ref=src, dst_ref=dst, send_sem=self.send.at[i], recv_sem=self.recv.at[i],
            device_id=dev, device_id_type=MESH,
        )
        copy.start()
        self.sent.append(copy)
        return copy

    def finish(self, count):
        assert len(self.sent) == count
        for copy in self.sent:
            copy.wait_send()


def gather_count(S, H):
    X, Y, Z = sizes(S, H)
    return (Z - 1) + 2 * Z * (X + Y - 2) + 2 * Z * (X - 1) * (Y - 1) + X * Y * Z


def gather(pc, mail, x_ref, out_ref, own_sem):
    X, Y, Z = pc.X, pc.Y, pc.Z
    R = x_ref.shape[0]
    half = R // 2

    def rows(part, **where):
        base = pl.multiple_of(pc.slot(**where) * R, R)
        if part is None:
            return out_ref.at[pl.ds(base, R)]
        return out_ref.at[pl.ds(pl.multiple_of(base + part * half, half), half)]

    own = pltpu.make_async_copy(x_ref, rows(None), own_sem)
    own.start()
    z_in, x_in, y_in, dga, dgb, sib = {}, {}, {}, {}, {}, []
    for dz in range(1, Z):
        z_in[dz] = mail.start(x_ref, rows(None), pc.dev(dz=dz))

    def column(dz):
        for part in (0, 1):
            src = x_ref.at[pl.ds(part * half, half)] if dz == 0 else rows(part, dz=-dz)
            for k in range(1, X):
                x_in[dz, k, part] = mail.start(src, rows(part, dz=-dz), pc.dev(dx=k))
            other = 1 - part
            src = x_ref.at[pl.ds(other * half, half)] if dz == 0 else rows(other, dz=-dz)
            for k in range(1, Y):
                y_in[dz, k, other] = mail.start(src, rows(other, dz=-dz), pc.dev(dy=k))
        src = x_ref if dz == 0 else rows(None, dz=-dz)
        sib.append(mail.start(src, rows(None, dz=-dz), pc.dev(dc=1)))

    column(0)
    for dz in range(Z):
        if dz + 1 < Z:
            z_in[dz + 1].wait_recv()
            column(dz + 1)
        for k in range(1, X):
            x_in[dz, k, 0].wait_recv()
            block = rows(0, dz=-dz, dx=-k)
            for m in range(1, Y):
                dga[dz, k, m] = mail.start(block, block, pc.dev(dy=m))
        for k in range(1, Y):
            y_in[dz, k, 1].wait_recv()
            block = rows(1, dz=-dz, dy=-k)
            for m in range(1, X):
                dgb[dz, k, m] = mail.start(block, block, pc.dev(dx=m))
        for k in range(1, X):
            x_in[dz, k, 1].wait_recv()
            block = rows(None, dz=-dz, dx=-k)
            sib.append(mail.start(block, block, pc.dev(dc=1)))
        for k in range(1, Y):
            y_in[dz, k, 0].wait_recv()
            block = rows(None, dz=-dz, dy=-k)
            sib.append(mail.start(block, block, pc.dev(dc=1)))
    for dz in range(Z):
        for k in range(1, X):
            for m in range(1, Y):
                dga[dz, k, m].wait_recv()
                dgb[dz, m, k].wait_recv()
                block = rows(None, dz=-dz, dx=-k, dy=-m)
                sib.append(mail.start(block, block, pc.dev(dc=1)))
    for copy in sib:
        copy.wait_recv()
    own.wait()


def scatter_parts(split):
    return (("y", 0), ("x", 1)) if split else (("x", None),)


def scatter_count(S, H, splits=(True,)):
    X, Y, Z = sizes(S, H)
    pieces = sum(len(scatter_parts(split)) for split in splits)
    return len(splits) * (Z + Z - 1) + pieces * Z * (X + Y - 2)


def scatter_scratch(S, H, R, W, split=True):
    X, Y, Z = sizes(S, H)
    out = [pltpu.VMEM((Z, Y, X, R, W), B16), pltpu.VMEM((Z, Y, X, R, W), B16), pltpu.VMEM((Z - 1, R, W), B16)]
    for axis, part in scatter_parts(split):
        rows = R if part is None else R // 2
        first, second = (Y, X) if axis == "y" else (X, Y)
        out += [pltpu.VMEM((Z, first - 1, second, rows, W), B16), pltpu.VMEM((Z, second - 1, rows, W), B16)]
    return out + [pltpu.SemaphoreType.DMA((Z,))]


def accumulate(dst, srcs, rows):
    def body(i, carry):
        at = pl.ds(pl.multiple_of(i * 16, 16), 16)
        total = dst.at[at][...].astype(F32)
        for src in srcs:
            total = total + src.at[at][...].astype(F32)
        dst.at[at][...] = total.astype(dst.dtype)
        return carry

    lax.fori_loop(0, rows // 16, body, 0)


def scatter_local(pc, jobs):
    X, Y, Z = pc.X, pc.Y, pc.Z
    own = {}
    for o, (p_ref, total, scratch, split) in enumerate(jobs):
        for dz in pc.order():
            own[o, dz] = pltpu.make_async_copy(
                p_ref.at[pc.at(dz=dz)[0], :, :, pc.c], scratch[0].at[dz], scratch[-1].at[dz]
            )
            own[o, dz].start()
    return own


def scatter(pc, mail, jobs, own, between=None):
    X, Y, Z = pc.X, pc.Y, pc.Z
    sib, one, two, zs = {}, {}, {}, {}

    def pieces(o):
        p_ref, total, scratch, split = jobs[o]
        R = p_ref.shape[4]
        for j, (axis, part) in enumerate(scatter_parts(split)):
            rows, size = (pl.ds(0, R), R) if part is None else (pl.ds(part * (R // 2), R // 2), R // 2)
            yield j, axis, rows, size, scratch[3 + 2 * j], scratch[4 + 2 * j]

    for dz in pc.order():
        for o, (p_ref, total, scratch, split) in enumerate(jobs):
            sib[o, dz] = mail.start(p_ref.at[pc.at(dz=dz)[0], :, :, 1 - pc.c], scratch[1].at[dz], pc.dev(dc=1))
    for dz in pc.order():
        for o, (p_ref, total, scratch, split) in enumerate(jobs):
            t0, r0 = scratch[0], scratch[1]
            own[o, dz].wait()
            sib[o, dz].wait_recv()
            for yy in range(Y):
                for xx in range(X):
                    accumulate(t0.at[dz, yy, xx], [r0.at[dz, yy, xx]], p_ref.shape[4])
            for j, axis, rows, size, r1, r2 in pieces(o):
                for k in range(1, Y if axis == "y" else X):
                    if axis == "y":
                        src, dev = t0.at[dz, pc.at(dy=k)[1], :, rows], pc.dev(dy=k)
                    else:
                        src, dev = t0.at[dz, :, pc.at(dx=k)[2], rows], pc.dev(dx=k)
                    one[o, dz, j, k] = mail.start(src, r1.at[dz, k - 1], dev)
    if between is not None:
        between()
    for dz in pc.order():
        for o, (p_ref, total, scratch, split) in enumerate(jobs):
            t0 = scratch[0]
            for j, axis, rows, size, r1, r2 in pieces(o):
                firsts = range(1, Y if axis == "y" else X)
                for k in firsts:
                    one[o, dz, j, k].wait_recv()
                for m in range(X if axis == "y" else Y):
                    dst = t0.at[dz, pc.y, m, rows] if axis == "y" else t0.at[dz, m, pc.x, rows]
                    accumulate(dst, [r1.at[dz, k - 1, m] for k in firsts], size)
                for k in range(1, X if axis == "y" else Y):
                    if axis == "y":
                        src, dev = t0.at[dz, pc.y, pc.at(dx=k)[2], rows], pc.dev(dx=k)
                    else:
                        src, dev = t0.at[dz, pc.at(dy=k)[1], pc.x, rows], pc.dev(dy=k)
                    two[o, dz, j, k] = mail.start(src, r2.at[dz, k - 1], dev)
    for dz in pc.order():
        for o, (p_ref, total, scratch, split) in enumerate(jobs):
            mine = scratch[0].at[dz, pc.y, pc.x]
            for j, axis, rows, size, r1, r2 in pieces(o):
                seconds = range(1, X if axis == "y" else Y)
                for k in seconds:
                    two[o, dz, j, k].wait_recv()
                accumulate(mine.at[rows], [r2.at[dz, k - 1] for k in seconds], size)
            if dz:
                zs[o, dz] = mail.start(mine, scratch[2].at[dz - 1], pc.dev(dz=dz))
    for o, (p_ref, total, scratch, split) in enumerate(jobs):
        for dz in range(1, Z):
            zs[o, dz].wait_recv()

        def last(i, carry, total=total, scratch=scratch):
            at = pl.ds(pl.multiple_of(i * 16, 16), 16)
            value = scratch[0].at[0, pc.y, pc.x, at][...].astype(F32)
            for k in range(Z - 1):
                value = value + scratch[2].at[k, at][...].astype(F32)
            total.at[at][...] = value
            return carry

        lax.fori_loop(0, p_ref.shape[4] // 16, last, 0)


ANY = pl.BlockSpec(memory_space=pl.ANY)
VMEM = pl.BlockSpec(memory_space=pltpu.VMEM)


def sems(count):
    return [pltpu.SemaphoreType.DMA((count,)), pltpu.SemaphoreType.DMA((count,))]


def talking(cid):
    return pltpu.CompilerParams(collective_id=cid, has_side_effects=True, vmem_limit_bytes=56 * 1024 * 1024)


def first_kernel(S, H, in_ref, gain_ref, named_ref, out_ref, rows, send, recv, own_sem):
    pc = Place(S, H)
    D = in_ref.shape[1]
    values = in_ref[...]
    rows[:, :D] = (values * inverse_rms(values) * gain_ref[...]).astype(B16)
    rows[:, D:] = named_ref[...]
    greet(pc.peers())
    mail = Mail(send, recv)
    gather(pc, mail, rows, out_ref, own_sem)
    mail.finish(gather_count(S, H))


def first_rows(hidden_in, gain, named, S, H):
    R, D = hidden_in.shape
    W = D + LANES
    return pl.pallas_call(
        functools.partial(first_kernel, S, H),
        out_shape=jax.ShapeDtypeStruct((S * H * R, W), B16),
        in_specs=[VMEM] * 3,
        out_specs=ANY,
        scratch_shapes=[pltpu.VMEM((R, W), B16), *sems(gather_count(S, H)), pltpu.SemaphoreType.DMA],
        compiler_params=talking(1),
    )(hidden_in, gain, named)


def blocks(part, S, H):
    X, Y, Z = sizes(S, H)
    return part.reshape(Z, Y, X, 2, part.shape[0] // (S * H), part.shape[1])


def second_kernel(S, H, width, p_ref, in_ref, gain_ref, out_ref, res_ref, mixed_ref, inv_ref, total, rows, *rest):
    scratch, (send, recv, own_sem) = rest[:-3], rest[-3:]
    pc = Place(S, H)
    D = in_ref.shape[1]
    jobs = [(p_ref, total, scratch, True)]
    own = scatter_local(pc, jobs)
    greet(pc.peers())
    mail = Mail(send, recv)
    scatter(pc, mail, jobs, own)
    mixed = total[:, :D]
    square = jnp.sum(total[:, D:], axis=1, keepdims=True)
    inv = lax.rsqrt(square / width + EPS)
    residual = in_ref[...] + inv * mixed
    mixed_ref[...] = mixed
    res_ref[...] = residual
    inv_ref[...] = jnp.broadcast_to(inv, inv_ref.shape)
    rows[...] = (residual * inverse_rms(residual) * gain_ref[...]).astype(B16)
    gather(pc, mail, rows, out_ref, own_sem)
    mail.finish(scatter_count(S, H) + gather_count(S, H))


def second_rows(part, hidden_in, gain, width, S, H):
    R, D = hidden_in.shape
    count = scatter_count(S, H) + gather_count(S, H)
    return pl.pallas_call(
        functools.partial(second_kernel, S, H, width),
        out_shape=[
            jax.ShapeDtypeStruct((S * H * R, D), B16),
            jax.ShapeDtypeStruct((R, D), F32),
            jax.ShapeDtypeStruct((R, D), F32),
            jax.ShapeDtypeStruct((R, LANES), F32),
        ],
        in_specs=[ANY, VMEM, VMEM],
        out_specs=[ANY, VMEM, VMEM, VMEM],
        scratch_shapes=[
            pltpu.VMEM((R, D + LANES), F32), pltpu.VMEM((R, D), B16), *scatter_scratch(S, H, R, D + LANES),
            *sems(count), pltpu.SemaphoreType.DMA,
        ],
        compiler_params=talking(2),
    )(blocks(part, S, H), hidden_in, gain)


def third_kernel(
    S, H, width, p_ref, probs_ref, res_ref, mixed_ref, inv_ref, grad_ref, gain_ref, router_ref,
    out_ref, gres_ref, gnorm_ref, grouter_ref, total, rows, probs, *rest,
):
    scratch, (send, recv, own_sem, probs_sem) = rest[:-4], rest[-4:]
    pc = Place(S, H)
    R, D = res_ref.shape
    jobs = [(p_ref, total, scratch, True)]
    own = scatter_local(pc, jobs)
    fetch = pltpu.make_async_copy(probs_ref.at[pl.ds(pl.multiple_of(pc.slot() * R, R), R)], probs, probs_sem)
    fetch.start()
    greet(pc.peers())
    mail = Mail(send, recv)
    scatter(pc, mail, jobs, own)
    fetch.wait()
    p = probs[...]
    gp = total[:, D:]
    glogits = (p * (gp - jnp.sum(p * gp, axis=1, keepdims=True))).astype(B16)
    gtwo = total[:, :D] + mm(glogits, router_ref[...], NT)
    residual = res_ref[...]
    inv_two = inverse_rms(residual)
    gain = gain_ref[...]
    gres = grad_ref[...] + rms_back(residual, inv_two, gain, gtwo)
    gres_ref[...] = gres
    inv = inv_ref[:, 0:1]
    cross = jnp.sum(gres * mixed_ref[...], axis=1, keepdims=True) * (inv * inv * inv) / width
    high, low = hi_lo(cross)
    lane = lax.broadcasted_iota(jnp.int32, (R, LANES), 1)
    rows[:, :D] = (inv * gres).astype(B16)
    rows[:, D:] = jnp.where(lane == 0, high.astype(F32), jnp.where(lane == 1, low.astype(F32), 0.0)).astype(B16)
    gnorm_ref[...] = jnp.sum(gtwo * residual * inv_two, axis=0, keepdims=True)
    grouter_ref[...] = mm((residual * inv_two * gain).astype(B16), glogits, TN).astype(B16)
    gather(pc, mail, rows, out_ref, own_sem)
    mail.finish(scatter_count(S, H) + gather_count(S, H))


def third_rows(part, probs, residual, mixed, inv_gate, out_grad, gain, router, width, S, H):
    R, D = residual.shape
    count = scatter_count(S, H) + gather_count(S, H)
    return pl.pallas_call(
        functools.partial(third_kernel, S, H, width),
        out_shape=[
            jax.ShapeDtypeStruct((S * H * R, D + LANES), B16),
            jax.ShapeDtypeStruct((R, D), F32),
            jax.ShapeDtypeStruct((1, D), F32),
            jax.ShapeDtypeStruct((D, LANES), B16),
        ],
        in_specs=[ANY, ANY] + [VMEM] * 6,
        out_specs=[ANY, VMEM, VMEM, VMEM],
        scratch_shapes=[
            pltpu.VMEM((R, D + LANES), F32), pltpu.VMEM((R, D + LANES), B16), pltpu.VMEM((R, LANES), F32),
            *scatter_scratch(S, H, R, D + LANES), *sems(count), pltpu.SemaphoreType.DMA, pltpu.SemaphoreType.DMA,
        ],
        compiler_params=talking(3),
    )(blocks(part, S, H), probs, residual, mixed, inv_gate, out_grad, gain, router)


def last_kernel(
    S, H, p_ref, e_ref, zx_ref, wo_ref, su_ref, sd_ref, small_ref, in_ref, gres_ref, gain_ref,
    gin_ref, extra_ref, norm_ref, zx_out, wo_out, su_out, sd_out, small_out,
    total, norm_in, *rest,
):
    half = len(rest) - 7
    main, extra = rest[: half - 6], rest[half - 6 : half]
    send, recv, all_send, all_recv, local_sem, norm_send, norm_recv = rest[half:]
    pc = Place(S, H)
    N = S * H
    me = pc.slot()
    seq, head = lax.axis_index("seq"), lax.axis_index("head")
    jobs = [(p_ref, total, main, True), (e_ref, extra_ref, extra, False)]
    own = scatter_local(pc, jobs)
    barrier = pltpu.get_barrier_semaphore()

    def other(m):
        to = (me + m) % N
        return to, (to // H, to % H)

    def hello(m, carry):
        pl.semaphore_signal(barrier, inc=1, device_id=other(m)[1], device_id_type=MESH)
        return carry

    lax.fori_loop(1, N, hello, 0)
    pl.semaphore_wait(barrier, N - 1)
    mail = Mail(send, recv)

    def to_group(m):
        to = (seq + m) % S
        return [
            pltpu.make_async_remote_copy(
                src_ref=src.at[to], dst_ref=dst.at[seq], send_sem=all_send.at[j, m], recv_sem=all_recv.at[j, m],
                device_id=(to, head), device_id_type=MESH,
            )
            for j, (src, dst) in enumerate(((zx_ref, zx_out), (wo_ref, wo_out)))
        ]

    def to_all(m):
        to, dev = other(m)
        return [
            pltpu.make_async_remote_copy(
                src_ref=src, dst_ref=dst.at[me], send_sem=all_send.at[2 + j, m], recv_sem=all_recv.at[2 + j, m],
                device_id=dev, device_id_type=MESH,
            )
            for j, (src, dst) in enumerate(((su_ref.at[to], su_out), (sd_ref.at[to], sd_out), (small_ref, small_out)))
        ]

    def each(function, make, count):
        def body(m, carry):
            for copy in make(m):
                function(copy)
            return carry

        lax.fori_loop(1, count, body, 0)

    stay = [
        pltpu.make_async_copy(src, dst, local_sem.at[j])
        for j, (src, dst) in enumerate(
            (
                (zx_ref.at[seq], zx_out.at[seq]), (wo_ref.at[seq], wo_out.at[seq]), (su_ref.at[me], su_out.at[me]),
                (sd_ref.at[me], sd_out.at[me]), (small_ref, small_out.at[me]),
            )
        )
    ]
    for copy in stay:
        copy.start()

    def exchange():
        each(lambda c: c.start(), to_group, S)
        each(lambda c: c.start(), to_all, N)

    scatter(pc, mail, jobs, own, exchange)
    values, gone = in_ref[...], total[...]
    inv = inverse_rms(values)
    gin_ref[...] = gres_ref[...] + rms_back(values, inv, gain_ref[...], gone)
    gnorm = jnp.sum(gone * values * inv, axis=0, keepdims=True)
    D = values.shape[1]
    norm_in[me] = jnp.zeros(norm_in.shape[1:], F32)
    for j in range(D // LANES):
        norm_in[me, j : j + 1, :] = gnorm[:, j * LANES : (j + 1) * LANES]

    def norm_to(m):
        return [
            pltpu.make_async_remote_copy(
                src_ref=norm_in.at[me], dst_ref=norm_in.at[me], send_sem=norm_send.at[m], recv_sem=norm_recv.at[m],
                device_id=other(m)[1], device_id_type=MESH,
            )
        ]

    each(lambda c: c.start(), norm_to, N)
    each(lambda c: c.wait_recv(), to_group, S)
    each(lambda c: c.wait_recv(), to_all, N)
    each(lambda c: c.wait_recv(), norm_to, N)

    def add(k, value):
        return value + norm_in[k]

    norm_ref[...] = lax.fori_loop(0, N, add, jnp.zeros(norm_ref.shape, F32))
    each(lambda c: c.wait_send(), to_group, S)
    each(lambda c: c.wait_send(), to_all, N)
    each(lambda c: c.wait_send(), norm_to, N)
    mail.finish(scatter_count(S, H, (True, False)))
    for copy in stay:
        copy.wait()


def last_rows(part, extra, zx, wo, su, sd, small, hidden_in, grad_res, gain, S, H):
    R, D = hidden_in.shape
    N = S * H
    rows = -(-(D // LANES) // 8) * 8
    count = scatter_count(S, H, (True, False))
    like = [jax.ShapeDtypeStruct(v.shape, v.dtype) for v in (zx, wo, su, sd)]
    return pl.pallas_call(
        functools.partial(last_kernel, S, H),
        out_shape=[
            jax.ShapeDtypeStruct((R, D), F32),
            jax.ShapeDtypeStruct((extra.shape[0] // N, extra.shape[1]), F32),
            jax.ShapeDtypeStruct((rows, LANES), F32),
            *like,
            jax.ShapeDtypeStruct((N,) + small.shape, F32),
        ],
        in_specs=[ANY] * 7 + [VMEM] * 3,
        out_specs=[VMEM] * 3 + [ANY] * 5,
        scratch_shapes=[
            pltpu.VMEM((R, D), F32), pltpu.VMEM((N, rows, LANES), F32), *scatter_scratch(S, H, R, D),
            *scatter_scratch(S, H, extra.shape[0] // N, extra.shape[1], False), *sems(count),
            pltpu.SemaphoreType.DMA((5, N)), pltpu.SemaphoreType.DMA((5, N)), pltpu.SemaphoreType.DMA((5,)),
            *sems(N),
        ],
        compiler_params=talking(4),
    )(blocks(part, S, H), blocks(extra, S, H), zx, wo, su, sd, small, hidden_in, grad_res, gain)


def seg_of(pos, ends_ref, count):
    found = jnp.zeros(pos.shape, jnp.int32)
    for k in range(count):
        found = found + (pos >= ends_ref[k]).astype(jnp.int32)
    return jnp.where(pos < 0, -1, found)


def exact(left, right):
    return jnp.dot(left, right, precision=lax.Precision.HIGHEST, preferred_element_type=F32)


def silu(values):
    return values / (1.0 + jnp.exp(-values))


def softplus(values):
    return jnp.maximum(values, 0.0) + jnp.log1p(jnp.exp(-jnp.abs(values)))


class Block:
    def __init__(self, i, pre, ext, z, taps_ref, rows_ref, ends_ref, count, state, C):
        n = BLOCK
        pos = i * n + lax.broadcasted_iota(jnp.int32, (n, 1), 0)
        pos_row = i * n + lax.broadcasted_iota(jnp.int32, (1, n), 1)
        seg, seg_row = seg_of(pos, ends_ref, count), seg_of(pos_row, ends_ref, count)
        self.joined = {k: ((pos >= k) & (seg_of(pos - k, ends_ref, count) == seg)).astype(F32) for k in (1, 2, 3)}
        self.later = {k: (seg_of(pos + k, ends_ref, count) == seg).astype(F32) for k in (1, 2, 3)}
        conv = taps_ref[3:4, :] * pre
        for k in (1, 2, 3):
            conv = conv + taps_ref[3 - k : 4 - k, :] * ext[8 - k : 8 - k + n, :] * self.joined[k]
        act = silu(conv)
        cp = act.shape[1] - 2 * state
        self.conv = conv
        self.x, self.b, self.c = act[:, :cp], act[:, cp : cp + state].astype(B16), act[:, cp + state :].astype(B16)
        self.m = [rows_ref[j : j + 1, :] for j in range(2)]
        self.skip, self.gain = rows_ref[2:3, :], rows_ref[3:4, :]
        self.C = C
        self.dtr = z + rows_ref[4:5, :]
        self.dt = softplus(self.dtr)
        self.decay = rows_ref[5:6, :]
        self.rate = -self.dt * self.decay
        row, col = lax.broadcasted_iota(jnp.int32, (n, n), 0), lax.broadcasted_iota(jnp.int32, (n, n), 1)
        lower = row >= col
        self.row, self.col = row, col
        logdec = exact(lower.astype(F32), self.rate)
        log_row = logdec.T
        linked = lower & (seg == seg_row)
        self.decays = [
            jnp.exp(jnp.where(linked, logdec[:, C + j : C + j + 1] - log_row[C + j : C + j + 1, :], -1e30)) for j in range(2)
        ]
        scores = mm(self.c, self.b, NT)
        self.mats = [(scores * d).astype(B16) for d in self.decays]
        before = jnp.where(i == 0, -1, seg_of(jnp.full((1, 1), i * n - 1, jnp.int32), ends_ref, count))
        final = seg_of(jnp.full((1, 1), i * n + n - 1, jnp.int32), ends_ref, count)
        last = logdec[n - 1 : n, :]
        self.carry = self.spread(jnp.where(seg == before, jnp.exp(logdec), 0.0))
        self.tail = self.spread(jnp.where(seg == final, jnp.exp(last - logdec), 0.0))
        self.keep = self.spread(jnp.where(final == before, jnp.exp(last), 0.0))
        self.dtc = self.spread(self.dt)
        self.xt = (self.dtc * self.x).astype(B16)
        self.low = [m.astype(B16) for m in self.m]
        self.xts = [self.xt * low for low in self.low]
        self.tail_xt = (self.tail * self.xt.astype(F32)).astype(B16)

    def spread(self, values):
        return values[:, self.C : self.C + 1] * self.m[0] + values[:, self.C + 1 : self.C + 2] * self.m[1]

    def inner(self):
        return mm(self.mats[0], self.xts[0]) + mm(self.mats[1], self.xts[1])


def mixer_forward_kernel(
    count, state, C, ends_ref, in_ref, w_ref, taps_ref, rows_ref, out_w_ref,
    pre_ref, z_ref, y_ref, st_ref, part_ref, held, ext,
):
    i = pl.program_id(0)
    depth = w_ref.shape[0]
    n, cp = BLOCK, z_ref.shape[1]

    @pl.when(i == 0)
    def _():
        held[...] = jnp.zeros_like(held)
        ext[0:8, :] = jnp.zeros((8, ext.shape[1]), F32)

    made = mm(in_ref[:, :depth], w_ref[...])
    z = made[:, :cp]
    pre = made[:, cp:]
    z_ref[...], pre_ref[...] = z, pre
    ext[8 : 8 + n, :] = pre
    blk = Block(i, pre, ext, z, taps_ref, rows_ref, ends_ref, count, state, C)
    ext[0:8, :] = pre[n - 8 :, :]
    st = held[...]
    st_ref[0] = st
    y = blk.inner() + blk.carry * mm(blk.c, st.astype(B16))
    held[...] = blk.keep * st + mm(blk.b, blk.tail_xt, TN)
    y = y + blk.skip * blk.x
    y_ref[...] = y
    gated = y * silu(z)
    part_ref[:, :depth] = mm((gated * blk.gain).astype(B16), out_w_ref[...]).astype(B16)
    high, rest = hi_lo(jnp.sum(gated * gated, axis=1, keepdims=True))
    lane = lax.broadcasted_iota(jnp.int32, (n, LANES), 1)
    part_ref[:, depth:] = jnp.where(lane == 0, high.astype(F32), jnp.where(lane == 1, rest.astype(F32), 0.0)).astype(B16)


def whole(shape):
    return pl.BlockSpec(shape, lambda i: (0,) * len(shape))


def params():
    return pltpu.CompilerParams(dimension_semantics=("arbitrary",), vmem_limit_bytes=60 * 1024 * 1024)


def mixer_forward(ends, gathered, in_w, taps, rows, out_w, state, C):
    T, depth = gathered.shape[0], in_w.shape[0]
    cp, nb = out_w.shape[0], gathered.shape[0] // BLOCK
    conv_width = cp + 2 * state

    def block(width):
        return pl.BlockSpec((BLOCK, width), lambda i: (i, 0))

    return pl.pallas_call(
        functools.partial(mixer_forward_kernel, ends.shape[0], state, C),
        grid=(nb,),
        in_specs=[
            pl.BlockSpec(memory_space=pltpu.SMEM), block(gathered.shape[1]), whole(in_w.shape), whole(taps.shape),
            whole(rows.shape), whole(out_w.shape),
        ],
        out_specs=[
            block(conv_width), block(cp), block(cp),
            pl.BlockSpec((1, state, cp), lambda i: (i, 0, 0)), block(depth + LANES),
        ],
        out_shape=[
            jax.ShapeDtypeStruct((T, conv_width), F32),
            jax.ShapeDtypeStruct((T, cp), F32),
            jax.ShapeDtypeStruct((T, cp), F32),
            jax.ShapeDtypeStruct((nb, state, cp), F32),
            jax.ShapeDtypeStruct((T, depth + LANES), B16),
        ],
        scratch_shapes=[pltpu.VMEM((state, cp), F32), pltpu.VMEM((BLOCK + 8, conv_width), F32)],
        compiler_params=params(),
    )(ends, gathered, in_w, taps, rows, out_w)


def mixer_backward_kernel(
    count, state, C, ends_ref, three_ref, one_ref, pre_ref, halo_ref, z_ref, y_ref, st_ref,
    w_ref, taps_ref, rows_ref, cols_ref, out_w_ref,
    part_ref, gzx_ref, gbc_ref, gout_ref, gtaps_ref, gvec_ref, held, ext, gext, gw_ref,
):
    step = pl.program_id(0)
    i = pl.num_programs(0) - 1 - step
    depth = w_ref.shape[0]
    n, cp = BLOCK, z_ref.shape[1]

    @pl.when(step == 0)
    def _():
        held[...] = jnp.zeros_like(held)
        gext[n : n + 8, :] = jnp.zeros((8, gext.shape[1]), F32)
        gw_ref[...] = jnp.zeros_like(gw_ref)
        gout_ref[...] = jnp.zeros_like(gout_ref)
        gtaps_ref[...] = jnp.zeros_like(gtaps_ref)
        gvec_ref[...] = jnp.zeros_like(gvec_ref)

    pre, z, y = pre_ref[...], z_ref[...], y_ref[...]
    ext[0:8, :] = jnp.where(i == 0, 0.0, halo_ref[...])
    ext[8 : 8 + n, :] = pre
    blk = Block(i, pre, ext, z, taps_ref, rows_ref, ends_ref, count, state, C)
    three = three_ref[:, :depth]
    pg = mm(three, out_w_ref[...], NT)
    cross = jnp.sum(three_ref[:, depth:].astype(F32), axis=1, keepdims=True)
    act_z = silu(z)
    gated = y * act_z
    gout_ref[...] += mm((gated * blk.gain).astype(B16), three, TN)
    grad_gated = pg * blk.gain - gated * cross
    gy = grad_gated * act_z
    gz = grad_gated * y * silu_grad(z)
    st = st_ref[0]
    st_low, grad = st.astype(B16), held[...]
    grad_low = grad.astype(B16)
    gy_low = gy.astype(B16)
    y_all = blk.inner() + blk.carry * mm(blk.c, st_low)
    back = sum(mm(blk.mats[j], gy_low * blk.low[j], TN) for j in range(2))
    gate = (blk.carry * gy_low.astype(F32)).astype(B16)
    tail_back = blk.tail * mm(blk.b, grad_low)
    pull = sum(mm(gy_low, blk.xts[j], NT) * blk.decays[j] for j in range(2)).astype(B16)
    g_c = mm(pull, blk.b) + mm(gate, st_low, NT)
    g_b = mm(pull, blk.c, TN) + mm(blk.tail_xt, grad_low, NT)
    held[...] = blk.keep * grad + mm(blk.c, gate, TN)
    g_xt = back + tail_back
    xt = blk.xt.astype(F32)
    cols = cols_ref[...]
    after = exact(gy_low.astype(F32) * y_all - xt * back, cols)
    used = exact(xt * tail_back, cols)
    through = exact(jnp.broadcast_to(blk.keep * jnp.sum(grad * st, axis=0, keepdims=True), (8, cp)), cols)[0:1, :]
    g_rate = (
        exact((blk.row <= blk.col).astype(F32), after) + exact((blk.row > blk.col).astype(F32), used) + through
    )
    g_dt = exact(g_xt * blk.x, cols) - g_rate * blk.decay
    g_dtr = g_dt / (1.0 + jnp.exp(-blk.dtr))
    g_x = g_xt * blk.dtc + blk.skip * gy
    for r, v in enumerate((pg * gated, g_dtr, g_rate * blk.rate, gy * blk.x)):
        gvec_ref[r : r + 1, :] += jnp.sum(v, axis=0, keepdims=True)
    gconv = jnp.concatenate([g_x, g_b, g_c], axis=1) * silu_grad(blk.conv)
    gext[0:n, :] = gconv
    gpre = taps_ref[3:4, :] * gconv
    gtaps_ref[3:4, :] += jnp.sum(gconv * pre, axis=0, keepdims=True)
    for k in (1, 2, 3):
        gpre = gpre + taps_ref[3 - k : 4 - k, :] * gext[k : n + k, :] * blk.later[k]
        gtaps_ref[3 - k : 4 - k, :] += jnp.sum(gconv * ext[8 - k : 8 - k + n, :] * blk.joined[k], axis=0, keepdims=True)
    gext[n : n + 8, :] = gconv[0:8, :]
    made = jnp.concatenate([gz + g_dtr, gpre], axis=1).astype(B16)
    part_ref[...] = mm(made, w_ref[...], NT).astype(B16)
    gw_ref[...] += mm(one_ref[:, :depth], made, TN)

    @pl.when(i == 0)
    def _():
        gzx_ref[...] = gw_ref[:, : 2 * cp].astype(B16)
        gbc_ref[...] = gw_ref[:, 2 * cp :].astype(B16)


def mixer_backward(ends, three, one, pre, z, y, states, in_w, taps, rows, cols, out_w, state, C):
    T, depth = three.shape[0], in_w.shape[0]
    cp, nb = out_w.shape[0], T // BLOCK
    conv_width = cp + 2 * state

    def block(width):
        return pl.BlockSpec((BLOCK, width), lambda k: (nb - 1 - k, 0))

    def halo(k):
        return (jnp.maximum((nb - 1 - k) * (BLOCK // 8) - 1, 0), 0)

    return pl.pallas_call(
        functools.partial(mixer_backward_kernel, ends.shape[0], state, C),
        grid=(nb,),
        in_specs=[
            pl.BlockSpec(memory_space=pltpu.SMEM), block(three.shape[1]), block(one.shape[1]), block(conv_width),
            pl.BlockSpec((8, conv_width), halo), block(cp), block(cp),
            pl.BlockSpec((1, state, cp), lambda k: (nb - 1 - k, 0, 0)),
            whole(in_w.shape), whole(taps.shape), whole(rows.shape), whole(cols.shape), whole(out_w.shape),
        ],
        out_specs=[
            block(depth), whole((depth, 2 * cp)), whole((depth, 2 * state)), whole(out_w.shape), whole((8, conv_width)),
            whole((8, cp)),
        ],
        out_shape=[
            jax.ShapeDtypeStruct((T, depth), B16),
            jax.ShapeDtypeStruct((depth, 2 * cp), B16),
            jax.ShapeDtypeStruct((depth, 2 * state), B16),
            jax.ShapeDtypeStruct(out_w.shape, F32),
            jax.ShapeDtypeStruct((8, conv_width), F32),
            jax.ShapeDtypeStruct((8, cp), F32),
        ],
        scratch_shapes=[
            pltpu.VMEM((state, cp), F32),
            pltpu.VMEM((BLOCK + 8, conv_width), F32),
            pltpu.VMEM((BLOCK + 8, conv_width), F32),
            pltpu.VMEM(in_w.shape, F32),
        ],
        compiler_params=params(),
    )(ends, three, one, pre, pre, z, y, states, in_w, taps, rows, cols, out_w)


def expert_kernel(
    F, two_ref, grad_ref, named_ref, up_ref, down_ref, mine_ref,
    out_ref, part_ref, probs_ref, gup_ref, gdown_ref,
):
    depth = two_ref.shape[1]

    @pl.when(pl.program_id(0) == 0)
    def _():
        gup_ref[...] = jnp.zeros_like(gup_ref)
        gdown_ref[...] = jnp.zeros_like(gdown_ref)

    two, grad = two_ref[...], grad_ref[...]
    mid = mm(two, up_ref[...])
    back = mm(grad, down_ref[...], NT)
    gate, lin = mid[:, :F], mid[:, F : 2 * F]
    s_gate, s_lin = mid[:, 2 * F : 2 * F + LANES], mid[:, 2 * F + LANES :]
    named = named_ref[...].astype(F32) > 0
    logits = jnp.where(named, s_gate, -1e30)
    odds = jnp.where(named, jnp.exp(logits - jnp.max(logits, axis=1, keepdims=True)), 0.0)
    probs = odds / jnp.sum(odds, axis=1, keepdims=True)
    probs_ref[...] = probs
    mine = mine_ref[...]
    weight = jnp.sum(probs * mine, axis=1, keepdims=True)
    s_back, back = back[:, F:], back[:, :F]
    act_gate, act_s = silu(gate), silu(s_gate)
    acting = act_gate * lin
    gp = jnp.sum(acting * back, axis=1, keepdims=True)
    back = weight * back
    down_in = jnp.concatenate([weight * acting, act_s * s_lin], axis=1).astype(B16)
    mid_grad = jnp.concatenate(
        [back * lin * silu_grad(gate), back * act_gate, s_back * s_lin * silu_grad(s_gate), s_back * act_s], axis=1
    ).astype(B16)
    out_ref[...] = mm(down_in, down_ref[...]).astype(B16)
    part_ref[:, :depth] = mm(mid_grad, up_ref[...], NT).astype(B16)
    part_ref[:, depth:] = (gp * mine).astype(B16)
    gup_ref[...] += mm(two, mid_grad, TN)
    gdown_ref[...] += mm(down_in, grad, TN)


def experts(two, all_grad, gathered, up_w, down_w, mine, F):
    T, depth = two.shape

    def block(width):
        return pl.BlockSpec((BLOCK, width), lambda i: (i, 0))

    return pl.pallas_call(
        functools.partial(expert_kernel, F),
        grid=(T // BLOCK,),
        in_specs=[
            block(depth), block(depth), pl.BlockSpec((BLOCK, LANES), lambda i: (i, depth // LANES)),
            whole(up_w.shape), whole(down_w.shape), whole(mine.shape),
        ],
        out_specs=[block(depth), block(depth + LANES), block(LANES), whole(up_w.shape), whole(down_w.shape)],
        out_shape=[
            jax.ShapeDtypeStruct((T, depth), B16),
            jax.ShapeDtypeStruct((T, depth + LANES), B16),
            jax.ShapeDtypeStruct((T, LANES), F32),
            jax.ShapeDtypeStruct(up_w.shape, F32),
            jax.ShapeDtypeStruct(down_w.shape, F32),
        ],
        compiler_params=params(),
    )(two, all_grad, gathered, up_w, down_w, mine)


def local(
    hidden_in, norm1_gain, w_zx, w_bc, w_dt, conv_x, conv_bc, dt_bias, a_log, d_skip, gate_gain,
    w_out, norm2_gain, router, expert_up, expert_down, shared_up, shared_down, out_grad,
    seq_lengths, routes,
):
    S, H = lax.axis_size("seq"), lax.axis_size("head")
    N = S * H
    s = lax.axis_index("seq")
    g = s * H + lax.axis_index("head")
    R, D = hidden_in.shape
    heads, inner = dt_bias.shape[0], conv_x.shape[1]
    size = inner // heads
    state = w_bc.shape[1] // 2
    width = inner * H
    C = inner // S
    CP = -(-(C + 2) // LANES) * LANES
    E = N // 2
    F = expert_down.shape[1]
    FS = shared_down.shape[0] // N
    per = D // N

    all_grad = lax.all_gather(out_grad.astype(B16), ("seq", "head"), axis=0, tiled=True)
    named = jnp.sum(
        (routes[:, :, None] == jnp.arange(E, dtype=jnp.int32)[None, None, :]).astype(F32), axis=1
    )
    named = jnp.pad(named.astype(B16), ((0, 0), (FS, LANES - FS - E)))
    gain1, gain2 = norm1_gain[None], norm2_gain[None]
    gathered = first_rows(hidden_in, gain1, named, S, H)

    firsts = [min(k * C // size, heads - 2) for k in range(S)]
    first = jnp.minimum(s * C // size, heads - 2)
    channel = jnp.arange(CP)
    masks = jnp.stack(
        [((channel < C) & ((s * C + channel) // size - first == j)).astype(F32) for j in range(2)]
    )

    def mine(values, axis, offset, length):
        return lax.dynamic_slice_in_dim(values, offset, length, axis)

    def channels(values, axis):
        cut = mine(values, axis, s * C, C)
        pads = [(0, 0)] * values.ndim
        pads[axis] = (0, CP - C)
        return jnp.pad(cut, pads)

    def in_free(values):
        return jnp.pad(values, [(0, 0)] * (values.ndim - 1) + [(C, CP - C - 2)])

    in_w = jnp.concatenate(
        [
            mine(w_zx[:, 0], 1, s * C, C), pad_lanes(mine(w_dt, 1, first, 2), CP - C),
            channels(w_zx[:, 1], 1), w_bc,
        ],
        axis=1,
    )
    taps = jnp.concatenate([channels(conv_x, 1), conv_bc], axis=1)
    bias, alog, skip = (mine(v, 0, first, 2) for v in (dt_bias, a_log, d_skip))
    gain = channels(gate_gain, 0)
    out_w = channels(w_out, 0)
    rows = jnp.concatenate(
        [masks, (skip @ masks)[None], gain[None], in_free(jnp.stack([bias, jnp.exp(alog)]))], axis=0
    )
    rows = jnp.pad(rows, ((0, 2), (0, 0)))
    cols = in_free(masks.T)
    ends = jnp.cumsum(seq_lengths)

    pre, z, y, states, part = mixer_forward(ends, gathered, in_w, taps, rows, out_w, state, C)
    two, residual, mixed, inv_gate = second_rows(part, hidden_in, gain2, width, S, H)

    sup = mine(shared_up, 2, g * FS, FS)
    router_w = jnp.pad(router, ((0, 0), (FS, LANES - FS - E)))
    up_w = jnp.concatenate(
        [
            expert_up[0].reshape(D, 2 * F), sup[:, 0], router_w[:, FS:], pad_lanes(sup[:, 1], LANES),
        ],
        axis=1,
    )
    down_w = jnp.concatenate([expert_down[0], mine(shared_down, 0, g * FS, FS), jnp.zeros((LANES - FS, D), B16)], axis=0)
    is_mine = (jnp.arange(LANES) == FS + g // 2).astype(F32)[None]
    out_part, two_part, probs, grad_up_all, grad_down_all = experts(
        two, all_grad, gathered, up_w, down_w, is_mine, F
    )
    out_sum = lax.psum_scatter(out_part, ("seq", "head"), scatter_dimension=0, tiled=True)
    three, grad_res, norm2_part, router_part = third_rows(
        two_part, probs, residual, mixed, inv_gate, out_grad, gain2, router_w, width, S, H
    )
    grad_up = grad_up_all[:, : 2 * F].reshape(expert_up.shape)
    grad_down = grad_down_all[:F].reshape(expert_down.shape)

    one_part, grad_zx_w, grad_bc_w, grad_out_w, tap_part, vec_part = mixer_backward(
        ends, three, gathered, pre, z, y, states, in_w, taps, rows, cols, out_w, state, C
    )
    pieces = (
        norm2_part, tap_part[:4, CP:], tap_part[:4, :C], vec_part[0, :C], vec_part[1, C : C + 2],
        vec_part[2, C : C + 2], masks @ vec_part[3],
    )
    flat = jnp.concatenate([v.reshape(-1) for v in pieces])
    room = -(-flat.shape[0] // (8 * LANES)) * (8 * LANES)
    flat = jnp.pad(flat, (0, room - flat.shape[0])).reshape(8, room // 8)
    tall = -(-per // 16) * 16
    extra = jnp.concatenate([grad_bc_w, router_part], axis=1).reshape(N, per, 2 * state + LANES)
    extra = jnp.pad(extra, ((0, 0), (0, tall - per), (0, 0))).reshape(N * tall, 2 * state + LANES)
    s_up = jnp.concatenate([grad_up_all[:, 2 * F : 2 * F + FS], grad_up_all[:, 2 * F + LANES :][:, :FS]], axis=1)
    s_down = grad_down_all[F : F + FS].reshape(FS, N, per).transpose(1, 0, 2)
    grad_in, extra_sum, norm1_sum, zx_in, wo_in, su_in, sd_in, small = last_rows(
        one_part,
        extra,
        grad_zx_w.reshape(S, D // S, 2 * CP),
        grad_out_w[:C].reshape(C, S, D // S).transpose(1, 0, 2).astype(B16),
        s_up.astype(B16).reshape(N, per, 2 * FS),
        s_down.astype(B16),
        flat, hidden_in, grad_res, gain1, S, H,
    )
    output = residual + out_sum.astype(F32)
    grad_norm1 = norm1_sum.reshape(-1)[:D]
    grad_bc, grad_router = extra_sum[:per, : 2 * state], extra_sum[:per, 2 * state :][:, FS : FS + E]
    zx_in = zx_in.astype(F32)
    grad_zx = jnp.stack([zx_in[:, :, :C], zx_in[:, :, CP : CP + C]], axis=2)
    grad_zx = grad_zx.transpose(1, 2, 0, 3).reshape(D // S, 2, inner)
    grad_w_dt = sum(
        jnp.pad(zx_in[k, :, C : C + 2], ((0, 0), (firsts[k], heads - 2 - firsts[k]))) for k in range(S)
    )
    grad_w_out = wo_in.reshape(inner, D // S).astype(F32)
    grad_shared_up = su_in.reshape(N, per, 2, FS).transpose(1, 2, 0, 3).reshape(per, 2, N * FS).astype(F32)
    grad_shared_down = sd_in.reshape(N * FS, per).astype(F32)

    small = small.reshape(N, room)
    at, found = 0, []
    for v in pieces:
        found.append(small[:, at : at + v.size].reshape((S, H) + v.shape))
        at += v.size
    grad_norm2, grad_conv_bc = found[0].sum((0, 1)).reshape(D), found[1].sum((0, 1))
    grad_conv_x = found[2].transpose(2, 1, 0, 3).reshape(4, width)
    grad_gate_gain = found[3].transpose(1, 0, 2).reshape(width)

    def by_head(v):
        return sum(
            jnp.pad(v[k], ((0, 0), (firsts[k], heads - 2 - firsts[k]))) for k in range(S)
        ).reshape(-1)

    grad_dt_bias, grad_a_log, grad_d_skip = (by_head(v) for v in found[4:])
    return (
        output, grad_in, grad_norm1, grad_zx, grad_bc, grad_w_dt, grad_conv_x, grad_conv_bc, grad_dt_bias,
        grad_a_log, grad_d_skip, grad_gate_gain, grad_w_out, grad_norm2, grad_router, grad_up, grad_down,
        grad_shared_up, grad_shared_down,
    )


def solution(mesh):
    return jax.shard_map(
        local,
        mesh=mesh,
        in_specs=(
            P(("seq", "head"), None),
            P(),
            P(None, None, "head"),
            P(),
            P(None, "head"),
            P(None, "head"),
            P(),
            P("head"),
            P("head"),
            P("head"),
            P("head"),
            P("head", None),
            P(),
            P(),
            P(("seq", "head"), None, None, None),
            P(("seq", "head"), None, None),
            P(),
            P(),
            P(("seq", "head"), None),
            P(),
            P(("seq", "head"), None),
        ),
        out_specs=(
            P(("seq", "head"), None),
            P(("seq", "head"), None),
            P(),
            P("seq", None, "head"),
            P(("seq", "head"), None),
            P("seq", "head"),
            P(),
            P(),
            P(),
            P(),
            P(),
            P(),
            P("head", "seq"),
            P(),
            P(("seq", "head"), None),
            P(("seq", "head"), None, None, None),
            P(("seq", "head"), None, None),
            P(("seq", "head"), None, None),
            P(None, ("seq", "head")),
        ),
        check_vma=False,
    )
```

```python
import functools
import jax
import jax.numpy as jnp
from jax import lax
from jax.experimental import pallas as pl
from jax.experimental.pallas import tpu as pltpu
from jax.sharding import PartitionSpec as P

MESH = pl.DeviceIdType.MESH
BLOCK = 256
EPS = 1e-05
LANES = 128
B16 = jnp.bfloat16
F32 = jnp.float32


def mm(left, right, dims=(((1,), (0,)), ((), ()))):
    return lax.dot_general(left, right, dims, preferred_element_type=F32)


NT = (((1,), (1,)), ((), ()))
TN = (((0,), (0,)), ((), ()))


def inverse_rms(values):
    return lax.rsqrt(jnp.mean(values * values, axis=-1, keepdims=True) + EPS)


def rms_back(values, inverse, gain, grad):
    weighted = grad * gain
    inner = jnp.mean(weighted * values, axis=-1, keepdims=True)
    return inverse * weighted - values * inverse**3 * inner


def silu_grad(values):
    sig = jax.nn.sigmoid(values)
    return sig * (1.0 + values * (1.0 - sig))


def pad_lanes(values, width):
    return jnp.pad(values, [(0, 0)] * (values.ndim - 1) + [(0, width - values.shape[-1])])


def hi_lo(values):
    high = values.astype(B16)
    return high, (values - high.astype(F32)).astype(B16)


def sizes(seq_size, head_size):
    return head_size // 2, head_size // 2, seq_size // (head_size // 2)


class Place:
    def __init__(self, seq_size, head_size):
        self.H = head_size
        self.X, self.Y, self.Z = sizes(seq_size, head_size)
        assert self.Z == 4
        seq, head = lax.axis_index("seq"), lax.axis_index("head")
        self.z, self.y = seq // self.Y, seq % self.Y
        self.x, self.c = head // 2, head % 2
        z = self.z
        self.partners = (z, z + 1 - 2 * (z % 2), (z + 2) % 4, 3 - z)

    def at(self, dz=0, dy=0, dx=0, dc=0):
        return (
            self.partners[dz],
            (self.y + dy) % self.Y if dy else self.y,
            (self.x + dx) % self.X if dx else self.x,
            1 - self.c if dc else self.c,
        )

    def dev(self, **where):
        z, y, x, c = self.at(**where)
        return (z * self.Y + y, x * 2 + c)

    def slot(self, **where):
        z, y, x, c = self.at(**where)
        return (z * self.Y + y) * self.H + x * 2 + c

    def peers(self):
        out = [self.dev(dz=1), self.dev(dz=2)]
        out += [self.dev(dy=k) for k in range(1, self.Y)]
        out += [self.dev(dx=k) for k in range(1, self.X)]
        return out + [self.dev(dc=1)]


def greet(peers):
    barrier = pltpu.get_barrier_semaphore()
    for peer in peers:
        pl.semaphore_signal(barrier, inc=1, device_id=peer, device_id_type=MESH)
    pl.semaphore_wait(barrier, len(peers))


class Mail:
    def __init__(self, send, recv):
        self.send, self.recv, self.made = send, recv, []

    def copy(self, src, dst, dev):
        i = len(self.made)
        self.made.append(
            pltpu.make_async_remote_copy(
                src_ref=src, dst_ref=dst, send_sem=self.send.at[i], recv_sem=self.recv.at[i],
                device_id=dev, device_id_type=MESH,
            )
        )
        return self.made[-1]

    def finish(self, count):
        assert len(self.made) == count
        for copy in self.made:
            copy.wait_send()


class Script(list):
    def stage(self):
        self.append([])

    def do(self, action):
        self[-1].append(action)

    def run(self, first=0, last=None):
        for stage in self[first:last]:
            for action in stage:
                action()


def gather_count(S, H):
    X, Y, Z = sizes(S, H)
    return (Z - 1) + 2 * Z * (X + Y - 2) + 2 * Z * (X - 1) * (Y - 1) + X * Y * Z


def gather(pc, mail, x_ref, out_ref, own_sem):
    X, Y, Z = pc.X, pc.Y, pc.Z
    R = x_ref.shape[0]
    half = R // 2
    script = Script()

    def rows(part, **where):
        base = pl.multiple_of(pc.slot(**where) * R, R)
        if part is None:
            return out_ref.at[pl.ds(base, R)]
        return out_ref.at[pl.ds(pl.multiple_of(base + part * half, half), half)]

    def send(src, dst, dev):
        copy = mail.copy(src, dst, dev)
        script.do(copy.start)
        return copy

    x_in, y_in, dga, dgb, sib = {}, {}, {}, {}, []

    def column(dz):
        for part in (0, 1):
            src = x_ref.at[pl.ds(part * half, half)] if dz == 0 else rows(part, dz=dz)
            for k in range(1, X):
                x_in[dz, k, part] = send(src, rows(part, dz=dz), pc.dev(dx=k))
            other = 1 - part
            src = x_ref.at[pl.ds(other * half, half)] if dz == 0 else rows(other, dz=dz)
            for k in range(1, Y):
                y_in[dz, k, other] = send(src, rows(other, dz=dz), pc.dev(dy=k))
        src = x_ref if dz == 0 else rows(None, dz=dz)
        sib.append(send(src, rows(None, dz=dz), pc.dev(dc=1)))

    def onward(dz):
        for k in range(1, X):
            script.do(x_in[dz, k, 0].wait_recv)
            block = rows(0, dz=dz, dx=-k)
            for m in range(1, Y):
                dga[dz, k, m] = send(block, block, pc.dev(dy=m))
        for k in range(1, Y):
            script.do(y_in[dz, k, 1].wait_recv)
            block = rows(1, dz=dz, dy=-k)
            for m in range(1, X):
                dgb[dz, k, m] = send(block, block, pc.dev(dx=m))
        for k in range(1, X):
            script.do(x_in[dz, k, 1].wait_recv)
            block = rows(None, dz=dz, dx=-k)
            sib.append(send(block, block, pc.dev(dc=1)))
        for k in range(1, Y):
            script.do(y_in[dz, k, 0].wait_recv)
            block = rows(None, dz=dz, dy=-k)
            sib.append(send(block, block, pc.dev(dc=1)))

    def corner(dz):
        for k in range(1, X):
            for m in range(1, Y):
                script.do(dga[dz, k, m].wait_recv)
                script.do(dgb[dz, m, k].wait_recv)
                block = rows(None, dz=dz, dx=-k, dy=-m)
                sib.append(send(block, block, pc.dev(dc=1)))

    own = pltpu.make_async_copy(x_ref, rows(None), own_sem)
    script.stage()
    script.do(own.start)
    first = send(x_ref, rows(None), pc.dev(dz=1))
    column(0)
    second = send(x_ref, rows(None), pc.dev(dz=2))
    script.stage()
    script.do(first.wait_recv)
    column(1)
    script.stage()
    onward(0)
    script.stage()
    script.do(second.wait_recv)
    third = send(rows(None, dz=2), rows(None, dz=2), pc.dev(dz=1))
    column(2)
    corner(0)
    script.stage()
    onward(1)
    script.stage()
    script.do(third.wait_recv)
    column(3)
    corner(1)
    script.stage()
    onward(2)
    corner(2)
    script.stage()
    onward(3)
    corner(3)
    for copy in sib:
        script.do(copy.wait_recv)
    script.do(own.wait)
    return script


def scatter_parts(split):
    return (("y", 0), ("x", 1)) if split else (("x", None),)


def scatter_count(S, H, splits=(True,)):
    X, Y, Z = sizes(S, H)
    pieces = sum(len(scatter_parts(split)) for split in splits)
    return len(splits) * (Z + Z - 1) + pieces * Z * (X + Y - 2)


def scatter_scratch(S, H, R, W, split=True):
    X, Y, Z = sizes(S, H)
    out = [pltpu.VMEM((Z, Y, X, R, W), B16), pltpu.VMEM((Z, Y, X, R, W), B16), pltpu.VMEM((Z - 1, R, W), B16)]
    for axis, part in scatter_parts(split):
        rows = R if part is None else R // 2
        first, second = (Y, X) if axis == "y" else (X, Y)
        out += [pltpu.VMEM((Z, first - 1, second, rows, W), B16), pltpu.VMEM((Z, second - 1, rows, W), B16)]
    return out + [pltpu.SemaphoreType.DMA((Z,))]


def accumulate(dst, srcs, rows):
    def action():
        def body(i, carry):
            at = pl.ds(pl.multiple_of(i * 16, 16), 16)
            total = dst.at[at][...].astype(F32)
            for src in srcs:
                total = total + src.at[at][...].astype(F32)
            dst.at[at][...] = total.astype(dst.dtype)
            return carry

        lax.fori_loop(0, rows // 16, body, 0)

    return action


ORDER = (3, 2, 1, 0)


def scatter(pc, mail, jobs):
    X, Y, Z = pc.X, pc.Y, pc.Z
    script = Script()
    own, sib, one, two, zs = {}, {}, {}, {}, {}

    def send(src, dst, dev):
        copy = mail.copy(src, dst, dev)
        script.do(copy.start)
        return copy

    def pieces(o):
        p_ref, total, scratch, split = jobs[o]
        R = p_ref.shape[4]
        for j, (axis, part) in enumerate(scatter_parts(split)):
            rows, size = (pl.ds(0, R), R) if part is None else (pl.ds(part * (R // 2), R // 2), R // 2)
            yield j, axis, rows, size, scratch[3 + 2 * j], scratch[4 + 2 * j]

    def cores(dz):
        for o, (p_ref, total, scratch, split) in enumerate(jobs):
            t0, r0 = scratch[0], scratch[1]
            script.do(own[o, dz].wait)
            script.do(sib[o, dz].wait_recv)
            for yy in range(Y):
                for xx in range(X):
                    script.do(accumulate(t0.at[dz, yy, xx], [r0.at[dz, yy, xx]], p_ref.shape[4]))
            for j, axis, rows, size, r1, r2 in pieces(o):
                for k in range(1, Y if axis == "y" else X):
                    if axis == "y":
                        src, dev = t0.at[dz, pc.at(dy=k)[1], :, rows], pc.dev(dy=k)
                    else:
                        src, dev = t0.at[dz, :, pc.at(dx=k)[2], rows], pc.dev(dx=k)
                    one[o, dz, j, k] = send(src, r1.at[dz, k - 1], dev)

    def firsts(dz):
        for o, (p_ref, total, scratch, split) in enumerate(jobs):
            t0 = scratch[0]
            for j, axis, rows, size, r1, r2 in pieces(o):
                steps = range(1, Y if axis == "y" else X)
                for k in steps:
                    script.do(one[o, dz, j, k].wait_recv)
                for m in range(X if axis == "y" else Y):
                    dst = t0.at[dz, pc.y, m, rows] if axis == "y" else t0.at[dz, m, pc.x, rows]
                    script.do(accumulate(dst, [r1.at[dz, k - 1, m] for k in steps], size))
                for k in range(1, X if axis == "y" else Y):
                    if axis == "y":
                        src, dev = t0.at[dz, pc.y, pc.at(dx=k)[2], rows], pc.dev(dx=k)
                    else:
                        src, dev = t0.at[dz, pc.at(dy=k)[1], pc.x, rows], pc.dev(dy=k)
                    two[o, dz, j, k] = send(src, r2.at[dz, k - 1], dev)

    def seconds(dz):
        for o, (p_ref, total, scratch, split) in enumerate(jobs):
            mine = scratch[0].at[dz, pc.y, pc.x]
            for j, axis, rows, size, r1, r2 in pieces(o):
                steps = range(1, X if axis == "y" else Y)
                for k in steps:
                    script.do(two[o, dz, j, k].wait_recv)
                script.do(accumulate(mine.at[rows], [r2.at[dz, k - 1] for k in steps], size))
            if dz == 2:
                script.do(zs[o, 3].wait_recv)
                script.do(accumulate(mine, [scratch[2].at[0]], p_ref.shape[4]))
            if dz:
                zs[o, dz] = send(mine, scratch[2].at[3 - dz], pc.dev(dz=2 if dz == 2 else 1))

    def last(p_ref, total, scratch):
        def body(i, carry):
            at = pl.ds(pl.multiple_of(i * 16, 16), 16)
            value = scratch[0].at[0, pc.y, pc.x, at][...].astype(F32)
            for k in (1, 2):
                value = value + scratch[2].at[k, at][...].astype(F32)
            total.at[at][...] = value
            return carry

        return lambda: lax.fori_loop(0, p_ref.shape[4] // 16, body, 0)

    script.stage()
    for o, (p_ref, total, scratch, split) in enumerate(jobs):
        for dz in ORDER:
            own[o, dz] = pltpu.make_async_copy(
                p_ref.at[pc.at(dz=dz)[0], :, :, pc.c], scratch[0].at[dz], scratch[-1].at[dz]
            )
            script.do(own[o, dz].start)
    script.stage()
    for dz in ORDER:
        for o, (p_ref, total, scratch, split) in enumerate(jobs):
            sib[o, dz] = send(p_ref.at[pc.at(dz=dz)[0], :, :, 1 - pc.c], scratch[1].at[dz], pc.dev(dc=1))
    script.stage()
    cores(3)
    cores(2)
    script.stage()
    cores(1)
    cores(0)
    script.stage()
    firsts(3)
    script.stage()
    firsts(2)
    seconds(3)
    script.stage()
    firsts(1)
    seconds(2)
    script.stage()
    firsts(0)
    seconds(1)
    script.stage()
    seconds(0)
    for o, (p_ref, total, scratch, split) in enumerate(jobs):
        for dz in (2, 1):
            script.do(zs[o, dz].wait_recv)
        script.do(last(p_ref, total, scratch))
    return script


ANY = pl.BlockSpec(memory_space=pl.ANY)
VMEM = pl.BlockSpec(memory_space=pltpu.VMEM)


def sems(count):
    return [pltpu.SemaphoreType.DMA((count,)), pltpu.SemaphoreType.DMA((count,))]


def talking(cid):
    return pltpu.CompilerParams(collective_id=cid, has_side_effects=True, vmem_limit_bytes=58 * 1024 * 1024)


def blocks(part, S, H):
    X, Y, Z = sizes(S, H)
    return part.reshape(Z, Y, X, 2, part.shape[0] // (S * H), part.shape[1])


def first_kernel(S, H, in_ref, gain_ref, named_ref, out_ref, rows, send, recv, own_sem):
    pc = Place(S, H)
    D = in_ref.shape[1]
    values = in_ref[...]
    rows[:, :D] = (values * inverse_rms(values) * gain_ref[...]).astype(B16)
    rows[:, D:] = named_ref[...]
    mail = Mail(send, recv)
    moves = gather(pc, mail, rows, out_ref, own_sem)
    greet(pc.peers())
    moves.run()
    mail.finish(gather_count(S, H))


def first_rows(hidden_in, gain, named, S, H):
    R, D = hidden_in.shape
    W = D + LANES
    return pl.pallas_call(
        functools.partial(first_kernel, S, H),
        out_shape=jax.ShapeDtypeStruct((S * H * R, W), B16),
        in_specs=[VMEM] * 3,
        out_specs=ANY,
        scratch_shapes=[pltpu.VMEM((R, W), B16), *sems(gather_count(S, H)), pltpu.SemaphoreType.DMA],
        compiler_params=talking(1),
    )(hidden_in, gain, named)


def second_kernel(S, H, width, p_ref, in_ref, gain_ref, out_ref, res_ref, mixed_ref, inv_ref, total, rows, *rest):
    scratch, (send, recv, own_sem) = rest[:-3], rest[-3:]
    pc = Place(S, H)
    D = in_ref.shape[1]
    mail = Mail(send, recv)
    sums = scatter(pc, mail, [(p_ref, total, scratch, True)])
    moves = gather(pc, mail, rows, out_ref, own_sem)
    sums.run(0, 1)
    greet(pc.peers())
    sums.run(1)
    mixed = total[:, :D]
    square = jnp.sum(total[:, D:], axis=1, keepdims=True)
    inv = lax.rsqrt(square / width + EPS)
    residual = in_ref[...] + inv * mixed
    rows[...] = (residual * inverse_rms(residual) * gain_ref[...]).astype(B16)
    moves.run(0, 1)
    mixed_ref[...] = mixed
    res_ref[...] = residual
    inv_ref[...] = jnp.broadcast_to(inv, inv_ref.shape)
    moves.run(1)
    mail.finish(scatter_count(S, H) + gather_count(S, H))


def second_rows(part, hidden_in, gain, width, S, H):
    R, D = hidden_in.shape
    count = scatter_count(S, H) + gather_count(S, H)
    return pl.pallas_call(
        functools.partial(second_kernel, S, H, width),
        out_shape=[
            jax.ShapeDtypeStruct((S * H * R, D), B16),
            jax.ShapeDtypeStruct((R, D), F32),
            jax.ShapeDtypeStruct((R, D), F32),
            jax.ShapeDtypeStruct((R, LANES), F32),
        ],
        in_specs=[ANY, VMEM, VMEM],
        out_specs=[ANY, VMEM, VMEM, VMEM],
        scratch_shapes=[
            pltpu.VMEM((R, D + LANES), F32), pltpu.VMEM((R, D), B16), *scatter_scratch(S, H, R, D + LANES),
            *sems(count), pltpu.SemaphoreType.DMA,
        ],
        compiler_params=talking(2),
    )(blocks(part, S, H), hidden_in, gain)


def third_kernel(
    S, H, width, p_ref, probs_ref, res_ref, mixed_ref, inv_ref, grad_ref, gain_ref, router_ref,
    out_ref, gres_ref, gnorm_ref, grouter_ref, total, rows, probs, *rest,
):
    scratch, (send, recv, own_sem, probs_sem) = rest[:-4], rest[-4:]
    pc = Place(S, H)
    R, D = res_ref.shape
    mail = Mail(send, recv)
    sums = scatter(pc, mail, [(p_ref, total, scratch, True)])
    moves = gather(pc, mail, rows, out_ref, own_sem)
    fetch = pltpu.make_async_copy(probs_ref.at[pl.ds(pl.multiple_of(pc.slot() * R, R), R)], probs, probs_sem)
    fetch.start()
    sums.run(0, 1)
    greet(pc.peers())
    sums.run(1)
    fetch.wait()
    p = probs[...]
    gp = total[:, D:]
    glogits = (p * (gp - jnp.sum(p * gp, axis=1, keepdims=True))).astype(B16)
    gtwo = total[:, :D] + mm(glogits, router_ref[...], NT)
    residual = res_ref[...]
    inv_two = inverse_rms(residual)
    gain = gain_ref[...]
    gres = grad_ref[...] + rms_back(residual, inv_two, gain, gtwo)
    inv = inv_ref[:, 0:1]
    cross = jnp.sum(gres * mixed_ref[...], axis=1, keepdims=True) * (inv * inv * inv) / width
    high, low = hi_lo(cross)
    lane = lax.broadcasted_iota(jnp.int32, (R, LANES), 1)
    rows[:, :D] = (inv * gres).astype(B16)
    rows[:, D:] = jnp.where(lane == 0, high.astype(F32), jnp.where(lane == 1, low.astype(F32), 0.0)).astype(B16)
    moves.run(0, 1)
    gres_ref[...] = gres
    gnorm_ref[...] = jnp.sum(gtwo * residual * inv_two, axis=0, keepdims=True)
    grouter_ref[...] = mm((residual * inv_two * gain).astype(B16), glogits, TN).astype(B16)
    moves.run(1)
    mail.finish(scatter_count(S, H) + gather_count(S, H))


def third_rows(part, probs, residual, mixed, inv_gate, out_grad, gain, router, width, S, H):
    R, D = residual.shape
    count = scatter_count(S, H) + gather_count(S, H)
    return pl.pallas_call(
        functools.partial(third_kernel, S, H, width),
        out_shape=[
            jax.ShapeDtypeStruct((S * H * R, D + LANES), B16),
            jax.ShapeDtypeStruct((R, D), F32),
            jax.ShapeDtypeStruct((1, D), F32),
            jax.ShapeDtypeStruct((D, LANES), B16),
        ],
        in_specs=[ANY, ANY] + [VMEM] * 6,
        out_specs=[ANY, VMEM, VMEM, VMEM],
        scratch_shapes=[
            pltpu.VMEM((R, D + LANES), F32), pltpu.VMEM((R, D + LANES), B16), pltpu.VMEM((R, LANES), F32),
            *scatter_scratch(S, H, R, D + LANES), *sems(count), pltpu.SemaphoreType.DMA, pltpu.SemaphoreType.DMA,
        ],
        compiler_params=talking(3),
    )(blocks(part, S, H), probs, residual, mixed, inv_gate, out_grad, gain, router)


def last_kernel(
    S, H, state, p_ref, e_ref, zx_ref, wo_ref, taps_ref, vec_ref, norms_ref, in_ref, gres_ref, gain_ref,
    gin_ref, extra_ref, sums_ref, each_ref, zx_out, wo_out, total, small, small_in, *rest,
):
    half = len(rest) - 6
    main, extra = rest[: half - 6], rest[half - 6 : half]
    send, recv, group_send, group_recv, local_sem, own_sem = rest[half:]
    pc = Place(S, H)
    seq, head = lax.axis_index("seq"), lax.axis_index("head")
    mail = Mail(send, recv)
    sums = scatter(pc, mail, [(p_ref, total, main, True), (e_ref, extra_ref, extra, False)])
    moves = gather(pc, mail, small, small_in, own_sem)
    group = []
    for m in range(1, S):
        to = (seq + m) % S
        for j, (src, dst) in enumerate(((zx_ref, zx_out), (wo_ref, wo_out))):
            group.append(
                pltpu.make_async_remote_copy(
                    src_ref=src.at[to], dst_ref=dst.at[seq], send_sem=group_send.at[j, m],
                    recv_sem=group_recv.at[j, m], device_id=(to, head), device_id_type=MESH,
                )
            )
    stay = [
        pltpu.make_async_copy(src.at[seq], dst.at[seq], local_sem.at[j])
        for j, (src, dst) in enumerate(((zx_ref, zx_out), (wo_ref, wo_out)))
    ]
    sums.run(0, 1)
    D = in_ref.shape[1]
    line = 0
    small[...] = jnp.zeros_like(small)
    for r in range(2):
        for j in range(D // LANES):
            small[line : line + 1, :] = norms_ref[r : r + 1, j * LANES : (j + 1) * LANES]
            line += 1
    wide = taps_ref.shape[1] - 2 * state
    for r in range(4):
        for j in range(2 * state // LANES):
            small[line : line + 1, :] = taps_ref[r : r + 1, wide + j * LANES : wide + (j + 1) * LANES]
            line += 1
    small[line : line + 4, :] = taps_ref[0:4, :wide]
    small[line + 4 : line + 8, :] = vec_ref[0:4, :]
    peers = pc.peers()
    barrier = pltpu.get_barrier_semaphore()
    for peer in peers:
        pl.semaphore_signal(barrier, inc=1, device_id=peer, device_id_type=MESH)
    for m in range(1, S):
        pl.semaphore_signal(barrier, inc=1, device_id=((seq + m) % S, head), device_id_type=MESH)
    pl.semaphore_wait(barrier, len(peers) + S - 1)
    sums.run(1, 3)
    moves.run(0, 1)
    for copy in stay + group:
        copy.start()
    sums.run(3, 4)
    moves.run(1, 2)
    for k in range(4, 9):
        sums.run(k, k + 1)
        if k < 8:
            moves.run(k - 2, k - 1)
    values, gone = in_ref[...], total[...]
    inv = inverse_rms(values)
    gin_ref[...] = gres_ref[...] + rms_back(values, inv, gain_ref[...], gone)
    moves.run(6)
    rows = small.shape[0]

    def add(k, value):
        return value + small_in[pl.ds(pl.multiple_of(k * rows, rows), line), :]

    sums_ref[...] = lax.fori_loop(0, S * H, add, jnp.zeros(sums_ref.shape, F32))
    for k in range(S * H):
        each_ref[k] = small_in[k * rows + line : k * rows + line + 8, :]
    for copy in group:
        copy.wait()
    for copy in stay:
        copy.wait()
    mail.finish(scatter_count(S, H, (True, False)) + gather_count(S, H))


def last_rows(part, extra, zx, wo, taps, vec, norms, hidden_in, grad_res, gain, state, S, H):
    R, D = hidden_in.shape
    N = S * H
    line = 2 * (D // LANES) + 4 * (2 * state // LANES)
    assert line % 8 == 0 and vec.shape[1] == LANES
    rows = -(-(line + 8) // 16) * 16
    tall = extra.shape[0] // N
    count = scatter_count(S, H, (True, False)) + gather_count(S, H)
    return pl.pallas_call(
        functools.partial(last_kernel, S, H, state),
        out_shape=[
            jax.ShapeDtypeStruct((R, D), F32),
            jax.ShapeDtypeStruct((tall, extra.shape[1]), F32),
            jax.ShapeDtypeStruct((line, LANES), F32),
            jax.ShapeDtypeStruct((N, 8, LANES), F32),
            jax.ShapeDtypeStruct(zx.shape, zx.dtype),
            jax.ShapeDtypeStruct(wo.shape, wo.dtype),
        ],
        in_specs=[ANY] * 4 + [VMEM] * 6,
        out_specs=[VMEM] * 4 + [ANY] * 2,
        scratch_shapes=[
            pltpu.VMEM((R, D), F32), pltpu.VMEM((rows, LANES), F32), pltpu.VMEM((N * rows, LANES), F32),
            *scatter_scratch(S, H, R, D), *scatter_scratch(S, H, tall, extra.shape[1], False), *sems(count),
            pltpu.SemaphoreType.DMA((2, S)), pltpu.SemaphoreType.DMA((2, S)), pltpu.SemaphoreType.DMA((2,)),
            pltpu.SemaphoreType.DMA,
        ],
        compiler_params=talking(4),
    )(blocks(part, S, H), blocks(extra, S, H), zx, wo, taps, vec, norms, hidden_in, grad_res, gain)


def seg_of(pos, ends_ref, count):
    found = jnp.zeros(pos.shape, jnp.int32)
    for k in range(count):
        found = found + (pos >= ends_ref[k]).astype(jnp.int32)
    return jnp.where(pos < 0, -1, found)


def exact(left, right):
    return jnp.dot(left, right, precision=lax.Precision.HIGHEST, preferred_element_type=F32)


def silu(values):
    return values / (1.0 + jnp.exp(-values))


def softplus(values):
    return jnp.maximum(values, 0.0) + jnp.log1p(jnp.exp(-jnp.abs(values)))


class Block:
    def __init__(self, i, pre, ext, z, taps_ref, rows_ref, ends_ref, count, state, C):
        n = BLOCK
        pos = i * n + lax.broadcasted_iota(jnp.int32, (n, 1), 0)
        pos_row = i * n + lax.broadcasted_iota(jnp.int32, (1, n), 1)
        seg, seg_row = seg_of(pos, ends_ref, count), seg_of(pos_row, ends_ref, count)
        self.joined = {k: ((pos >= k) & (seg_of(pos - k, ends_ref, count) == seg)).astype(F32) for k in (1, 2, 3)}
        self.later = {k: (seg_of(pos + k, ends_ref, count) == seg).astype(F32) for k in (1, 2, 3)}
        conv = taps_ref[3:4, :] * pre
        for k in (1, 2, 3):
            conv = conv + taps_ref[3 - k : 4 - k, :] * ext[8 - k : 8 - k + n, :] * self.joined[k]
        act = silu(conv)
        cp = act.shape[1] - 2 * state
        self.conv = conv
        self.x, self.b, self.c = act[:, :cp], act[:, cp : cp + state].astype(B16), act[:, cp + state :].astype(B16)
        self.m = [rows_ref[j : j + 1, :] for j in range(2)]
        self.skip, self.gain = rows_ref[2:3, :], rows_ref[3:4, :]
        self.C = C
        self.dtr = z + rows_ref[4:5, :]
        self.dt = softplus(self.dtr)
        self.decay = rows_ref[5:6, :]
        self.rate = -self.dt * self.decay
        row, col = lax.broadcasted_iota(jnp.int32, (n, n), 0), lax.broadcasted_iota(jnp.int32, (n, n), 1)
        lower = row >= col
        self.row, self.col = row, col
        logdec = exact(lower.astype(F32), self.rate)
        log_row = logdec.T
        linked = lower & (seg == seg_row)
        self.decays = [
            jnp.exp(jnp.where(linked, logdec[:, C + j : C + j + 1] - log_row[C + j : C + j + 1, :], -1e30)) for j in range(2)
        ]
        scores = mm(self.c, self.b, NT)
        self.mats = [(scores * d).astype(B16) for d in self.decays]
        before = jnp.where(i == 0, -1, seg_of(jnp.full((1, 1), i * n - 1, jnp.int32), ends_ref, count))
        final = seg_of(jnp.full((1, 1), i * n + n - 1, jnp.int32), ends_ref, count)
        last = logdec[n - 1 : n, :]
        self.carry = self.spread(jnp.where(seg == before, jnp.exp(logdec), 0.0))
        self.tail = self.spread(jnp.where(seg == final, jnp.exp(last - logdec), 0.0))
        self.keep = self.spread(jnp.where(final == before, jnp.exp(last), 0.0))
        self.dtc = self.spread(self.dt)
        self.xt = (self.dtc * self.x).astype(B16)
        self.low = [m.astype(B16) for m in self.m]
        self.xts = [self.xt * low for low in self.low]
        self.tail_xt = (self.tail * self.xt.astype(F32)).astype(B16)

    def spread(self, values):
        return values[:, self.C : self.C + 1] * self.m[0] + values[:, self.C + 1 : self.C + 2] * self.m[1]

    def inner(self):
        return mm(self.mats[0], self.xts[0]) + mm(self.mats[1], self.xts[1])


def mixer_forward_kernel(
    S, H, count, state, C, ends_ref, in_ref, w_ref, taps_ref, rows_ref, out_w_ref, grad_ref,
    pre_ref, z_ref, y_ref, st_ref, part_ref, all_ref, held, ext, send, recv, own_sem,
):
    i = pl.program_id(0)
    pc = Place(S, H)
    mail = Mail(send, recv)
    moves = gather(pc, mail, grad_ref, all_ref, own_sem)
    ready = pl.num_programs(0) - 1

    @pl.when(i == 0)
    def _():
        greet(pc.peers())
        moves.run(0, 1)

    for step, stage in ((2, 1), (3, 2), (4, 3), (5, 4), (6, 5)):

        @pl.when(i == step)
        def _():
            moves.run(stage, stage + 1)

    depth = w_ref.shape[0]
    n, cp = BLOCK, z_ref.shape[1]

    @pl.when(i == 0)
    def _():
        held[...] = jnp.zeros_like(held)
        ext[0:8, :] = jnp.zeros((8, ext.shape[1]), F32)

    made = mm(in_ref[:, :depth], w_ref[...])
    z = made[:, :cp]
    pre = made[:, cp:]
    z_ref[...], pre_ref[...] = z, pre
    ext[8 : 8 + n, :] = pre
    blk = Block(i, pre, ext, z, taps_ref, rows_ref, ends_ref, count, state, C)
    ext[0:8, :] = pre[n - 8 :, :]
    st = held[...]
    st_ref[0] = st
    y = blk.inner() + blk.carry * mm(blk.c, st.astype(B16))
    held[...] = blk.keep * st + mm(blk.b, blk.tail_xt, TN)
    y = y + blk.skip * blk.x
    y_ref[...] = y
    gated = y * silu(z)
    part_ref[:, :depth] = mm((gated * blk.gain).astype(B16), out_w_ref[...]).astype(B16)
    high, rest = hi_lo(jnp.sum(gated * gated, axis=1, keepdims=True))
    lane = lax.broadcasted_iota(jnp.int32, (n, LANES), 1)
    part_ref[:, depth:] = jnp.where(lane == 0, high.astype(F32), jnp.where(lane == 1, rest.astype(F32), 0.0)).astype(B16)

    @pl.when(i == ready)
    def _():
        moves.run(6)
        mail.finish(gather_count(S, H))


def whole(shape):
    return pl.BlockSpec(shape, lambda i: (0,) * len(shape))


def params():
    return pltpu.CompilerParams(dimension_semantics=("arbitrary",), vmem_limit_bytes=60 * 1024 * 1024)


def mixer_forward(ends, gathered, in_w, taps, rows, out_w, grad, state, C, S, H):
    T, depth = gathered.shape[0], in_w.shape[0]
    cp, nb = out_w.shape[0], gathered.shape[0] // BLOCK
    conv_width = cp + 2 * state

    def block(width):
        return pl.BlockSpec((BLOCK, width), lambda i: (i, 0))

    return pl.pallas_call(
        functools.partial(mixer_forward_kernel, S, H, ends.shape[0], state, C),
        grid=(nb,),
        in_specs=[
            pl.BlockSpec(memory_space=pltpu.SMEM), block(gathered.shape[1]), whole(in_w.shape), whole(taps.shape),
            whole(rows.shape), whole(out_w.shape), VMEM,
        ],
        out_specs=[
            block(conv_width), block(cp), block(cp),
            pl.BlockSpec((1, state, cp), lambda i: (i, 0, 0)), block(depth + LANES), ANY,
        ],
        out_shape=[
            jax.ShapeDtypeStruct((T, conv_width), F32),
            jax.ShapeDtypeStruct((T, cp), F32),
            jax.ShapeDtypeStruct((T, cp), F32),
            jax.ShapeDtypeStruct((nb, state, cp), F32),
            jax.ShapeDtypeStruct((T, depth + LANES), B16),
            jax.ShapeDtypeStruct((T, depth), B16),
        ],
        scratch_shapes=[
            pltpu.VMEM((state, cp), F32), pltpu.VMEM((BLOCK + 8, conv_width), F32), *sems(gather_count(S, H)),
            pltpu.SemaphoreType.DMA,
        ],
        compiler_params=talking(5),
    )(ends, gathered, in_w, taps, rows, out_w, grad)


def mixer_backward_kernel(
    S, H, count, state, C, ends_ref, three_ref, one_ref, pre_ref, halo_ref, z_ref, y_ref, st_ref,
    w_ref, taps_ref, rows_ref, cols_ref, out_w_ref, p_ref, sh_ref, res_ref,
    part_ref, gzx_ref, gbc_ref, gout_ref, gtaps_ref, gvec_ref, gnorm_ref, sh_out, output_ref,
    held, ext, gext, gw_ref, total, *rest,
):
    step = pl.program_id(0)
    i = pl.num_programs(0) - 1 - step
    depth = w_ref.shape[0]
    n, cp = BLOCK, z_ref.shape[1]

    scratch, (send, recv, sh_send, sh_recv, sh_sem) = rest[:-5], rest[-5:]
    pc = Place(S, H)
    N, me = S * H, pc.slot()
    mail = Mail(send, recv)
    sums = scatter(pc, mail, [(p_ref, total, scratch, True)])
    stay = pltpu.make_async_copy(sh_ref.at[me], sh_out.at[me], sh_sem)

    def to_all(function, first, last):
        def body(m, carry):
            to = (me + m) % N
            function(
                pltpu.make_async_remote_copy(
                    src_ref=sh_ref.at[to], dst_ref=sh_out.at[me], send_sem=sh_send.at[m], recv_sem=sh_recv.at[m],
                    device_id=(to // H, to % H), device_id_type=MESH,
                )
            )
            return carry

        lax.fori_loop(first, last, body, 0)

    @pl.when(step == 0)
    def _():
        sums.run(0, 1)
        stay.start()
        barrier = pltpu.get_barrier_semaphore()

        def hello(m, carry):
            to = (me + m) % N
            pl.semaphore_signal(barrier, inc=1, device_id=(to // H, to % H), device_id_type=MESH)
            return carry

        lax.fori_loop(1, N, hello, 0)
        pl.semaphore_wait(barrier, N - 1)
        sums.run(1, 2)

    for when, stage in ((1, 2), (2, 3), (3, 4), (4, 5), (5, 6), (6, 7)):

        @pl.when(step == when)
        def _():
            sums.run(stage, stage + 1)

    @pl.when(step == 1)
    def _():
        to_all(lambda copy: copy.start(), 1, N)

    @pl.when(step == 0)
    def _():
        gnorm_ref[...] = jnp.zeros_like(gnorm_ref)
        held[...] = jnp.zeros_like(held)
        gext[n : n + 8, :] = jnp.zeros((8, gext.shape[1]), F32)
        gw_ref[...] = jnp.zeros_like(gw_ref)
        gout_ref[...] = jnp.zeros_like(gout_ref)
        gtaps_ref[...] = jnp.zeros_like(gtaps_ref)
        gvec_ref[...] = jnp.zeros_like(gvec_ref)

    pre, z, y = pre_ref[...], z_ref[...], y_ref[...]
    ext[0:8, :] = jnp.where(i == 0, 0.0, halo_ref[...])
    ext[8 : 8 + n, :] = pre
    blk = Block(i, pre, ext, z, taps_ref, rows_ref, ends_ref, count, state, C)
    three = three_ref[:, :depth]
    pg = mm(three, out_w_ref[...], NT)
    cross = jnp.sum(three_ref[:, depth:].astype(F32), axis=1, keepdims=True)
    act_z = silu(z)
    gated = y * act_z
    gout_ref[...] += mm((gated * blk.gain).astype(B16), three, TN)
    grad_gated = pg * blk.gain - gated * cross
    gy = grad_gated * act_z
    gz = grad_gated * y * silu_grad(z)
    st = st_ref[0]
    st_low, grad = st.astype(B16), held[...]
    grad_low = grad.astype(B16)
    gy_low = gy.astype(B16)
    y_all = blk.inner() + blk.carry * mm(blk.c, st_low)
    back = sum(mm(blk.mats[j], gy_low * blk.low[j], TN) for j in range(2))
    gate = (blk.carry * gy_low.astype(F32)).astype(B16)
    tail_back = blk.tail * mm(blk.b, grad_low)
    pull = sum(mm(gy_low, blk.xts[j], NT) * blk.decays[j] for j in range(2)).astype(B16)
    g_c = mm(pull, blk.b) + mm(gate, st_low, NT)
    g_b = mm(pull, blk.c, TN) + mm(blk.tail_xt, grad_low, NT)
    held[...] = blk.keep * grad + mm(blk.c, gate, TN)
    g_xt = back + tail_back
    xt = blk.xt.astype(F32)
    cols = cols_ref[...]
    after = exact(gy_low.astype(F32) * y_all - xt * back, cols)
    used = exact(xt * tail_back, cols)
    through = exact(jnp.broadcast_to(blk.keep * jnp.sum(grad * st, axis=0, keepdims=True), (8, cp)), cols)[0:1, :]
    g_rate = (
        exact((blk.row <= blk.col).astype(F32), after) + exact((blk.row > blk.col).astype(F32), used) + through
    )
    g_dt = exact(g_xt * blk.x, cols) - g_rate * blk.decay
    g_dtr = g_dt / (1.0 + jnp.exp(-blk.dtr))
    g_x = g_xt * blk.dtc + blk.skip * gy
    for r, v in enumerate((pg * gated, g_dtr, g_rate * blk.rate, gy * blk.x)):
        gvec_ref[r : r + 1, :] += jnp.sum(v, axis=0, keepdims=True)
    gconv = jnp.concatenate([g_x, g_b, g_c], axis=1) * silu_grad(blk.conv)
    gext[0:n, :] = gconv
    gpre = taps_ref[3:4, :] * gconv
    gtaps_ref[3:4, :] += jnp.sum(gconv * pre, axis=0, keepdims=True)
    for k in (1, 2, 3):
        gpre = gpre + taps_ref[3 - k : 4 - k, :] * gext[k : n + k, :] * blk.later[k]
        gtaps_ref[3 - k : 4 - k, :] += jnp.sum(gconv * ext[8 - k : 8 - k + n, :] * blk.joined[k], axis=0, keepdims=True)
    gext[n : n + 8, :] = gconv[0:8, :]
    made = jnp.concatenate([gz + g_dtr, gpre], axis=1).astype(B16)
    one = one_ref[:, :depth]
    part = mm(made, w_ref[...], NT)
    part_ref[...] = part.astype(B16)
    gnorm_ref[...] += jnp.sum(part * one.astype(F32), axis=0, keepdims=True)
    gw_ref[...] += mm(made, one, TN)

    @pl.when(i == 0)
    def _():
        gzx_ref[...] = gw_ref[: 2 * cp, :].astype(B16)
        gbc_ref[...] = gw_ref[2 * cp :, :].astype(B16)
        gvec_ref[3:4, :] = exact(gvec_ref[...], cols)[3:4, :]
        sums.run(8)
        output_ref[...] = res_ref[...] + total[...]
        to_all(lambda copy: copy.wait(), 1, N)
        stay.wait()
        mail.finish(scatter_count(S, H))


def mixer_backward(ends, three, one, pre, z, y, states, in_w, taps, rows, cols, out_w, out_part, shared, residual, state, C, S, H):
    T, depth = three.shape[0], in_w.shape[0]
    cp, nb = out_w.shape[0], T // BLOCK
    conv_width = cp + 2 * state
    R = residual.shape[0]

    def block(width):
        return pl.BlockSpec((BLOCK, width), lambda k: (nb - 1 - k, 0))

    def halo(k):
        return (jnp.maximum((nb - 1 - k) * (BLOCK // 8) - 1, 0), 0)

    return pl.pallas_call(
        functools.partial(mixer_backward_kernel, S, H, ends.shape[0], state, C),
        grid=(nb,),
        in_specs=[
            pl.BlockSpec(memory_space=pltpu.SMEM), block(three.shape[1]), block(one.shape[1]), block(conv_width),
            pl.BlockSpec((8, conv_width), halo), block(cp), block(cp),
            pl.BlockSpec((1, state, cp), lambda k: (nb - 1 - k, 0, 0)),
            whole(in_w.shape), whole(taps.shape), whole(rows.shape), whole(cols.shape), whole(out_w.shape),
            ANY, ANY, whole(residual.shape),
        ],
        out_specs=[
            block(depth), whole((2 * cp, depth)), whole((2 * state, depth)), whole(out_w.shape), whole((8, conv_width)),
            whole((8, cp)), whole((1, depth)), ANY, whole(residual.shape),
        ],
        out_shape=[
            jax.ShapeDtypeStruct((T, depth), B16),
            jax.ShapeDtypeStruct((2 * cp, depth), B16),
            jax.ShapeDtypeStruct((2 * state, depth), B16),
            jax.ShapeDtypeStruct(out_w.shape, F32),
            jax.ShapeDtypeStruct((8, conv_width), F32),
            jax.ShapeDtypeStruct((8, cp), F32),
            jax.ShapeDtypeStruct((1, depth), F32),
            jax.ShapeDtypeStruct(shared.shape, shared.dtype),
            jax.ShapeDtypeStruct(residual.shape, F32),
        ],
        scratch_shapes=[
            pltpu.VMEM((state, cp), F32),
            pltpu.VMEM((BLOCK + 8, conv_width), F32),
            pltpu.VMEM((BLOCK + 8, conv_width), F32),
            pltpu.VMEM((in_w.shape[1], depth), F32),
            pltpu.VMEM(residual.shape, F32),
            *scatter_scratch(S, H, R, depth),
            *sems(scatter_count(S, H)),
            *sems(S * H),
            pltpu.SemaphoreType.DMA,
        ],
        compiler_params=talking(6),
    )(ends, three, one, pre, pre, z, y, states, in_w, taps, rows, cols, out_w, blocks(out_part, S, H), shared, residual)


def expert_kernel(
    F, FS, two_ref, grad_ref, named_ref, up_ref, down_ref, mine_ref,
    out_ref, part_ref, probs_ref, gup_ref, gdown_ref, gsh_ref, gs_ref,
):
    depth = two_ref.shape[1]

    @pl.when(pl.program_id(0) == 0)
    def _():
        gup_ref[...] = jnp.zeros_like(gup_ref)
        gdown_ref[...] = jnp.zeros_like(gdown_ref)
        gs_ref[...] = jnp.zeros_like(gs_ref)

    two, grad = two_ref[...], grad_ref[...]
    mid = mm(two, up_ref[...])
    back = mm(grad, down_ref[...], NT)
    gate, lin = mid[:, :F], mid[:, F : 2 * F]
    s_gate, s_lin = mid[:, 2 * F : 2 * F + LANES], mid[:, 2 * F + LANES :]
    named = named_ref[...].astype(F32) > 0
    logits = jnp.where(named, s_gate, -1e30)
    odds = jnp.where(named, jnp.exp(logits - jnp.max(logits, axis=1, keepdims=True)), 0.0)
    probs = odds / jnp.sum(odds, axis=1, keepdims=True)
    probs_ref[...] = probs
    mine = mine_ref[...]
    weight = jnp.sum(probs * mine, axis=1, keepdims=True)
    s_back, back = back[:, F:], back[:, :F]
    act_gate, act_s = silu(gate), silu(s_gate)
    acting = act_gate * lin
    gp = jnp.sum(acting * back, axis=1, keepdims=True)
    back = weight * back
    down_in = jnp.concatenate([weight * acting, act_s * s_lin], axis=1).astype(B16)
    mid_grad = jnp.concatenate(
        [back * lin * silu_grad(gate), back * act_gate, s_back * s_lin * silu_grad(s_gate), s_back * act_s], axis=1
    ).astype(B16)
    out_ref[...] = mm(down_in, down_ref[...]).astype(B16)
    part_ref[:, :depth] = mm(mid_grad, up_ref[...], NT).astype(B16)
    part_ref[:, depth:] = (gp * mine).astype(B16)
    gup_ref[...] += mm(two, mid_grad[:, : 2 * F], TN)
    gdown_ref[...] += mm(down_in[:, :F], grad, TN)
    gs_ref[: 2 * LANES, :] += mm(mid_grad[:, 2 * F :], two, TN)
    gs_ref[2 * LANES :, :] += mm(down_in[:, F:], grad, TN)

    @pl.when(pl.program_id(0) == pl.num_programs(0) - 1)
    def _():
        for k in range(3):
            gsh_ref[k] = gs_ref[k * LANES : k * LANES + gsh_ref.shape[1], :].astype(B16)


def experts(two, all_grad, gathered, up_w, down_w, mine, F, FS):
    T, depth = two.shape
    tall = -(-FS // 16) * 16

    def block(width):
        return pl.BlockSpec((BLOCK, width), lambda i: (i, 0))

    return pl.pallas_call(
        functools.partial(expert_kernel, F, FS),
        grid=(T // BLOCK,),
        in_specs=[
            block(depth), block(depth), pl.BlockSpec((BLOCK, LANES), lambda i: (i, depth // LANES)),
            whole(up_w.shape), whole(down_w.shape), whole(mine.shape),
        ],
        out_specs=[
            block(depth), block(depth + LANES), block(LANES), whole((depth, 2 * F)), whole((F, depth)),
            whole((3, tall, depth)),
        ],
        out_shape=[
            jax.ShapeDtypeStruct((T, depth), B16),
            jax.ShapeDtypeStruct((T, depth + LANES), B16),
            jax.ShapeDtypeStruct((T, LANES), F32),
            jax.ShapeDtypeStruct((depth, 2 * F), F32),
            jax.ShapeDtypeStruct((F, depth), F32),
            jax.ShapeDtypeStruct((3, tall, depth), B16),
        ],
        scratch_shapes=[pltpu.VMEM((3 * LANES, depth), F32)],
        compiler_params=params(),
    )(two, all_grad, gathered, up_w, down_w, mine)


def local(
    hidden_in, norm1_gain, w_zx, w_bc, w_dt, conv_x, conv_bc, dt_bias, a_log, d_skip, gate_gain,
    w_out, norm2_gain, router, expert_up, expert_down, shared_up, shared_down, out_grad,
    seq_lengths, routes,
):
    S, H = lax.axis_size("seq"), lax.axis_size("head")
    N = S * H
    s = lax.axis_index("seq")
    g = s * H + lax.axis_index("head")
    R, D = hidden_in.shape
    heads, inner = dt_bias.shape[0], conv_x.shape[1]
    size = inner // heads
    state = w_bc.shape[1] // 2
    width = inner * H
    C = inner // S
    CP = -(-(C + 2) // LANES) * LANES
    E = N // 2
    F = expert_down.shape[1]
    FS = shared_down.shape[0] // N
    per = D // N

    named = jnp.sum(
        (routes[:, :, None] == jnp.arange(E, dtype=jnp.int32)[None, None, :]).astype(F32), axis=1
    )
    named = jnp.pad(named.astype(B16), ((0, 0), (FS, LANES - FS - E)))
    gain1, gain2 = norm1_gain[None], norm2_gain[None]
    gathered = first_rows(hidden_in, gain1, named, S, H)

    firsts = [min(k * C // size, heads - 2) for k in range(S)]
    first = jnp.minimum(s * C // size, heads - 2)
    channel = jnp.arange(CP)
    masks = jnp.stack(
        [((channel < C) & ((s * C + channel) // size - first == j)).astype(F32) for j in range(2)]
    )

    def mine(values, axis, offset, length):
        return lax.dynamic_slice_in_dim(values, offset, length, axis)

    def channels(values, axis):
        cut = mine(values, axis, s * C, C)
        pads = [(0, 0)] * values.ndim
        pads[axis] = (0, CP - C)
        return jnp.pad(cut, pads)

    def in_free(values):
        return jnp.pad(values, [(0, 0)] * (values.ndim - 1) + [(C, CP - C - 2)])

    zx_w = mine(w_zx, 2, s * C, C)
    in_w = jnp.concatenate(
        [
            zx_w[:, 0], pad_lanes(mine(w_dt, 1, first, 2), CP - C), pad_lanes(zx_w[:, 1], CP), w_bc,
        ],
        axis=1,
    )
    taps = jnp.concatenate([channels(conv_x, 1), conv_bc], axis=1)
    bias, alog, skip = (mine(v, 0, first, 2) for v in (dt_bias, a_log, d_skip))
    gain = channels(gate_gain, 0)
    out_w = channels(w_out, 0)
    rows = jnp.concatenate(
        [masks, (skip @ masks)[None], gain[None], in_free(jnp.stack([bias, jnp.exp(alog)]))], axis=0
    )
    rows = jnp.pad(rows, ((0, 2), (0, 0)))
    cols = in_free(masks.T)
    ends = jnp.cumsum(seq_lengths)

    pre, z, y, states, part, all_grad = mixer_forward(
        ends, gathered, in_w, taps, rows, out_w, out_grad.astype(B16), state, C, S, H
    )
    two, residual, mixed, inv_gate = second_rows(part, hidden_in, gain2, width, S, H)

    sup = mine(shared_up, 2, g * FS, FS)
    router_w = jnp.pad(router, ((0, 0), (FS, LANES - FS - E)))
    up_w = jnp.concatenate(
        [
            expert_up[0].reshape(D, 2 * F), sup[:, 0], router_w[:, FS:], pad_lanes(sup[:, 1], LANES),
        ],
        axis=1,
    )
    down_w = jnp.concatenate([expert_down[0], mine(shared_down, 0, g * FS, FS), jnp.zeros((LANES - FS, D), B16)], axis=0)
    is_mine = (jnp.arange(LANES) == FS + g // 2).astype(F32)[None]
    out_part, two_part, probs, grad_up, grad_down, grad_shared = experts(
        two, all_grad, gathered, up_w, down_w, is_mine, F, FS
    )
    three, grad_res, norm2_part, router_part = third_rows(
        two_part, probs, residual, mixed, inv_gate, out_grad, gain2, router_w, width, S, H
    )
    tall_s = grad_shared.shape[1]
    shared = grad_shared.reshape(3 * tall_s, N, per).transpose(1, 0, 2)
    one_part, grad_zx_w, grad_bc_w, grad_out_w, tap_part, vec_part, norm1_part, sh_in, output = mixer_backward(
        ends, three, gathered, pre, z, y, states, in_w, taps, rows, cols, out_w, out_part, shared, residual,
        state, C, S, H,
    )
    tall = -(-per // 16) * 16
    extra = jnp.concatenate([grad_bc_w.T, router_part], axis=1).reshape(N, per, 2 * state + LANES)
    extra = jnp.pad(extra, ((0, 0), (0, tall - per), (0, 0))).reshape(N * tall, 2 * state + LANES)
    cut = -(-(C + 2) // 16) * 16
    zx_rows = jnp.concatenate([grad_zx_w[:cut], grad_zx_w[CP : CP + C]], axis=0)
    zx_rows = jnp.pad(zx_rows, ((0, -(cut + C) % 16), (0, 0)))
    wo_rows = jnp.pad(grad_out_w[:C].astype(B16), ((0, -C % 16), (0, 0)))

    def by_seq(values):
        return values.reshape(values.shape[0], S, D // S).transpose(1, 0, 2)

    grad_in, extra_sum, sums, singles, zx_in, wo_in = last_rows(
        one_part, extra, by_seq(zx_rows), by_seq(wo_rows), tap_part, vec_part,
        jnp.concatenate([norm1_part, norm2_part], axis=0), hidden_in, grad_res, gain1, state, S, H,
    )
    grad_bc, grad_router = extra_sum[:per, : 2 * state], extra_sum[:per, 2 * state :][:, FS : FS + E]
    grad_zx = jnp.stack([zx_in[:, :C], zx_in[:, cut : cut + C]], axis=0)
    grad_zx = grad_zx.transpose(3, 0, 1, 2).reshape(D // S, 2, inner).astype(F32)
    pick = jnp.asarray(
        [[[float(firsts[k] + j == h) for h in range(heads)] for j in range(2)] for k in range(S)], F32
    )
    exactly = lax.Precision.HIGHEST
    grad_w_dt = jnp.einsum("kjd,kjh->dh", zx_in[:, C : C + 2].astype(F32), pick, precision=exactly)
    grad_w_out = wo_in[:, :C].reshape(inner, D // S).astype(F32)
    sh_in = sh_in.reshape(N, 3, tall_s, per)[:, :, :FS]
    grad_shared_up = sh_in[:, :2].transpose(3, 1, 0, 2).reshape(per, 2, N * FS).astype(F32)
    grad_shared_down = sh_in[:, 2].reshape(N * FS, per).astype(F32)
    lines = D // LANES
    grad_norm1 = sums[:lines].reshape(D) / norm1_gain
    grad_norm2 = sums[lines : 2 * lines].reshape(D)
    grad_conv_bc = sums[2 * lines :].reshape(4, 2 * state)
    singles = singles.reshape(S, H, 8, LANES)
    by_channel = singles[:, :, :5, :C].transpose(2, 1, 0, 3).reshape(5, width)
    grad_conv_x, grad_gate_gain = by_channel[:4], by_channel[4]
    by_head = jnp.einsum("kgrj,kjh->rgh", singles[:, :, 5:, C : C + 2], pick, precision=exactly).reshape(3, heads * H)
    grad_dt_bias, grad_a_log, grad_d_skip = by_head[0], by_head[1], by_head[2]
    grad_up, grad_down = grad_up.reshape(expert_up.shape), grad_down.reshape(expert_down.shape)
    return (
        output, grad_in, grad_norm1, grad_zx, grad_bc, grad_w_dt, grad_conv_x, grad_conv_bc, grad_dt_bias,
        grad_a_log, grad_d_skip, grad_gate_gain, grad_w_out, grad_norm2, grad_router, grad_up, grad_down,
        grad_shared_up, grad_shared_down,
    )


def solution(mesh):
    return jax.shard_map(
        local,
        mesh=mesh,
        in_specs=(
            P(("seq", "head"), None),
            P(),
            P(None, None, "head"),
            P(),
            P(None, "head"),
            P(None, "head"),
            P(),
            P("head"),
            P("head"),
            P("head"),
            P("head"),
            P("head", None),
            P(),
            P(),
            P(("seq", "head"), None, None, None),
            P(("seq", "head"), None, None),
            P(),
            P(),
            P(("seq", "head"), None),
            P(),
            P(("seq", "head"), None),
        ),
        out_specs=(
            P(("seq", "head"), None),
            P(("seq", "head"), None),
            P(),
            P("seq", None, "head"),
            P(("seq", "head"), None),
            P("seq", "head"),
            P(),
            P(),
            P(),
            P(),
            P(),
            P(),
            P("head", "seq"),
            P(),
            P(("seq", "head"), None),
            P(("seq", "head"), None, None, None),
            P(("seq", "head"), None, None),
            P(("seq", "head"), None, None),
            P(None, ("seq", "head")),
        ),
        check_vma=False,
    )
```

```python
import functools
import jax
import jax.numpy as jnp
from jax import lax
from jax.experimental import pallas as pl
from jax.experimental.pallas import tpu as pltpu
from jax.sharding import PartitionSpec as P

MESH = pl.DeviceIdType.MESH
BLOCK = 256
EPS = 1e-05
LANES = 128
B16 = jnp.bfloat16
F32 = jnp.float32


def mm(left, right, dims=(((1,), (0,)), ((), ()))):
    return lax.dot_general(left, right, dims, preferred_element_type=F32)


NT = (((1,), (1,)), ((), ()))
TN = (((0,), (0,)), ((), ()))


def inverse_rms(values):
    return lax.rsqrt(jnp.mean(values * values, axis=-1, keepdims=True) + EPS)


def rms_back(values, inverse, gain, grad):
    weighted = grad * gain
    inner = jnp.mean(weighted * values, axis=-1, keepdims=True)
    return inverse * weighted - values * inverse**3 * inner


def silu_grad(values):
    sig = jax.nn.sigmoid(values)
    return sig * (1.0 + values * (1.0 - sig))


def pad_lanes(values, width):
    return jnp.pad(values, [(0, 0)] * (values.ndim - 1) + [(0, width - values.shape[-1])])


def hi_lo(values):
    high = values.astype(B16)
    return high, (values - high.astype(F32)).astype(B16)


def sizes(seq_size, head_size):
    return head_size // 2, head_size // 2, seq_size // (head_size // 2)


class Place:
    def __init__(self, seq_size, head_size):
        self.H = head_size
        self.X, self.Y, self.Z = sizes(seq_size, head_size)
        assert self.Z == 4
        seq, head = lax.axis_index("seq"), lax.axis_index("head")
        self.z, self.y = seq // self.Y, seq % self.Y
        self.x, self.c = head // 2, head % 2
        z = self.z
        self.partners = (z, z + 1 - 2 * (z % 2), (z + 2) % 4, 3 - z)

    def at(self, dz=0, dy=0, dx=0, dc=0):
        return (
            self.partners[dz],
            (self.y + dy) % self.Y if dy else self.y,
            (self.x + dx) % self.X if dx else self.x,
            1 - self.c if dc else self.c,
        )

    def dev(self, **where):
        z, y, x, c = self.at(**where)
        return (z * self.Y + y, x * 2 + c)

    def slot(self, **where):
        z, y, x, c = self.at(**where)
        return (z * self.Y + y) * self.H + x * 2 + c

    def partner(self, dz):
        return (self.z // 2 + dz // 2) % 2 * 2 + (self.z + dz) % 2

    def peers(self, direct=False):
        out = [self.dev(dz=k) for k in range(1, 4 if direct else 3)]
        out += [self.dev(dy=k) for k in range(1, self.Y)]
        out += [self.dev(dx=k) for k in range(1, self.X)]
        return out + [self.dev(dc=1)]


def greet(peers):
    barrier = pltpu.get_barrier_semaphore()
    for peer in peers:
        pl.semaphore_signal(barrier, inc=1, device_id=peer, device_id_type=MESH)
    pl.semaphore_wait(barrier, len(peers))


class Mail:
    def __init__(self, send, recv):
        self.send, self.recv, self.made = send, recv, []

    def copy(self, src, dst, dev):
        i = len(self.made)
        self.made.append(
            pltpu.make_async_remote_copy(
                src_ref=src, dst_ref=dst, send_sem=self.send.at[i], recv_sem=self.recv.at[i],
                device_id=dev, device_id_type=MESH,
            )
        )
        return self.made[-1]

    def finish(self, count):
        assert len(self.made) == count
        for copy in self.made:
            copy.wait_send()


class Script(list):
    def stage(self):
        self.append([])

    def do(self, action):
        self[-1].append(action)

    def run(self, first=0, last=None):
        for stage in self[first:last]:
            for action in stage:
                action()


def gather_count(S, H):
    X, Y, Z = sizes(S, H)
    return (Z - 1) + 2 * Z * (X + Y - 2) + 2 * Z * (X - 1) * (Y - 1) + X * Y * Z


def gather(pc, mail, x_ref, out_ref, own_sem, planes=False):
    X, Y, Z = pc.X, pc.Y, pc.Z
    R = x_ref.shape[0]
    half = R // 2
    script = Script()

    def rows(part, **where):
        base = pl.multiple_of(pc.slot(**where) * R, R)
        if part is None:
            return out_ref.at[pl.ds(base, R)]
        return out_ref.at[pl.ds(pl.multiple_of(base + part * half, half), half)]

    def send(src, dst, dev):
        copy = mail.copy(src, dst, dev)
        script.do(copy.start)
        return copy

    x_in, y_in, dga, dgb = {}, {}, {}, {}
    sib = {dz: [] for dz in range(Z)}

    def column(dz):
        for part in (0, 1):
            src = x_ref.at[pl.ds(part * half, half)] if dz == 0 else rows(part, dz=dz)
            for k in range(1, X):
                x_in[dz, k, part] = send(src, rows(part, dz=dz), pc.dev(dx=k))
            other = 1 - part
            src = x_ref.at[pl.ds(other * half, half)] if dz == 0 else rows(other, dz=dz)
            for k in range(1, Y):
                y_in[dz, k, other] = send(src, rows(other, dz=dz), pc.dev(dy=k))
        src = x_ref if dz == 0 else rows(None, dz=dz)
        sib[dz].append(send(src, rows(None, dz=dz), pc.dev(dc=1)))

    def onward(dz):
        for k in range(1, X):
            script.do(x_in[dz, k, 0].wait_recv)
            block = rows(0, dz=dz, dx=-k)
            for m in range(1, Y):
                dga[dz, k, m] = send(block, block, pc.dev(dy=m))
        for k in range(1, Y):
            script.do(y_in[dz, k, 1].wait_recv)
            block = rows(1, dz=dz, dy=-k)
            for m in range(1, X):
                dgb[dz, k, m] = send(block, block, pc.dev(dx=m))
        for k in range(1, X):
            script.do(x_in[dz, k, 1].wait_recv)
            block = rows(None, dz=dz, dx=-k)
            sib[dz].append(send(block, block, pc.dev(dc=1)))
        for k in range(1, Y):
            script.do(y_in[dz, k, 0].wait_recv)
            block = rows(None, dz=dz, dy=-k)
            sib[dz].append(send(block, block, pc.dev(dc=1)))

    def corner(dz):
        for k in range(1, X):
            for m in range(1, Y):
                script.do(dga[dz, k, m].wait_recv)
                script.do(dgb[dz, m, k].wait_recv)
                block = rows(None, dz=dz, dx=-k, dy=-m)
                sib[dz].append(send(block, block, pc.dev(dc=1)))

    own = pltpu.make_async_copy(x_ref, rows(None), own_sem)
    script.stage()
    script.do(own.start)
    first = send(x_ref, rows(None), pc.dev(dz=1))
    column(0)
    second = send(x_ref, rows(None), pc.dev(dz=2))
    script.stage()
    script.do(first.wait_recv)
    column(1)
    script.stage()
    onward(0)
    script.stage()
    corner(0)
    script.stage()
    script.do(second.wait_recv)
    third = send(rows(None, dz=2), rows(None, dz=2), pc.dev(dz=1))
    column(2)
    script.stage()
    onward(1)
    script.stage()
    script.do(third.wait_recv)
    column(3)
    script.stage()
    corner(1)
    for dz in (2, 3):
        script.stage()
        onward(dz)
        script.stage()
        corner(dz)
    if not planes:
        for dz in range(Z):
            for copy in sib[dz]:
                script.do(copy.wait_recv)
        script.do(own.wait)
        return script
    for dz in range(Z):
        script.stage()
        for copy in sib[dz]:
            script.do(copy.wait_recv)
        if dz == 0:
            script.do(own.wait)
    return script


def scatter_parts(split):
    return (("y", 0), ("x", 1)) if split else (("x", None),)


def scatter_count(S, H, splits=(True,)):
    X, Y, Z = sizes(S, H)
    pieces = sum(len(scatter_parts(split)) for split in splits)
    return len(splits) * (Z + Z - 1) + pieces * Z * (X + Y - 2)


def sum_scratch(S, H, R, W, split=True):
    X, Y, Z = sizes(S, H)
    out = [pltpu.VMEM((Z, Y, X, R, W), B16), pltpu.VMEM((Z - 1, R, W), B16)]
    for axis, part in scatter_parts(split):
        rows = R if part is None else R // 2
        first, second = (Y, X) if axis == "y" else (X, Y)
        out += [pltpu.VMEM((Z, first - 1, second, rows, W), B16), pltpu.VMEM((Z, second - 1, rows, W), B16)]
    return out


def scatter_scratch(S, H, R, W, split=True):
    X, Y, Z = sizes(S, H)
    return [pltpu.VMEM((Z, Y, X, R, W), B16), *sum_scratch(S, H, R, W, split), pltpu.SemaphoreType.DMA((Z,))]


def accumulate(dst, srcs, rows):
    def action():
        def body(i, carry):
            at = pl.ds(pl.multiple_of(i * 16, 16), 16)
            total = dst.at[at][...].astype(F32)
            for src in srcs:
                total = total + src.at[at][...].astype(F32)
            dst.at[at][...] = total.astype(dst.dtype)
            return carry

        lax.fori_loop(0, rows // 16, body, 0)

    return action


ORDER = (3, 2, 1, 0)


class Sum:
    def __init__(self, pc, mail, script, cell, theirs, buffers, R, split=True, direct=False, ends=None):
        self.ends = ends
        self.pc, self.mail, self.script, self.cell, self.theirs = pc, mail, script, cell, theirs
        self.r0, self.r3, self.buffers, self.R, self.split, self.direct = buffers[0], buffers[1], buffers[2:], R, split, direct
        self.sib, self.one, self.two, self.zs = {}, {}, {}, {}

    def send(self, src, dst, dev):
        copy = self.mail.copy(src, dst, dev)
        self.script.do(copy.start)
        return copy

    def pieces(self):
        R = self.R
        for j, (axis, part) in enumerate(scatter_parts(self.split)):
            rows, size = (pl.ds(0, R), R) if part is None else (pl.ds(part * (R // 2), R // 2), R // 2)
            yield j, axis, rows, size, self.buffers[2 * j], self.buffers[2 * j + 1]

    def across(self, dz):
        self.sib[dz] = self.send(self.theirs(dz), self.r0.at[dz], self.pc.dev(dc=1))

    def cores(self, dz):
        pc, whole = self.pc, pl.ds(0, self.R)
        self.script.do(self.sib[dz].wait_recv)
        for yy in range(pc.Y):
            for xx in range(pc.X):
                self.script.do(accumulate(self.cell(dz, yy, xx, whole), [self.r0.at[dz, yy, xx]], self.R))
        for j, axis, rows, size, r1, r2 in self.pieces():
            for k in range(1, pc.Y if axis == "y" else pc.X):
                if axis == "y":
                    src, dev = self.cell(dz, pc.at(dy=k)[1], slice(None), rows), pc.dev(dy=k)
                else:
                    src, dev = self.cell(dz, slice(None), pc.at(dx=k)[2], rows), pc.dev(dx=k)
                self.one[dz, j, k] = self.send(src, r1.at[dz, k - 1], dev)

    def firsts(self, dz):
        pc = self.pc
        for j, axis, rows, size, r1, r2 in self.pieces():
            steps = range(1, pc.Y if axis == "y" else pc.X)
            for k in steps:
                self.script.do(self.one[dz, j, k].wait_recv)
            for m in range(pc.X if axis == "y" else pc.Y):
                dst = self.cell(dz, pc.y, m, rows) if axis == "y" else self.cell(dz, m, pc.x, rows)
                self.script.do(accumulate(dst, [r1.at[dz, k - 1, m] for k in steps], size))
            for k in range(1, pc.X if axis == "y" else pc.Y):
                if axis == "y":
                    src, dev = self.cell(dz, pc.y, pc.at(dx=k)[2], rows), pc.dev(dx=k)
                else:
                    src, dev = self.cell(dz, pc.at(dy=k)[1], pc.x, rows), pc.dev(dy=k)
                self.two[dz, j, k] = self.send(src, r2.at[dz, k - 1], dev)

    def seconds(self, dz):
        pc = self.pc
        for j, axis, rows, size, r1, r2 in self.pieces():
            steps = range(1, pc.X if axis == "y" else pc.Y)
            for k in steps:
                self.script.do(self.two[dz, j, k].wait_recv)
            mine = self.cell(dz, pc.y, pc.x, rows)
            self.script.do(accumulate(mine, [r2.at[dz, k - 1] for k in steps], size))
        mine = self.cell(dz, pc.y, pc.x, pl.ds(0, self.R))
        if self.ends is not None:
            self.homeward(dz, mine)
            return
        if self.direct:
            if dz:
                self.zs[dz] = self.send(mine, self.r3.at[dz - 1], pc.dev(dz=dz))
            return
        if dz == 2:
            self.script.do(self.zs[3].wait_recv)
            self.script.do(accumulate(mine, [self.r3.at[0]], self.R))
        if dz:
            self.zs[dz] = self.send(mine, self.r3.at[3 - dz], pc.dev(dz=2 if dz == 2 else 1))

    def homeward(self, plane, mine):
        pc, (zsend, zrecv) = self.pc, self.ends
        at = (pc.z - plane + 3) % 4
        copy = pltpu.make_async_remote_copy(
            src_ref=mine, dst_ref=self.r3.at[at], send_sem=zsend.at[plane], recv_sem=zrecv.at[at],
            device_id=(plane * pc.Y + pc.y, pc.x * 2 + pc.c), device_id_type=MESH,
        )
        self.zs[plane] = copy

        def start():
            @pl.when(pc.z != plane)
            def _():
                copy.start()

        self.script.do(start)

    def home(self, total):
        pc, (zsend, zrecv) = self.pc, self.ends
        mine = self.cell(pc.z, pc.y, pc.x, pl.ds(0, self.R))
        copies = [
            pltpu.make_async_remote_copy(
                src_ref=mine, dst_ref=self.r3.at[k], send_sem=zsend.at[0], recv_sem=zrecv.at[k],
                device_id=pc.dev(dz=1), device_id_type=MESH,
            )
            for k in range(3)
        ]

        def body(i, carry):
            at = pl.ds(pl.multiple_of(i * 16, 16), 16)
            value = mine.at[at][...].astype(F32)
            for k in range(3):
                value = value + self.r3.at[k, at][...].astype(F32)
            total.at[at][...] = value
            return carry

        def sent():
            for plane in range(4):

                @pl.when(pc.z != plane)
                def _():
                    self.zs[plane].wait_send()

        for copy in copies:
            self.script.do(copy.wait_recv)
        self.script.do(lambda: lax.fori_loop(0, self.R // 16, body, 0))
        self.script.do(sent)

    def last(self, total):
        ends = (1, 2, 3) if self.direct else (2, 1)
        slots = (0, 1, 2) if self.direct else (1, 2)
        for dz in ends:
            self.script.do(self.zs[dz].wait_recv)
        pc, mine = self.pc, self.cell(0, self.pc.y, self.pc.x, pl.ds(0, self.R))

        def body(i, carry):
            at = pl.ds(pl.multiple_of(i * 16, 16), 16)
            value = mine.at[at][...].astype(F32)
            for k in slots:
                value = value + self.r3.at[k, at][...].astype(F32)
            total.at[at][...] = value
            return carry

        self.script.do(lambda: lax.fori_loop(0, self.R // 16, body, 0))


def scatter(pc, mail, jobs):
    script = Script()
    own, sums = {}, []

    def make(p_ref, t0, scratch, split):
        return Sum(
            pc, mail, script, lambda dz, yy, xx, rows: t0.at[dz, yy, xx, rows],
            lambda dz: p_ref.at[pc.at(dz=dz)[0], :, :, 1 - pc.c], scratch[1:-1], p_ref.shape[4], split,
        )

    for p_ref, total, scratch, split in jobs:
        sums.append(make(p_ref, scratch[0], scratch, split))
    script.stage()
    for o, (p_ref, total, scratch, split) in enumerate(jobs):
        for dz in ORDER:
            own[o, dz] = pltpu.make_async_copy(
                p_ref.at[pc.at(dz=dz)[0], :, :, pc.c], scratch[0].at[dz], scratch[-1].at[dz]
            )
            script.do(own[o, dz].start)
    script.stage()
    for dz in ORDER:
        for each in sums:
            each.across(dz)

    def cores(dz):
        for o, each in enumerate(sums):
            script.do(own[o, dz].wait)
            each.cores(dz)

    script.stage()
    cores(3)
    cores(2)
    script.stage()
    cores(1)
    cores(0)
    script.stage()
    for dz in ORDER:
        if dz < 3:
            script.stage()
        for each in sums:
            each.firsts(dz)
        if dz < 3:
            for each in sums:
                each.seconds(dz + 1)
    script.stage()
    for each, (p_ref, total, scratch, split) in zip(sums, jobs):
        each.seconds(0)
        each.last(total)
    return script


ANY = pl.BlockSpec(memory_space=pl.ANY)
VMEM = pl.BlockSpec(memory_space=pltpu.VMEM)


def sems(count):
    return [pltpu.SemaphoreType.DMA((count,)), pltpu.SemaphoreType.DMA((count,))]


def talking(cid):
    return pltpu.CompilerParams(collective_id=cid, has_side_effects=True, vmem_limit_bytes=60 * 1024 * 1024)


def blocks(part, S, H):
    X, Y, Z = sizes(S, H)
    return part.reshape(Z, Y, X, 2, part.shape[0] // (S * H), part.shape[1])


def first_kernel(S, H, in_ref, gain_ref, named_ref, out_ref, rows, send, recv, own_sem):
    pc = Place(S, H)
    D = in_ref.shape[1]
    values = in_ref[...]
    rows[:, :D] = (values * inverse_rms(values) * gain_ref[...]).astype(B16)
    rows[:, D:] = named_ref[...]
    mail = Mail(send, recv)
    moves = gather(pc, mail, rows, out_ref, own_sem)
    greet(pc.peers())
    moves.run()
    mail.finish(gather_count(S, H))


def first_rows(hidden_in, gain, named, S, H):
    R, D = hidden_in.shape
    W = D + LANES
    return pl.pallas_call(
        functools.partial(first_kernel, S, H),
        out_shape=jax.ShapeDtypeStruct((S * H * R, W), B16),
        in_specs=[VMEM] * 3,
        out_specs=ANY,
        scratch_shapes=[pltpu.VMEM((R, W), B16), *sems(gather_count(S, H)), pltpu.SemaphoreType.DMA],
        compiler_params=talking(1),
    )(hidden_in, gain, named)


def seg_of(pos, ends_ref, count):
    found = jnp.zeros(pos.shape, jnp.int32)
    for k in range(count):
        found = found + (pos >= ends_ref[k]).astype(jnp.int32)
    return jnp.where(pos < 0, -1, found)


def exact(left, right):
    return jnp.dot(left, right, precision=lax.Precision.HIGHEST, preferred_element_type=F32)


def silu(values):
    return values / (1.0 + jnp.exp(-values))


def softplus(values):
    return jnp.maximum(values, 0.0) + jnp.log1p(jnp.exp(-jnp.abs(values)))


class Block:
    def __init__(self, i, pre, ext, z, taps_ref, rows_ref, ends_ref, count, state, C):
        n = BLOCK
        pos = i * n + lax.broadcasted_iota(jnp.int32, (n, 1), 0)
        pos_row = i * n + lax.broadcasted_iota(jnp.int32, (1, n), 1)
        seg, seg_row = seg_of(pos, ends_ref, count), seg_of(pos_row, ends_ref, count)
        self.joined = {k: ((pos >= k) & (seg_of(pos - k, ends_ref, count) == seg)).astype(F32) for k in (1, 2, 3)}
        self.later = {k: (seg_of(pos + k, ends_ref, count) == seg).astype(F32) for k in (1, 2, 3)}
        conv = taps_ref[3:4, :] * pre
        for k in (1, 2, 3):
            conv = conv + taps_ref[3 - k : 4 - k, :] * ext[8 - k : 8 - k + n, :] * self.joined[k]
        act = silu(conv)
        cp = act.shape[1] - 2 * state
        self.conv = conv
        self.x, self.b, self.c = act[:, :cp], act[:, cp : cp + state].astype(B16), act[:, cp + state :].astype(B16)
        self.m = [rows_ref[j : j + 1, :] for j in range(2)]
        self.skip, self.gain = rows_ref[2:3, :], rows_ref[3:4, :]
        self.C = C
        self.dtr = z + rows_ref[4:5, :]
        self.dt = softplus(self.dtr)
        self.decay = rows_ref[5:6, :]
        self.rate = -self.dt * self.decay
        row, col = lax.broadcasted_iota(jnp.int32, (n, n), 0), lax.broadcasted_iota(jnp.int32, (n, n), 1)
        lower = row >= col
        self.row, self.col = row, col
        logdec = exact(lower.astype(F32), self.rate)
        log_row = logdec.T
        linked = lower & (seg == seg_row)
        self.decays = [
            jnp.exp(jnp.where(linked, logdec[:, C + j : C + j + 1] - log_row[C + j : C + j + 1, :], -1e30)) for j in range(2)
        ]
        scores = mm(self.c, self.b, NT)
        self.mats = [(scores * d).astype(B16) for d in self.decays]
        before = jnp.where(i == 0, -1, seg_of(jnp.full((1, 1), i * n - 1, jnp.int32), ends_ref, count))
        final = seg_of(jnp.full((1, 1), i * n + n - 1, jnp.int32), ends_ref, count)
        last = logdec[n - 1 : n, :]
        self.carry = self.spread(jnp.where(seg == before, jnp.exp(logdec), 0.0))
        self.tail = self.spread(jnp.where(seg == final, jnp.exp(last - logdec), 0.0))
        self.keep = self.spread(jnp.where(final == before, jnp.exp(last), 0.0))
        self.dtc = self.spread(self.dt)
        self.xt = (self.dtc * self.x).astype(B16)
        self.low = [m.astype(B16) for m in self.m]
        self.xts = [self.xt * low for low in self.low]
        self.tail_xt = (self.tail * self.xt.astype(F32)).astype(B16)

    def spread(self, values):
        return values[:, self.C : self.C + 1] * self.m[0] + values[:, self.C + 1 : self.C + 2] * self.m[1]

    def inner(self):
        return mm(self.mats[0], self.xts[0]) + mm(self.mats[1], self.xts[1])


def mixer_forward_kernel(
    S, H, count, state, C, ends_ref, in_ref, w_ref, taps_ref, rows_ref, out_w_ref, grad_ref,
    pre_ref, z_ref, y_ref, st_ref, part_ref, all_ref, held, ext, send, recv, own_sem,
):
    i = pl.program_id(0)
    pc = Place(S, H)
    mail = Mail(send, recv)
    moves = gather(pc, mail, grad_ref, all_ref, own_sem)
    ready = pl.num_programs(0) - 1

    @pl.when(i == 0)
    def _():
        greet(pc.peers())
        moves.run(0, 1)

    for step, stage, until in ((1, 1, 2), (2, 2, 3), (3, 3, 5), (4, 5, 7), (5, 7, 9), (6, 9, 11)):

        @pl.when(i == step)
        def _():
            moves.run(stage, until)

    depth = w_ref.shape[0]
    n, cp = BLOCK, z_ref.shape[1]

    @pl.when(i == 0)
    def _():
        held[...] = jnp.zeros_like(held)
        ext[0:8, :] = jnp.zeros((8, ext.shape[1]), F32)

    made = mm(in_ref[:, :depth], w_ref[...])
    z = made[:, :cp]
    pre = made[:, cp:]
    z_ref[...], pre_ref[...] = z, pre
    ext[8 : 8 + n, :] = pre
    blk = Block(i, pre, ext, z, taps_ref, rows_ref, ends_ref, count, state, C)
    ext[0:8, :] = pre[n - 8 :, :]
    st = held[...]
    st_ref[0] = st
    y = blk.inner() + blk.carry * mm(blk.c, st.astype(B16))
    held[...] = blk.keep * st + mm(blk.b, blk.tail_xt, TN)
    y = y + blk.skip * blk.x
    y_ref[...] = y
    gated = y * silu(z)
    part_ref[:, :depth] = mm((gated * blk.gain).astype(B16), out_w_ref[...]).astype(B16)
    high, rest = hi_lo(jnp.sum(gated * gated, axis=1, keepdims=True))
    lane = lax.broadcasted_iota(jnp.int32, (n, LANES), 1)
    part_ref[:, depth:] = jnp.where(lane == 0, high.astype(F32), jnp.where(lane == 1, rest.astype(F32), 0.0)).astype(B16)

    @pl.when(i == ready)
    def _():
        moves.run(11)
        mail.finish(gather_count(S, H))


def whole(shape):
    return pl.BlockSpec(shape, lambda i: (0,) * len(shape))


def params():
    return pltpu.CompilerParams(dimension_semantics=("arbitrary",), vmem_limit_bytes=60 * 1024 * 1024)


def mixer_forward(ends, gathered, in_w, taps, rows, out_w, grad, state, C, S, H):
    T, depth = gathered.shape[0], in_w.shape[0]
    cp, nb = out_w.shape[0], gathered.shape[0] // BLOCK
    conv_width = cp + 2 * state

    def block(width):
        return pl.BlockSpec((BLOCK, width), lambda i: (i, 0))

    return pl.pallas_call(
        functools.partial(mixer_forward_kernel, S, H, ends.shape[0], state, C),
        grid=(nb,),
        in_specs=[
            pl.BlockSpec(memory_space=pltpu.SMEM), block(gathered.shape[1]), whole(in_w.shape), whole(taps.shape),
            whole(rows.shape), whole(out_w.shape), VMEM,
        ],
        out_specs=[
            block(conv_width), block(cp), block(cp),
            pl.BlockSpec((1, state, cp), lambda i: (i, 0, 0)), block(depth + LANES), ANY,
        ],
        out_shape=[
            jax.ShapeDtypeStruct((T, conv_width), F32),
            jax.ShapeDtypeStruct((T, cp), F32),
            jax.ShapeDtypeStruct((T, cp), F32),
            jax.ShapeDtypeStruct((nb, state, cp), F32),
            jax.ShapeDtypeStruct((T, depth + LANES), B16),
            jax.ShapeDtypeStruct((T, depth), B16),
        ],
        scratch_shapes=[
            pltpu.VMEM((state, cp), F32), pltpu.VMEM((BLOCK + 8, conv_width), F32), *sems(gather_count(S, H)),
            pltpu.SemaphoreType.DMA,
        ],
        compiler_params=talking(5),
    )(ends, gathered, in_w, taps, rows, out_w, grad)


def mixer_backward_kernel(
    S, H, beside, count, state, C, ends_ref, three_ref, one_ref, pre_ref, halo_ref, z_ref, y_ref, st_ref,
    w_ref, taps_ref, rows_ref, cols_ref, out_w_ref, p_ref, sh_ref, res_ref, gres_ref, in_ref, gain_ref, norm2_ref, router_ref,
    sh_out, output_ref, gin_ref, extra_ref, small_out, zx_out, wo_out,
    held, ext, gext, gw_ref, gout_ref, gtaps_ref, gvec_ref, gnorm_ref, total, parts, extra, zx_ref, wo_ref, small, joint,
    *rest,
):
    step = pl.program_id(0)
    i = pl.num_programs(0) - 1 - step
    depth = w_ref.shape[0]
    n, cp = BLOCK, z_ref.shape[1]

    n1, n2 = 8 if beside else 0, 6
    scratch, main, side = rest[:n1], rest[n1 : n1 + n2], rest[n1 + n2 : n1 + n2 + 4]
    send, recv, sh_send, sh_recv, send2, recv2, zsend, zrecv, group_send, group_recv, sh_sem, local_sem = rest[n1 + n2 + 4 :]
    pc = Place(S, H)
    X, Y, Z = pc.X, pc.Y, pc.Z
    N, me, R = S * H, pc.slot(), res_ref.shape[0]
    seq, head = lax.axis_index("seq"), lax.axis_index("head")
    mail = Mail(send, recv)
    sums = scatter(pc, mail, [(p_ref, total, scratch, True)]) if beside else Script([[] for _ in range(9)])

    mail2 = Mail(send2, recv2)
    acts = Script()
    ones = Sum(
        pc, mail2, acts, lambda dz, yy, xx, rows: parts.at[dz, yy, xx, pc.c, rows], lambda dz: parts.at[dz, :, :, 1 - pc.c],
        main, R, ends=(zsend, zrecv),
    )
    for dz in range(Z):
        acts.stage()
        ones.across(dz)
        acts.stage()
        ones.cores(dz)
        acts.stage()
        ones.firsts(dz)
        acts.stage()
        ones.seconds(dz)
    acts.stage()
    ones.home(total)
    tall = extra.shape[4]
    sides = Script()
    other = Sum(
        pc, mail2, sides, lambda dz, yy, xx, rows: extra.at[pc.at(dz=dz)[0], yy, xx, pc.c, rows],
        lambda dz: extra.at[pc.at(dz=dz)[0], :, :, 1 - pc.c],
        side, tall, split=False, direct=True,
    )
    sides.stage()
    for dz in ORDER:
        other.across(dz)
    sides.stage()
    for dz in ORDER:
        other.cores(dz)
    sides.stage()
    for dz in ORDER:
        other.firsts(dz)
    sides.stage()
    for dz in ORDER:
        other.seconds(dz)
    other.last(extra_ref)
    group, keep_here, column, row = [], [], [], []
    for j, (src, dst) in enumerate(((zx_ref, zx_out), (wo_ref, wo_out))):
        keep_here.append(pltpu.make_async_copy(src.at[seq], dst.at[seq], local_sem.at[j]))
        for m in range(1, S):
            to = (seq + m) % S
            group.append(
                pltpu.make_async_remote_copy(
                    src_ref=src.at[to], dst_ref=dst.at[seq], send_sem=group_send.at[j, m],
                    recv_sem=group_recv.at[j, m], device_id=(to, head), device_id_type=MESH,
                )
            )
    for m in range(1, S):
        column.append(
            pltpu.make_async_remote_copy(
                src_ref=small.at[seq], dst_ref=small.at[seq], send_sem=group_send.at[2, m], recv_sem=group_recv.at[2, m],
                device_id=((seq + m) % S, head), device_id_type=MESH,
            )
        )
    for m in range(1, H):
        row.append(
            pltpu.make_async_remote_copy(
                src_ref=joint, dst_ref=small_out.at[head], send_sem=group_send.at[3, m], recv_sem=group_recv.at[3, m],
                device_id=(seq, (head + m) % H), device_id_type=MESH,
            )
        )
    keep_joint = pltpu.make_async_copy(joint, small_out.at[head], local_sem.at[2])
    total_steps = Y * Z
    before = {k: [] for k in range(total_steps)}
    for k, stage in ((2, 2), (3, 3), (4, 4), (5, 5), (6, 6), (7, 7)):
        before[k].append((sums, stage))
    final_acts = []
    for dz in (3, 2, 1, 0):
        for late, stage in ((0, 0), (1, 1), (3, 2), (4, 3)):
            k = (Z - dz) * Y + late
            if k < total_steps:
                before[k].append((acts, 4 * dz + stage))
    final_acts = [(acts, 4 * dz + stage) for dz, stage in ((0, 0), (3, 3), (2, 2), (2, 3), (1, 1), (1, 2), (0, 1), (1, 3), (0, 2), (0, 3))]
    final_acts = [entry for entry in final_acts if all(entry not in before[k] for k in before)]
    stay = pltpu.make_async_copy(sh_ref.at[me], sh_out.at[me], sh_sem)

    def to_all(function, first, last):
        def body(m, carry):
            to = (me + m) % N
            function(
                pltpu.make_async_remote_copy(
                    src_ref=sh_ref.at[to], dst_ref=sh_out.at[me], send_sem=sh_send.at[m], recv_sem=sh_recv.at[m],
                    device_id=(to // H, to % H), device_id_type=MESH,
                )
            )
            return carry

        lax.fori_loop(first, last, body, 0)

    @pl.when(step == 0)
    def _():
        sums.run(0, 1)
        stay.start()
        barrier = pltpu.get_barrier_semaphore()

        def hello(m, carry):
            to = (me + m) % N
            pl.semaphore_signal(barrier, inc=1, device_id=(to // H, to % H), device_id_type=MESH)
            return carry

        lax.fori_loop(1, N, hello, 0)
        pl.semaphore_wait(barrier, N - 1)
        sums.run(1, 2)

    for at in range(1, total_steps):
        if before[at]:

            @pl.when(step == at)
            def _():
                for script, stage in before[at]:
                    script.run(stage, stage + 1)

    @pl.when(step == 1)
    def _():
        to_all(lambda copy: copy.start(), 1, N)

    @pl.when(step == 0)
    def _():
        gnorm_ref[...] = jnp.zeros_like(gnorm_ref)
        held[...] = jnp.zeros_like(held)
        gext[n : n + 8, :] = jnp.zeros((8, gext.shape[1]), F32)
        gw_ref[...] = jnp.zeros_like(gw_ref)
        extra[...] = jnp.zeros_like(extra)
        zx_ref[...] = jnp.zeros_like(zx_ref)
        wo_ref[...] = jnp.zeros_like(wo_ref)
        gout_ref[...] = jnp.zeros_like(gout_ref)
        gtaps_ref[...] = jnp.zeros_like(gtaps_ref)
        gvec_ref[...] = jnp.zeros_like(gvec_ref)

    pre, z, y = pre_ref[...], z_ref[...], y_ref[...]
    ext[0:8, :] = jnp.where(i == 0, 0.0, halo_ref[...])
    ext[8 : 8 + n, :] = pre
    blk = Block(i, pre, ext, z, taps_ref, rows_ref, ends_ref, count, state, C)
    three = three_ref[:, :depth]
    pg = mm(three, out_w_ref[...], NT)
    cross = jnp.sum(three_ref[:, depth:].astype(F32), axis=1, keepdims=True)
    act_z = silu(z)
    gated = y * act_z
    gout_ref[...] += mm((gated * blk.gain).astype(B16), three, TN)
    grad_gated = pg * blk.gain - gated * cross
    gy = grad_gated * act_z
    gz = grad_gated * y * silu_grad(z)
    st = st_ref[0]
    st_low, grad = st.astype(B16), held[...]
    grad_low = grad.astype(B16)
    gy_low = gy.astype(B16)
    y_all = blk.inner() + blk.carry * mm(blk.c, st_low)
    back = sum(mm(blk.mats[j], gy_low * blk.low[j], TN) for j in range(2))
    gate = (blk.carry * gy_low.astype(F32)).astype(B16)
    tail_back = blk.tail * mm(blk.b, grad_low)
    pull = sum(mm(gy_low, blk.xts[j], NT) * blk.decays[j] for j in range(2)).astype(B16)
    g_c = mm(pull, blk.b) + mm(gate, st_low, NT)
    g_b = mm(pull, blk.c, TN) + mm(blk.tail_xt, grad_low, NT)
    held[...] = blk.keep * grad + mm(blk.c, gate, TN)
    g_xt = back + tail_back
    xt = blk.xt.astype(F32)
    cols = cols_ref[...]
    after = exact(gy_low.astype(F32) * y_all - xt * back, cols)
    used = exact(xt * tail_back, cols)
    through = exact(jnp.broadcast_to(blk.keep * jnp.sum(grad * st, axis=0, keepdims=True), (8, cp)), cols)[0:1, :]
    g_rate = (
        exact((blk.row <= blk.col).astype(F32), after) + exact((blk.row > blk.col).astype(F32), used) + through
    )
    g_dt = exact(g_xt * blk.x, cols) - g_rate * blk.decay
    g_dtr = g_dt / (1.0 + jnp.exp(-blk.dtr))
    g_x = g_xt * blk.dtc + blk.skip * gy
    for r, v in enumerate((pg * gated, g_dtr, g_rate * blk.rate, gy * blk.x)):
        gvec_ref[r : r + 1, :] += jnp.sum(v, axis=0, keepdims=True)
    gconv = jnp.concatenate([g_x, g_b, g_c], axis=1) * silu_grad(blk.conv)
    gext[0:n, :] = gconv
    gpre = taps_ref[3:4, :] * gconv
    gtaps_ref[3:4, :] += jnp.sum(gconv * pre, axis=0, keepdims=True)
    for k in (1, 2, 3):
        gpre = gpre + taps_ref[3 - k : 4 - k, :] * gext[k : n + k, :] * blk.later[k]
        gtaps_ref[3 - k : 4 - k, :] += jnp.sum(gconv * ext[8 - k : 8 - k + n, :] * blk.joined[k], axis=0, keepdims=True)
    gext[n : n + 8, :] = gconv[0:8, :]
    made = jnp.concatenate([gz + g_dtr, gpre], axis=1).astype(B16)
    one = one_ref[:, :depth]
    part = mm(made, w_ref[...], NT)
    part_low = part.astype(B16)
    for xx in range(X):
        for cc in range(2):
            at = slice((xx * 2 + cc) * R, (xx * 2 + cc + 1) * R)
            parts[i // Y, i % Y, xx, cc] = part_low[at]
    gnorm_ref[...] += jnp.sum(part * one.astype(F32), axis=0, keepdims=True)
    gw_ref[...] += mm(made, one, TN)

    @pl.when(i == 0)
    def _():
        acts.run(0, 1)
        line = 0
        for ref in (gnorm_ref, norm2_ref):
            for j in range(depth // LANES):
                small[seq, line : line + 1, :] = ref[0:1, j * LANES : (j + 1) * LANES]
                line += 1
        for r in range(4):
            for j in range(2 * state // LANES):
                small[seq, line : line + 1, :] = gtaps_ref[r : r + 1, cp + j * LANES : cp + (j + 1) * LANES]
                line += 1
        small[seq, line : line + 4, :] = gtaps_ref[0:4, :cp]
        small[seq, line + 4 : line + 7, :] = gvec_ref[0:3, :]
        small[seq, line + 7 : line + 8, :] = exact(gvec_ref[...], cols)[3:4, :]
        for copy in column:
            copy.start()
        wide = depth // S
        cut = zx_ref.shape[1]
        for t in range(S):
            at = slice(t * wide, (t + 1) * wide)
            zx_ref[t, :, :wide] = gw_ref[:cut, at].astype(B16)
            zx_ref[t, :, wide:] = gw_ref[cp : cp + cut, at].astype(B16)
            wo_ref[t] = gout_ref[: wo_ref.shape[1], at].astype(B16)
        for copy in keep_here + group:
            copy.start()
        for script, stage in final_acts[1:5]:
            script.run(stage, stage + 1)
        per = depth // N
        bc = gw_ref[2 * cp :, :].T
        router = router_ref[...].astype(F32)
        for t in range(N):
            at = slice(t * per, (t + 1) * per)
            where = (t // (Y * X * 2), t // (X * 2) % Y, t // 2 % X, t % 2)
            extra[(*where, slice(0, per), slice(0, 2 * state))] = bc[at].astype(B16)
            extra[(*where, slice(0, per), slice(2 * state, 2 * state + LANES))] = router[at].astype(B16)
        sides.run(0, 1)
        for script, stage in final_acts[5:7]:
            script.run(stage, stage + 1)
        sides.run(1, 2)
        for copy in column:
            copy.wait_recv()
        joint[0:line, :] = functools.reduce(jnp.add, [small[t, 0:line, :] for t in range(S)])
        for t in range(S):
            joint[line + 8 * t : line + 8 * t + 8, :] = small[t, line : line + 8, :]
        keep_joint.start()
        for copy in row:
            copy.start()
        for script, stage in final_acts[7:]:
            script.run(stage, stage + 1)
        sides.run(2, 3)
        sums.run(8)
        output_ref[...] = res_ref[...] + total[...] if beside else res_ref[...]
        sides.run(3)
        acts.run(4 * Z)
        values, gone = in_ref[...], total[...]
        gin_ref[...] = gres_ref[...] + rms_back(values, inverse_rms(values), gain_ref[...], gone)
        for copy in row:
            copy.wait()
        for copy in column:
            copy.wait_send()
        keep_joint.wait()
        to_all(lambda copy: copy.wait(), 1, N)
        for copy in keep_here + group:
            copy.wait()
        stay.wait()
        mail.finish(scatter_count(S, H) if beside else 0)
        mail2.finish(scatter_count(S, H) - 3 + scatter_count(S, H, (False,)))


def mixer_backward(
    ends, three, one, pre, z, y, states, in_w, taps, rows, cols, out_w, out_part, shared, residual, grad_res, hidden_in, gain,
    norm2, router_part, state, C, S, H,
):
    T, depth = three.shape[0], in_w.shape[0]
    cp, nb = out_w.shape[0], T // BLOCK
    conv_width = cp + 2 * state
    R, N = residual.shape[0], S * H
    X, Y, Z = sizes(S, H)
    line = 2 * (depth // LANES) + 4 * (2 * state // LANES)
    tall = -(-(depth // N) // 16) * 16
    zx_rows = -(-(C + 2) // 16) * 16
    beside = Y == 2
    wo_rows = -(-C // 16) * 16
    assert line % 8 == 0 and cp == LANES and R * H == BLOCK
    sent = scatter_count(S, H) - 3 + scatter_count(S, H, (False,))

    def block(width, kept=2):
        return pl.BlockSpec((BLOCK, width), lambda k: (nb - 1 - k, 0), pipeline_mode=pl.Buffered(kept))

    kept = 2 if beside else 1

    def halo(k):
        return (jnp.maximum((nb - 1 - k) * (BLOCK // 8) - 1, 0), 0)

    return pl.pallas_call(
        functools.partial(mixer_backward_kernel, S, H, beside, ends.shape[0], state, C),
        grid=(nb,),
        in_specs=[
            pl.BlockSpec(memory_space=pltpu.SMEM), block(three.shape[1]), block(one.shape[1], kept), block(conv_width, kept),
            pl.BlockSpec((8, conv_width), halo), block(cp), block(cp),
            pl.BlockSpec((1, state, cp), lambda k: (nb - 1 - k, 0, 0)),
            VMEM, VMEM, VMEM, VMEM, VMEM, ANY, ANY, VMEM, VMEM, VMEM, VMEM, VMEM, VMEM,
        ],
        out_specs=[ANY, VMEM, VMEM, VMEM, ANY, ANY, ANY],
        out_shape=[
            jax.ShapeDtypeStruct(shared.shape, shared.dtype),
            jax.ShapeDtypeStruct((R, depth), F32),
            jax.ShapeDtypeStruct((R, depth), F32),
            jax.ShapeDtypeStruct((tall, 2 * state + LANES), F32),
            jax.ShapeDtypeStruct((H, line + 8 * S, LANES), F32),
            jax.ShapeDtypeStruct((S, zx_rows, 2 * (depth // S)), B16),
            jax.ShapeDtypeStruct((S, wo_rows, depth // S), B16),
        ],
        scratch_shapes=[
            pltpu.VMEM((state, cp), F32),
            pltpu.VMEM((BLOCK + 8, conv_width), F32),
            pltpu.VMEM((BLOCK + 8, conv_width), F32),
            pltpu.VMEM((in_w.shape[1], depth), F32),
            pltpu.VMEM(out_w.shape, F32),
            pltpu.VMEM((8, conv_width), F32),
            pltpu.VMEM((8, cp), F32),
            pltpu.VMEM((1, depth), F32),
            pltpu.VMEM((R, depth), F32),
            pltpu.VMEM((Z, Y, X, 2, R, depth), B16),
            pltpu.VMEM((Z, Y, X, 2, tall, 2 * state + LANES), B16),
            pltpu.VMEM((S, zx_rows, 2 * (depth // S)), B16),
            pltpu.VMEM((S, wo_rows, depth // S), B16),
            pltpu.VMEM((S, line + 8, LANES), F32),
            pltpu.VMEM((line + 8 * S, LANES), F32),
            *(scatter_scratch(S, H, R, depth) if beside else []),
            *sum_scratch(S, H, R, depth),
            *sum_scratch(S, H, tall, 2 * state + LANES, False),
            *sems(scatter_count(S, H)),
            *sems(N),
            *sems(sent),
            pltpu.SemaphoreType.DMA((4,)), pltpu.SemaphoreType.DMA((3,)),
            pltpu.SemaphoreType.DMA((4, S)), pltpu.SemaphoreType.DMA((4, S)),
            pltpu.SemaphoreType.DMA, pltpu.SemaphoreType.DMA((3,)),
        ],
        compiler_params=talking(6),
    )(
        ends, three, one, pre, pre, z, y, states, in_w, taps, rows, cols, out_w, blocks(out_part, S, H), shared, residual,
        grad_res, hidden_in, gain, norm2, router_part,
    )


def expert_block(F, two, grad, named, mine, up_ref, down_ref, gup_ref, gdown_ref, gs_ref):
    mid = mm(two, up_ref[...])
    back = mm(grad, down_ref[...], NT)
    gate, lin = mid[:, :F], mid[:, F : 2 * F]
    s_gate, s_lin = mid[:, 2 * F : 2 * F + LANES], mid[:, 2 * F + LANES :]
    named = named.astype(F32) > 0
    logits = jnp.where(named, s_gate, -1e30)
    odds = jnp.where(named, jnp.exp(logits - jnp.max(logits, axis=1, keepdims=True)), 0.0)
    probs = odds / jnp.sum(odds, axis=1, keepdims=True)
    weight = jnp.sum(probs * mine, axis=1, keepdims=True)
    s_back, back = back[:, F:], back[:, :F]
    act_gate, act_s = silu(gate), silu(s_gate)
    acting = act_gate * lin
    gp = jnp.sum(acting * back, axis=1, keepdims=True)
    back = weight * back
    down_in = jnp.concatenate([weight * acting, act_s * s_lin], axis=1).astype(B16)
    mid_grad = jnp.concatenate(
        [back * lin * silu_grad(gate), back * act_gate, s_back * s_lin * silu_grad(s_gate), s_back * act_s], axis=1
    ).astype(B16)
    gup_ref[...] += mm(two, mid_grad[:, : 2 * F], TN)
    gdown_ref[...] += mm(down_in[:, :F], grad, TN)
    gs_ref[: 2 * LANES, :] += mm(mid_grad[:, 2 * F :], two, TN)
    gs_ref[2 * LANES :, :] += mm(down_in[:, F:], grad, TN)
    out = mm(down_in, down_ref[...]).astype(B16)
    part = mm(mid_grad, up_ref[...], NT).astype(B16)
    return out, part, (gp * mine).astype(B16), probs


def expert_kernel(
    S, H, F, width, p_ref, in_ref, gain_ref, grad_ref, named_ref, up_ref, down_ref, mine_ref, router_ref, ograd_ref,
    rows_ref, res_ref, gres_ref, gnorm_ref, grouter_ref, out_ref, gup_out, gdown_ref, gsh_ref,
    gup_ref, total, rows, two, grads, names, parts, stage_out, probs, gs_ref, *rest,
):
    buffers, (send1, recv1, send2, recv2, own_sem, load_sem, name_sem, grad_sem, out_sem) = rest[:-9], rest[-9:]
    pc = Place(S, H)
    X, Y, Z = pc.X, pc.Y, pc.Z
    R, D = in_ref.shape
    n = BLOCK
    mail1, mail2 = Mail(send1, recv1), Mail(send2, recv2)

    def cell(dz, yy, xx, rows):
        return parts.at[dz, yy, xx, pc.c, rows]

    sums = Script()
    first = Sum(
        pc, mail1, sums, cell, lambda dz: p_ref.at[pc.at(dz=dz)[0], :, :, 1 - pc.c], buffers, R
    )
    own = {
        dz: pltpu.make_async_copy(p_ref.at[pc.at(dz=dz)[0], :, :, pc.c], parts.at[dz, :, :, pc.c], load_sem.at[dz])
        for dz in ORDER
    }
    for copy in own.values():
        copy.start()
    sums.stage()
    for dz in ORDER:
        first.across(dz)
    for dz in ORDER:
        sums.do(own[dz].wait)
        first.cores(dz)
    for dz in ORDER:
        first.firsts(dz)
        if dz < 3:
            first.seconds(dz + 1)
    first.seconds(0)
    first.last(total)

    moves = gather(pc, mail2, rows, two, own_sem, planes=True)
    acts = Script()
    second = Sum(pc, mail2, acts, cell, lambda dz: parts.at[dz, :, :, 1 - pc.c], buffers, R, direct=True)
    for dz in range(Z):
        acts.stage()
        second.across(dz)
        acts.stage()
        second.cores(dz)
        acts.stage()
        second.firsts(dz)
        acts.stage()
        second.seconds(dz)
    acts.stage()
    second.last(total)

    def seq_of(k):
        return pc.partner(k // Y) * Y + k % Y

    def loads(k, slot):
        at = pl.ds(pl.multiple_of(seq_of(k) * n, n), n)
        return [
            pltpu.make_async_copy(grad_ref.at[at], grads.at[slot], grad_sem.at[slot]),
            pltpu.make_async_copy(named_ref.at[at, pl.ds(D, LANES)], names.at[slot], name_sem.at[slot]),
        ]

    def store(k, slot):
        at = pl.ds(pl.multiple_of(seq_of(k) * n, n), n)
        return pltpu.make_async_copy(stage_out.at[slot], out_ref.at[at], out_sem.at[slot])

    for copy in loads(0, 0):
        copy.start()
    gup_ref[...] = jnp.zeros_like(gup_ref)
    gdown_ref[...] = jnp.zeros_like(gdown_ref)
    gs_ref[...] = jnp.zeros_like(gs_ref)
    greet(pc.peers(direct=True))
    sums.run()
    gain = gain_ref[...]
    mixed = total[:, :D]
    square = jnp.sum(total[:, D:], axis=1, keepdims=True)
    inv = lax.rsqrt(square / width + EPS)
    residual = in_ref[...] + inv * mixed
    res_ref[...] = residual
    rows[...] = (residual * inverse_rms(residual) * gain).astype(B16)
    gres_ref[...] = mixed
    cube = inv * inv * inv / width
    moves.run(0, 5)
    for copy in mail1.made:
        copy.wait_send()
    moves.run(12, 13)

    count = Y * Z
    before = {k: [] for k in range(count)}
    after = []
    for dz in range(Z):
        for late, stage in ((0, 0), (1, 1), (3, 2), (4, 3)):
            k = (dz + 1) * Y + late
            before.get(k, after).append((acts, 4 * dz + stage))
    after = [(acts, 4 * dz + stage) for dz, stage in ((3, 0), (1, 2), (1, 3), (2, 2), (3, 1), (2, 3), (3, 2), (3, 3))]
    after = [entry for entry in after if all(entry not in before[k] for k in before)]
    for k, stage in (
        (0, 5), (1, 6), (1, 7), (Y, 8), (Y, 13), (Y + 1, 9), (Y + 1, 10), (2 * Y, 11), (2 * Y, 14), (3 * Y, 15),
    ):
        before[k].append((moves, stage))
    mine = mine_ref[...]

    def step(k, carry):
        for at in range(count):
            if before[at]:

                @pl.when(k == at)
                def _():
                    for script, stage in before[at]:
                        script.run(stage, stage + 1)

        slot = k % 2

        @pl.when(k + 1 < count)
        def _():
            for copy in loads(k + 1, 1 - slot):
                copy.start()

        for copy in loads(k, slot):
            copy.wait()
        block = two[pl.ds(pl.multiple_of(seq_of(k) * n, n), n), :]
        out, part, gp, chance = expert_block(
            F, block, grads[slot], names[slot], mine, up_ref, down_ref, gup_ref, gdown_ref, gs_ref
        )
        for xx in range(X):
            for cc in range(2):
                at = slice((xx * 2 + cc) * R, (xx * 2 + cc + 1) * R)
                parts[k // Y, k % Y, xx, cc, :, :D] = part[at]
                parts[k // Y, k % Y, xx, cc, :, D:] = gp[at]

        @pl.when(k == pc.y)
        def _():
            probs[...] = chance

        @pl.when(k >= 2)
        def _():
            store(k - 2, slot).wait()

        stage_out[slot] = out
        store(k, slot).start()
        return carry

    lax.fori_loop(0, count, step, 0)
    for script, stage in after[:1]:
        script.run(stage, stage + 1)
    for k in range(2):
        gup_out[0, :, k, :] = gup_ref[:, k * F : (k + 1) * F]
    for script, stage in after[1:]:
        script.run(stage, stage + 1)
    for k in range(3):
        gsh_ref[k] = gs_ref[k * LANES : k * LANES + gsh_ref.shape[1], :].astype(B16)
    head = lax.axis_index("head")
    p = probs[pl.ds(pl.multiple_of(head * R, R), R), :]
    acts.run(4 * Z)
    gp = total[:, D:]
    glogits = (p * (gp - jnp.sum(p * gp, axis=1, keepdims=True))).astype(B16)
    gtwo = total[:, :D] + mm(glogits, router_ref[...], NT)
    residual = res_ref[...]
    inv_two = inverse_rms(residual)
    mixed = gres_ref[...]
    gres = ograd_ref[...] + rms_back(residual, inv_two, gain, gtwo)
    cross = jnp.sum(gres * mixed, axis=1, keepdims=True) * cube
    high, low = hi_lo(cross)
    lane = lax.broadcasted_iota(jnp.int32, (R, LANES), 1)
    rows_ref[:, :D] = (inv * gres).astype(B16)
    rows_ref[:, D:] = jnp.where(lane == 0, high.astype(F32), jnp.where(lane == 1, low.astype(F32), 0.0)).astype(B16)
    gres_ref[...] = gres
    gnorm_ref[...] = jnp.sum(gtwo * residual * inv_two, axis=0, keepdims=True)
    grouter_ref[...] = mm((residual * inv_two * gain).astype(B16), glogits, TN).astype(B16)
    for k in (count - 2, count - 1):
        store(k, k % 2).wait()
    mail2.finish(gather_count(S, H) + scatter_count(S, H))


def experts(part, hidden_in, gain, all_grad, gathered, up_w, down_w, mine, router, out_grad, F, FS, width, S, H):
    R, D = hidden_in.shape
    X, Y, Z = sizes(S, H)
    T, W = S * H * R, D + LANES
    tall = -(-FS // 16) * 16
    assert R * H == BLOCK
    return pl.pallas_call(
        functools.partial(expert_kernel, S, H, F, width),
        out_shape=[
            jax.ShapeDtypeStruct((R, W), B16),
            jax.ShapeDtypeStruct((R, D), F32),
            jax.ShapeDtypeStruct((R, D), F32),
            jax.ShapeDtypeStruct((1, D), F32),
            jax.ShapeDtypeStruct((D, LANES), B16),
            jax.ShapeDtypeStruct((T, D), B16),
            jax.ShapeDtypeStruct((1, D, 2, F), F32),
            jax.ShapeDtypeStruct((F, D), F32),
            jax.ShapeDtypeStruct((3, tall, D), B16),
        ],
        in_specs=[ANY, VMEM, VMEM, ANY, ANY] + [VMEM] * 5,
        out_specs=[VMEM] * 5 + [ANY] + [VMEM] * 3,
        scratch_shapes=[
            pltpu.VMEM((D, 2 * F), F32), pltpu.VMEM((R, W), F32), pltpu.VMEM((R, D), B16), pltpu.VMEM((T, D), B16),
            pltpu.VMEM((2, BLOCK, D), B16), pltpu.VMEM((2, BLOCK, LANES), B16),
            pltpu.VMEM((Z, Y, X, 2, R, W), B16), pltpu.VMEM((2, BLOCK, D), B16), pltpu.VMEM((BLOCK, LANES), F32),
            pltpu.VMEM((3 * LANES, D), F32), *sum_scratch(S, H, R, W),
            *sems(scatter_count(S, H)), *sems(scatter_count(S, H) + gather_count(S, H)),
            pltpu.SemaphoreType.DMA, pltpu.SemaphoreType.DMA((Z,)), pltpu.SemaphoreType.DMA((2,)),
            pltpu.SemaphoreType.DMA((2,)), pltpu.SemaphoreType.DMA((2,)),
        ],
        compiler_params=talking(2),
    )(blocks(part, S, H), hidden_in, gain, all_grad, gathered, up_w, down_w, mine, router, out_grad)


def third_kernel(S, H, rows_ref, out_ref, send, recv, own_sem):
    pc = Place(S, H)
    mail = Mail(send, recv)
    moves = gather(pc, mail, rows_ref, out_ref, own_sem)
    greet(pc.peers())
    moves.run()
    mail.finish(gather_count(S, H))


def third_rows(rows, S, H):
    R, W = rows.shape
    return pl.pallas_call(
        functools.partial(third_kernel, S, H),
        out_shape=jax.ShapeDtypeStruct((S * H * R, W), B16),
        in_specs=[VMEM],
        out_specs=ANY,
        scratch_shapes=[*sems(gather_count(S, H)), pltpu.SemaphoreType.DMA],
        compiler_params=talking(3),
    )(rows)


def finish_kernel(
    S, H, C, FS, state, zx_ref, wo_ref, sh_ref, small_ref, pick_ref, gain_ref,
    zx_out, dt_out, wo_out, up_out, down_out, norm1_out, norm2_out, taps_out, bc_out, gate_out, heads_out,
):
    wide = wo_ref.shape[2]
    heads = dt_out.shape[1]
    dt = jnp.zeros(dt_out.shape, F32)
    for t in range(S):
        turned = zx_ref[t].astype(F32).T
        at = slice(t * C, (t + 1) * C)
        zx_out[:, 0, at] = turned[:wide, :C]
        zx_out[:, 1, at] = turned[wide:, :C]
        dt = dt + exact(turned[:wide, :], pick_ref[t, : turned.shape[1], :])
        wo_out[at, :] = wo_ref[t, :C, :].astype(F32)
    dt_out[...] = dt
    N, tall, per = sh_ref.shape[0], sh_ref.shape[1] // 3, sh_ref.shape[2]
    for k in range(2):
        rows = sh_ref[:, k * tall : (k + 1) * tall, :].astype(F32)[:, :FS, :]
        up_out[:, k, :] = rows.reshape(N * FS, per).T
    down_out[...] = sh_ref[:, 2 * tall :, :].astype(F32)[:, :FS, :].reshape(N * FS, per)
    lines = gain_ref.shape[1] // LANES
    total = small_ref[0, : 2 * lines + 4 * (2 * state // LANES), :]
    for h in range(1, H):
        total = total + small_ref[h, : total.shape[0], :]
    for j in range(lines):
        at = slice(j * LANES, (j + 1) * LANES)
        norm1_out[:, at] = total[j : j + 1, :] / gain_ref[:, at]
        norm2_out[:, at] = total[lines + j : lines + j + 1, :]
    line = 2 * lines
    for r in range(4):
        for j in range(2 * state // LANES):
            bc_out[r : r + 1, j * LANES : (j + 1) * LANES] = total[line : line + 1, :]
            line += 1
    for h in range(H):
        by_head = jnp.zeros((8, heads), F32)
        for t in range(S):
            ours = small_ref[h, line + 8 * t : line + 8 * t + 8, :]
            at = slice((h * S + t) * C, (h * S + t + 1) * C)
            taps_out[:, at] = ours[0:4, :C]
            gate_out[:, at] = ours[4:5, :C]
            by_head = by_head + exact(ours, pick_ref[t])
        for r in range(3):
            heads_out[r : r + 1, h * heads : (h + 1) * heads] = by_head[5 + r : 6 + r, :]


def finish(zx, wo, shared, small, pick, gain, C, FS, state, S, H):
    N, per, wide, heads, D = shared.shape[0], shared.shape[2], wo.shape[2], pick.shape[2], gain.shape[1]
    shapes = (
        (wide, 2, S * C), (wide, heads), (S * C, wide), (per, 2, N * FS), (N * FS, per), (1, D), (1, D), (4, S * H * C),
        (4, 2 * state), (1, S * H * C), (3, H * heads),
    )
    return pl.pallas_call(
        functools.partial(finish_kernel, S, H, C, FS, state),
        out_shape=[jax.ShapeDtypeStruct(shape, F32) for shape in shapes],
        in_specs=[VMEM] * 6,
        out_specs=[VMEM] * len(shapes),
        compiler_params=pltpu.CompilerParams(vmem_limit_bytes=56 * 1024 * 1024),
    )(zx, wo, shared, small, pick, gain)


def local(
    hidden_in, norm1_gain, w_zx, w_bc, w_dt, conv_x, conv_bc, dt_bias, a_log, d_skip, gate_gain,
    w_out, norm2_gain, router, expert_up, expert_down, shared_up, shared_down, out_grad,
    seq_lengths, routes,
):
    S, H = lax.axis_size("seq"), lax.axis_size("head")
    N = S * H
    s = lax.axis_index("seq")
    g = s * H + lax.axis_index("head")
    R, D = hidden_in.shape
    heads, inner = dt_bias.shape[0], conv_x.shape[1]
    size = inner // heads
    state = w_bc.shape[1] // 2
    width = inner * H
    C = inner // S
    CP = -(-(C + 2) // LANES) * LANES
    E = N // 2
    F = expert_down.shape[1]
    FS = shared_down.shape[0] // N
    per = D // N

    named = jnp.sum(
        (routes[:, :, None] == jnp.arange(E, dtype=jnp.int32)[None, None, :]).astype(F32), axis=1
    )
    named = jnp.pad(named.astype(B16), ((0, 0), (FS, LANES - FS - E)))
    gain1, gain2 = norm1_gain[None], norm2_gain[None]
    gathered = first_rows(hidden_in, gain1, named, S, H)

    firsts = [min(k * C // size, heads - 2) for k in range(S)]
    first = jnp.minimum(s * C // size, heads - 2)
    channel = jnp.arange(CP)
    masks = jnp.stack(
        [((channel < C) & ((s * C + channel) // size - first == j)).astype(F32) for j in range(2)]
    )

    def mine(values, axis, offset, length):
        return lax.dynamic_slice_in_dim(values, offset, length, axis)

    def channels(values, axis):
        cut = mine(values, axis, s * C, C)
        pads = [(0, 0)] * values.ndim
        pads[axis] = (0, CP - C)
        return jnp.pad(cut, pads)

    def in_free(values):
        return jnp.pad(values, [(0, 0)] * (values.ndim - 1) + [(C, CP - C - 2)])

    zx_w = mine(w_zx, 2, s * C, C)
    in_w = jnp.concatenate(
        [
            zx_w[:, 0], pad_lanes(mine(w_dt, 1, first, 2), CP - C), pad_lanes(zx_w[:, 1], CP), w_bc,
        ],
        axis=1,
    )
    taps = jnp.concatenate([channels(conv_x, 1), conv_bc], axis=1)
    bias, alog, skip = (mine(v, 0, first, 2) for v in (dt_bias, a_log, d_skip))
    gain = channels(gate_gain, 0)
    out_w = channels(w_out, 0)
    rows = jnp.concatenate(
        [masks, (skip @ masks)[None], gain[None], in_free(jnp.stack([bias, jnp.exp(alog)]))], axis=0
    )
    rows = jnp.pad(rows, ((0, 2), (0, 0)))
    cols = in_free(masks.T)
    ends = jnp.cumsum(seq_lengths)

    pre, z, y, states, part, all_grad = mixer_forward(
        ends, gathered, in_w, taps, rows, out_w, out_grad.astype(B16), state, C, S, H
    )

    sup = mine(shared_up, 2, g * FS, FS)
    router_w = jnp.pad(router, ((0, 0), (FS, LANES - FS - E)))
    up_w = jnp.concatenate(
        [
            expert_up[0].reshape(D, 2 * F), sup[:, 0], router_w[:, FS:], pad_lanes(sup[:, 1], LANES),
        ],
        axis=1,
    )
    down_w = jnp.concatenate([expert_down[0], mine(shared_down, 0, g * FS, FS), jnp.zeros((LANES - FS, D), B16)], axis=0)
    is_mine = (jnp.arange(LANES) == FS + g // 2).astype(F32)[None]
    rows_three, residual, grad_res, norm2_part, router_part, out_part, grad_up, grad_down, grad_shared = experts(
        part, hidden_in, gain2, all_grad, gathered, up_w, down_w, is_mine, router_w, out_grad, F, FS, width, S, H
    )
    three = third_rows(rows_three, S, H)

    tall_s = grad_shared.shape[1]
    shared = grad_shared.reshape(3 * tall_s, N, per).transpose(1, 0, 2)
    sh_in, output, grad_in, extra_sum, small, zx_in, wo_in = mixer_backward(
        ends, three, gathered, pre, z, y, states, in_w, taps, rows, cols, out_w, out_part, shared, residual,
        grad_res, hidden_in, gain1, norm2_part, router_part, state, C, S, H,
    )
    if H > 4:
        output = output + lax.psum_scatter(out_part, ("seq", "head"), scatter_dimension=0, tiled=True).astype(F32)
    grad_bc, grad_router = extra_sum[:per, : 2 * state], extra_sum[:per, 2 * state :][:, FS : FS + E]
    pick = jnp.asarray(
        [[[float(c >= C and firsts[k] + c - C == h) for h in range(heads)] for c in range(LANES)] for k in range(S)], F32
    ) * (jnp.arange(LANES) < C + 2).astype(F32)[None, :, None]
    grad_zx, grad_w_dt, grad_w_out, grad_shared_up, grad_shared_down, *found = finish(
        zx_in, wo_in, sh_in, small, pick, gain1, C, FS, state, S, H
    )
    grad_norm1, grad_norm2, grad_conv_x, grad_conv_bc, grad_gate_gain, by_head = found
    grad_norm1, grad_norm2, grad_gate_gain = (v.reshape(-1) for v in (grad_norm1, grad_norm2, grad_gate_gain))
    grad_dt_bias, grad_a_log, grad_d_skip = by_head[0], by_head[1], by_head[2]
    return (
        output, grad_in, grad_norm1, grad_zx, grad_bc, grad_w_dt, grad_conv_x, grad_conv_bc, grad_dt_bias,
        grad_a_log, grad_d_skip, grad_gate_gain, grad_w_out, grad_norm2, grad_router, grad_up, grad_down[None],
        grad_shared_up, grad_shared_down,
    )


def solution(mesh):
    return jax.shard_map(
        local,
        mesh=mesh,
        in_specs=(
            P(("seq", "head"), None),
            P(),
            P(None, None, "head"),
            P(),
            P(None, "head"),
            P(None, "head"),
            P(),
            P("head"),
            P("head"),
            P("head"),
            P("head"),
            P("head", None),
            P(),
            P(),
            P(("seq", "head"), None, None, None),
            P(("seq", "head"), None, None),
            P(),
            P(),
            P(("seq", "head"), None),
            P(),
            P(("seq", "head"), None),
        ),
        out_specs=(
            P(("seq", "head"), None),
            P(("seq", "head"), None),
            P(),
            P("seq", None, "head"),
            P(("seq", "head"), None),
            P("seq", "head"),
            P(),
            P(),
            P(),
            P(),
            P(),
            P(),
            P("head", "seq"),
            P(),
            P(("seq", "head"), None),
            P(("seq", "head"), None, None, None),
            P(("seq", "head"), None, None),
            P(("seq", "head"), None, None),
            P(None, ("seq", "head")),
        ),
        check_vma=False,
    )
```

```python
import functools
import jax
import jax.numpy as jnp
import numpy as np
from jax import lax
from jax.experimental import pallas as pl
from jax.experimental.pallas import tpu as pltpu
from jax.sharding import PartitionSpec as P

MESH = pl.DeviceIdType.MESH
BLOCK = 256
EPS = 1e-05
LANES = 128
B16 = jnp.bfloat16
F32 = jnp.float32


def mm(left, right, dims=(((1,), (0,)), ((), ()))):
    return lax.dot_general(left, right, dims, preferred_element_type=F32)


NT = (((1,), (1,)), ((), ()))
TN = (((0,), (0,)), ((), ()))


def inverse_rms(values):
    return lax.rsqrt(jnp.mean(values * values, axis=-1, keepdims=True) + EPS)


def rms_back(values, inverse, gain, grad):
    weighted = grad * gain
    inner = jnp.mean(weighted * values, axis=-1, keepdims=True)
    return inverse * weighted - values * inverse**3 * inner


def silu_grad(values):
    sig = jax.nn.sigmoid(values)
    return sig * (1.0 + values * (1.0 - sig))


def pad_lanes(values, width):
    return jnp.pad(values, [(0, 0)] * (values.ndim - 1) + [(0, width - values.shape[-1])])


def hi_lo(values):
    high = values.astype(B16)
    return high, (values - high.astype(F32)).astype(B16)


def sizes(seq_size, head_size):
    return head_size // 2, head_size // 2, seq_size // (head_size // 2)


class Place:
    def __init__(self, seq_size, head_size):
        self.H = head_size
        self.X, self.Y, self.Z = sizes(seq_size, head_size)
        assert self.Z == 4
        seq, head = lax.axis_index("seq"), lax.axis_index("head")
        self.z, self.y = seq // self.Y, seq % self.Y
        self.x, self.c = head // 2, head % 2
        z = self.z
        self.partners = (z, z + 1 - 2 * (z % 2), (z + 2) % 4, 3 - z)

    def at(self, dz=0, dy=0, dx=0, dc=0):
        return (
            self.partners[dz],
            (self.y + dy) % self.Y if dy else self.y,
            (self.x + dx) % self.X if dx else self.x,
            1 - self.c if dc else self.c,
        )

    def dev(self, **where):
        z, y, x, c = self.at(**where)
        return (z * self.Y + y, x * 2 + c)

    def slot(self, **where):
        z, y, x, c = self.at(**where)
        return (z * self.Y + y) * self.H + x * 2 + c

    def partner(self, dz):
        return (self.z // 2 + dz // 2) % 2 * 2 + (self.z + dz) % 2

    def peers(self, direct=False):
        out = [self.dev(dz=k) for k in range(1, 4 if direct else 3)]
        out += [self.dev(dy=k) for k in range(1, self.Y)]
        out += [self.dev(dx=k) for k in range(1, self.X)]
        return out + [self.dev(dc=1)]


def greet(peers):
    barrier = pltpu.get_barrier_semaphore()
    for peer in peers:
        pl.semaphore_signal(barrier, inc=1, device_id=peer, device_id_type=MESH)
    pl.semaphore_wait(barrier, len(peers))


class Mail:
    def __init__(self, send, recv):
        self.send, self.recv, self.made = send, recv, []

    def copy(self, src, dst, dev):
        i = len(self.made)
        self.made.append(
            pltpu.make_async_remote_copy(
                src_ref=src, dst_ref=dst, send_sem=self.send.at[i], recv_sem=self.recv.at[i],
                device_id=dev, device_id_type=MESH,
            )
        )
        return self.made[-1]

    def finish(self, count):
        assert len(self.made) == count
        for copy in self.made:
            copy.wait_send()


class Script(list):
    def stage(self):
        self.append([])

    def do(self, action):
        self[-1].append(action)

    def run(self, first=0, last=None):
        for stage in self[first:last]:
            for action in stage:
                action()


def gather_count(S, H):
    X, Y, Z = sizes(S, H)
    return (Z - 1) + 2 * Z * (X + Y - 2) + 2 * Z * (X - 1) * (Y - 1) + X * Y * Z


def gather(pc, mail, x_ref, out_ref, own_sem, planes=False):
    X, Y, Z = pc.X, pc.Y, pc.Z
    R = x_ref.shape[0]
    half = R // 2
    script = Script()

    def rows(part, **where):
        base = pl.multiple_of(pc.slot(**where) * R, R)
        if part is None:
            return out_ref.at[pl.ds(base, R)]
        return out_ref.at[pl.ds(pl.multiple_of(base + part * half, half), half)]

    def send(src, dst, dev):
        copy = mail.copy(src, dst, dev)
        script.do(copy.start)
        return copy

    x_in, y_in, dga, dgb = {}, {}, {}, {}
    sib = {dz: [] for dz in range(Z)}

    def column(dz):
        for part in (0, 1):
            src = x_ref.at[pl.ds(part * half, half)] if dz == 0 else rows(part, dz=dz)
            for k in range(1, X):
                x_in[dz, k, part] = send(src, rows(part, dz=dz), pc.dev(dx=k))
            other = 1 - part
            src = x_ref.at[pl.ds(other * half, half)] if dz == 0 else rows(other, dz=dz)
            for k in range(1, Y):
                y_in[dz, k, other] = send(src, rows(other, dz=dz), pc.dev(dy=k))
        src = x_ref if dz == 0 else rows(None, dz=dz)
        sib[dz].append(send(src, rows(None, dz=dz), pc.dev(dc=1)))

    def onward(dz):
        for k in range(1, X):
            script.do(x_in[dz, k, 0].wait_recv)
            block = rows(0, dz=dz, dx=-k)
            for m in range(1, Y):
                dga[dz, k, m] = send(block, block, pc.dev(dy=m))
        for k in range(1, Y):
            script.do(y_in[dz, k, 1].wait_recv)
            block = rows(1, dz=dz, dy=-k)
            for m in range(1, X):
                dgb[dz, k, m] = send(block, block, pc.dev(dx=m))
        for k in range(1, X):
            script.do(x_in[dz, k, 1].wait_recv)
            block = rows(None, dz=dz, dx=-k)
            sib[dz].append(send(block, block, pc.dev(dc=1)))
        for k in range(1, Y):
            script.do(y_in[dz, k, 0].wait_recv)
            block = rows(None, dz=dz, dy=-k)
            sib[dz].append(send(block, block, pc.dev(dc=1)))

    def corner(dz):
        for k in range(1, X):
            for m in range(1, Y):
                script.do(dga[dz, k, m].wait_recv)
                script.do(dgb[dz, m, k].wait_recv)
                block = rows(None, dz=dz, dx=-k, dy=-m)
                sib[dz].append(send(block, block, pc.dev(dc=1)))

    own = pltpu.make_async_copy(x_ref, rows(None), own_sem)
    script.stage()
    script.do(own.start)
    first = send(x_ref, rows(None), pc.dev(dz=1))
    column(0)
    second = send(x_ref, rows(None), pc.dev(dz=2))
    script.stage()
    script.do(first.wait_recv)
    column(1)
    script.stage()
    onward(0)
    script.stage()
    corner(0)
    script.stage()
    script.do(second.wait_recv)
    third = send(rows(None, dz=2), rows(None, dz=2), pc.dev(dz=1))
    column(2)
    script.stage()
    onward(1)
    script.stage()
    script.do(third.wait_recv)
    column(3)
    script.stage()
    corner(1)
    for dz in (2, 3):
        script.stage()
        onward(dz)
        script.stage()
        corner(dz)
    if not planes:
        for dz in range(Z):
            for copy in sib[dz]:
                script.do(copy.wait_recv)
        script.do(own.wait)
        return script
    for dz in range(Z):
        script.stage()
        for copy in sib[dz]:
            script.do(copy.wait_recv)
        if dz == 0:
            script.do(own.wait)
    return script


def scatter_parts(split):
    return (("y", 0), ("x", 1)) if split else (("x", None),)


def scatter_count(S, H, splits=(True,)):
    X, Y, Z = sizes(S, H)
    pieces = sum(len(scatter_parts(split)) for split in splits)
    return len(splits) * (Z + Z - 1) + pieces * Z * (X + Y - 2)


def sum_scratch(S, H, R, W, split=True):
    X, Y, Z = sizes(S, H)
    out = [pltpu.VMEM((Z, Y, X, R, W), B16), pltpu.VMEM((Z - 1, R, W), B16)]
    for axis, part in scatter_parts(split):
        rows = R if part is None else R // 2
        first, second = (Y, X) if axis == "y" else (X, Y)
        out += [pltpu.VMEM((Z, first - 1, second, rows, W), B16), pltpu.VMEM((Z, second - 1, rows, W), B16)]
    return out


def scatter_scratch(S, H, R, W, split=True):
    X, Y, Z = sizes(S, H)
    return [pltpu.VMEM((Z, Y, X, R, W), B16), *sum_scratch(S, H, R, W, split), pltpu.SemaphoreType.DMA((Z,))]


def accumulate(dst, srcs, rows):
    def action():
        def body(i, carry):
            at = pl.ds(pl.multiple_of(i * 16, 16), 16)
            total = dst.at[at][...].astype(F32)
            for src in srcs:
                total = total + src.at[at][...].astype(F32)
            dst.at[at][...] = total.astype(dst.dtype)
            return carry

        lax.fori_loop(0, rows // 16, body, 0)

    return action


ORDER = (3, 2, 1, 0)


class Sum:
    def __init__(self, pc, mail, script, cell, theirs, buffers, R, split=True, direct=False, ends=None):
        self.ends = ends
        self.pc, self.mail, self.script, self.cell, self.theirs = pc, mail, script, cell, theirs
        self.r0, self.r3, self.buffers, self.R, self.split, self.direct = buffers[0], buffers[1], buffers[2:], R, split, direct
        self.sib, self.one, self.two, self.zs = {}, {}, {}, {}

    def send(self, src, dst, dev):
        copy = self.mail.copy(src, dst, dev)
        self.script.do(copy.start)
        return copy

    def pieces(self):
        R = self.R
        for j, (axis, part) in enumerate(scatter_parts(self.split)):
            rows, size = (pl.ds(0, R), R) if part is None else (pl.ds(part * (R // 2), R // 2), R // 2)
            yield j, axis, rows, size, self.buffers[2 * j], self.buffers[2 * j + 1]

    def across(self, dz):
        self.sib[dz] = self.send(self.theirs(dz), self.r0.at[dz], self.pc.dev(dc=1))

    def cores(self, dz):
        pc, whole = self.pc, pl.ds(0, self.R)
        self.script.do(self.sib[dz].wait_recv)
        for yy in range(pc.Y):
            for xx in range(pc.X):
                self.script.do(accumulate(self.cell(dz, yy, xx, whole), [self.r0.at[dz, yy, xx]], self.R))
        for j, axis, rows, size, r1, r2 in self.pieces():
            for k in range(1, pc.Y if axis == "y" else pc.X):
                if axis == "y":
                    src, dev = self.cell(dz, pc.at(dy=k)[1], slice(None), rows), pc.dev(dy=k)
                else:
                    src, dev = self.cell(dz, slice(None), pc.at(dx=k)[2], rows), pc.dev(dx=k)
                self.one[dz, j, k] = self.send(src, r1.at[dz, k - 1], dev)

    def firsts(self, dz):
        pc = self.pc
        for j, axis, rows, size, r1, r2 in self.pieces():
            steps = range(1, pc.Y if axis == "y" else pc.X)
            for k in steps:
                self.script.do(self.one[dz, j, k].wait_recv)
            for m in range(pc.X if axis == "y" else pc.Y):
                dst = self.cell(dz, pc.y, m, rows) if axis == "y" else self.cell(dz, m, pc.x, rows)
                self.script.do(accumulate(dst, [r1.at[dz, k - 1, m] for k in steps], size))
            for k in range(1, pc.X if axis == "y" else pc.Y):
                if axis == "y":
                    src, dev = self.cell(dz, pc.y, pc.at(dx=k)[2], rows), pc.dev(dx=k)
                else:
                    src, dev = self.cell(dz, pc.at(dy=k)[1], pc.x, rows), pc.dev(dy=k)
                self.two[dz, j, k] = self.send(src, r2.at[dz, k - 1], dev)

    def seconds(self, dz):
        pc = self.pc
        for j, axis, rows, size, r1, r2 in self.pieces():
            steps = range(1, pc.X if axis == "y" else pc.Y)
            for k in steps:
                self.script.do(self.two[dz, j, k].wait_recv)
            mine = self.cell(dz, pc.y, pc.x, rows)
            self.script.do(accumulate(mine, [r2.at[dz, k - 1] for k in steps], size))
        mine = self.cell(dz, pc.y, pc.x, pl.ds(0, self.R))
        if self.ends is not None:
            self.homeward(dz, mine)
            return
        if self.direct:
            if dz:
                self.zs[dz] = self.send(mine, self.r3.at[dz - 1], pc.dev(dz=dz))
            return
        if dz == 2:
            self.script.do(self.zs[3].wait_recv)
            self.script.do(accumulate(mine, [self.r3.at[0]], self.R))
        if dz:
            self.zs[dz] = self.send(mine, self.r3.at[3 - dz], pc.dev(dz=2 if dz == 2 else 1))

    def homeward(self, plane, mine):
        pc, (zsend, zrecv) = self.pc, self.ends
        at = (pc.z - plane + 3) % 4
        copy = pltpu.make_async_remote_copy(
            src_ref=mine, dst_ref=self.r3.at[at], send_sem=zsend.at[plane], recv_sem=zrecv.at[at],
            device_id=(plane * pc.Y + pc.y, pc.x * 2 + pc.c), device_id_type=MESH,
        )
        self.zs[plane] = copy

        def start():
            @pl.when(pc.z != plane)
            def _():
                copy.start()

        self.script.do(start)

    def home(self, total):
        pc, (zsend, zrecv) = self.pc, self.ends
        mine = self.cell(pc.z, pc.y, pc.x, pl.ds(0, self.R))
        copies = [
            pltpu.make_async_remote_copy(
                src_ref=mine, dst_ref=self.r3.at[k], send_sem=zsend.at[0], recv_sem=zrecv.at[k],
                device_id=pc.dev(dz=1), device_id_type=MESH,
            )
            for k in range(3)
        ]

        def body(i, carry):
            at = pl.ds(pl.multiple_of(i * 16, 16), 16)
            value = mine.at[at][...].astype(F32)
            for k in range(3):
                value = value + self.r3.at[k, at][...].astype(F32)
            total.at[at][...] = value
            return carry

        def sent():
            for plane in range(4):

                @pl.when(pc.z != plane)
                def _():
                    self.zs[plane].wait_send()

        for copy in copies:
            self.script.do(copy.wait_recv)
        self.script.do(lambda: lax.fori_loop(0, self.R // 16, body, 0))
        self.script.do(sent)

    def last(self, total):
        ends = (1, 2, 3) if self.direct else (2, 1)
        slots = (0, 1, 2) if self.direct else (1, 2)
        for dz in ends:
            self.script.do(self.zs[dz].wait_recv)
        pc, mine = self.pc, self.cell(0, self.pc.y, self.pc.x, pl.ds(0, self.R))

        def body(i, carry):
            at = pl.ds(pl.multiple_of(i * 16, 16), 16)
            value = mine.at[at][...].astype(F32)
            for k in slots:
                value = value + self.r3.at[k, at][...].astype(F32)
            total.at[at][...] = value
            return carry

        self.script.do(lambda: lax.fori_loop(0, self.R // 16, body, 0))


def scatter(pc, mail, jobs):
    script = Script()
    own, sums = {}, []

    def make(p_ref, t0, scratch, split):
        return Sum(
            pc, mail, script, lambda dz, yy, xx, rows: t0.at[dz, yy, xx, rows],
            lambda dz: p_ref.at[pc.at(dz=dz)[0], :, :, 1 - pc.c], scratch[1:-1], p_ref.shape[4], split,
        )

    for p_ref, total, scratch, split in jobs:
        sums.append(make(p_ref, scratch[0], scratch, split))
    script.stage()
    for o, (p_ref, total, scratch, split) in enumerate(jobs):
        for dz in ORDER:
            own[o, dz] = pltpu.make_async_copy(
                p_ref.at[pc.at(dz=dz)[0], :, :, pc.c], scratch[0].at[dz], scratch[-1].at[dz]
            )
            script.do(own[o, dz].start)
    script.stage()
    for dz in ORDER:
        for each in sums:
            each.across(dz)

    def cores(dz):
        for o, each in enumerate(sums):
            script.do(own[o, dz].wait)
            each.cores(dz)

    script.stage()
    cores(3)
    cores(2)
    script.stage()
    cores(1)
    cores(0)
    script.stage()
    for dz in ORDER:
        if dz < 3:
            script.stage()
        for each in sums:
            each.firsts(dz)
        if dz < 3:
            for each in sums:
                each.seconds(dz + 1)
    script.stage()
    for each, (p_ref, total, scratch, split) in zip(sums, jobs):
        each.seconds(0)
        each.last(total)
    return script


ANY = pl.BlockSpec(memory_space=pl.ANY)
VMEM = pl.BlockSpec(memory_space=pltpu.VMEM)


def sems(count):
    return [pltpu.SemaphoreType.DMA((count,)), pltpu.SemaphoreType.DMA((count,))]


def talking(cid):
    return pltpu.CompilerParams(collective_id=cid, has_side_effects=True, vmem_limit_bytes=60 * 1024 * 1024)


def blocks(part, S, H):
    X, Y, Z = sizes(S, H)
    return part.reshape(Z, Y, X, 2, part.shape[0] // (S * H), part.shape[1])


def first_kernel(S, H, in_ref, gain_ref, named_ref, out_ref, rows, send, recv, own_sem):
    pc = Place(S, H)
    D = in_ref.shape[1]
    values = in_ref[...]
    rows[:, :D] = (values * inverse_rms(values) * gain_ref[...]).astype(B16)
    rows[:, D:] = named_ref[...]
    mail = Mail(send, recv)
    moves = gather(pc, mail, rows, out_ref, own_sem)
    greet(pc.peers())
    moves.run()
    mail.finish(gather_count(S, H))


def first_rows(hidden_in, gain, named, S, H):
    R, D = hidden_in.shape
    W = D + LANES
    return pl.pallas_call(
        functools.partial(first_kernel, S, H),
        out_shape=jax.ShapeDtypeStruct((S * H * R, W), B16),
        in_specs=[VMEM] * 3,
        out_specs=ANY,
        scratch_shapes=[pltpu.VMEM((R, W), B16), *sems(gather_count(S, H)), pltpu.SemaphoreType.DMA],
        compiler_params=talking(1),
    )(hidden_in, gain, named)


def seg_of(pos, ends_ref, count):
    found = jnp.zeros(pos.shape, jnp.int32)
    for k in range(count):
        found = found + (pos >= ends_ref[k]).astype(jnp.int32)
    return jnp.where(pos < 0, -1, found)


def exact(left, right):
    return jnp.dot(left, right, precision=lax.Precision.HIGHEST, preferred_element_type=F32)


def silu(values):
    return values / (1.0 + jnp.exp(-values))


def softplus(values):
    return jnp.maximum(values, 0.0) + jnp.log1p(jnp.exp(-jnp.abs(values)))


class Block:
    def __init__(self, i, pre, ext, z, taps_ref, rows_ref, ends_ref, count, state, C):
        n = BLOCK
        pos = i * n + lax.broadcasted_iota(jnp.int32, (n, 1), 0)
        pos_row = i * n + lax.broadcasted_iota(jnp.int32, (1, n), 1)
        seg, seg_row = seg_of(pos, ends_ref, count), seg_of(pos_row, ends_ref, count)
        self.joined = {k: ((pos >= k) & (seg_of(pos - k, ends_ref, count) == seg)).astype(F32) for k in (1, 2, 3)}
        self.later = {k: (seg_of(pos + k, ends_ref, count) == seg).astype(F32) for k in (1, 2, 3)}
        conv = taps_ref[3:4, :] * pre
        for k in (1, 2, 3):
            conv = conv + taps_ref[3 - k : 4 - k, :] * ext[8 - k : 8 - k + n, :] * self.joined[k]
        act = silu(conv)
        cp = act.shape[1] - 2 * state
        self.conv = conv
        self.x, self.b, self.c = act[:, :cp], act[:, cp : cp + state].astype(B16), act[:, cp + state :].astype(B16)
        self.m = [rows_ref[j : j + 1, :] for j in range(2)]
        self.skip, self.gain = rows_ref[2:3, :], rows_ref[3:4, :]
        self.C = C
        self.dtr = z + rows_ref[4:5, :]
        self.dt = softplus(self.dtr)
        self.decay = rows_ref[5:6, :]
        self.rate = -self.dt * self.decay
        row, col = lax.broadcasted_iota(jnp.int32, (n, n), 0), lax.broadcasted_iota(jnp.int32, (n, n), 1)
        lower = row >= col
        self.row, self.col = row, col
        logdec = exact(lower.astype(F32), self.rate)
        log_row = logdec.T
        linked = lower & (seg == seg_row)
        self.decays = [
            jnp.exp(jnp.where(linked, logdec[:, C + j : C + j + 1] - log_row[C + j : C + j + 1, :], -1e30)) for j in range(2)
        ]
        scores = mm(self.c, self.b, NT)
        self.mats = [(scores * d).astype(B16) for d in self.decays]
        before = jnp.where(i == 0, -1, seg_of(jnp.full((1, 1), i * n - 1, jnp.int32), ends_ref, count))
        final = seg_of(jnp.full((1, 1), i * n + n - 1, jnp.int32), ends_ref, count)
        last = logdec[n - 1 : n, :]
        self.carry = self.spread(jnp.where(seg == before, jnp.exp(logdec), 0.0))
        self.tail = self.spread(jnp.where(seg == final, jnp.exp(last - logdec), 0.0))
        self.keep = self.spread(jnp.where(final == before, jnp.exp(last), 0.0))
        self.dtc = self.spread(self.dt)
        self.xt = (self.dtc * self.x).astype(B16)
        self.low = [m.astype(B16) for m in self.m]
        self.xts = [self.xt * low for low in self.low]
        self.tail_xt = (self.tail * self.xt.astype(F32)).astype(B16)

    def spread(self, values):
        return values[:, self.C : self.C + 1] * self.m[0] + values[:, self.C + 1 : self.C + 2] * self.m[1]

    def inner(self):
        return mm(self.mats[0], self.xts[0]) + mm(self.mats[1], self.xts[1])


def mixer_forward_kernel(
    S, H, count, state, C, ends_ref, in_ref, w_ref, taps_ref, rows_ref, out_w_ref, grad_ref,
    pre_ref, z_ref, y_ref, st_ref, total_ref, all_ref, held, ext, parts, *rest,
):
    i = pl.program_id(0)
    pc = Place(S, H)
    buffers, (send, recv, zsend, zrecv, own_sem) = rest[:-5], rest[-5:]
    X, Y, Z = pc.X, pc.Y, pc.Z
    R = grad_ref.shape[0]
    mail = Mail(send, recv)
    moves = gather(pc, mail, grad_ref, all_ref, own_sem)
    acts = Script()
    sums = Sum(
        pc, mail, acts, lambda dz, yy, xx, rows: parts.at[dz, yy, xx, pc.c, rows], lambda dz: parts.at[dz, :, :, 1 - pc.c],
        buffers, R, ends=(zsend, zrecv),
    )
    for dz in range(Z):
        acts.stage()
        sums.across(dz)
        acts.stage()
        sums.cores(dz)
        acts.stage()
        sums.firsts(dz)
        acts.stage()
        sums.seconds(dz)
    acts.stage()
    sums.home(total_ref)
    ready = Y * Z - 1
    before = {k: [] for k in range(Y * Z)}
    for dz in range(Z):
        for late, stage in ((0, 0), (1, 1), (3, 2), (4, 3)):
            k = (dz + 1) * Y + late
            if k <= ready:
                before[k].append((acts, 4 * dz + stage))
    final_acts = [
        (acts, 4 * dz + stage)
        for dz, stage in ((3, 0), (0, 3), (1, 2), (1, 3), (2, 1), (2, 2), (3, 1), (2, 3), (3, 2), (3, 3))
    ]
    final_acts = [entry for entry in final_acts if all(entry not in before[k] for k in before)]

    @pl.when(i == 0)
    def _():
        greet(pc.peers(direct=True))
        moves.run(0, 1)

    for step, stage, until in ((1, 1, 2), (2, 2, 3), (3, 3, 5), (4, 5, 7), (5, 7, 9), (6, 9, 11)):

        @pl.when(i == step)
        def _():
            moves.run(stage, until)

    for at in range(1, Y * Z):
        if before[at]:

            @pl.when(i == at)
            def _():
                for script, stage in before[at]:
                    script.run(stage, stage + 1)

    depth = w_ref.shape[0]
    n, cp = BLOCK, z_ref.shape[1]

    @pl.when(i == 0)
    def _():
        held[...] = jnp.zeros_like(held)
        ext[0:8, :] = jnp.zeros((8, ext.shape[1]), F32)

    made = mm(in_ref[:, :depth], w_ref[...])
    z = made[:, :cp]
    pre = made[:, cp:]
    z_ref[...], pre_ref[...] = z, pre
    ext[8 : 8 + n, :] = pre
    blk = Block(i, pre, ext, z, taps_ref, rows_ref, ends_ref, count, state, C)
    ext[0:8, :] = pre[n - 8 :, :]
    st = held[...]
    st_ref[0] = st
    y = blk.inner() + blk.carry * mm(blk.c, st.astype(B16))
    held[...] = blk.keep * st + mm(blk.b, blk.tail_xt, TN)
    y = y + blk.skip * blk.x
    y_ref[...] = y
    gated = y * silu(z)
    part = mm((gated * blk.gain).astype(B16), out_w_ref[...]).astype(B16)
    high, rest = hi_lo(jnp.sum(gated * gated, axis=1, keepdims=True))
    lane = lax.broadcasted_iota(jnp.int32, (n, LANES), 1)
    tail = jnp.where(lane == 0, high.astype(F32), jnp.where(lane == 1, rest.astype(F32), 0.0)).astype(B16)
    for xx in range(X):
        for cc in range(2):
            at = slice((xx * 2 + cc) * R, (xx * 2 + cc + 1) * R)
            parts[i // Y, i % Y, xx, cc, :, :depth] = part[at]
            parts[i // Y, i % Y, xx, cc, :, depth:] = tail[at]

    @pl.when(i == ready)
    def _():
        for script, stage in final_acts[:4]:
            script.run(stage, stage + 1)
        moves.run(11)
        for script, stage in final_acts[4:]:
            script.run(stage, stage + 1)
        acts.run(4 * Z)
        mail.finish(gather_count(S, H) + scatter_count(S, H) - 3)


def whole(shape):
    return pl.BlockSpec(shape, lambda i: (0,) * len(shape))


def params():
    return pltpu.CompilerParams(dimension_semantics=("arbitrary",), vmem_limit_bytes=60 * 1024 * 1024)


def mixer_forward(ends, gathered, in_w, taps, rows, out_w, grad, state, C, S, H):
    T, depth = gathered.shape[0], in_w.shape[0]
    X, Y, Z = sizes(S, H)
    R = grad.shape[0]
    cp, nb = out_w.shape[0], gathered.shape[0] // BLOCK
    conv_width = cp + 2 * state

    def block(width):
        return pl.BlockSpec((BLOCK, width), lambda i: (i, 0))

    return pl.pallas_call(
        functools.partial(mixer_forward_kernel, S, H, ends.shape[0], state, C),
        grid=(nb,),
        in_specs=[
            pl.BlockSpec(memory_space=pltpu.SMEM), block(gathered.shape[1]), whole(in_w.shape), whole(taps.shape),
            whole(rows.shape), whole(out_w.shape), VMEM,
        ],
        out_specs=[
            block(conv_width), block(cp), block(cp),
            pl.BlockSpec((1, state, cp), lambda i: (i, 0, 0)), VMEM, ANY,
        ],
        out_shape=[
            jax.ShapeDtypeStruct((T, conv_width), F32),
            jax.ShapeDtypeStruct((T, cp), F32),
            jax.ShapeDtypeStruct((T, cp), F32),
            jax.ShapeDtypeStruct((nb, state, cp), F32),
            jax.ShapeDtypeStruct((R, depth + LANES), F32),
            jax.ShapeDtypeStruct((T, depth), B16),
        ],
        scratch_shapes=[
            pltpu.VMEM((state, cp), F32), pltpu.VMEM((BLOCK + 8, conv_width), F32),
            pltpu.VMEM((Z, Y, X, 2, R, depth + LANES), B16), *sum_scratch(S, H, R, depth + LANES),
            *sems(gather_count(S, H) + scatter_count(S, H) - 3),
            pltpu.SemaphoreType.DMA((4,)), pltpu.SemaphoreType.DMA((3,)), pltpu.SemaphoreType.DMA,
        ],
        compiler_params=talking(5),
    )(ends, gathered, in_w, taps, rows, out_w, grad)


def mixer_backward_kernel(
    S, H, beside, count, state, C, ends_ref, three_ref, one_ref, pre_ref, halo_ref, z_ref, y_ref, st_ref,
    w_ref, taps_ref, rows_ref, cols_ref, out_w_ref, p_ref, res_ref, gres_ref, in_ref, gain_ref, norm2_ref, router_ref,
    output_ref, gin_ref, extra_ref, small_out, zx_out, wo_out,
    held, ext, gext, gw_ref, gout_ref, gtaps_ref, gvec_ref, gnorm_ref, total, parts, extra, zx_ref, wo_ref, small, joint,
    *rest,
):
    step = pl.program_id(0)
    i = pl.num_programs(0) - 1 - step
    depth = w_ref.shape[0]
    n, cp = BLOCK, z_ref.shape[1]

    n1, n2 = 8 if beside else 0, 6
    scratch, main, side = rest[:n1], rest[n1 : n1 + n2], rest[n1 + n2 : n1 + n2 + 4]
    send, recv, send2, recv2, zsend, zrecv, group_send, group_recv, local_sem = rest[n1 + n2 + 4 :]
    pc = Place(S, H)
    X, Y, Z = pc.X, pc.Y, pc.Z
    N, me, R = S * H, pc.slot(), res_ref.shape[0]
    seq, head = lax.axis_index("seq"), lax.axis_index("head")
    mail = Mail(send, recv)
    sums = scatter(pc, mail, [(p_ref, total, scratch, True)]) if beside else Script([[] for _ in range(9)])

    mail2 = Mail(send2, recv2)
    acts = Script()
    ones = Sum(
        pc, mail2, acts, lambda dz, yy, xx, rows: parts.at[dz, yy, xx, pc.c, rows], lambda dz: parts.at[dz, :, :, 1 - pc.c],
        main, R, ends=(zsend, zrecv),
    )
    for dz in range(Z):
        acts.stage()
        ones.across(dz)
        acts.stage()
        ones.cores(dz)
        acts.stage()
        ones.firsts(dz)
        acts.stage()
        ones.seconds(dz)
    acts.stage()
    ones.home(total)
    tall = extra.shape[4]
    sides = Script()
    other = Sum(
        pc, mail2, sides, lambda dz, yy, xx, rows: extra.at[pc.at(dz=dz)[0], yy, xx, pc.c, rows],
        lambda dz: extra.at[pc.at(dz=dz)[0], :, :, 1 - pc.c],
        side, tall, split=False, direct=True,
    )
    sides.stage()
    for dz in ORDER:
        other.across(dz)
    sides.stage()
    for dz in ORDER:
        other.cores(dz)
    sides.stage()
    for dz in ORDER:
        other.firsts(dz)
    sides.stage()
    for dz in ORDER:
        other.seconds(dz)
    other.last(extra_ref)
    group, keep_here, column, row = [], [], [], []
    for j, (src, dst) in enumerate(((zx_ref, zx_out), (wo_ref, wo_out))):
        keep_here.append(pltpu.make_async_copy(src.at[seq], dst.at[seq], local_sem.at[j]))
        for m in range(1, S):
            to = (seq + m) % S
            group.append(
                pltpu.make_async_remote_copy(
                    src_ref=src.at[to], dst_ref=dst.at[seq], send_sem=group_send.at[j, m],
                    recv_sem=group_recv.at[j, m], device_id=(to, head), device_id_type=MESH,
                )
            )
    for m in range(1, S):
        column.append(
            pltpu.make_async_remote_copy(
                src_ref=small.at[seq], dst_ref=small.at[seq], send_sem=group_send.at[2, m], recv_sem=group_recv.at[2, m],
                device_id=((seq + m) % S, head), device_id_type=MESH,
            )
        )
    for m in range(1, H):
        row.append(
            pltpu.make_async_remote_copy(
                src_ref=joint, dst_ref=small_out.at[head], send_sem=group_send.at[3, m], recv_sem=group_recv.at[3, m],
                device_id=(seq, (head + m) % H), device_id_type=MESH,
            )
        )
    keep_joint = pltpu.make_async_copy(joint, small_out.at[head], local_sem.at[2])
    total_steps = Y * Z
    before = {k: [] for k in range(total_steps)}
    for k, stage in ((2, 2), (3, 3), (4, 4), (5, 5), (6, 6), (7, 7)):
        before[k].append((sums, stage))
    final_acts = []
    for dz in (3, 2, 1, 0):
        for late, stage in ((0, 0), (1, 1), (3, 2), (4, 3)):
            k = (Z - dz) * Y + late
            if k < total_steps:
                before[k].append((acts, 4 * dz + stage))
    final_acts = [(acts, 4 * dz + stage) for dz, stage in ((0, 0), (3, 3), (2, 2), (2, 3), (1, 1), (1, 2), (0, 1), (1, 3), (0, 2), (0, 3))]
    final_acts = [entry for entry in final_acts if all(entry not in before[k] for k in before)]
    @pl.when(step == 0)
    def _():
        sums.run(0, 1)
        greet([((seq + m) % S, head) for m in range(1, S)] + [(seq, (head + m) % H) for m in range(1, H)])
        sums.run(1, 2)

    for at in range(1, total_steps):
        if before[at]:

            @pl.when(step == at)
            def _():
                for script, stage in before[at]:
                    script.run(stage, stage + 1)

    @pl.when(step == 0)
    def _():
        gnorm_ref[...] = jnp.zeros_like(gnorm_ref)
        held[...] = jnp.zeros_like(held)
        gext[n : n + 8, :] = jnp.zeros((8, gext.shape[1]), F32)
        gw_ref[...] = jnp.zeros_like(gw_ref)
        extra[...] = jnp.zeros_like(extra)
        zx_ref[...] = jnp.zeros_like(zx_ref)
        wo_ref[...] = jnp.zeros_like(wo_ref)
        gout_ref[...] = jnp.zeros_like(gout_ref)
        gtaps_ref[...] = jnp.zeros_like(gtaps_ref)
        gvec_ref[...] = jnp.zeros_like(gvec_ref)

    pre, z, y = pre_ref[...], z_ref[...], y_ref[...]
    ext[0:8, :] = jnp.where(i == 0, 0.0, halo_ref[...])
    ext[8 : 8 + n, :] = pre
    blk = Block(i, pre, ext, z, taps_ref, rows_ref, ends_ref, count, state, C)
    three = three_ref[:, :depth]
    pg = mm(three, out_w_ref[...], NT)
    cross = jnp.sum(three_ref[:, depth:].astype(F32), axis=1, keepdims=True)
    act_z = silu(z)
    gated = y * act_z
    gout_ref[...] += mm((gated * blk.gain).astype(B16), three, TN)
    grad_gated = pg * blk.gain - gated * cross
    gy = grad_gated * act_z
    gz = grad_gated * y * silu_grad(z)
    st = st_ref[0]
    st_low, grad = st.astype(B16), held[...]
    grad_low = grad.astype(B16)
    gy_low = gy.astype(B16)
    y_all = blk.inner() + blk.carry * mm(blk.c, st_low)
    back = sum(mm(blk.mats[j], gy_low * blk.low[j], TN) for j in range(2))
    gate = (blk.carry * gy_low.astype(F32)).astype(B16)
    tail_back = blk.tail * mm(blk.b, grad_low)
    pull = sum(mm(gy_low, blk.xts[j], NT) * blk.decays[j] for j in range(2)).astype(B16)
    g_c = mm(pull, blk.b) + mm(gate, st_low, NT)
    g_b = mm(pull, blk.c, TN) + mm(blk.tail_xt, grad_low, NT)
    held[...] = blk.keep * grad + mm(blk.c, gate, TN)
    g_xt = back + tail_back
    xt = blk.xt.astype(F32)
    cols = cols_ref[...]
    after = exact(gy_low.astype(F32) * y_all - xt * back, cols)
    used = exact(xt * tail_back, cols)
    through = exact(jnp.broadcast_to(blk.keep * jnp.sum(grad * st, axis=0, keepdims=True), (8, cp)), cols)[0:1, :]
    g_rate = (
        exact((blk.row <= blk.col).astype(F32), after) + exact((blk.row > blk.col).astype(F32), used) + through
    )
    g_dt = exact(g_xt * blk.x, cols) - g_rate * blk.decay
    g_dtr = g_dt / (1.0 + jnp.exp(-blk.dtr))
    g_x = g_xt * blk.dtc + blk.skip * gy
    for r, v in enumerate((pg * gated, g_dtr, g_rate * blk.rate, gy * blk.x)):
        gvec_ref[r : r + 1, :] += jnp.sum(v, axis=0, keepdims=True)
    gconv = jnp.concatenate([g_x, g_b, g_c], axis=1) * silu_grad(blk.conv)
    gext[0:n, :] = gconv
    gpre = taps_ref[3:4, :] * gconv
    gtaps_ref[3:4, :] += jnp.sum(gconv * pre, axis=0, keepdims=True)
    for k in (1, 2, 3):
        gpre = gpre + taps_ref[3 - k : 4 - k, :] * gext[k : n + k, :] * blk.later[k]
        gtaps_ref[3 - k : 4 - k, :] += jnp.sum(gconv * ext[8 - k : 8 - k + n, :] * blk.joined[k], axis=0, keepdims=True)
    gext[n : n + 8, :] = gconv[0:8, :]
    made = jnp.concatenate([gz + g_dtr, gpre], axis=1).astype(B16)
    one = one_ref[:, :depth]
    part = mm(made, w_ref[...], NT)
    part_low = part.astype(B16)
    for xx in range(X):
        for cc in range(2):
            at = slice((xx * 2 + cc) * R, (xx * 2 + cc + 1) * R)
            parts[i // Y, i % Y, xx, cc] = part_low[at]
    gnorm_ref[...] += jnp.sum(part * one.astype(F32), axis=0, keepdims=True)
    gw_ref[...] += mm(made, one, TN)

    @pl.when(i == 0)
    def _():
        acts.run(0, 1)
        line = 0
        for ref in (gnorm_ref, norm2_ref):
            for j in range(depth // LANES):
                small[seq, line : line + 1, :] = ref[0:1, j * LANES : (j + 1) * LANES]
                line += 1
        for r in range(4):
            for j in range(2 * state // LANES):
                small[seq, line : line + 1, :] = gtaps_ref[r : r + 1, cp + j * LANES : cp + (j + 1) * LANES]
                line += 1
        small[seq, line : line + 4, :] = gtaps_ref[0:4, :cp]
        small[seq, line + 4 : line + 7, :] = gvec_ref[0:3, :]
        small[seq, line + 7 : line + 8, :] = exact(gvec_ref[...], cols)[3:4, :]
        for copy in column:
            copy.start()
        wide = depth // S
        cut = zx_ref.shape[1]
        for t in range(S):
            at = slice(t * wide, (t + 1) * wide)
            zx_ref[t, :, :wide] = gw_ref[:cut, at].astype(B16)
            zx_ref[t, :, wide:] = gw_ref[cp : cp + cut, at].astype(B16)
            wo_ref[t] = gout_ref[: wo_ref.shape[1], at].astype(B16)
        for copy in keep_here + group:
            copy.start()
        for script, stage in final_acts[1:5]:
            script.run(stage, stage + 1)
        per = depth // N
        bc = gw_ref[2 * cp :, :].T
        router = router_ref[...].astype(F32)
        for t in range(N):
            at = slice(t * per, (t + 1) * per)
            where = (t // (Y * X * 2), t // (X * 2) % Y, t // 2 % X, t % 2)
            extra[(*where, slice(0, per), slice(0, 2 * state))] = bc[at].astype(B16)
            extra[(*where, slice(0, per), slice(2 * state, 2 * state + LANES))] = router[at].astype(B16)
        sides.run(0, 1)
        for script, stage in final_acts[5:7]:
            script.run(stage, stage + 1)
        sides.run(1, 2)
        for copy in column:
            copy.wait_recv()
        joint[0:line, :] = functools.reduce(jnp.add, [small[t, 0:line, :] for t in range(S)])
        for t in range(S):
            joint[line + 8 * t : line + 8 * t + 8, :] = small[t, line : line + 8, :]
        keep_joint.start()
        for copy in row:
            copy.start()
        for script, stage in final_acts[7:]:
            script.run(stage, stage + 1)
        sides.run(2, 3)
        sums.run(8)
        output_ref[...] = res_ref[...] + total[...] if beside else res_ref[...]
        sides.run(3)
        acts.run(4 * Z)
        values, gone = in_ref[...], total[...]
        gin_ref[...] = gres_ref[...] + rms_back(values, inverse_rms(values), gain_ref[...], gone)
        for copy in row:
            copy.wait()
        for copy in column:
            copy.wait_send()
        keep_joint.wait()
        for copy in keep_here + group:
            copy.wait()
        mail.finish(scatter_count(S, H) if beside else 0)
        mail2.finish(scatter_count(S, H) - 3 + scatter_count(S, H, (False,)))


def mixer_backward(
    ends, three, one, pre, z, y, states, in_w, taps, rows, cols, out_w, out_part, residual, grad_res, hidden_in, gain,
    norm2, router_part, state, C, S, H,
):
    T, depth = three.shape[0], in_w.shape[0]
    cp, nb = out_w.shape[0], T // BLOCK
    conv_width = cp + 2 * state
    R, N = residual.shape[0], S * H
    X, Y, Z = sizes(S, H)
    line = 2 * (depth // LANES) + 4 * (2 * state // LANES)
    tall = -(-(depth // N) // 16) * 16
    zx_rows = -(-(C + 2) // 16) * 16
    beside = Y == 2
    wo_rows = -(-C // 16) * 16
    assert line % 8 == 0 and cp == LANES and R * H == BLOCK
    sent = scatter_count(S, H) - 3 + scatter_count(S, H, (False,))

    def block(width, kept=2):
        return pl.BlockSpec((BLOCK, width), lambda k: (nb - 1 - k, 0), pipeline_mode=pl.Buffered(kept))

    kept = 2 if beside else 1

    def halo(k):
        return (jnp.maximum((nb - 1 - k) * (BLOCK // 8) - 1, 0), 0)

    return pl.pallas_call(
        functools.partial(mixer_backward_kernel, S, H, beside, ends.shape[0], state, C),
        grid=(nb,),
        in_specs=[
            pl.BlockSpec(memory_space=pltpu.SMEM), block(three.shape[1]), block(one.shape[1], kept), block(conv_width, kept),
            pl.BlockSpec((8, conv_width), halo), block(cp), block(cp),
            pl.BlockSpec((1, state, cp), lambda k: (nb - 1 - k, 0, 0)),
            VMEM, VMEM, VMEM, VMEM, VMEM, ANY, VMEM, VMEM, VMEM, VMEM, VMEM, VMEM,
        ],
        out_specs=[VMEM, VMEM, VMEM, ANY, ANY, ANY],
        out_shape=[
            jax.ShapeDtypeStruct((R, depth), F32),
            jax.ShapeDtypeStruct((R, depth), F32),
            jax.ShapeDtypeStruct((tall, 2 * state + LANES), F32),
            jax.ShapeDtypeStruct((H, line + 8 * S, LANES), F32),
            jax.ShapeDtypeStruct((S, zx_rows, 2 * (depth // S)), B16),
            jax.ShapeDtypeStruct((S, wo_rows, depth // S), B16),
        ],
        scratch_shapes=[
            pltpu.VMEM((state, cp), F32),
            pltpu.VMEM((BLOCK + 8, conv_width), F32),
            pltpu.VMEM((BLOCK + 8, conv_width), F32),
            pltpu.VMEM((in_w.shape[1], depth), F32),
            pltpu.VMEM(out_w.shape, F32),
            pltpu.VMEM((8, conv_width), F32),
            pltpu.VMEM((8, cp), F32),
            pltpu.VMEM((1, depth), F32),
            pltpu.VMEM((R, depth), F32),
            pltpu.VMEM((Z, Y, X, 2, R, depth), B16),
            pltpu.VMEM((Z, Y, X, 2, tall, 2 * state + LANES), B16),
            pltpu.VMEM((S, zx_rows, 2 * (depth // S)), B16),
            pltpu.VMEM((S, wo_rows, depth // S), B16),
            pltpu.VMEM((S, line + 8, LANES), F32),
            pltpu.VMEM((line + 8 * S, LANES), F32),
            *(scatter_scratch(S, H, R, depth) if beside else []),
            *sum_scratch(S, H, R, depth),
            *sum_scratch(S, H, tall, 2 * state + LANES, False),
            *sems(scatter_count(S, H)),
            *sems(sent),
            pltpu.SemaphoreType.DMA((4,)), pltpu.SemaphoreType.DMA((3,)),
            pltpu.SemaphoreType.DMA((4, S)), pltpu.SemaphoreType.DMA((4, S)),
            pltpu.SemaphoreType.DMA((3,)),
        ],
        compiler_params=talking(6),
    )(
        ends, three, one, pre, pre, z, y, states, in_w, taps, rows, cols, out_w, blocks(out_part, S, H), residual,
        grad_res, hidden_in, gain, norm2, router_part,
    )


def expert_block(F, two, grad, named, mine, up_ref, down_ref, gup_ref, gdown_ref, gs_ref):
    mid = mm(two, up_ref[...])
    back = mm(grad, down_ref[...], NT)
    gate, lin = mid[:, :F], mid[:, F : 2 * F]
    s_gate, s_lin = mid[:, 2 * F : 2 * F + LANES], mid[:, 2 * F + LANES :]
    named = named.astype(F32) > 0
    logits = jnp.where(named, s_gate, -1e30)
    odds = jnp.where(named, jnp.exp(logits - jnp.max(logits, axis=1, keepdims=True)), 0.0)
    probs = odds / jnp.sum(odds, axis=1, keepdims=True)
    weight = jnp.sum(probs * mine, axis=1, keepdims=True)
    s_back, back = back[:, F:], back[:, :F]
    act_gate, act_s = silu(gate), silu(s_gate)
    acting = act_gate * lin
    gp = jnp.sum(acting * back, axis=1, keepdims=True)
    back = weight * back
    down_in = jnp.concatenate([weight * acting, act_s * s_lin], axis=1).astype(B16)
    mid_grad = jnp.concatenate(
        [back * lin * silu_grad(gate), back * act_gate, s_back * s_lin * silu_grad(s_gate), s_back * act_s], axis=1
    ).astype(B16)
    gup_ref[...] += mm(two, mid_grad[:, : 2 * F], TN)
    gdown_ref[...] += mm(down_in[:, :F], grad, TN)
    gs_ref[: 2 * LANES, :] += mm(mid_grad[:, 2 * F :], two, TN)
    gs_ref[2 * LANES :, :] += mm(down_in[:, F:], grad, TN)
    out = mm(down_in, down_ref[...]).astype(B16)
    part = mm(mid_grad, up_ref[...], NT).astype(B16)
    return out, part, (gp * mine).astype(B16), probs


def expert_kernel(
    S, H, F, width, total_ref, in_ref, gain_ref, grad_ref, named_ref, up_ref, down_ref, mine_ref, router_ref, ograd_ref,
    three_ref, res_ref, gres_ref, gnorm_ref, grouter_ref, out_ref, gup_out, gdown_ref, sh_out,
    gup_ref, total, rows, two, grads, names, parts, stage_out, probs, gs_ref, *rest,
):
    buffers, (rows3, pieces, send2, recv2, sh_send, sh_recv, own_sem, own3_sem, sh_sem, name_sem, grad_sem, out_sem) = (
        rest[:-12], rest[-12:]
    )
    pc = Place(S, H)
    X, Y, Z = pc.X, pc.Y, pc.Z
    R, D = in_ref.shape
    n = BLOCK
    N, me = S * H, pc.slot()
    mail2 = Mail(send2, recv2)
    stay = pltpu.make_async_copy(pieces.at[me], sh_out.at[me], sh_sem)

    def to_all(function):
        def body(m, carry):
            to = (me + m) % N
            function(
                pltpu.make_async_remote_copy(
                    src_ref=pieces.at[to], dst_ref=sh_out.at[me], send_sem=sh_send.at[m], recv_sem=sh_recv.at[m],
                    device_id=(to // H, to % H), device_id_type=MESH,
                )
            )
            return carry

        lax.fori_loop(1, N, body, 0)

    def cell(dz, yy, xx, rows):
        return parts.at[dz, yy, xx, pc.c, rows]

    moves = gather(pc, mail2, rows, two, own_sem, planes=True)
    onward = gather(pc, mail2, rows3, three_ref, own3_sem)
    acts = Script()
    second = Sum(pc, mail2, acts, cell, lambda dz: parts.at[dz, :, :, 1 - pc.c], buffers, R, direct=True)
    for dz in range(Z):
        acts.stage()
        second.across(dz)
        acts.stage()
        second.cores(dz)
        acts.stage()
        second.firsts(dz)
        acts.stage()
        second.seconds(dz)
    acts.stage()
    second.last(total)

    def seq_of(k):
        return pc.partner(k // Y) * Y + k % Y

    def loads(k, slot):
        at = pl.ds(pl.multiple_of(seq_of(k) * n, n), n)
        return [
            pltpu.make_async_copy(grad_ref.at[at], grads.at[slot], grad_sem.at[slot]),
            pltpu.make_async_copy(named_ref.at[at, pl.ds(D, LANES)], names.at[slot], name_sem.at[slot]),
        ]

    def store(k, slot):
        at = pl.ds(pl.multiple_of(seq_of(k) * n, n), n)
        return pltpu.make_async_copy(stage_out.at[slot], out_ref.at[at], out_sem.at[slot])

    for copy in loads(0, 0):
        copy.start()
    gain = gain_ref[...]
    mixed = total_ref[:, :D]
    square = jnp.sum(total_ref[:, D:], axis=1, keepdims=True)
    inv = lax.rsqrt(square / width + EPS)
    residual = in_ref[...] + inv * mixed
    res_ref[...] = residual
    rows[...] = (residual * inverse_rms(residual) * gain).astype(B16)
    cube = inv * inv * inv / width
    barrier = pltpu.get_barrier_semaphore()

    def hello(m, carry):
        to = (me + m) % N
        pl.semaphore_signal(barrier, inc=1, device_id=(to // H, to % H), device_id_type=MESH)
        return carry

    lax.fori_loop(1, N, hello, 0)
    pl.semaphore_wait(barrier, N - 1)
    moves.run(0, 1)
    gup_ref[...] = jnp.zeros_like(gup_ref)
    gdown_ref[...] = jnp.zeros_like(gdown_ref)
    gs_ref[...] = jnp.zeros_like(gs_ref)
    moves.run(1, 5)
    moves.run(12, 13)

    count = Y * Z
    before = {k: [] for k in range(count)}
    after = []
    for dz in range(Z):
        for late, stage in ((0, 0), (1, 1), (3, 2), (4, 3)):
            k = (dz + 1) * Y + late
            before.get(k, after).append((acts, 4 * dz + stage))
    after = [(acts, 4 * dz + stage) for dz, stage in ((3, 0), (1, 2), (1, 3), (2, 2), (3, 1), (2, 3), (3, 2), (3, 3))]
    after = [entry for entry in after if all(entry not in before[k] for k in before)]
    for k, stage in (
        (0, 5), (1, 6), (1, 7), (Y, 8), (Y, 13), (Y + 1, 9), (Y + 1, 10), (2 * Y, 11), (2 * Y, 14), (3 * Y, 15),
    ):
        before[k].append((moves, stage))
    mine = mine_ref[...]

    def step(k, carry):
        for at in range(count):
            if before[at]:

                @pl.when(k == at)
                def _():
                    for script, stage in before[at]:
                        script.run(stage, stage + 1)

        slot = k % 2

        @pl.when(k + 1 < count)
        def _():
            for copy in loads(k + 1, 1 - slot):
                copy.start()

        for copy in loads(k, slot):
            copy.wait()
        block = two[pl.ds(pl.multiple_of(seq_of(k) * n, n), n), :]
        out, part, gp, chance = expert_block(
            F, block, grads[slot], names[slot], mine, up_ref, down_ref, gup_ref, gdown_ref, gs_ref
        )
        for xx in range(X):
            for cc in range(2):
                at = slice((xx * 2 + cc) * R, (xx * 2 + cc + 1) * R)
                parts[k // Y, k % Y, xx, cc, :, :D] = part[at]
                parts[k // Y, k % Y, xx, cc, :, D:] = gp[at]

        @pl.when(k == pc.y)
        def _():
            probs[...] = chance

        @pl.when(k >= 2)
        def _():
            store(k - 2, slot).wait()

        stage_out[slot] = out
        store(k, slot).start()
        return carry

    lax.fori_loop(0, count, step, 0)
    for script, stage in after[:1]:
        script.run(stage, stage + 1)
    for k in range(2):
        gup_out[0, :, k, :] = gup_ref[:, k * F : (k + 1) * F]
    per, FS = D // N, pieces.shape[2] // 3
    turned = jnp.concatenate([gs_ref[k * LANES : k * LANES + FS, :] for k in range(3)], axis=0).T
    for k in range(N):
        pieces[k, :per, :] = turned[k * per : (k + 1) * per, :].astype(B16)
        if per < pieces.shape[1]:
            pieces[k, per:, :] = jnp.zeros((pieces.shape[1] - per, 3 * FS), B16)
    for script, stage in after[1:]:
        script.run(stage, stage + 1)
    head = lax.axis_index("head")
    p = probs[pl.ds(pl.multiple_of(head * R, R), R), :]
    acts.run(4 * Z)
    gp = total[:, D:]
    glogits = (p * (gp - jnp.sum(p * gp, axis=1, keepdims=True))).astype(B16)
    gtwo = total[:, :D] + mm(glogits, router_ref[...], NT)
    residual = res_ref[...]
    inv_two = inverse_rms(residual)
    gres = ograd_ref[...] + rms_back(residual, inv_two, gain, gtwo)
    cross = jnp.sum(gres * mixed, axis=1, keepdims=True) * cube
    high, low = hi_lo(cross)
    lane = lax.broadcasted_iota(jnp.int32, (R, LANES), 1)
    rows3[:, :D] = (inv * gres).astype(B16)
    rows3[:, D:] = jnp.where(lane == 0, high.astype(F32), jnp.where(lane == 1, low.astype(F32), 0.0)).astype(B16)
    onward.run(0, 1)
    stay.start()
    to_all(lambda copy: copy.start())
    gres_ref[...] = gres
    gnorm_ref[...] = jnp.sum(gtwo * residual * inv_two, axis=0, keepdims=True)
    grouter_ref[...] = mm((residual * inv_two * gain).astype(B16), glogits, TN).astype(B16)
    for k in (count - 2, count - 1):
        store(k, k % 2).wait()
    onward.run(1)
    to_all(lambda copy: copy.wait())
    stay.wait()
    mail2.finish(2 * gather_count(S, H) + scatter_count(S, H))


def experts(total, hidden_in, gain, all_grad, gathered, up_w, down_w, mine, router, out_grad, F, FS, width, S, H):
    R, D = hidden_in.shape
    X, Y, Z = sizes(S, H)
    T, W = S * H * R, D + LANES
    tall = -(-(D // (S * H)) // 16) * 16
    assert R * H == BLOCK
    return pl.pallas_call(
        functools.partial(expert_kernel, S, H, F, width),
        out_shape=[
            jax.ShapeDtypeStruct((T, W), B16),
            jax.ShapeDtypeStruct((R, D), F32),
            jax.ShapeDtypeStruct((R, D), F32),
            jax.ShapeDtypeStruct((1, D), F32),
            jax.ShapeDtypeStruct((D, LANES), B16),
            jax.ShapeDtypeStruct((T, D), B16),
            jax.ShapeDtypeStruct((1, D, 2, F), F32),
            jax.ShapeDtypeStruct((F, D), F32),
            jax.ShapeDtypeStruct((S * H, tall, 3 * FS), B16),
        ],
        in_specs=[VMEM, VMEM, VMEM, ANY, ANY] + [VMEM] * 5,
        out_specs=[ANY] + [VMEM] * 4 + [ANY] + [VMEM] * 2 + [ANY],
        scratch_shapes=[
            pltpu.VMEM((D, 2 * F), F32), pltpu.VMEM((R, W), F32), pltpu.VMEM((R, D), B16), pltpu.VMEM((T, D), B16),
            pltpu.VMEM((2, BLOCK, D), B16), pltpu.VMEM((2, BLOCK, LANES), B16),
            pltpu.VMEM((Z, Y, X, 2, R, W), B16), pltpu.VMEM((2, BLOCK, D), B16), pltpu.VMEM((BLOCK, LANES), F32),
            pltpu.VMEM((3 * LANES, D), F32), *sum_scratch(S, H, R, W),
            pltpu.VMEM((R, W), B16), pltpu.VMEM((S * H, tall, 3 * FS), B16),
            *sems(scatter_count(S, H) + 2 * gather_count(S, H)), *sems(S * H),
            pltpu.SemaphoreType.DMA, pltpu.SemaphoreType.DMA, pltpu.SemaphoreType.DMA, pltpu.SemaphoreType.DMA((2,)),
            pltpu.SemaphoreType.DMA((2,)), pltpu.SemaphoreType.DMA((2,)),
        ],
        compiler_params=talking(2),
    )(total, hidden_in, gain, all_grad, gathered, up_w, down_w, mine, router, out_grad)


def finish_kernel(
    S, H, C, FS, state, zx_ref, wo_ref, sh_ref, small_ref, pick_ref, kcip_ref, gain_ref, a_in, b_in, c_in, d_in,
    zx_out, dt_out, wo_out, up_out, down_out, norm1_out, norm2_out, taps_out, bc_out, gate_out, heads_out,
    a_out, b_out, c_out, d_out, a_way, b_way, c_way, d_way, sem,
):
    ways = ((a_in, a_way, a_out), (b_in, b_way, b_out), (c_in, c_way, c_out), (d_in, d_way, d_out))
    held = [pltpu.make_async_copy(src, way, sem.at[0, k]) for k, (src, way, dst) in enumerate(ways)]
    gone = [pltpu.make_async_copy(way, dst, sem.at[1, k]) for k, (src, way, dst) in enumerate(ways)]
    for copy in held:
        copy.start()
    wide = wo_ref.shape[2]
    heads = dt_out.shape[0]
    dt = jnp.zeros(dt_out.shape, F32)
    for t in range(S):
        piece = zx_ref[t].astype(F32)
        turned = piece.T
        at = slice(t * C, (t + 1) * C)
        zx_out[:, 0, at] = turned[:wide, :C]
        zx_out[:, 1, at] = turned[wide:, :C]
        dt = dt + exact(kcip_ref[t, :, : piece.shape[0]], piece[:, :wide])
        wo_out[:, at] = wo_ref[t].astype(F32).T[:, :C]
    dt_out[...] = dt
    for come, go in zip(held, gone):
        come.wait()
        go.start()
    for t in range(S * H):
        piece = sh_ref[t].astype(F32)[: up_out.shape[0]]
        at = slice(t * FS, (t + 1) * FS)
        for k in range(2):
            up_out[:, k, at] = piece[:, k * FS : (k + 1) * FS]
        down_out[:, at] = piece[:, 2 * FS :]
    lines = gain_ref.shape[1] // LANES
    total = small_ref[0, : 2 * lines + 4 * (2 * state // LANES), :]
    for h in range(1, H):
        total = total + small_ref[h, : total.shape[0], :]
    for j in range(lines):
        at = slice(j * LANES, (j + 1) * LANES)
        norm1_out[:, at] = total[j : j + 1, :] / gain_ref[:, at]
        norm2_out[:, at] = total[lines + j : lines + j + 1, :]
    line = 2 * lines
    for r in range(4):
        for j in range(2 * state // LANES):
            bc_out[r : r + 1, j * LANES : (j + 1) * LANES] = total[line : line + 1, :]
            line += 1
    for h in range(H):
        by_head = jnp.zeros((8, heads), F32)
        for t in range(S):
            ours = small_ref[h, line + 8 * t : line + 8 * t + 8, :]
            at = slice((h * S + t) * C, (h * S + t + 1) * C)
            taps_out[:, at] = ours[0:4, :C]
            gate_out[:, at] = ours[4:5, :C]
            by_head = by_head + exact(ours, pick_ref[t])
        for r in range(3):
            heads_out[r : r + 1, h * heads : (h + 1) * heads] = by_head[5 + r : 6 + r, :]
    for copy in gone:
        copy.wait()


def finish(zx, wo, shared, small, pick, gain, made, C, FS, state, S, H):
    N, wide, heads, D = S * H, wo.shape[2], pick.shape[2], gain.shape[1]
    per = D // N
    shapes = (
        (wide, 2, S * C), (heads, wide), (wide, S * C), (per, 2, N * FS), (per, N * FS), (1, D), (1, D), (4, S * H * C),
        (4, 2 * state), (1, S * H * C), (3, H * heads),
    )
    return pl.pallas_call(
        functools.partial(finish_kernel, S, H, C, FS, state),
        out_shape=[jax.ShapeDtypeStruct(shape, F32) for shape in shapes + tuple(v.shape for v in made)],
        in_specs=[VMEM] * 7 + [ANY] * 4,
        out_specs=[VMEM] * len(shapes) + [ANY] * 4,
        scratch_shapes=[*(pltpu.VMEM(v.shape, F32) for v in made), pltpu.SemaphoreType.DMA((2, 4))],
        compiler_params=pltpu.CompilerParams(vmem_limit_bytes=56 * 1024 * 1024),
    )(zx, wo, shared, small, pick, pick.transpose(0, 2, 1), gain, *made)


def local(
    hidden_in, norm1_gain, w_zx, w_bc, w_dt, conv_x, conv_bc, dt_bias, a_log, d_skip, gate_gain,
    w_out, norm2_gain, router, expert_up, expert_down, shared_up, shared_down, out_grad,
    seq_lengths, routes,
):
    S, H = lax.axis_size("seq"), lax.axis_size("head")
    N = S * H
    s = lax.axis_index("seq")
    g = s * H + lax.axis_index("head")
    R, D = hidden_in.shape
    heads, inner = dt_bias.shape[0], conv_x.shape[1]
    size = inner // heads
    state = w_bc.shape[1] // 2
    width = inner * H
    C = inner // S
    CP = -(-(C + 2) // LANES) * LANES
    E = N // 2
    F = expert_down.shape[1]
    FS = shared_down.shape[0] // N
    per = D // N

    named = jnp.sum(
        (routes[:, :, None] == jnp.arange(E, dtype=jnp.int32)[None, None, :]).astype(F32), axis=1
    )
    named = jnp.pad(named.astype(B16), ((0, 0), (FS, LANES - FS - E)))
    gain1, gain2 = norm1_gain[None], norm2_gain[None]
    gathered = first_rows(hidden_in, gain1, named, S, H)

    firsts = [min(k * C // size, heads - 2) for k in range(S)]
    first = jnp.minimum(s * C // size, heads - 2)
    channel = jnp.arange(CP)
    masks = jnp.stack(
        [((channel < C) & ((s * C + channel) // size - first == j)).astype(F32) for j in range(2)]
    )

    def mine(values, axis, offset, length):
        return lax.dynamic_slice_in_dim(values, offset, length, axis)

    def channels(values, axis):
        cut = mine(values, axis, s * C, C)
        pads = [(0, 0)] * values.ndim
        pads[axis] = (0, CP - C)
        return jnp.pad(cut, pads)

    def in_free(values):
        return jnp.pad(values, [(0, 0)] * (values.ndim - 1) + [(C, CP - C - 2)])

    zx_w = mine(w_zx, 2, s * C, C)
    in_w = jnp.concatenate(
        [
            zx_w[:, 0], pad_lanes(mine(w_dt, 1, first, 2), CP - C), pad_lanes(zx_w[:, 1], CP), w_bc,
        ],
        axis=1,
    )
    taps = jnp.concatenate([channels(conv_x, 1), conv_bc], axis=1)
    bias, alog, skip = (mine(v, 0, first, 2) for v in (dt_bias, a_log, d_skip))
    gain = channels(gate_gain, 0)
    out_w = channels(w_out, 0)
    rows = jnp.concatenate(
        [masks, (skip @ masks)[None], gain[None], in_free(jnp.stack([bias, jnp.exp(alog)]))], axis=0
    )
    rows = jnp.pad(rows, ((0, 2), (0, 0)))
    cols = in_free(masks.T)
    ends = jnp.cumsum(seq_lengths)

    pre, z, y, states, mixed, all_grad = mixer_forward(
        ends, gathered, in_w, taps, rows, out_w, out_grad.astype(B16), state, C, S, H
    )

    sup = mine(shared_up, 2, g * FS, FS)
    router_w = jnp.pad(router, ((0, 0), (FS, LANES - FS - E)))
    up_w = jnp.concatenate(
        [
            expert_up[0].reshape(D, 2 * F), sup[:, 0], router_w[:, FS:], pad_lanes(sup[:, 1], LANES),
        ],
        axis=1,
    )
    down_w = jnp.concatenate([expert_down[0], mine(shared_down, 0, g * FS, FS), jnp.zeros((LANES - FS, D), B16)], axis=0)
    is_mine = (jnp.arange(LANES) == FS + g // 2).astype(F32)[None]
    three, residual, grad_res, norm2_part, router_part, out_part, grad_up, grad_down, sh_in = experts(
        mixed, hidden_in, gain2, all_grad, gathered, up_w, down_w, is_mine, router_w, out_grad, F, FS, width, S, H
    )

    output, grad_in, extra_sum, small, zx_in, wo_in = mixer_backward(
        ends, three, gathered, pre, z, y, states, in_w, taps, rows, cols, out_w, out_part, residual,
        grad_res, hidden_in, gain1, norm2_part, router_part, state, C, S, H,
    )
    if H > 4:
        output = output + lax.psum_scatter(out_part, ("seq", "head"), scatter_dimension=0, tiled=True).astype(F32)
    grad_bc, grad_router = extra_sum[:per, : 2 * state], extra_sum[:per, 2 * state :][:, FS : FS + E]
    pick = np.array(
        [[[C <= c < C + 2 and firsts[k] + c - C == h for h in range(heads)] for c in range(LANES)] for k in range(S)], np.float32
    )
    grad_zx, grad_w_dt, grad_w_out, grad_shared_up, grad_shared_down, *found = finish(
        zx_in, wo_in, sh_in, small, pick, gain1, (grad_up, grad_down[None], output, grad_in), C, FS, state, S, H
    )
    grad_norm1, grad_norm2, grad_conv_x, grad_conv_bc, grad_gate_gain, by_head, *made = found
    grad_up, grad_down, output, grad_in = made
    grad_norm1, grad_norm2, grad_gate_gain = (v.reshape(-1) for v in (grad_norm1, grad_norm2, grad_gate_gain))
    grad_dt_bias, grad_a_log, grad_d_skip = by_head[0], by_head[1], by_head[2]
    return (
        output, grad_in, grad_norm1, grad_zx, grad_bc, grad_w_dt.T, grad_conv_x, grad_conv_bc, grad_dt_bias,
        grad_a_log, grad_d_skip, grad_gate_gain, grad_w_out.T, grad_norm2, grad_router, grad_up, grad_down,
        grad_shared_up, grad_shared_down.T,
    )


def solution(mesh):
    return jax.shard_map(
        local,
        mesh=mesh,
        in_specs=(
            P(("seq", "head"), None),
            P(),
            P(None, None, "head"),
            P(),
            P(None, "head"),
            P(None, "head"),
            P(),
            P("head"),
            P("head"),
            P("head"),
            P("head"),
            P("head", None),
            P(),
            P(),
            P(("seq", "head"), None, None, None),
            P(("seq", "head"), None, None),
            P(),
            P(),
            P(("seq", "head"), None),
            P(),
            P(("seq", "head"), None),
        ),
        out_specs=(
            P(("seq", "head"), None),
            P(("seq", "head"), None),
            P(),
            P("seq", None, "head"),
            P(("seq", "head"), None),
            P("seq", "head"),
            P(),
            P(),
            P(),
            P(),
            P(),
            P(),
            P("head", "seq"),
            P(),
            P(("seq", "head"), None),
            P(("seq", "head"), None, None, None),
            P(("seq", "head"), None, None),
            P(("seq", "head"), None, None),
            P(None, ("seq", "head")),
        ),
        check_vma=False,
    )
```

```python
import functools
import jax
import jax.numpy as jnp
import numpy as np
from jax import lax
from jax.experimental import pallas as pl
from jax.experimental.pallas import tpu as pltpu
from jax.sharding import PartitionSpec as P

MESH = pl.DeviceIdType.MESH
BLOCK = 256
EPS = 1e-05
LANES = 128
B16 = jnp.bfloat16
F32 = jnp.float32


def mm(left, right, dims=(((1,), (0,)), ((), ()))):
    return lax.dot_general(left, right, dims, preferred_element_type=F32)


NT = (((1,), (1,)), ((), ()))
TN = (((0,), (0,)), ((), ()))


def inverse_rms(values):
    return lax.rsqrt(jnp.mean(values * values, axis=-1, keepdims=True) + EPS)


def rms_back(values, inverse, gain, grad):
    weighted = grad * gain
    inner = jnp.mean(weighted * values, axis=-1, keepdims=True)
    return inverse * weighted - values * inverse**3 * inner


def silu_grad(values):
    sig = jax.nn.sigmoid(values)
    return sig * (1.0 + values * (1.0 - sig))


def pad_lanes(values, width):
    return jnp.pad(values, [(0, 0)] * (values.ndim - 1) + [(0, width - values.shape[-1])])


def hi_lo(values):
    high = values.astype(B16)
    return high, (values - high.astype(F32)).astype(B16)


def sizes(seq_size, head_size):
    return head_size // 2, head_size // 2, seq_size // (head_size // 2)


class Place:
    def __init__(self, seq_size, head_size):
        self.H = head_size
        self.X, self.Y, self.Z = sizes(seq_size, head_size)
        assert self.Z == 4
        seq, head = lax.axis_index("seq"), lax.axis_index("head")
        self.z, self.y = seq // self.Y, seq % self.Y
        self.x, self.c = head // 2, head % 2
        z = self.z
        self.partners = (z, z + 1 - 2 * (z % 2), (z + 2) % 4, 3 - z)

    def at(self, dz=0, dy=0, dx=0, dc=0):
        return (
            self.partners[dz],
            (self.y + dy) % self.Y if dy else self.y,
            (self.x + dx) % self.X if dx else self.x,
            1 - self.c if dc else self.c,
        )

    def dev(self, **where):
        z, y, x, c = self.at(**where)
        return (z * self.Y + y, x * 2 + c)

    def slot(self, **where):
        z, y, x, c = self.at(**where)
        return (z * self.Y + y) * self.H + x * 2 + c

    def partner(self, dz):
        return (self.z // 2 + dz // 2) % 2 * 2 + (self.z + dz) % 2

    def peers(self, direct=False):
        out = [self.dev(dz=k) for k in range(1, 4 if direct else 3)]
        out += [self.dev(dy=k) for k in range(1, self.Y)]
        out += [self.dev(dx=k) for k in range(1, self.X)]
        return out + [self.dev(dc=1)]


def greet(peers):
    barrier = pltpu.get_barrier_semaphore()
    for peer in peers:
        pl.semaphore_signal(barrier, inc=1, device_id=peer, device_id_type=MESH)
    pl.semaphore_wait(barrier, len(peers))


class Mail:
    def __init__(self, send, recv):
        self.send, self.recv, self.made = send, recv, []

    def copy(self, src, dst, dev):
        i = len(self.made)
        self.made.append(
            pltpu.make_async_remote_copy(
                src_ref=src, dst_ref=dst, send_sem=self.send.at[i], recv_sem=self.recv.at[i],
                device_id=dev, device_id_type=MESH,
            )
        )
        return self.made[-1]

    def finish(self, count):
        assert len(self.made) == count
        for copy in self.made:
            copy.wait_send()


class Script(list):
    def stage(self):
        self.append([])

    def do(self, action):
        self[-1].append(action)

    def run(self, first=0, last=None):
        for stage in self[first:last]:
            for action in stage:
                action()


def gather_count(S, H):
    X, Y, Z = sizes(S, H)
    return (Z - 1) + 2 * Z * (X + Y - 2) + 2 * Z * (X - 1) * (Y - 1) + X * Y * Z


def gather(pc, mail, x_ref, out_ref, own_sem, planes=False):
    X, Y, Z = pc.X, pc.Y, pc.Z
    R = x_ref.shape[0]
    half = R // 2
    script = Script()

    def rows(part, **where):
        base = pl.multiple_of(pc.slot(**where) * R, R)
        if part is None:
            return out_ref.at[pl.ds(base, R)]
        return out_ref.at[pl.ds(pl.multiple_of(base + part * half, half), half)]

    def send(src, dst, dev):
        copy = mail.copy(src, dst, dev)
        script.do(copy.start)
        return copy

    x_in, y_in, dga, dgb = {}, {}, {}, {}
    sib = {dz: [] for dz in range(Z)}

    def column(dz):
        for part in (0, 1):
            src = x_ref.at[pl.ds(part * half, half)] if dz == 0 else rows(part, dz=dz)
            for k in range(1, X):
                x_in[dz, k, part] = send(src, rows(part, dz=dz), pc.dev(dx=k))
            other = 1 - part
            src = x_ref.at[pl.ds(other * half, half)] if dz == 0 else rows(other, dz=dz)
            for k in range(1, Y):
                y_in[dz, k, other] = send(src, rows(other, dz=dz), pc.dev(dy=k))
        src = x_ref if dz == 0 else rows(None, dz=dz)
        sib[dz].append(send(src, rows(None, dz=dz), pc.dev(dc=1)))

    def onward(dz):
        for k in range(1, X):
            script.do(x_in[dz, k, 0].wait_recv)
            block = rows(0, dz=dz, dx=-k)
            for m in range(1, Y):
                dga[dz, k, m] = send(block, block, pc.dev(dy=m))
        for k in range(1, Y):
            script.do(y_in[dz, k, 1].wait_recv)
            block = rows(1, dz=dz, dy=-k)
            for m in range(1, X):
                dgb[dz, k, m] = send(block, block, pc.dev(dx=m))
        for k in range(1, X):
            script.do(x_in[dz, k, 1].wait_recv)
            block = rows(None, dz=dz, dx=-k)
            sib[dz].append(send(block, block, pc.dev(dc=1)))
        for k in range(1, Y):
            script.do(y_in[dz, k, 0].wait_recv)
            block = rows(None, dz=dz, dy=-k)
            sib[dz].append(send(block, block, pc.dev(dc=1)))

    def corner(dz):
        for k in range(1, X):
            for m in range(1, Y):
                script.do(dga[dz, k, m].wait_recv)
                script.do(dgb[dz, m, k].wait_recv)
                block = rows(None, dz=dz, dx=-k, dy=-m)
                sib[dz].append(send(block, block, pc.dev(dc=1)))

    own = pltpu.make_async_copy(x_ref, rows(None), own_sem)
    script.stage()
    script.do(own.start)
    first = send(x_ref, rows(None), pc.dev(dz=1))
    column(0)
    second = send(x_ref, rows(None), pc.dev(dz=2))
    script.stage()
    script.do(first.wait_recv)
    column(1)
    script.stage()
    onward(0)
    script.stage()
    corner(0)
    script.stage()
    script.do(second.wait_recv)
    third = send(rows(None, dz=2), rows(None, dz=2), pc.dev(dz=1))
    column(2)
    script.stage()
    onward(1)
    script.stage()
    script.do(third.wait_recv)
    column(3)
    script.stage()
    corner(1)
    for dz in (2, 3):
        script.stage()
        onward(dz)
        script.stage()
        corner(dz)
    if not planes:
        for dz in range(Z):
            for copy in sib[dz]:
                script.do(copy.wait_recv)
        script.do(own.wait)
        return script
    for dz in range(Z):
        script.stage()
        for copy in sib[dz]:
            script.do(copy.wait_recv)
        if dz == 0:
            script.do(own.wait)
    return script


def scatter_parts(split):
    return (("y", 0), ("x", 1)) if split else (("x", None),)


def scatter_count(S, H, splits=(True,)):
    X, Y, Z = sizes(S, H)
    pieces = sum(len(scatter_parts(split)) for split in splits)
    return len(splits) * (Z + Z - 1) + pieces * Z * (X + Y - 2)


def sum_scratch(S, H, R, W, split=True):
    X, Y, Z = sizes(S, H)
    out = [pltpu.VMEM((Z, Y, X, R, W), B16), pltpu.VMEM((Z - 1, R, W), B16)]
    for axis, part in scatter_parts(split):
        rows = R if part is None else R // 2
        first, second = (Y, X) if axis == "y" else (X, Y)
        out += [pltpu.VMEM((Z, first - 1, second, rows, W), B16), pltpu.VMEM((Z, second - 1, rows, W), B16)]
    return out


def scatter_scratch(S, H, R, W, split=True):
    X, Y, Z = sizes(S, H)
    return [pltpu.VMEM((Z, Y, X, R, W), B16), *sum_scratch(S, H, R, W, split), pltpu.SemaphoreType.DMA((Z,))]


def accumulate(dst, srcs, rows):
    def action():
        def body(i, carry):
            at = pl.ds(pl.multiple_of(i * 16, 16), 16)
            total = dst.at[at][...].astype(F32)
            for src in srcs:
                total = total + src.at[at][...].astype(F32)
            dst.at[at][...] = total.astype(dst.dtype)
            return carry

        lax.fori_loop(0, rows // 16, body, 0)

    return action


ORDER = (3, 2, 1, 0)


class Sum:
    def __init__(self, pc, mail, script, cell, theirs, buffers, R, split=True, direct=False, ends=None):
        self.ends = ends
        self.pc, self.mail, self.script, self.cell, self.theirs = pc, mail, script, cell, theirs
        self.r0, self.r3, self.buffers, self.R, self.split, self.direct = buffers[0], buffers[1], buffers[2:], R, split, direct
        self.sib, self.one, self.two, self.zs = {}, {}, {}, {}

    def send(self, src, dst, dev):
        copy = self.mail.copy(src, dst, dev)
        self.script.do(copy.start)
        return copy

    def pieces(self):
        R = self.R
        for j, (axis, part) in enumerate(scatter_parts(self.split)):
            rows, size = (pl.ds(0, R), R) if part is None else (pl.ds(part * (R // 2), R // 2), R // 2)
            yield j, axis, rows, size, self.buffers[2 * j], self.buffers[2 * j + 1]

    def across(self, dz):
        self.sib[dz] = self.send(self.theirs(dz), self.r0.at[dz], self.pc.dev(dc=1))

    def cores(self, dz):
        pc, whole = self.pc, pl.ds(0, self.R)
        self.script.do(self.sib[dz].wait_recv)
        for yy in range(pc.Y):
            for xx in range(pc.X):
                self.script.do(accumulate(self.cell(dz, yy, xx, whole), [self.r0.at[dz, yy, xx]], self.R))
        for j, axis, rows, size, r1, r2 in self.pieces():
            for k in range(1, pc.Y if axis == "y" else pc.X):
                if axis == "y":
                    src, dev = self.cell(dz, pc.at(dy=k)[1], slice(None), rows), pc.dev(dy=k)
                else:
                    src, dev = self.cell(dz, slice(None), pc.at(dx=k)[2], rows), pc.dev(dx=k)
                self.one[dz, j, k] = self.send(src, r1.at[dz, k - 1], dev)

    def firsts(self, dz):
        pc = self.pc
        for j, axis, rows, size, r1, r2 in self.pieces():
            steps = range(1, pc.Y if axis == "y" else pc.X)
            for k in steps:
                self.script.do(self.one[dz, j, k].wait_recv)
            for m in range(pc.X if axis == "y" else pc.Y):
                dst = self.cell(dz, pc.y, m, rows) if axis == "y" else self.cell(dz, m, pc.x, rows)
                self.script.do(accumulate(dst, [r1.at[dz, k - 1, m] for k in steps], size))
            for k in range(1, pc.X if axis == "y" else pc.Y):
                if axis == "y":
                    src, dev = self.cell(dz, pc.y, pc.at(dx=k)[2], rows), pc.dev(dx=k)
                else:
                    src, dev = self.cell(dz, pc.at(dy=k)[1], pc.x, rows), pc.dev(dy=k)
                self.two[dz, j, k] = self.send(src, r2.at[dz, k - 1], dev)

    def seconds(self, dz):
        pc = self.pc
        for j, axis, rows, size, r1, r2 in self.pieces():
            steps = range(1, pc.X if axis == "y" else pc.Y)
            for k in steps:
                self.script.do(self.two[dz, j, k].wait_recv)
            mine = self.cell(dz, pc.y, pc.x, rows)
            self.script.do(accumulate(mine, [r2.at[dz, k - 1] for k in steps], size))
        mine = self.cell(dz, pc.y, pc.x, pl.ds(0, self.R))
        if self.ends is not None:
            self.homeward(dz, mine)
            return
        if self.direct:
            if dz:
                self.zs[dz] = self.send(mine, self.r3.at[dz - 1], pc.dev(dz=dz))
            return
        if dz == 2:
            self.script.do(self.zs[3].wait_recv)
            self.script.do(accumulate(mine, [self.r3.at[0]], self.R))
        if dz:
            self.zs[dz] = self.send(mine, self.r3.at[3 - dz], pc.dev(dz=2 if dz == 2 else 1))

    def homeward(self, plane, mine):
        pc, (zsend, zrecv) = self.pc, self.ends
        at = (pc.z - plane + 3) % 4
        copy = pltpu.make_async_remote_copy(
            src_ref=mine, dst_ref=self.r3.at[at], send_sem=zsend.at[plane], recv_sem=zrecv.at[at],
            device_id=(plane * pc.Y + pc.y, pc.x * 2 + pc.c), device_id_type=MESH,
        )
        self.zs[plane] = copy

        def start():
            @pl.when(pc.z != plane)
            def _():
                copy.start()

        self.script.do(start)

    def home(self, total):
        pc, (zsend, zrecv) = self.pc, self.ends
        mine = self.cell(pc.z, pc.y, pc.x, pl.ds(0, self.R))
        copies = [
            pltpu.make_async_remote_copy(
                src_ref=mine, dst_ref=self.r3.at[k], send_sem=zsend.at[0], recv_sem=zrecv.at[k],
                device_id=pc.dev(dz=1), device_id_type=MESH,
            )
            for k in range(3)
        ]

        def body(i, carry):
            at = pl.ds(pl.multiple_of(i * 16, 16), 16)
            value = mine.at[at][...].astype(F32)
            for k in range(3):
                value = value + self.r3.at[k, at][...].astype(F32)
            total.at[at][...] = value
            return carry

        def sent():
            for plane in range(4):

                @pl.when(pc.z != plane)
                def _():
                    self.zs[plane].wait_send()

        for copy in copies:
            self.script.do(copy.wait_recv)
        self.script.do(lambda: lax.fori_loop(0, self.R // 16, body, 0))
        self.script.do(sent)

    def last(self, total):
        ends = (1, 2, 3) if self.direct else (2, 1)
        slots = (0, 1, 2) if self.direct else (1, 2)
        for dz in ends:
            self.script.do(self.zs[dz].wait_recv)
        pc, mine = self.pc, self.cell(0, self.pc.y, self.pc.x, pl.ds(0, self.R))

        def body(i, carry):
            at = pl.ds(pl.multiple_of(i * 16, 16), 16)
            value = mine.at[at][...].astype(F32)
            for k in slots:
                value = value + self.r3.at[k, at][...].astype(F32)
            total.at[at][...] = value
            return carry

        self.script.do(lambda: lax.fori_loop(0, self.R // 16, body, 0))


def scatter(pc, mail, jobs):
    script = Script()
    own, sums = {}, []

    def make(p_ref, t0, scratch, split):
        return Sum(
            pc, mail, script, lambda dz, yy, xx, rows: t0.at[dz, yy, xx, rows],
            lambda dz: p_ref.at[pc.at(dz=dz)[0], :, :, 1 - pc.c], scratch[1:-1], p_ref.shape[4], split,
        )

    for p_ref, total, scratch, split in jobs:
        sums.append(make(p_ref, scratch[0], scratch, split))
    script.stage()
    for o, (p_ref, total, scratch, split) in enumerate(jobs):
        for dz in ORDER:
            own[o, dz] = pltpu.make_async_copy(
                p_ref.at[pc.at(dz=dz)[0], :, :, pc.c], scratch[0].at[dz], scratch[-1].at[dz]
            )
            script.do(own[o, dz].start)
    script.stage()
    for dz in ORDER:
        for each in sums:
            each.across(dz)

    def cores(dz):
        for o, each in enumerate(sums):
            script.do(own[o, dz].wait)
            each.cores(dz)

    script.stage()
    cores(3)
    cores(2)
    script.stage()
    cores(1)
    cores(0)
    script.stage()
    for dz in ORDER:
        if dz < 3:
            script.stage()
        for each in sums:
            each.firsts(dz)
        if dz < 3:
            for each in sums:
                each.seconds(dz + 1)
    script.stage()
    for each, (p_ref, total, scratch, split) in zip(sums, jobs):
        each.seconds(0)
        each.last(total)
    return script


ANY = pl.BlockSpec(memory_space=pl.ANY)
VMEM = pl.BlockSpec(memory_space=pltpu.VMEM)


def sems(count):
    return [pltpu.SemaphoreType.DMA((count,)), pltpu.SemaphoreType.DMA((count,))]


def talking(cid):
    return pltpu.CompilerParams(collective_id=cid, has_side_effects=True, vmem_limit_bytes=60 * 1024 * 1024)


def blocks(part, S, H):
    X, Y, Z = sizes(S, H)
    return part.reshape(Z, Y, X, 2, part.shape[0] // (S * H), part.shape[1])


def first_kernel(
    S, H, C, FS, size, in_ref, gain_ref, routes_ref, conv_ref, conv_bc_ref, gate_ref, zx_ref, bc_ref, dt_ref, up_ref, router_ref,
    shared_ref, bias_ref, alog_ref, skip_ref,
    out_ref, rows_ref, taps_ref, cols_ref, in_w_ref, up_w_ref, rows, window, zx_own, up_own, send, recv, own_sem, window_sem,
):
    pc = Place(S, H)
    R, D = in_ref.shape
    base = pl.multiple_of(pc.slot() * FS // LANES * LANES, LANES)
    fetch = pltpu.make_async_copy(shared_ref.at[:, :, pl.ds(base, LANES)], window, window_sem.at[0])
    fetch_zx = pltpu.make_async_copy(zx_ref, zx_own, window_sem.at[1])
    fetch_up = pltpu.make_async_copy(up_ref, up_own, window_sem.at[2])
    for copy in (fetch_zx, fetch_up, fetch):
        copy.start()
    values = in_ref[...]
    rows[:, :D] = (values * inverse_rms(values) * gain_ref[...].reshape(1, D)).astype(B16)
    line = lax.broadcasted_iota(jnp.int32, (LANES, R), 0)
    named = jnp.zeros((LANES, R), F32)
    for k in range(routes_ref.shape[0]):
        named = named + (routes_ref[k : k + 1, :] == line - FS).astype(F32)
    rows[:, D:] = named.T.astype(B16)
    mail = Mail(send, recv)
    moves = gather(pc, mail, rows, out_ref, own_sem)
    greet(pc.peers())
    moves.run(0, 1)

    heads, inner, width = bias_ref.shape[0], conv_ref.shape[1], rows_ref.shape[1]
    start = lax.axis_index("seq") * C
    first = jnp.minimum(start // size, heads - 2)
    lane = lax.broadcasted_iota(jnp.int32, (1, width), 1)
    masks = []
    for j in range(2):
        low = (first + j) * size - start
        masks.append(((lane < C) & (lane >= low) & (lane < low + size)).astype(F32))
    cut = (
        lax.broadcasted_iota(jnp.int32, (inner, width), 0) == start + lax.broadcasted_iota(jnp.int32, (inner, width), 1)
    ) & (lax.broadcasted_iota(jnp.int32, (inner, width), 1) < C)
    ours = exact(jnp.concatenate([conv_ref[...], gate_ref[...].reshape(1, inner), jnp.zeros((3, inner), F32)], axis=0), cut.astype(F32))
    taps_ref[:, :width] = ours[0:4, :]
    taps_ref[:, width:] = conv_bc_ref[...]

    def pair(ref):
        return jnp.where(lane == C, ref[first], ref[first + 1])

    free = (lane == C) | (lane == C + 1)
    rows_ref[0:1, :] = masks[0]
    rows_ref[1:2, :] = masks[1]
    rows_ref[2:3, :] = skip_ref[first] * masks[0] + skip_ref[first + 1] * masks[1]
    rows_ref[3:4, :] = ours[4:5, :]
    rows_ref[4:5, :] = jnp.where(free, pair(bias_ref), 0.0)
    rows_ref[5:6, :] = jnp.where(free, jnp.exp(pair(alog_ref)), 0.0)
    rows_ref[6:8, :] = jnp.zeros((2, width), F32)
    channel = lax.broadcasted_iota(jnp.int32, cols_ref.shape, 0)
    slot = lax.broadcasted_iota(jnp.int32, cols_ref.shape, 1) - C
    low = (first + slot) * size - start
    cols_ref[...] = (
        (slot >= 0) & (slot < 2) & (channel < C) & (channel >= low) & (channel < low + size)
    ).astype(F32)
    moves.run(1, 2)

    def take(depth, at):
        row = lax.broadcasted_iota(jnp.int32, (depth, width), 0)
        col = lax.broadcasted_iota(jnp.int32, (depth, width), 1)
        return at(row, col).astype(B16)

    fetch_zx.wait()
    zx = zx_own[...].reshape(D, 2 * inner)
    ours = take(inner, lambda row, col: (row == start + col) & (col < C))
    steps = take(heads, lambda row, col: (row - first == col - C) & (col >= C) & (col < C + 2))
    in_w_ref[:, :width] = (mm(zx[:, :inner], ours) + mm(dt_ref[...], steps, TN)).astype(B16)
    in_w_ref[:, width : 2 * width] = mm(zx[:, inner:], ours).astype(B16)
    in_w_ref[:, 2 * width :] = bc_ref[...]
    moves.run(2, 3)
    up = 2 * up_ref.shape[2]
    fetch_up.wait()
    up_w_ref[:, :up] = up_own[...].reshape(D, up)
    fetch.wait()
    shared = window[...].reshape(D, 2 * LANES)
    offset = pc.slot() * FS - base
    units = take(LANES, lambda row, col: (row == offset + col) & (col < FS))
    names = take(router_ref.shape[0], lambda row, col: col == FS + row)
    up_w_ref[:, up : up + LANES] = (mm(shared[:, :LANES], units) + mm(router_ref[...], names, TN)).astype(B16)
    up_w_ref[:, up + LANES :] = mm(shared[:, LANES:], units).astype(B16)
    moves.run(3)
    mail.finish(gather_count(S, H))


def first_rows(
    hidden_in, gain, routes, conv_x, conv_bc, gate, w_zx, w_bc, w_dt, up, router, shared, bias, alog, skip, C, CP, FS, S, H
):
    R, D = hidden_in.shape
    assert CP == LANES and LANES % FS == 0
    W = D + LANES
    scalars = pl.BlockSpec(memory_space=pltpu.SMEM)
    return pl.pallas_call(
        functools.partial(first_kernel, S, H, C, FS, conv_x.shape[1] // bias.shape[0]),
        out_shape=[
            jax.ShapeDtypeStruct((S * H * R, W), B16),
            jax.ShapeDtypeStruct((8, CP), F32),
            jax.ShapeDtypeStruct((4, CP + conv_bc.shape[1]), F32),
            jax.ShapeDtypeStruct((CP, LANES), F32),
            jax.ShapeDtypeStruct((D, 2 * CP + w_bc.shape[1]), B16),
            jax.ShapeDtypeStruct((D, 2 * up.shape[2] + 2 * LANES), B16),
        ],
        in_specs=[VMEM] * 6 + [ANY, VMEM, VMEM, ANY, VMEM, ANY] + [scalars] * 3,
        out_specs=[ANY] + [VMEM] * 5,
        scratch_shapes=[
            pltpu.VMEM((R, W), B16), pltpu.VMEM((D, 2, LANES), B16), pltpu.VMEM(w_zx.shape, B16), pltpu.VMEM(up.shape, B16),
            *sems(gather_count(S, H)), pltpu.SemaphoreType.DMA, pltpu.SemaphoreType.DMA((3,)),
        ],
        compiler_params=talking(1),
    )(hidden_in, gain, routes, conv_x, conv_bc, gate, w_zx, w_bc, w_dt, up, router, shared, bias, alog, skip)


def seg_of(pos, lengths_ref, count):
    found, end = jnp.zeros(pos.shape, jnp.int32), 0
    for k in range(count):
        end = end + lengths_ref[k]
        found = found + (pos >= end).astype(jnp.int32)
    return jnp.where(pos < 0, -1, found)


def exact(left, right):
    return jnp.dot(left, right, precision=lax.Precision.HIGHEST, preferred_element_type=F32)


def silu(values):
    return values / (1.0 + jnp.exp(-values))


def softplus(values):
    return jnp.maximum(values, 0.0) + jnp.log1p(jnp.exp(-jnp.abs(values)))


class Block:
    def __init__(self, i, pre, ext, z, taps_ref, rows_ref, lengths_ref, count, state, C):
        n = BLOCK
        pos_row = i * n + lax.broadcasted_iota(jnp.int32, (1, n), 1)
        around = seg_of(i * n - 8 + lax.broadcasted_iota(jnp.int32, (n + 16, 1), 0), lengths_ref, count)
        seg, seg_row = around[8 : 8 + n], seg_of(pos_row, lengths_ref, count)
        self.joined = {k: (around[8 - k : 8 - k + n] == seg).astype(F32) for k in (1, 2, 3)}
        self.later = {k: (around[8 + k : 8 + k + n] == seg).astype(F32) for k in (1, 2, 3)}
        conv = taps_ref[3:4, :] * pre
        for k in (1, 2, 3):
            conv = conv + taps_ref[3 - k : 4 - k, :] * ext[8 - k : 8 - k + n, :] * self.joined[k]
        act = silu(conv)
        cp = act.shape[1] - 2 * state
        self.conv = conv
        self.x, self.b, self.c = act[:, :cp], act[:, cp : cp + state].astype(B16), act[:, cp + state :].astype(B16)
        self.m = [rows_ref[j : j + 1, :] for j in range(2)]
        self.skip, self.gain = rows_ref[2:3, :], rows_ref[3:4, :]
        self.C = C
        self.dtr = z + rows_ref[4:5, :]
        self.dt = softplus(self.dtr)
        self.decay = rows_ref[5:6, :]
        self.rate = -self.dt * self.decay
        row, col = lax.broadcasted_iota(jnp.int32, (n, n), 0), lax.broadcasted_iota(jnp.int32, (n, n), 1)
        lower = row >= col
        self.row, self.col = row, col
        logdec = exact(lower.astype(F32), self.rate)
        log_row = logdec.T
        linked = lower & (seg == seg_row)
        self.decays = [
            jnp.exp(jnp.where(linked, logdec[:, C + j : C + j + 1] - log_row[C + j : C + j + 1, :], -1e30)) for j in range(2)
        ]
        scores = mm(self.c, self.b, NT)
        self.mats = [(scores * d).astype(B16) for d in self.decays]
        before = jnp.where(i == 0, -1, seg_of(jnp.full((1, 1), i * n - 1, jnp.int32), lengths_ref, count))
        final = seg_of(jnp.full((1, 1), i * n + n - 1, jnp.int32), lengths_ref, count)
        last = logdec[n - 1 : n, :]
        self.carry = self.spread(jnp.where(seg == before, jnp.exp(logdec), 0.0))
        self.tail = self.spread(jnp.where(seg == final, jnp.exp(last - logdec), 0.0))
        self.keep = self.spread(jnp.where(final == before, jnp.exp(last), 0.0))
        self.dtc = self.spread(self.dt)
        self.xt = (self.dtc * self.x).astype(B16)
        self.low = [m.astype(B16) for m in self.m]
        self.xts = [self.xt * low for low in self.low]
        self.tail_xt = (self.tail * self.xt.astype(F32)).astype(B16)

    def spread(self, values):
        return values[:, self.C : self.C + 1] * self.m[0] + values[:, self.C + 1 : self.C + 2] * self.m[1]

    def inner(self):
        return mm(self.mats[0], self.xts[0]) + mm(self.mats[1], self.xts[1])


def mixer_forward_kernel(
    S, H, count, state, C, lengths_ref, in_ref, w_ref, taps_ref, rows_ref, out_w_ref, grad_ref,
    pre_ref, z_ref, y_ref, st_ref, total_ref, all_ref, held, ext, parts, grad_low, *rest,
):
    i = pl.program_id(0)
    pc = Place(S, H)
    buffers, (send, recv, zsend, zrecv, own_sem) = rest[:-5], rest[-5:]
    X, Y, Z = pc.X, pc.Y, pc.Z
    R = grad_ref.shape[0]
    mail = Mail(send, recv)
    moves = gather(pc, mail, grad_low, all_ref, own_sem)
    acts = Script()
    sums = Sum(
        pc, mail, acts, lambda dz, yy, xx, rows: parts.at[dz, yy, xx, pc.c, rows], lambda dz: parts.at[dz, :, :, 1 - pc.c],
        buffers, R, ends=(zsend, zrecv),
    )
    for dz in range(Z):
        acts.stage()
        sums.across(dz)
        acts.stage()
        sums.cores(dz)
        acts.stage()
        sums.firsts(dz)
        acts.stage()
        sums.seconds(dz)
    acts.stage()
    sums.home(total_ref)
    ready = Y * Z - 1
    before = {k: [] for k in range(Y * Z)}
    for dz in range(Z):
        for late, stage in ((0, 0), (1, 1), (3, 2), (4, 3)):
            k = (dz + 1) * Y + late
            if k <= ready:
                before[k].append((acts, 4 * dz + stage))
    final_acts = [
        (acts, 4 * dz + stage)
        for dz, stage in ((3, 0), (0, 3), (1, 2), (1, 3), (2, 1), (2, 2), (3, 1), (2, 3), (3, 2), (3, 3))
    ]
    final_acts = [entry for entry in final_acts if all(entry not in before[k] for k in before)]

    @pl.when(i == 0)
    def _():
        grad_low[...] = grad_ref[...].astype(B16)
        greet(pc.peers(direct=True))
        moves.run(0, 1)

    for step, stage, until in ((1, 1, 2), (2, 2, 3), (3, 3, 5), (4, 5, 7), (5, 7, 9), (6, 9, 11)):

        @pl.when(i == step)
        def _():
            moves.run(stage, until)

    for at in range(1, Y * Z):
        if before[at]:

            @pl.when(i == at)
            def _():
                for script, stage in before[at]:
                    script.run(stage, stage + 1)

    depth = w_ref.shape[0]
    n, cp = BLOCK, z_ref.shape[1]

    @pl.when(i == 0)
    def _():
        held[...] = jnp.zeros_like(held)
        ext[0:8, :] = jnp.zeros((8, ext.shape[1]), F32)

    made = mm(in_ref[:, :depth], w_ref[...])
    z = made[:, :cp]
    pre = made[:, cp:]
    z_ref[...], pre_ref[...] = z, pre
    ext[8 : 8 + n, :] = pre
    blk = Block(i, pre, ext, z, taps_ref, rows_ref, lengths_ref, count, state, C)
    ext[0:8, :] = pre[n - 8 :, :]
    st = held[...]
    st_ref[0] = st
    y = blk.inner() + blk.carry * mm(blk.c, st.astype(B16))
    held[...] = blk.keep * st + mm(blk.b, blk.tail_xt, TN)
    y = y + blk.skip * blk.x
    y_ref[...] = y
    gated = y * silu(z)
    part = mm((gated * blk.gain).astype(B16), out_w_ref[...]).astype(B16)
    high, rest = hi_lo(jnp.sum(gated * gated, axis=1, keepdims=True))
    lane = lax.broadcasted_iota(jnp.int32, (n, LANES), 1)
    tail = jnp.where(lane == 0, high.astype(F32), jnp.where(lane == 1, rest.astype(F32), 0.0)).astype(B16)
    for xx in range(X):
        for cc in range(2):
            at = slice((xx * 2 + cc) * R, (xx * 2 + cc + 1) * R)
            parts[i // Y, i % Y, xx, cc, :, :depth] = part[at]
            parts[i // Y, i % Y, xx, cc, :, depth:] = tail[at]

    @pl.when(i == ready)
    def _():
        for script, stage in final_acts[:4]:
            script.run(stage, stage + 1)
        moves.run(11)
        for script, stage in final_acts[4:]:
            script.run(stage, stage + 1)
        acts.run(4 * Z)
        mail.finish(gather_count(S, H) + scatter_count(S, H) - 3)


def whole(shape):
    return pl.BlockSpec(shape, lambda i: (0,) * len(shape))


def params():
    return pltpu.CompilerParams(dimension_semantics=("arbitrary",), vmem_limit_bytes=60 * 1024 * 1024)


def mixer_forward(lengths, gathered, in_w, taps, rows, out_w, grad, state, C, S, H):
    T, depth = gathered.shape[0], in_w.shape[0]
    X, Y, Z = sizes(S, H)
    R = grad.shape[0]
    cp, nb = out_w.shape[0], gathered.shape[0] // BLOCK
    conv_width = cp + 2 * state

    def block(width):
        return pl.BlockSpec((BLOCK, width), lambda i: (i, 0))

    return pl.pallas_call(
        functools.partial(mixer_forward_kernel, S, H, lengths.shape[0], state, C),
        grid=(nb,),
        in_specs=[
            pl.BlockSpec(memory_space=pltpu.SMEM), block(gathered.shape[1]), whole(in_w.shape), whole(taps.shape),
            whole(rows.shape), whole(out_w.shape), VMEM,
        ],
        out_specs=[
            block(conv_width), block(cp), block(cp),
            pl.BlockSpec((1, state, cp), lambda i: (i, 0, 0)), VMEM, ANY,
        ],
        out_shape=[
            jax.ShapeDtypeStruct((T, conv_width), F32),
            jax.ShapeDtypeStruct((T, cp), F32),
            jax.ShapeDtypeStruct((T, cp), F32),
            jax.ShapeDtypeStruct((nb, state, cp), F32),
            jax.ShapeDtypeStruct((R, depth + LANES), F32),
            jax.ShapeDtypeStruct((T, depth), B16),
        ],
        scratch_shapes=[
            pltpu.VMEM((state, cp), F32), pltpu.VMEM((BLOCK + 8, conv_width), F32),
            pltpu.VMEM((Z, Y, X, 2, R, depth + LANES), B16), pltpu.VMEM((R, depth), B16), *sum_scratch(S, H, R, depth + LANES),
            *sems(gather_count(S, H) + scatter_count(S, H) - 3),
            pltpu.SemaphoreType.DMA((4,)), pltpu.SemaphoreType.DMA((3,)), pltpu.SemaphoreType.DMA,
        ],
        compiler_params=talking(5),
    )(lengths, gathered, in_w, taps, rows, out_w, grad)


def mixer_backward_kernel(
    S, H, beside, count, state, C, lengths_ref, three_ref, one_ref, pre_ref, halo_ref, z_ref, y_ref, st_ref,
    w_ref, taps_ref, rows_ref, cols_ref, out_w_ref, p_ref, res_ref, gres_ref, in_ref, gain_ref, norm2_ref, router_ref,
    output_ref, gin_ref, extra_ref, small_out, zx_out, wo_out,
    held, ext, gext, gw_ref, gout_ref, gtaps_ref, gvec_ref, gnorm_ref, total, parts, extra, zx_ref, wo_ref, small, joint,
    *rest,
):
    step = pl.program_id(0)
    i = pl.num_programs(0) - 1 - step
    depth = w_ref.shape[0]
    n, cp = BLOCK, z_ref.shape[1]

    n1, n2 = 8 if beside else 0, 6
    scratch, main, side = rest[:n1], rest[n1 : n1 + n2], rest[n1 + n2 : n1 + n2 + 4]
    send, recv, send2, recv2, zsend, zrecv, group_send, group_recv, local_sem = rest[n1 + n2 + 4 :]
    pc = Place(S, H)
    X, Y, Z = pc.X, pc.Y, pc.Z
    N, me, R = S * H, pc.slot(), res_ref.shape[0]
    seq, head = lax.axis_index("seq"), lax.axis_index("head")
    mail = Mail(send, recv)
    sums = scatter(pc, mail, [(p_ref, total, scratch, True)]) if beside else Script([[] for _ in range(9)])

    mail2 = Mail(send2, recv2)
    acts = Script()
    ones = Sum(
        pc, mail2, acts, lambda dz, yy, xx, rows: parts.at[dz, yy, xx, pc.c, rows], lambda dz: parts.at[dz, :, :, 1 - pc.c],
        main, R, ends=(zsend, zrecv),
    )
    for dz in range(Z):
        acts.stage()
        ones.across(dz)
        acts.stage()
        ones.cores(dz)
        acts.stage()
        ones.firsts(dz)
        acts.stage()
        ones.seconds(dz)
    acts.stage()
    ones.home(total)
    tall = extra.shape[4]
    sides = Script()
    other = Sum(
        pc, mail2, sides, lambda dz, yy, xx, rows: extra.at[pc.at(dz=dz)[0], yy, xx, pc.c, rows],
        lambda dz: extra.at[pc.at(dz=dz)[0], :, :, 1 - pc.c],
        side, tall, split=False, direct=True,
    )
    sides.stage()
    for dz in ORDER:
        other.across(dz)
    sides.stage()
    for dz in ORDER:
        other.cores(dz)
    sides.stage()
    for dz in ORDER:
        other.firsts(dz)
    sides.stage()
    for dz in ORDER:
        other.seconds(dz)
    other.last(extra_ref)
    group, keep_here, column, row = [], [], [], []
    for j, (src, dst) in enumerate(((zx_ref, zx_out), (wo_ref, wo_out))):
        keep_here.append(pltpu.make_async_copy(src.at[seq], dst.at[seq], local_sem.at[j]))
        for m in range(1, S):
            to = (seq + m) % S
            group.append(
                pltpu.make_async_remote_copy(
                    src_ref=src.at[to], dst_ref=dst.at[seq], send_sem=group_send.at[j, m],
                    recv_sem=group_recv.at[j, m], device_id=(to, head), device_id_type=MESH,
                )
            )
    for m in range(1, S):
        column.append(
            pltpu.make_async_remote_copy(
                src_ref=small.at[seq], dst_ref=small.at[seq], send_sem=group_send.at[2, m], recv_sem=group_recv.at[2, m],
                device_id=((seq + m) % S, head), device_id_type=MESH,
            )
        )
    for m in range(1, H):
        row.append(
            pltpu.make_async_remote_copy(
                src_ref=joint, dst_ref=small_out.at[head], send_sem=group_send.at[3, m], recv_sem=group_recv.at[3, m],
                device_id=(seq, (head + m) % H), device_id_type=MESH,
            )
        )
    keep_joint = pltpu.make_async_copy(joint, small_out.at[head], local_sem.at[2])
    total_steps = Y * Z
    before = {k: [] for k in range(total_steps)}
    for k, stage in ((2, 2), (3, 3), (4, 4), (5, 5), (6, 6), (7, 7)):
        before[k].append((sums, stage))
    final_acts = []
    for dz in (3, 2, 1, 0):
        for late, stage in ((0, 0), (1, 1), (3, 2), (4, 3)):
            k = (Z - dz) * Y + late
            if k < total_steps:
                before[k].append((acts, 4 * dz + stage))
    final_acts = [(acts, 4 * dz + stage) for dz, stage in ((0, 0), (3, 3), (2, 2), (2, 3), (1, 1), (1, 2), (0, 1), (1, 3), (0, 2), (0, 3))]
    final_acts = [entry for entry in final_acts if all(entry not in before[k] for k in before)]
    @pl.when(step == 0)
    def _():
        sums.run(0, 1)
        greet([((seq + m) % S, head) for m in range(1, S)] + [(seq, (head + m) % H) for m in range(1, H)])
        sums.run(1, 2)

    for at in range(1, total_steps):
        if before[at]:

            @pl.when(step == at)
            def _():
                for script, stage in before[at]:
                    script.run(stage, stage + 1)

    @pl.when(step == 0)
    def _():
        gnorm_ref[...] = jnp.zeros_like(gnorm_ref)
        held[...] = jnp.zeros_like(held)
        gext[n : n + 8, :] = jnp.zeros((8, gext.shape[1]), F32)
        gw_ref[...] = jnp.zeros_like(gw_ref)
        extra[...] = jnp.zeros_like(extra)
        zx_ref[...] = jnp.zeros_like(zx_ref)
        wo_ref[...] = jnp.zeros_like(wo_ref)
        gout_ref[...] = jnp.zeros_like(gout_ref)
        gtaps_ref[...] = jnp.zeros_like(gtaps_ref)
        gvec_ref[...] = jnp.zeros_like(gvec_ref)

    pre, z, y = pre_ref[...], z_ref[...], y_ref[...]
    ext[0:8, :] = jnp.where(i == 0, 0.0, halo_ref[...])
    ext[8 : 8 + n, :] = pre
    blk = Block(i, pre, ext, z, taps_ref, rows_ref, lengths_ref, count, state, C)
    three = three_ref[:, :depth]
    pg = mm(three, out_w_ref[...], NT)
    cross = jnp.sum(three_ref[:, depth:].astype(F32), axis=1, keepdims=True)
    act_z = silu(z)
    gated = y * act_z
    gout_ref[...] += mm((gated * blk.gain).astype(B16), three, TN)
    grad_gated = pg * blk.gain - gated * cross
    gy = grad_gated * act_z
    gz = grad_gated * y * silu_grad(z)
    st = st_ref[0]
    st_low, grad = st.astype(B16), held[...]
    grad_low = grad.astype(B16)
    gy_low = gy.astype(B16)
    y_all = blk.inner() + blk.carry * mm(blk.c, st_low)
    back = sum(mm(blk.mats[j], gy_low * blk.low[j], TN) for j in range(2))
    gate = (blk.carry * gy_low.astype(F32)).astype(B16)
    tail_back = blk.tail * mm(blk.b, grad_low)
    pull = sum(mm(gy_low, blk.xts[j], NT) * blk.decays[j] for j in range(2)).astype(B16)
    g_c = mm(pull, blk.b) + mm(gate, st_low, NT)
    g_b = mm(pull, blk.c, TN) + mm(blk.tail_xt, grad_low, NT)
    held[...] = blk.keep * grad + mm(blk.c, gate, TN)
    g_xt = back + tail_back
    xt = blk.xt.astype(F32)
    cols = cols_ref[...]
    after = exact(gy_low.astype(F32) * y_all - xt * back, cols)
    used = exact(xt * tail_back, cols)
    through = exact(jnp.broadcast_to(blk.keep * jnp.sum(grad * st, axis=0, keepdims=True), (8, cp)), cols)[0:1, :]
    g_rate = (
        exact((blk.row <= blk.col).astype(F32), after) + exact((blk.row > blk.col).astype(F32), used) + through
    )
    g_dt = exact(g_xt * blk.x, cols) - g_rate * blk.decay
    g_dtr = g_dt / (1.0 + jnp.exp(-blk.dtr))
    g_x = g_xt * blk.dtc + blk.skip * gy
    for r, v in enumerate((pg * gated, g_dtr, g_rate * blk.rate, gy * blk.x)):
        gvec_ref[r : r + 1, :] += jnp.sum(v, axis=0, keepdims=True)
    gconv = jnp.concatenate([g_x, g_b, g_c], axis=1) * silu_grad(blk.conv)
    gext[0:n, :] = gconv
    gpre = taps_ref[3:4, :] * gconv
    gtaps_ref[3:4, :] += jnp.sum(gconv * pre, axis=0, keepdims=True)
    for k in (1, 2, 3):
        gpre = gpre + taps_ref[3 - k : 4 - k, :] * gext[k : n + k, :] * blk.later[k]
        gtaps_ref[3 - k : 4 - k, :] += jnp.sum(gconv * ext[8 - k : 8 - k + n, :] * blk.joined[k], axis=0, keepdims=True)
    gext[n : n + 8, :] = gconv[0:8, :]
    made = jnp.concatenate([gz + g_dtr, gpre], axis=1).astype(B16)
    one = one_ref[:, :depth]
    part = mm(made, w_ref[...], NT)
    part_low = part.astype(B16)
    for xx in range(X):
        for cc in range(2):
            at = slice((xx * 2 + cc) * R, (xx * 2 + cc + 1) * R)
            parts[i // Y, i % Y, xx, cc] = part_low[at]
    gnorm_ref[...] += jnp.sum(part * one.astype(F32), axis=0, keepdims=True)
    gw_ref[...] += mm(made, one, TN)

    @pl.when(i == 0)
    def _():
        acts.run(0, 1)
        line = 0
        for ref in (gnorm_ref, norm2_ref):
            for j in range(depth // LANES):
                small[seq, line : line + 1, :] = ref[0:1, j * LANES : (j + 1) * LANES]
                line += 1
        for r in range(4):
            for j in range(2 * state // LANES):
                small[seq, line : line + 1, :] = gtaps_ref[r : r + 1, cp + j * LANES : cp + (j + 1) * LANES]
                line += 1
        small[seq, line : line + 4, :] = gtaps_ref[0:4, :cp]
        small[seq, line + 4 : line + 7, :] = gvec_ref[0:3, :]
        small[seq, line + 7 : line + 8, :] = exact(gvec_ref[...], cols)[3:4, :]
        for copy in column:
            copy.start()
        wide = depth // S
        cut = zx_ref.shape[1]
        for t in range(S):
            at = slice(t * wide, (t + 1) * wide)
            zx_ref[t, :, :wide] = gw_ref[:cut, at].astype(B16)
            zx_ref[t, :, wide:] = gw_ref[cp : cp + cut, at].astype(B16)
            wo_ref[t] = gout_ref[: wo_ref.shape[1], at].astype(B16)
        for copy in keep_here + group:
            copy.start()
        for script, stage in final_acts[1:5]:
            script.run(stage, stage + 1)
        per = depth // N
        bc = gw_ref[2 * cp :, :].T
        router = router_ref[...].astype(F32)
        for t in range(N):
            at = slice(t * per, (t + 1) * per)
            where = (t // (Y * X * 2), t // (X * 2) % Y, t // 2 % X, t % 2)
            extra[(*where, slice(0, per), slice(0, 2 * state))] = bc[at].astype(B16)
            extra[(*where, slice(0, per), slice(2 * state, 2 * state + LANES))] = router[at].astype(B16)
        sides.run(0, 1)
        for script, stage in final_acts[5:7]:
            script.run(stage, stage + 1)
        sides.run(1, 2)
        for copy in column:
            copy.wait_recv()
        joint[0:line, :] = functools.reduce(jnp.add, [small[t, 0:line, :] for t in range(S)])
        for t in range(S):
            joint[line + 8 * t : line + 8 * t + 8, :] = small[t, line : line + 8, :]
        keep_joint.start()
        for copy in row:
            copy.start()
        for script, stage in final_acts[7:]:
            script.run(stage, stage + 1)
        sides.run(2, 3)
        sums.run(8)
        output_ref[...] = res_ref[...] + total[...] if beside else res_ref[...]
        sides.run(3)
        acts.run(4 * Z)
        values, gone = in_ref[...], total[...]
        gin_ref[...] = gres_ref[...] + rms_back(values, inverse_rms(values), gain_ref[...].reshape(1, depth), gone)
        for copy in row:
            copy.wait()
        for copy in column:
            copy.wait_send()
        keep_joint.wait()
        for copy in keep_here + group:
            copy.wait()
        mail.finish(scatter_count(S, H) if beside else 0)
        mail2.finish(scatter_count(S, H) - 3 + scatter_count(S, H, (False,)))


def mixer_backward(
    lengths, three, one, pre, z, y, states, in_w, taps, rows, cols, out_w, out_part, residual, grad_res, hidden_in, gain,
    norm2, router_part, state, C, S, H,
):
    T, depth = three.shape[0], in_w.shape[0]
    cp, nb = out_w.shape[0], T // BLOCK
    conv_width = cp + 2 * state
    R, N = residual.shape[0], S * H
    X, Y, Z = sizes(S, H)
    line = 2 * (depth // LANES) + 4 * (2 * state // LANES)
    tall = -(-(depth // N) // 16) * 16
    zx_rows = -(-(C + 2) // 16) * 16
    beside = Y == 2
    wo_rows = -(-C // 16) * 16
    assert line % 8 == 0 and cp == LANES and R * H == BLOCK
    sent = scatter_count(S, H) - 3 + scatter_count(S, H, (False,))

    def block(width, kept=2):
        return pl.BlockSpec((BLOCK, width), lambda k: (nb - 1 - k, 0), pipeline_mode=pl.Buffered(kept))

    kept = 2 if beside else 1

    def halo(k):
        return (jnp.maximum((nb - 1 - k) * (BLOCK // 8) - 1, 0), 0)

    return pl.pallas_call(
        functools.partial(mixer_backward_kernel, S, H, beside, lengths.shape[0], state, C),
        grid=(nb,),
        in_specs=[
            pl.BlockSpec(memory_space=pltpu.SMEM), block(three.shape[1]), block(one.shape[1], kept), block(conv_width, kept),
            pl.BlockSpec((8, conv_width), halo), block(cp), block(cp),
            pl.BlockSpec((1, state, cp), lambda k: (nb - 1 - k, 0, 0)),
            VMEM, VMEM, VMEM, VMEM, VMEM, ANY, VMEM, VMEM, VMEM, VMEM, VMEM, VMEM,
        ],
        out_specs=[VMEM, VMEM, VMEM, ANY, ANY, ANY],
        out_shape=[
            jax.ShapeDtypeStruct((R, depth), F32),
            jax.ShapeDtypeStruct((R, depth), F32),
            jax.ShapeDtypeStruct((tall, 2 * state + LANES), F32),
            jax.ShapeDtypeStruct((H, line + 8 * S, LANES), F32),
            jax.ShapeDtypeStruct((S, zx_rows, 2 * (depth // S)), B16),
            jax.ShapeDtypeStruct((S, wo_rows, depth // S), B16),
        ],
        scratch_shapes=[
            pltpu.VMEM((state, cp), F32),
            pltpu.VMEM((BLOCK + 8, conv_width), F32),
            pltpu.VMEM((BLOCK + 8, conv_width), F32),
            pltpu.VMEM((in_w.shape[1], depth), F32),
            pltpu.VMEM(out_w.shape, F32),
            pltpu.VMEM((8, conv_width), F32),
            pltpu.VMEM((8, cp), F32),
            pltpu.VMEM((1, depth), F32),
            pltpu.VMEM((R, depth), F32),
            pltpu.VMEM((Z, Y, X, 2, R, depth), B16),
            pltpu.VMEM((Z, Y, X, 2, tall, 2 * state + LANES), B16),
            pltpu.VMEM((S, zx_rows, 2 * (depth // S)), B16),
            pltpu.VMEM((S, wo_rows, depth // S), B16),
            pltpu.VMEM((S, line + 8, LANES), F32),
            pltpu.VMEM((line + 8 * S, LANES), F32),
            *(scatter_scratch(S, H, R, depth) if beside else []),
            *sum_scratch(S, H, R, depth),
            *sum_scratch(S, H, tall, 2 * state + LANES, False),
            *sems(scatter_count(S, H)),
            *sems(sent),
            pltpu.SemaphoreType.DMA((4,)), pltpu.SemaphoreType.DMA((3,)),
            pltpu.SemaphoreType.DMA((4, S)), pltpu.SemaphoreType.DMA((4, S)),
            pltpu.SemaphoreType.DMA((3,)),
        ],
        compiler_params=talking(6),
    )(
        lengths, three, one, pre, pre, z, y, states, in_w, taps, rows, cols, out_w, blocks(out_part, S, H), residual,
        grad_res, hidden_in, gain, norm2, router_part,
    )


def expert_block(F, two, grad, named, mine, up_ref, down_ref, gup_ref, gdown_ref, gs_ref):
    mid = mm(two, up_ref[...])
    back = mm(grad, down_ref[...], NT)
    gate, lin = mid[:, :F], mid[:, F : 2 * F]
    s_gate, s_lin = mid[:, 2 * F : 2 * F + LANES], mid[:, 2 * F + LANES :]
    named = named.astype(F32) > 0
    logits = jnp.where(named, s_gate, -1e30)
    odds = jnp.where(named, jnp.exp(logits - jnp.max(logits, axis=1, keepdims=True)), 0.0)
    probs = odds / jnp.sum(odds, axis=1, keepdims=True)
    weight = jnp.sum(probs * mine, axis=1, keepdims=True)
    s_back, back = back[:, F:], back[:, :F]
    act_gate, act_s = silu(gate), silu(s_gate)
    acting = act_gate * lin
    gp = jnp.sum(acting * back, axis=1, keepdims=True)
    back = weight * back
    down_in = jnp.concatenate([weight * acting, act_s * s_lin], axis=1).astype(B16)
    mid_grad = jnp.concatenate(
        [back * lin * silu_grad(gate), back * act_gate, s_back * s_lin * silu_grad(s_gate), s_back * act_s], axis=1
    ).astype(B16)
    gup_ref[...] += mm(two, mid_grad[:, : 2 * F], TN)
    gdown_ref[...] += mm(down_in[:, :F], grad, TN)
    gs_ref[: 2 * LANES, :] += mm(mid_grad[:, 2 * F :], two, TN)
    gs_ref[2 * LANES :, :] += mm(down_in[:, F:], grad, TN)
    out = mm(down_in, down_ref[...]).astype(B16)
    part = mm(mid_grad, up_ref[...], NT).astype(B16)
    return out, part, (gp * mine).astype(B16), probs


def expert_kernel(
    S, H, F, width, total_ref, in_ref, gain_ref, grad_ref, named_ref, up_ref, down_ref, mine_ref, ograd_ref,
    three_ref, res_ref, gres_ref, gnorm_ref, grouter_ref, out_ref, gup_out, gdown_ref, sh_out,
    gup_ref, total, rows, two, grads, names, parts, stage_out, probs, gs_ref, *rest,
):
    buffers, (rows3, pieces, send2, recv2, sh_send, sh_recv, own_sem, own3_sem, sh_sem, name_sem, grad_sem, out_sem) = (
        rest[:-12], rest[-12:]
    )
    pc = Place(S, H)
    X, Y, Z = pc.X, pc.Y, pc.Z
    R, D = in_ref.shape
    n = BLOCK
    N, me = S * H, pc.slot()
    mail2 = Mail(send2, recv2)
    stay = pltpu.make_async_copy(pieces.at[me], sh_out.at[me], sh_sem)

    def to_all(function):
        def body(m, carry):
            to = (me + m) % N
            function(
                pltpu.make_async_remote_copy(
                    src_ref=pieces.at[to], dst_ref=sh_out.at[me], send_sem=sh_send.at[m], recv_sem=sh_recv.at[m],
                    device_id=(to // H, to % H), device_id_type=MESH,
                )
            )
            return carry

        lax.fori_loop(1, N, body, 0)

    def cell(dz, yy, xx, rows):
        return parts.at[dz, yy, xx, pc.c, rows]

    moves = gather(pc, mail2, rows, two, own_sem, planes=True)
    onward = gather(pc, mail2, rows3, three_ref, own3_sem)
    acts = Script()
    second = Sum(pc, mail2, acts, cell, lambda dz: parts.at[dz, :, :, 1 - pc.c], buffers, R, direct=True)
    for dz in range(Z):
        acts.stage()
        second.across(dz)
        acts.stage()
        second.cores(dz)
        acts.stage()
        second.firsts(dz)
        acts.stage()
        second.seconds(dz)
    acts.stage()
    second.last(total)

    def seq_of(k):
        return pc.partner(k // Y) * Y + k % Y

    def loads(k, slot):
        at = pl.ds(pl.multiple_of(seq_of(k) * n, n), n)
        return [
            pltpu.make_async_copy(grad_ref.at[at], grads.at[slot], grad_sem.at[slot]),
            pltpu.make_async_copy(named_ref.at[at, pl.ds(D, LANES)], names.at[slot], name_sem.at[slot]),
        ]

    def store(k, slot):
        at = pl.ds(pl.multiple_of(seq_of(k) * n, n), n)
        return pltpu.make_async_copy(stage_out.at[slot], out_ref.at[at], out_sem.at[slot])

    for copy in loads(0, 0):
        copy.start()
    gain = gain_ref[...].reshape(1, D)
    mixed = total_ref[:, :D]
    square = jnp.sum(total_ref[:, D:], axis=1, keepdims=True)
    inv = lax.rsqrt(square / width + EPS)
    residual = in_ref[...] + inv * mixed
    res_ref[...] = residual
    rows[...] = (residual * inverse_rms(residual) * gain).astype(B16)
    cube = inv * inv * inv / width
    barrier = pltpu.get_barrier_semaphore()

    def hello(m, carry):
        to = (me + m) % N
        pl.semaphore_signal(barrier, inc=1, device_id=(to // H, to % H), device_id_type=MESH)
        return carry

    lax.fori_loop(1, N, hello, 0)
    pl.semaphore_wait(barrier, N - 1)
    moves.run(0, 1)
    gup_ref[...] = jnp.zeros_like(gup_ref)
    gdown_ref[...] = jnp.zeros_like(gdown_ref)
    gs_ref[...] = jnp.zeros_like(gs_ref)
    moves.run(1, 5)
    moves.run(12, 13)

    count = Y * Z
    before = {k: [] for k in range(count)}
    after = []
    for dz in range(Z):
        for late, stage in ((0, 0), (1, 1), (3, 2), (4, 3)):
            k = (dz + 1) * Y + late
            before.get(k, after).append((acts, 4 * dz + stage))
    after = [(acts, 4 * dz + stage) for dz, stage in ((3, 0), (1, 2), (1, 3), (2, 2), (3, 1), (2, 3), (3, 2), (3, 3))]
    after = [entry for entry in after if all(entry not in before[k] for k in before)]
    for k, stage in (
        (0, 5), (1, 6), (1, 7), (Y, 8), (Y, 13), (Y + 1, 9), (Y + 1, 10), (2 * Y, 11), (2 * Y, 14), (3 * Y, 15),
    ):
        before[k].append((moves, stage))
    mine = mine_ref[...]

    def step(k, carry):
        for at in range(count):
            if before[at]:

                @pl.when(k == at)
                def _():
                    for script, stage in before[at]:
                        script.run(stage, stage + 1)

        slot = k % 2

        @pl.when(k + 1 < count)
        def _():
            for copy in loads(k + 1, 1 - slot):
                copy.start()

        for copy in loads(k, slot):
            copy.wait()
        block = two[pl.ds(pl.multiple_of(seq_of(k) * n, n), n), :]
        out, part, gp, chance = expert_block(
            F, block, grads[slot], names[slot], mine, up_ref, down_ref, gup_ref, gdown_ref, gs_ref
        )
        for xx in range(X):
            for cc in range(2):
                at = slice((xx * 2 + cc) * R, (xx * 2 + cc + 1) * R)
                parts[k // Y, k % Y, xx, cc, :, :D] = part[at]
                parts[k // Y, k % Y, xx, cc, :, D:] = gp[at]

        @pl.when(k == pc.y)
        def _():
            probs[...] = chance

        @pl.when(k >= 2)
        def _():
            store(k - 2, slot).wait()

        stage_out[slot] = out
        store(k, slot).start()
        return carry

    lax.fori_loop(0, count, step, 0)
    for script, stage in after[:1]:
        script.run(stage, stage + 1)
    for k in range(2):
        gup_out[0, :, k, :] = gup_ref[:, k * F : (k + 1) * F]
    per, FS = D // N, pieces.shape[2] // 3
    turned = jnp.concatenate([gs_ref[k * LANES : k * LANES + FS, :] for k in range(3)], axis=0).T
    for k in range(N):
        pieces[k, :per, :] = turned[k * per : (k + 1) * per, :].astype(B16)
        if per < pieces.shape[1]:
            pieces[k, per:, :] = jnp.zeros((pieces.shape[1] - per, 3 * FS), B16)
    for script, stage in after[1:]:
        script.run(stage, stage + 1)
    head = lax.axis_index("head")
    p = probs[pl.ds(pl.multiple_of(head * R, R), R), :]
    acts.run(4 * Z)
    gp = total[:, D:]
    glogits = (p * (gp - jnp.sum(p * gp, axis=1, keepdims=True))).astype(B16)
    gtwo = total[:, :D] + mm(glogits, up_ref[:, 2 * F : 2 * F + LANES], NT)
    residual = res_ref[...]
    inv_two = inverse_rms(residual)
    gres = ograd_ref[...] + rms_back(residual, inv_two, gain, gtwo)
    cross = jnp.sum(gres * mixed, axis=1, keepdims=True) * cube
    high, low = hi_lo(cross)
    lane = lax.broadcasted_iota(jnp.int32, (R, LANES), 1)
    rows3[:, :D] = (inv * gres).astype(B16)
    rows3[:, D:] = jnp.where(lane == 0, high.astype(F32), jnp.where(lane == 1, low.astype(F32), 0.0)).astype(B16)
    onward.run(0, 1)
    stay.start()
    to_all(lambda copy: copy.start())
    gres_ref[...] = gres
    gnorm_ref[...] = jnp.sum(gtwo * residual * inv_two, axis=0, keepdims=True)
    grouter_ref[...] = mm((residual * inv_two * gain).astype(B16), glogits, TN).astype(B16)
    for k in (count - 2, count - 1):
        store(k, k % 2).wait()
    onward.run(1)
    to_all(lambda copy: copy.wait())
    stay.wait()
    mail2.finish(2 * gather_count(S, H) + scatter_count(S, H))


def experts(total, hidden_in, gain, all_grad, gathered, up_w, down_w, mine, out_grad, F, FS, width, S, H):
    R, D = hidden_in.shape
    X, Y, Z = sizes(S, H)
    T, W = S * H * R, D + LANES
    tall = -(-(D // (S * H)) // 16) * 16
    assert R * H == BLOCK
    return pl.pallas_call(
        functools.partial(expert_kernel, S, H, F, width),
        out_shape=[
            jax.ShapeDtypeStruct((T, W), B16),
            jax.ShapeDtypeStruct((R, D), F32),
            jax.ShapeDtypeStruct((R, D), F32),
            jax.ShapeDtypeStruct((1, D), F32),
            jax.ShapeDtypeStruct((D, LANES), B16),
            jax.ShapeDtypeStruct((T, D), B16),
            jax.ShapeDtypeStruct((1, D, 2, F), F32),
            jax.ShapeDtypeStruct((F, D), F32),
            jax.ShapeDtypeStruct((S * H, tall, 3 * FS), B16),
        ],
        in_specs=[VMEM, VMEM, VMEM, ANY, ANY] + [VMEM] * 4,
        out_specs=[ANY] + [VMEM] * 4 + [ANY] + [VMEM] * 2 + [ANY],
        scratch_shapes=[
            pltpu.VMEM((D, 2 * F), F32), pltpu.VMEM((R, W), F32), pltpu.VMEM((R, D), B16), pltpu.VMEM((T, D), B16),
            pltpu.VMEM((2, BLOCK, D), B16), pltpu.VMEM((2, BLOCK, LANES), B16),
            pltpu.VMEM((Z, Y, X, 2, R, W), B16), pltpu.VMEM((2, BLOCK, D), B16), pltpu.VMEM((BLOCK, LANES), F32),
            pltpu.VMEM((3 * LANES, D), F32), *sum_scratch(S, H, R, W),
            pltpu.VMEM((R, W), B16), pltpu.VMEM((S * H, tall, 3 * FS), B16),
            *sems(scatter_count(S, H) + 2 * gather_count(S, H)), *sems(S * H),
            pltpu.SemaphoreType.DMA, pltpu.SemaphoreType.DMA, pltpu.SemaphoreType.DMA, pltpu.SemaphoreType.DMA((2,)),
            pltpu.SemaphoreType.DMA((2,)), pltpu.SemaphoreType.DMA((2,)),
        ],
        compiler_params=talking(2),
    )(total, hidden_in, gain, all_grad, gathered, up_w, down_w, mine, out_grad)


def finish_kernel(
    S, H, C, FS, state, zx_ref, wo_ref, sh_ref, small_ref, pick_ref, kcip_ref, gain_ref, a_in, b_in, c_in, d_in,
    zx_out, dt_out, wo_out, up_out, down_out, norm1_out, norm2_out, taps_out, bc_out, gate_out, heads_out,
    a_out, b_out, c_out, d_out, a_way, b_way, c_way, d_way, sem,
):
    ways = ((a_in, a_way, a_out), (b_in, b_way, b_out), (c_in, c_way, c_out), (d_in, d_way, d_out))
    held = [pltpu.make_async_copy(src, way, sem.at[0, k]) for k, (src, way, dst) in enumerate(ways)]
    gone = [pltpu.make_async_copy(way, dst, sem.at[1, k]) for k, (src, way, dst) in enumerate(ways)]
    for copy in held:
        copy.start()
    wide = wo_ref.shape[2]
    heads = dt_out.shape[0]
    dt = jnp.zeros(dt_out.shape, F32)
    for t in range(S):
        piece = zx_ref[t].astype(F32)
        turned = piece.T
        at = slice(t * C, (t + 1) * C)
        zx_out[:, 0, at] = turned[:wide, :C]
        zx_out[:, 1, at] = turned[wide:, :C]
        dt = dt + exact(kcip_ref[t, :, : piece.shape[0]], piece[:, :wide])
        wo_out[:, at] = wo_ref[t].astype(F32).T[:, :C]
    dt_out[...] = dt
    for come, go in zip(held, gone):
        come.wait()
        go.start()
    for t in range(S * H):
        piece = sh_ref[t].astype(F32)[: up_out.shape[0]]
        at = slice(t * FS, (t + 1) * FS)
        for k in range(2):
            up_out[:, k, at] = piece[:, k * FS : (k + 1) * FS]
        down_out[:, at] = piece[:, 2 * FS :]
    gain = gain_ref[...].reshape(1, gain_ref.shape[0])
    lines = gain.shape[1] // LANES
    total = small_ref[0, : 2 * lines + 4 * (2 * state // LANES), :]
    for h in range(1, H):
        total = total + small_ref[h, : total.shape[0], :]
    for j in range(lines):
        at = slice(j * LANES, (j + 1) * LANES)
        norm1_out[:, at] = total[j : j + 1, :] / gain[:, at]
        norm2_out[:, at] = total[lines + j : lines + j + 1, :]
    line = 2 * lines
    for r in range(4):
        for j in range(2 * state // LANES):
            bc_out[r : r + 1, j * LANES : (j + 1) * LANES] = total[line : line + 1, :]
            line += 1
    for h in range(H):
        by_head = jnp.zeros((8, heads), F32)
        for t in range(S):
            ours = small_ref[h, line + 8 * t : line + 8 * t + 8, :]
            at = slice((h * S + t) * C, (h * S + t + 1) * C)
            taps_out[:, at] = ours[0:4, :C]
            gate_out[:, at] = ours[4:5, :C]
            by_head = by_head + exact(ours, pick_ref[t])
        for r in range(3):
            heads_out[r : r + 1, h * heads : (h + 1) * heads] = by_head[5 + r : 6 + r, :]
    for copy in gone:
        copy.wait()


def finish(zx, wo, shared, small, pick, gain, made, C, FS, state, S, H):
    N, wide, heads, D = S * H, wo.shape[2], pick.shape[2], gain.shape[0]
    per = D // N
    shapes = (
        (wide, 2, S * C), (heads, wide), (wide, S * C), (per, 2, N * FS), (per, N * FS), (1, D), (1, D), (4, S * H * C),
        (4, 2 * state), (1, S * H * C), (3, H * heads),
    )
    return pl.pallas_call(
        functools.partial(finish_kernel, S, H, C, FS, state),
        out_shape=[jax.ShapeDtypeStruct(shape, F32) for shape in shapes + tuple(v.shape for v in made)],
        in_specs=[VMEM] * 7 + [ANY] * 4,
        out_specs=[VMEM] * len(shapes) + [ANY] * 4,
        scratch_shapes=[*(pltpu.VMEM(v.shape, F32) for v in made), pltpu.SemaphoreType.DMA((2, 4))],
        compiler_params=pltpu.CompilerParams(vmem_limit_bytes=56 * 1024 * 1024),
    )(zx, wo, shared, small, pick, pick.transpose(0, 2, 1), gain, *made)


def local(
    hidden_in, norm1_gain, w_zx, w_bc, w_dt, conv_x, conv_bc, dt_bias, a_log, d_skip, gate_gain,
    w_out, norm2_gain, router, expert_up, expert_down, shared_up, shared_down, out_grad,
    seq_lengths, routes,
):
    S, H = lax.axis_size("seq"), lax.axis_size("head")
    N = S * H
    s = lax.axis_index("seq")
    g = s * H + lax.axis_index("head")
    R, D = hidden_in.shape
    heads, inner = dt_bias.shape[0], conv_x.shape[1]
    size = inner // heads
    state = w_bc.shape[1] // 2
    width = inner * H
    C = inner // S
    CP = -(-(C + 2) // LANES) * LANES
    E = N // 2
    F = expert_down.shape[1]
    FS = shared_down.shape[0] // N
    per = D // N

    gain1, gain2 = norm1_gain, norm2_gain
    gathered, rows, taps, cols, in_w, up_w = first_rows(
        hidden_in, gain1, routes.T, conv_x, conv_bc, gate_gain, w_zx, w_bc, w_dt.T, expert_up[0], router.T, shared_up,
        dt_bias, a_log, d_skip, C, CP, FS, S, H
    )

    firsts = [min(k * C // size, heads - 2) for k in range(S)]

    def mine(values, axis, offset, length):
        return lax.dynamic_slice_in_dim(values, offset, length, axis)

    def channels(values, axis):
        cut = mine(values, axis, s * C, C)
        pads = [(0, 0)] * values.ndim
        pads[axis] = (0, CP - C)
        return jnp.pad(cut, pads)

    out_w = channels(w_out, 0)

    pre, z, y, states, mixed, all_grad = mixer_forward(
        seq_lengths, gathered, in_w, taps, rows, out_w, out_grad, state, C, S, H
    )

    down_w = jnp.concatenate([expert_down[0], mine(shared_down, 0, g * FS, FS), jnp.zeros((LANES - FS, D), B16)], axis=0)
    is_mine = (jnp.arange(LANES) == FS + g // 2).astype(F32)[None]
    three, residual, grad_res, norm2_part, router_part, out_part, grad_up, grad_down, sh_in = experts(
        mixed, hidden_in, gain2, all_grad, gathered, up_w, down_w, is_mine, out_grad, F, FS, width, S, H
    )

    output, grad_in, extra_sum, small, zx_in, wo_in = mixer_backward(
        seq_lengths, three, gathered, pre, z, y, states, in_w, taps, rows, cols, out_w, out_part, residual,
        grad_res, hidden_in, gain1, norm2_part, router_part, state, C, S, H,
    )
    if H > 4:
        output = output + lax.psum_scatter(out_part, ("seq", "head"), scatter_dimension=0, tiled=True).astype(F32)
    grad_bc, grad_router = extra_sum[:per, : 2 * state], extra_sum[:per, 2 * state :][:, FS : FS + E]
    pick = np.array(
        [[[C <= c < C + 2 and firsts[k] + c - C == h for h in range(heads)] for c in range(LANES)] for k in range(S)], np.float32
    )
    grad_zx, grad_w_dt, grad_w_out, grad_shared_up, grad_shared_down, *found = finish(
        zx_in, wo_in, sh_in, small, pick, gain1, (grad_up, grad_down[None], output, grad_in), C, FS, state, S, H
    )
    grad_norm1, grad_norm2, grad_conv_x, grad_conv_bc, grad_gate_gain, by_head, *made = found
    grad_up, grad_down, output, grad_in = made
    grad_norm1, grad_norm2, grad_gate_gain = (v.reshape(-1) for v in (grad_norm1, grad_norm2, grad_gate_gain))
    grad_dt_bias, grad_a_log, grad_d_skip = by_head[0], by_head[1], by_head[2]
    return (
        output, grad_in, grad_norm1, grad_zx, grad_bc, grad_w_dt.T, grad_conv_x, grad_conv_bc, grad_dt_bias,
        grad_a_log, grad_d_skip, grad_gate_gain, grad_w_out.T, grad_norm2, grad_router, grad_up, grad_down,
        grad_shared_up, grad_shared_down.T,
    )


def solution(mesh):
    return jax.shard_map(
        local,
        mesh=mesh,
        in_specs=(
            P(("seq", "head"), None),
            P(),
            P(None, None, "head"),
            P(),
            P(None, "head"),
            P(None, "head"),
            P(),
            P("head"),
            P("head"),
            P("head"),
            P("head"),
            P("head", None),
            P(),
            P(),
            P(("seq", "head"), None, None, None),
            P(("seq", "head"), None, None),
            P(),
            P(),
            P(("seq", "head"), None),
            P(),
            P(("seq", "head"), None),
        ),
        out_specs=(
            P(("seq", "head"), None),
            P(("seq", "head"), None),
            P(),
            P("seq", None, "head"),
            P(("seq", "head"), None),
            P("seq", "head"),
            P(),
            P(),
            P(),
            P(),
            P(),
            P(),
            P("head", "seq"),
            P(),
            P(("seq", "head"), None),
            P(("seq", "head"), None, None, None),
            P(("seq", "head"), None, None),
            P(("seq", "head"), None, None),
            P(None, ("seq", "head")),
        ),
        check_vma=False,
    )
```

```python
import functools
import jax
import jax.numpy as jnp
import numpy as np
from jax import lax
from jax.experimental import pallas as pl
from jax.experimental.pallas import tpu as pltpu
from jax.sharding import PartitionSpec as P

MESH = pl.DeviceIdType.MESH
BLOCK = 256
EPS = 1e-05
LANES = 128
B16 = jnp.bfloat16
F32 = jnp.float32


def mm(left, right, dims=(((1,), (0,)), ((), ()))):
    return lax.dot_general(left, right, dims, preferred_element_type=F32)


NT = (((1,), (1,)), ((), ()))
TN = (((0,), (0,)), ((), ()))


def inverse_rms(values):
    return lax.rsqrt(jnp.mean(values * values, axis=-1, keepdims=True) + EPS)


def rms_back(values, inverse, gain, grad):
    weighted = grad * gain
    inner = jnp.mean(weighted * values, axis=-1, keepdims=True)
    return inverse * weighted - values * inverse**3 * inner


def silu_grad(values):
    sig = jax.nn.sigmoid(values)
    return sig * (1.0 + values * (1.0 - sig))


def pad_lanes(values, width):
    return jnp.pad(values, [(0, 0)] * (values.ndim - 1) + [(0, width - values.shape[-1])])


def hi_lo(values):
    high = values.astype(B16)
    return high, (values - high.astype(F32)).astype(B16)


def sizes(seq_size, head_size):
    return head_size // 2, head_size // 2, seq_size // (head_size // 2)


class Place:
    def __init__(self, seq_size, head_size):
        self.H = head_size
        self.X, self.Y, self.Z = sizes(seq_size, head_size)
        assert self.Z == 4
        seq, head = lax.axis_index("seq"), lax.axis_index("head")
        self.z, self.y = seq // self.Y, seq % self.Y
        self.x, self.c = head // 2, head % 2
        z = self.z
        self.partners = (z, z + 1 - 2 * (z % 2), (z + 2) % 4, 3 - z)

    def at(self, dz=0, dy=0, dx=0, dc=0):
        return (
            self.partners[dz],
            (self.y + dy) % self.Y if dy else self.y,
            (self.x + dx) % self.X if dx else self.x,
            1 - self.c if dc else self.c,
        )

    def dev(self, **where):
        z, y, x, c = self.at(**where)
        return (z * self.Y + y, x * 2 + c)

    def slot(self, **where):
        z, y, x, c = self.at(**where)
        return (z * self.Y + y) * self.H + x * 2 + c

    def partner(self, dz):
        return (self.z // 2 + dz // 2) % 2 * 2 + (self.z + dz) % 2

    def peers(self, direct=False):
        out = [self.dev(dz=k) for k in range(1, 4 if direct else 3)]
        out += [self.dev(dy=k) for k in range(1, self.Y)]
        out += [self.dev(dx=k) for k in range(1, self.X)]
        return out + [self.dev(dc=1)]


def hail(peers):
    for peer in peers:
        pl.semaphore_signal(pltpu.get_barrier_semaphore(), inc=1, device_id=peer, device_id_type=MESH)


def settle(count):
    pl.semaphore_wait(pltpu.get_barrier_semaphore(), count)


class Mail:
    def __init__(self, send, recv):
        self.send, self.recv, self.made = send, recv, []

    def copy(self, src, dst, dev):
        i = len(self.made)
        self.made.append(
            pltpu.make_async_remote_copy(
                src_ref=src, dst_ref=dst, send_sem=self.send.at[i], recv_sem=self.recv.at[i],
                device_id=dev, device_id_type=MESH,
            )
        )
        return self.made[-1]

    def finish(self, count):
        assert len(self.made) == count
        for copy in self.made:
            copy.wait_send()


class Script(list):
    def stage(self):
        self.append([])

    def do(self, action):
        self[-1].append(action)

    def run(self, first=0, last=None):
        for stage in self[first:last]:
            for action in stage:
                action()


def gather_count(S, H):
    X, Y, Z = sizes(S, H)
    return (Z - 1) + 2 * Z * (X + Y - 2) + 2 * Z * (X - 1) * (Y - 1) + X * Y * Z


def gather(pc, mail, x_ref, out_ref, own_sem, planes=False):
    X, Y, Z = pc.X, pc.Y, pc.Z
    R = x_ref.shape[0]
    half = R // 2
    script = Script()

    def rows(part, **where):
        base = pl.multiple_of(pc.slot(**where) * R, R)
        if part is None:
            return out_ref.at[pl.ds(base, R)]
        return out_ref.at[pl.ds(pl.multiple_of(base + part * half, half), half)]

    def send(src, dst, dev):
        copy = mail.copy(src, dst, dev)
        script.do(copy.start)
        return copy

    x_in, y_in, dga, dgb = {}, {}, {}, {}
    sib = {dz: [] for dz in range(Z)}

    def column(dz):
        for part in (0, 1):
            src = x_ref.at[pl.ds(part * half, half)] if dz == 0 else rows(part, dz=dz)
            for k in range(1, X):
                x_in[dz, k, part] = send(src, rows(part, dz=dz), pc.dev(dx=k))
            other = 1 - part
            src = x_ref.at[pl.ds(other * half, half)] if dz == 0 else rows(other, dz=dz)
            for k in range(1, Y):
                y_in[dz, k, other] = send(src, rows(other, dz=dz), pc.dev(dy=k))
        src = x_ref if dz == 0 else rows(None, dz=dz)
        sib[dz].append(send(src, rows(None, dz=dz), pc.dev(dc=1)))

    def onward(dz):
        for k in range(1, X):
            script.do(x_in[dz, k, 0].wait_recv)
            block = rows(0, dz=dz, dx=-k)
            for m in range(1, Y):
                dga[dz, k, m] = send(block, block, pc.dev(dy=m))
        for k in range(1, Y):
            script.do(y_in[dz, k, 1].wait_recv)
            block = rows(1, dz=dz, dy=-k)
            for m in range(1, X):
                dgb[dz, k, m] = send(block, block, pc.dev(dx=m))
        for k in range(1, X):
            script.do(x_in[dz, k, 1].wait_recv)
            block = rows(None, dz=dz, dx=-k)
            sib[dz].append(send(block, block, pc.dev(dc=1)))
        for k in range(1, Y):
            script.do(y_in[dz, k, 0].wait_recv)
            block = rows(None, dz=dz, dy=-k)
            sib[dz].append(send(block, block, pc.dev(dc=1)))

    def corner(dz):
        for k in range(1, X):
            for m in range(1, Y):
                script.do(dga[dz, k, m].wait_recv)
                script.do(dgb[dz, m, k].wait_recv)
                block = rows(None, dz=dz, dx=-k, dy=-m)
                sib[dz].append(send(block, block, pc.dev(dc=1)))

    own = pltpu.make_async_copy(x_ref, rows(None), own_sem)
    script.stage()
    script.do(own.start)
    first = send(x_ref, rows(None), pc.dev(dz=1))
    column(0)
    second = send(x_ref, rows(None), pc.dev(dz=2))
    script.stage()
    script.do(first.wait_recv)
    column(1)
    script.stage()
    onward(0)
    script.stage()
    corner(0)
    script.stage()
    script.do(second.wait_recv)
    third = send(rows(None, dz=2), rows(None, dz=2), pc.dev(dz=1))
    column(2)
    script.stage()
    onward(1)
    script.stage()
    script.do(third.wait_recv)
    column(3)
    script.stage()
    corner(1)
    for dz in (2, 3):
        script.stage()
        onward(dz)
        script.stage()
        corner(dz)
    if not planes:
        for dz in range(Z):
            for copy in sib[dz]:
                script.do(copy.wait_recv)
        script.do(own.wait)
        return script
    for dz in range(Z):
        script.stage()
        for copy in sib[dz]:
            script.do(copy.wait_recv)
        if dz == 0:
            script.do(own.wait)
    return script


def scatter_parts(split):
    return (("y", 0), ("x", 1)) if split else (("x", None),)


def scatter_count(S, H, splits=(True,)):
    X, Y, Z = sizes(S, H)
    pieces = sum(len(scatter_parts(split)) for split in splits)
    return len(splits) * (Z + Z - 1) + pieces * Z * (X + Y - 2)


def sum_scratch(S, H, R, W, split=True):
    X, Y, Z = sizes(S, H)
    out = [pltpu.VMEM((Z, Y, X, R, W), B16), pltpu.VMEM((Z - 1, R, W), B16)]
    for axis, part in scatter_parts(split):
        rows = R if part is None else R // 2
        first, second = (Y, X) if axis == "y" else (X, Y)
        out += [pltpu.VMEM((Z, first - 1, second, rows, W), B16), pltpu.VMEM((Z, second - 1, rows, W), B16)]
    return out


def scatter_scratch(S, H, R, W, split=True):
    X, Y, Z = sizes(S, H)
    return [pltpu.VMEM((Z, Y, X, R, W), B16), *sum_scratch(S, H, R, W, split), pltpu.SemaphoreType.DMA((Z,))]


def accumulate(dst, srcs, rows):
    def action():
        def body(i, carry):
            at = pl.ds(pl.multiple_of(i * 16, 16), 16)
            total = dst.at[at][...].astype(F32)
            for src in srcs:
                total = total + src.at[at][...].astype(F32)
            dst.at[at][...] = total.astype(dst.dtype)
            return carry

        lax.fori_loop(0, rows // 16, body, 0)

    return action


ORDER = (3, 2, 1, 0)


class Sum:
    def __init__(self, pc, mail, script, cell, theirs, buffers, R, split=True, direct=False, ends=None):
        self.ends = ends
        self.pc, self.mail, self.script, self.cell, self.theirs = pc, mail, script, cell, theirs
        self.r0, self.r3, self.buffers, self.R, self.split, self.direct = buffers[0], buffers[1], buffers[2:], R, split, direct
        self.sib, self.one, self.two, self.zs = {}, {}, {}, {}

    def send(self, src, dst, dev):
        copy = self.mail.copy(src, dst, dev)
        self.script.do(copy.start)
        return copy

    def pieces(self):
        R = self.R
        for j, (axis, part) in enumerate(scatter_parts(self.split)):
            rows, size = (pl.ds(0, R), R) if part is None else (pl.ds(part * (R // 2), R // 2), R // 2)
            yield j, axis, rows, size, self.buffers[2 * j], self.buffers[2 * j + 1]

    def across(self, dz):
        self.sib[dz] = self.send(self.theirs(dz), self.r0.at[dz], self.pc.dev(dc=1))

    def cores(self, dz):
        pc, whole = self.pc, pl.ds(0, self.R)
        self.script.do(self.sib[dz].wait_recv)
        for yy in range(pc.Y):
            for xx in range(pc.X):
                self.script.do(accumulate(self.cell(dz, yy, xx, whole), [self.r0.at[dz, yy, xx]], self.R))
        for j, axis, rows, size, r1, r2 in self.pieces():
            for k in range(1, pc.Y if axis == "y" else pc.X):
                if axis == "y":
                    src, dev = self.cell(dz, pc.at(dy=k)[1], slice(None), rows), pc.dev(dy=k)
                else:
                    src, dev = self.cell(dz, slice(None), pc.at(dx=k)[2], rows), pc.dev(dx=k)
                self.one[dz, j, k] = self.send(src, r1.at[dz, k - 1], dev)

    def firsts(self, dz):
        pc = self.pc
        for j, axis, rows, size, r1, r2 in self.pieces():
            steps = range(1, pc.Y if axis == "y" else pc.X)
            for k in steps:
                self.script.do(self.one[dz, j, k].wait_recv)
            for m in range(pc.X if axis == "y" else pc.Y):
                dst = self.cell(dz, pc.y, m, rows) if axis == "y" else self.cell(dz, m, pc.x, rows)
                self.script.do(accumulate(dst, [r1.at[dz, k - 1, m] for k in steps], size))
            for k in range(1, pc.X if axis == "y" else pc.Y):
                if axis == "y":
                    src, dev = self.cell(dz, pc.y, pc.at(dx=k)[2], rows), pc.dev(dx=k)
                else:
                    src, dev = self.cell(dz, pc.at(dy=k)[1], pc.x, rows), pc.dev(dy=k)
                self.two[dz, j, k] = self.send(src, r2.at[dz, k - 1], dev)

    def seconds(self, dz):
        pc = self.pc
        for j, axis, rows, size, r1, r2 in self.pieces():
            steps = range(1, pc.X if axis == "y" else pc.Y)
            for k in steps:
                self.script.do(self.two[dz, j, k].wait_recv)
            mine = self.cell(dz, pc.y, pc.x, rows)
            self.script.do(accumulate(mine, [r2.at[dz, k - 1] for k in steps], size))
        mine = self.cell(dz, pc.y, pc.x, pl.ds(0, self.R))
        if self.ends is not None:
            self.homeward(dz, mine)
            return
        if self.direct:
            if dz:
                self.zs[dz] = self.send(mine, self.r3.at[dz - 1], pc.dev(dz=dz))
            return
        if dz == 2:
            self.script.do(self.zs[3].wait_recv)
            self.script.do(accumulate(mine, [self.r3.at[0]], self.R))
        if dz:
            self.zs[dz] = self.send(mine, self.r3.at[3 - dz], pc.dev(dz=2 if dz == 2 else 1))

    def homeward(self, plane, mine):
        pc, (zsend, zrecv) = self.pc, self.ends
        at = (pc.z - plane + 3) % 4
        copy = pltpu.make_async_remote_copy(
            src_ref=mine, dst_ref=self.r3.at[at], send_sem=zsend.at[plane], recv_sem=zrecv.at[at],
            device_id=(plane * pc.Y + pc.y, pc.x * 2 + pc.c), device_id_type=MESH,
        )
        self.zs[plane] = copy

        def start():
            @pl.when(pc.z != plane)
            def _():
                copy.start()

        self.script.do(start)

    def home(self, total):
        pc, (zsend, zrecv) = self.pc, self.ends
        mine = self.cell(pc.z, pc.y, pc.x, pl.ds(0, self.R))
        copies = [
            pltpu.make_async_remote_copy(
                src_ref=mine, dst_ref=self.r3.at[k], send_sem=zsend.at[0], recv_sem=zrecv.at[k],
                device_id=pc.dev(dz=1), device_id_type=MESH,
            )
            for k in range(3)
        ]

        def body(i, carry):
            at = pl.ds(pl.multiple_of(i * 16, 16), 16)
            value = mine.at[at][...].astype(F32)
            for k in range(3):
                value = value + self.r3.at[k, at][...].astype(F32)
            total.at[at][...] = value
            return carry

        def sent():
            for plane in range(4):

                @pl.when(pc.z != plane)
                def _():
                    self.zs[plane].wait_send()

        for copy in copies:
            self.script.do(copy.wait_recv)
        self.script.do(lambda: lax.fori_loop(0, self.R // 16, body, 0))
        self.script.do(sent)

    def last(self, total):
        ends = (1, 2, 3) if self.direct else (2, 1)
        slots = (0, 1, 2) if self.direct else (1, 2)
        for dz in ends:
            self.script.do(self.zs[dz].wait_recv)
        pc, mine = self.pc, self.cell(0, self.pc.y, self.pc.x, pl.ds(0, self.R))

        def body(i, carry):
            at = pl.ds(pl.multiple_of(i * 16, 16), 16)
            value = mine.at[at][...].astype(F32)
            for k in slots:
                value = value + self.r3.at[k, at][...].astype(F32)
            total.at[at][...] = value
            return carry

        self.script.do(lambda: lax.fori_loop(0, self.R // 16, body, 0))


def scatter(pc, mail, jobs):
    script = Script()
    own, sums = {}, []

    def make(p_ref, t0, scratch, split):
        return Sum(
            pc, mail, script, lambda dz, yy, xx, rows: t0.at[dz, yy, xx, rows],
            lambda dz: p_ref.at[pc.at(dz=dz)[0], :, :, 1 - pc.c], scratch[1:-1], p_ref.shape[4], split,
        )

    for p_ref, total, scratch, split in jobs:
        sums.append(make(p_ref, scratch[0], scratch, split))
    script.stage()
    for o, (p_ref, total, scratch, split) in enumerate(jobs):
        for dz in ORDER:
            own[o, dz] = pltpu.make_async_copy(
                p_ref.at[pc.at(dz=dz)[0], :, :, pc.c], scratch[0].at[dz], scratch[-1].at[dz]
            )
            script.do(own[o, dz].start)
    script.stage()
    for dz in ORDER:
        for each in sums:
            each.across(dz)

    def cores(dz):
        for o, each in enumerate(sums):
            script.do(own[o, dz].wait)
            each.cores(dz)

    script.stage()
    cores(3)
    cores(2)
    script.stage()
    cores(1)
    cores(0)
    script.stage()
    for dz in ORDER:
        if dz < 3:
            script.stage()
        for each in sums:
            each.firsts(dz)
        if dz < 3:
            for each in sums:
                each.seconds(dz + 1)
    script.stage()
    for each, (p_ref, total, scratch, split) in zip(sums, jobs):
        each.seconds(0)
        each.last(total)
    return script


ANY = pl.BlockSpec(memory_space=pl.ANY)
VMEM = pl.BlockSpec(memory_space=pltpu.VMEM)


def sems(count):
    return [pltpu.SemaphoreType.DMA((count,)), pltpu.SemaphoreType.DMA((count,))]


def talking(cid):
    return pltpu.CompilerParams(collective_id=cid, has_side_effects=True, vmem_limit_bytes=60 * 1024 * 1024)


def blocks(part, S, H):
    X, Y, Z = sizes(S, H)
    return part.reshape(Z, Y, X, 2, part.shape[0] // (S * H), part.shape[1])


def first_kernel(
    S, H, C, FS, size, in_ref, gain_ref, routes_ref, conv_ref, conv_bc_ref, gate_ref, zx_ref, bc_ref, dt_ref, up_ref, router_ref,
    shared_ref, bias_ref, alog_ref, skip_ref,
    out_ref, rows_ref, taps_ref, cols_ref, in_w_ref, up_w_ref, rows, window, zx_own, up_own, send, recv, own_sem, window_sem,
):
    pc = Place(S, H)
    R, D = in_ref.shape
    peers = pc.peers()
    hail(peers)
    base = pl.multiple_of(pc.slot() * FS // LANES * LANES, LANES)
    fetch = pltpu.make_async_copy(shared_ref.at[:, :, pl.ds(base, LANES)], window, window_sem.at[0])
    fetch_zx = pltpu.make_async_copy(zx_ref, zx_own, window_sem.at[1])
    fetch_up = pltpu.make_async_copy(up_ref, up_own, window_sem.at[2])
    for copy in (fetch_zx, fetch_up, fetch):
        copy.start()
    values = in_ref[...]
    rows[:, :D] = (values * inverse_rms(values) * gain_ref[...].reshape(1, D)).astype(B16)
    line = lax.broadcasted_iota(jnp.int32, (LANES, R), 0)
    named = jnp.zeros((LANES, R), F32)
    for k in range(routes_ref.shape[0]):
        named = named + (routes_ref[k : k + 1, :] == line - FS).astype(F32)
    rows[:, D:] = named.T.astype(B16)
    mail = Mail(send, recv)
    moves = gather(pc, mail, rows, out_ref, own_sem)
    settle(len(peers))
    moves.run(0, 1)

    heads, inner, width = bias_ref.shape[0], conv_ref.shape[1], rows_ref.shape[1]
    start = lax.axis_index("seq") * C
    first = jnp.minimum(start // size, heads - 2)
    lane = lax.broadcasted_iota(jnp.int32, (1, width), 1)
    masks = []
    for j in range(2):
        low = (first + j) * size - start
        masks.append(((lane < C) & (lane >= low) & (lane < low + size)).astype(F32))
    cut = (
        lax.broadcasted_iota(jnp.int32, (inner, width), 0) == start + lax.broadcasted_iota(jnp.int32, (inner, width), 1)
    ) & (lax.broadcasted_iota(jnp.int32, (inner, width), 1) < C)
    ours = exact(jnp.concatenate([conv_ref[...], gate_ref[...].reshape(1, inner), jnp.zeros((3, inner), F32)], axis=0), cut.astype(F32))
    taps_ref[:, :width] = ours[0:4, :]
    taps_ref[:, width:] = conv_bc_ref[...]

    def pair(ref):
        return jnp.where(lane == C, ref[first], ref[first + 1])

    free = (lane == C) | (lane == C + 1)
    rows_ref[0:1, :] = masks[0]
    rows_ref[1:2, :] = masks[1]
    rows_ref[2:3, :] = skip_ref[first] * masks[0] + skip_ref[first + 1] * masks[1]
    rows_ref[3:4, :] = ours[4:5, :]
    rows_ref[4:5, :] = jnp.where(free, pair(bias_ref), 0.0)
    rows_ref[5:6, :] = jnp.where(free, jnp.exp(pair(alog_ref)), 0.0)
    rows_ref[6:8, :] = jnp.zeros((2, width), F32)
    channel = lax.broadcasted_iota(jnp.int32, cols_ref.shape, 0)
    slot = lax.broadcasted_iota(jnp.int32, cols_ref.shape, 1) - C
    low = (first + slot) * size - start
    cols_ref[...] = (
        (slot >= 0) & (slot < 2) & (channel < C) & (channel >= low) & (channel < low + size)
    ).astype(F32)
    moves.run(1, 2)

    def take(depth, at):
        row = lax.broadcasted_iota(jnp.int32, (depth, width), 0)
        col = lax.broadcasted_iota(jnp.int32, (depth, width), 1)
        return at(row, col).astype(B16)

    fetch_zx.wait()
    zx = zx_own[...].reshape(D, 2 * inner)
    ours = take(inner, lambda row, col: (row == start + col) & (col < C))
    steps = take(heads, lambda row, col: (row - first == col - C) & (col >= C) & (col < C + 2))
    in_w_ref[:, :width] = (mm(zx[:, :inner], ours) + mm(dt_ref[...], steps, TN)).astype(B16)
    in_w_ref[:, width : 2 * width] = mm(zx[:, inner:], ours).astype(B16)
    in_w_ref[:, 2 * width :] = bc_ref[...]
    moves.run(2, 3)
    up = 2 * up_ref.shape[2]
    fetch_up.wait()
    up_w_ref[:, :up] = up_own[...].reshape(D, up)
    fetch.wait()
    shared = window[...].reshape(D, 2 * LANES)
    offset = pc.slot() * FS - base
    units = take(LANES, lambda row, col: (row == offset + col) & (col < FS))
    names = take(router_ref.shape[0], lambda row, col: col == FS + row)
    up_w_ref[:, up : up + LANES] = (mm(shared[:, :LANES], units) + mm(router_ref[...], names, TN)).astype(B16)
    up_w_ref[:, up + LANES :] = mm(shared[:, LANES:], units).astype(B16)
    moves.run(3)
    mail.finish(gather_count(S, H))


def first_rows(
    hidden_in, gain, routes, conv_x, conv_bc, gate, w_zx, w_bc, w_dt, up, router, shared, bias, alog, skip, C, CP, FS, S, H
):
    R, D = hidden_in.shape
    assert CP == LANES and LANES % FS == 0
    W = D + LANES
    scalars = pl.BlockSpec(memory_space=pltpu.SMEM)
    return pl.pallas_call(
        functools.partial(first_kernel, S, H, C, FS, conv_x.shape[1] // bias.shape[0]),
        out_shape=[
            jax.ShapeDtypeStruct((S * H * R, W), B16),
            jax.ShapeDtypeStruct((8, CP), F32),
            jax.ShapeDtypeStruct((4, CP + conv_bc.shape[1]), F32),
            jax.ShapeDtypeStruct((CP, LANES), F32),
            jax.ShapeDtypeStruct((D, 2 * CP + w_bc.shape[1]), B16),
            jax.ShapeDtypeStruct((D, 2 * up.shape[2] + 2 * LANES), B16),
        ],
        in_specs=[VMEM] * 6 + [ANY, VMEM, VMEM, ANY, VMEM, ANY] + [scalars] * 3,
        out_specs=[ANY] + [VMEM] * 5,
        scratch_shapes=[
            pltpu.VMEM((R, W), B16), pltpu.VMEM((D, 2, LANES), B16), pltpu.VMEM(w_zx.shape, B16), pltpu.VMEM(up.shape, B16),
            *sems(gather_count(S, H)), pltpu.SemaphoreType.DMA, pltpu.SemaphoreType.DMA((3,)),
        ],
        compiler_params=talking(1),
    )(hidden_in, gain, routes, conv_x, conv_bc, gate, w_zx, w_bc, w_dt, up, router, shared, bias, alog, skip)


def seg_of(pos, lengths_ref, count):
    found, end = jnp.zeros(pos.shape, jnp.int32), 0
    for k in range(count):
        end = end + lengths_ref[k]
        found = found + (pos >= end).astype(jnp.int32)
    return jnp.where(pos < 0, -1, found)


def exact(left, right):
    return jnp.dot(left, right, precision=lax.Precision.HIGHEST, preferred_element_type=F32)


def silu(values):
    return values / (1.0 + jnp.exp(-values))


def softplus(values):
    return jnp.maximum(values, 0.0) + jnp.log1p(jnp.exp(-jnp.abs(values)))


class Block:
    def __init__(self, i, pre, ext, z, taps_ref, rows_ref, lengths_ref, count, state, C):
        n = BLOCK
        pos_row = i * n + lax.broadcasted_iota(jnp.int32, (1, n), 1)
        around = seg_of(i * n - 8 + lax.broadcasted_iota(jnp.int32, (n + 16, 1), 0), lengths_ref, count)
        seg, seg_row = around[8 : 8 + n], seg_of(pos_row, lengths_ref, count)
        self.joined = {k: (around[8 - k : 8 - k + n] == seg).astype(F32) for k in (1, 2, 3)}
        self.later = {k: (around[8 + k : 8 + k + n] == seg).astype(F32) for k in (1, 2, 3)}
        conv = taps_ref[3:4, :] * pre
        for k in (1, 2, 3):
            conv = conv + taps_ref[3 - k : 4 - k, :] * ext[8 - k : 8 - k + n, :] * self.joined[k]
        act = silu(conv)
        cp = act.shape[1] - 2 * state
        self.conv = conv
        self.x, self.b, self.c = act[:, :cp], act[:, cp : cp + state].astype(B16), act[:, cp + state :].astype(B16)
        self.m = [rows_ref[j : j + 1, :] for j in range(2)]
        self.skip, self.gain = rows_ref[2:3, :], rows_ref[3:4, :]
        self.C = C
        self.dtr = z + rows_ref[4:5, :]
        self.dt = softplus(self.dtr)
        self.decay = rows_ref[5:6, :]
        self.rate = -self.dt * self.decay
        row, col = lax.broadcasted_iota(jnp.int32, (n, n), 0), lax.broadcasted_iota(jnp.int32, (n, n), 1)
        lower = row >= col
        self.row, self.col = row, col
        logdec = exact(lower.astype(F32), self.rate)
        log_row = logdec.T
        linked = lower & (seg == seg_row)
        self.decays = [
            jnp.exp(jnp.where(linked, logdec[:, C + j : C + j + 1] - log_row[C + j : C + j + 1, :], -1e30)) for j in range(2)
        ]
        scores = mm(self.c, self.b, NT)
        self.mats = [(scores * d).astype(B16) for d in self.decays]
        before = jnp.where(i == 0, -1, seg_of(jnp.full((1, 1), i * n - 1, jnp.int32), lengths_ref, count))
        final = seg_of(jnp.full((1, 1), i * n + n - 1, jnp.int32), lengths_ref, count)
        last = logdec[n - 1 : n, :]
        self.carry = self.spread(jnp.where(seg == before, jnp.exp(logdec), 0.0))
        self.tail = self.spread(jnp.where(seg == final, jnp.exp(last - logdec), 0.0))
        self.keep = self.spread(jnp.where(final == before, jnp.exp(last), 0.0))
        self.dtc = self.spread(self.dt)
        self.xt = (self.dtc * self.x).astype(B16)
        self.low = [m.astype(B16) for m in self.m]
        self.xts = [self.xt * low for low in self.low]
        self.tail_xt = (self.tail * self.xt.astype(F32)).astype(B16)

    def spread(self, values):
        return values[:, self.C : self.C + 1] * self.m[0] + values[:, self.C + 1 : self.C + 2] * self.m[1]

    def inner(self):
        return mm(self.mats[0], self.xts[0]) + mm(self.mats[1], self.xts[1])


def mixer_forward_kernel(
    S, H, count, state, C, lengths_ref, in_ref, w_ref, taps_ref, rows_ref, out_w_ref, grad_ref,
    pre_ref, z_ref, y_ref, st_ref, total_ref, all_ref, held, ext, parts, grad_low, *rest,
):
    i = pl.program_id(0)
    pc = Place(S, H)
    buffers, (send, recv, zsend, zrecv, own_sem) = rest[:-5], rest[-5:]
    X, Y, Z = pc.X, pc.Y, pc.Z
    R = grad_ref.shape[0]
    mail = Mail(send, recv)
    moves = gather(pc, mail, grad_low, all_ref, own_sem)
    acts = Script()
    sums = Sum(
        pc, mail, acts, lambda dz, yy, xx, rows: parts.at[dz, yy, xx, pc.c, rows], lambda dz: parts.at[dz, :, :, 1 - pc.c],
        buffers, R, ends=(zsend, zrecv),
    )
    for dz in range(Z):
        acts.stage()
        sums.across(dz)
        acts.stage()
        sums.cores(dz)
        acts.stage()
        sums.firsts(dz)
        acts.stage()
        sums.seconds(dz)
    acts.stage()
    sums.home(total_ref)
    ready = Y * Z - 1
    before = {k: [] for k in range(Y * Z)}
    for dz in range(Z):
        for late, stage in ((0, 0), (1, 1), (3, 2), (4, 3)):
            k = (dz + 1) * Y + late
            if k <= ready:
                before[k].append((acts, 4 * dz + stage))
    final_acts = [
        (acts, 4 * dz + stage)
        for dz, stage in ((3, 0), (0, 3), (1, 2), (1, 3), (2, 1), (2, 2), (3, 1), (2, 3), (3, 2), (3, 3))
    ]
    final_acts = [entry for entry in final_acts if all(entry not in before[k] for k in before)]

    @pl.when(i == 0)
    def _():
        peers = pc.peers(direct=True)
        hail(peers)
        grad_low[...] = grad_ref[...].astype(B16)
        settle(len(peers))
        moves.run(0, 1)

    for step, stage, until in ((1, 1, 2), (2, 2, 3), (3, 3, 5), (4, 5, 7), (5, 7, 9), (6, 9, 11)):

        @pl.when(i == step)
        def _():
            moves.run(stage, until)

    for at in range(1, Y * Z):
        if before[at]:

            @pl.when(i == at)
            def _():
                for script, stage in before[at]:
                    script.run(stage, stage + 1)

    depth = w_ref.shape[0]
    n, cp = BLOCK, z_ref.shape[1]

    @pl.when(i == 0)
    def _():
        held[...] = jnp.zeros_like(held)
        ext[0:8, :] = jnp.zeros((8, ext.shape[1]), F32)

    made = mm(in_ref[:, :depth], w_ref[...])
    z = made[:, :cp]
    pre = made[:, cp:]
    z_ref[...], pre_ref[...] = z, pre
    ext[8 : 8 + n, :] = pre
    blk = Block(i, pre, ext, z, taps_ref, rows_ref, lengths_ref, count, state, C)
    ext[0:8, :] = pre[n - 8 :, :]
    st = held[...]
    st_ref[0] = st
    y = blk.inner() + blk.carry * mm(blk.c, st.astype(B16))
    held[...] = blk.keep * st + mm(blk.b, blk.tail_xt, TN)
    y = y + blk.skip * blk.x
    y_ref[...] = y
    gated = y * silu(z)
    part = mm((gated * blk.gain).astype(B16), out_w_ref[...]).astype(B16)
    high, rest = hi_lo(jnp.sum(gated * gated, axis=1, keepdims=True))
    lane = lax.broadcasted_iota(jnp.int32, (n, LANES), 1)
    tail = jnp.where(lane == 0, high.astype(F32), jnp.where(lane == 1, rest.astype(F32), 0.0)).astype(B16)
    for xx in range(X):
        for cc in range(2):
            at = slice((xx * 2 + cc) * R, (xx * 2 + cc + 1) * R)
            parts[i // Y, i % Y, xx, cc, :, :depth] = part[at]
            parts[i // Y, i % Y, xx, cc, :, depth:] = tail[at]

    @pl.when(i == ready)
    def _():
        for script, stage in final_acts[:4]:
            script.run(stage, stage + 1)
        moves.run(11)
        for script, stage in final_acts[4:]:
            script.run(stage, stage + 1)
        acts.run(4 * Z)
        mail.finish(gather_count(S, H) + scatter_count(S, H) - 3)


def whole(shape):
    return pl.BlockSpec(shape, lambda i: (0,) * len(shape))


def params():
    return pltpu.CompilerParams(dimension_semantics=("arbitrary",), vmem_limit_bytes=60 * 1024 * 1024)


def mixer_forward(lengths, gathered, in_w, taps, rows, out_w, grad, state, C, S, H):
    T, depth = gathered.shape[0], in_w.shape[0]
    X, Y, Z = sizes(S, H)
    R = grad.shape[0]
    cp, nb = out_w.shape[0], gathered.shape[0] // BLOCK
    conv_width = cp + 2 * state

    def block(width):
        return pl.BlockSpec((BLOCK, width), lambda i: (i, 0))

    return pl.pallas_call(
        functools.partial(mixer_forward_kernel, S, H, lengths.shape[0], state, C),
        grid=(nb,),
        in_specs=[
            pl.BlockSpec(memory_space=pltpu.SMEM), block(gathered.shape[1]), whole(in_w.shape), whole(taps.shape),
            whole(rows.shape), whole(out_w.shape), VMEM,
        ],
        out_specs=[
            block(conv_width), block(cp), block(cp),
            pl.BlockSpec((1, state, cp), lambda i: (i, 0, 0)), VMEM, ANY,
        ],
        out_shape=[
            jax.ShapeDtypeStruct((T, conv_width), F32),
            jax.ShapeDtypeStruct((T, cp), F32),
            jax.ShapeDtypeStruct((T, cp), F32),
            jax.ShapeDtypeStruct((nb, state, cp), F32),
            jax.ShapeDtypeStruct((R, depth + LANES), F32),
            jax.ShapeDtypeStruct((T, depth), B16),
        ],
        scratch_shapes=[
            pltpu.VMEM((state, cp), F32), pltpu.VMEM((BLOCK + 8, conv_width), F32),
            pltpu.VMEM((Z, Y, X, 2, R, depth + LANES), B16), pltpu.VMEM((R, depth), B16), *sum_scratch(S, H, R, depth + LANES),
            *sems(gather_count(S, H) + scatter_count(S, H) - 3),
            pltpu.SemaphoreType.DMA((4,)), pltpu.SemaphoreType.DMA((3,)), pltpu.SemaphoreType.DMA,
        ],
        compiler_params=talking(5),
    )(lengths, gathered, in_w, taps, rows, out_w, grad)


def mixer_backward_kernel(
    S, H, beside, count, state, C, lengths_ref, three_ref, one_ref, pre_ref, halo_ref, z_ref, y_ref, st_ref,
    w_ref, taps_ref, rows_ref, cols_ref, out_w_ref, p_ref, res_ref, gres_ref, in_ref, gain_ref, norm2_ref, router_ref,
    output_ref, gin_ref, extra_ref, small_out, zx_out, wo_out,
    held, ext, gext, gw_ref, gout_ref, gtaps_ref, gvec_ref, gnorm_ref, total, parts, extra, zx_ref, wo_ref, small, joint,
    *rest,
):
    step = pl.program_id(0)
    i = pl.num_programs(0) - 1 - step
    depth = w_ref.shape[0]
    n, cp = BLOCK, z_ref.shape[1]

    n1, n2 = 8 if beside else 0, 6
    scratch, main, side = rest[:n1], rest[n1 : n1 + n2], rest[n1 + n2 : n1 + n2 + 4]
    send, recv, send2, recv2, zsend, zrecv, group_send, group_recv, local_sem = rest[n1 + n2 + 4 :]
    pc = Place(S, H)
    X, Y, Z = pc.X, pc.Y, pc.Z
    N, me, R = S * H, pc.slot(), res_ref.shape[0]
    seq, head = lax.axis_index("seq"), lax.axis_index("head")
    mail = Mail(send, recv)
    sums = scatter(pc, mail, [(p_ref, total, scratch, True)]) if beside else Script([[] for _ in range(9)])

    mail2 = Mail(send2, recv2)
    acts = Script()
    ones = Sum(
        pc, mail2, acts, lambda dz, yy, xx, rows: parts.at[dz, yy, xx, pc.c, rows], lambda dz: parts.at[dz, :, :, 1 - pc.c],
        main, R, ends=(zsend, zrecv),
    )
    for dz in range(Z):
        acts.stage()
        ones.across(dz)
        acts.stage()
        ones.cores(dz)
        acts.stage()
        ones.firsts(dz)
        acts.stage()
        ones.seconds(dz)
    acts.stage()
    ones.home(total)
    tall = extra.shape[4]
    sides = Script()
    other = Sum(
        pc, mail2, sides, lambda dz, yy, xx, rows: extra.at[pc.at(dz=dz)[0], yy, xx, pc.c, rows],
        lambda dz: extra.at[pc.at(dz=dz)[0], :, :, 1 - pc.c],
        side, tall, split=False, direct=True,
    )
    sides.stage()
    for dz in ORDER:
        other.across(dz)
    sides.stage()
    for dz in ORDER:
        other.cores(dz)
    sides.stage()
    for dz in ORDER:
        other.firsts(dz)
    sides.stage()
    for dz in ORDER:
        other.seconds(dz)
    other.last(extra_ref)
    group, keep_here, column, row = [], [], [], []
    for j, (src, dst) in enumerate(((zx_ref, zx_out), (wo_ref, wo_out))):
        keep_here.append(pltpu.make_async_copy(src.at[seq], dst.at[seq], local_sem.at[j]))
        for m in range(1, S):
            to = (seq + m) % S
            group.append(
                pltpu.make_async_remote_copy(
                    src_ref=src.at[to], dst_ref=dst.at[seq], send_sem=group_send.at[j, m],
                    recv_sem=group_recv.at[j, m], device_id=(to, head), device_id_type=MESH,
                )
            )
    for m in range(1, S):
        column.append(
            pltpu.make_async_remote_copy(
                src_ref=small.at[seq], dst_ref=small.at[seq], send_sem=group_send.at[2, m], recv_sem=group_recv.at[2, m],
                device_id=((seq + m) % S, head), device_id_type=MESH,
            )
        )
    for m in range(1, H):
        row.append(
            pltpu.make_async_remote_copy(
                src_ref=joint, dst_ref=small_out.at[head], send_sem=group_send.at[3, m], recv_sem=group_recv.at[3, m],
                device_id=(seq, (head + m) % H), device_id_type=MESH,
            )
        )
    keep_joint = pltpu.make_async_copy(joint, small_out.at[head], local_sem.at[2])
    total_steps = Y * Z
    before = {k: [] for k in range(total_steps)}
    for k, stage in ((2, 2), (3, 3), (4, 4), (5, 5), (6, 6), (7, 7)):
        before[k].append((sums, stage))
    final_acts = []
    for dz in (3, 2, 1, 0):
        for late, stage in ((0, 0), (1, 1), (3, 2), (4, 3)):
            k = (Z - dz) * Y + late
            if k < total_steps:
                before[k].append((acts, 4 * dz + stage))
    final_acts = [(acts, 4 * dz + stage) for dz, stage in ((0, 0), (3, 3), (2, 2), (2, 3), (1, 1), (1, 2), (0, 1), (1, 3), (0, 2), (0, 3))]
    final_acts = [entry for entry in final_acts if all(entry not in before[k] for k in before)]
    @pl.when(step == 0)
    def _():
        hail([((seq + m) % S, head) for m in range(1, S)] + [(seq, (head + m) % H) for m in range(1, H)])
        sums.run(0, 1)

    @pl.when(step == 0)
    def _():
        gnorm_ref[...] = jnp.zeros_like(gnorm_ref)
        held[...] = jnp.zeros_like(held)
        gext[n : n + 8, :] = jnp.zeros((8, gext.shape[1]), F32)
        gw_ref[...] = jnp.zeros_like(gw_ref)
        extra[...] = jnp.zeros_like(extra)
        zx_ref[...] = jnp.zeros_like(zx_ref)
        wo_ref[...] = jnp.zeros_like(wo_ref)
        settle(S + H - 2)
        sums.run(1, 2)
        gout_ref[...] = jnp.zeros_like(gout_ref)
        gtaps_ref[...] = jnp.zeros_like(gtaps_ref)
        gvec_ref[...] = jnp.zeros_like(gvec_ref)

    for at in range(1, total_steps):
        if before[at]:

            @pl.when(step == at)
            def _():
                for script, stage in before[at]:
                    script.run(stage, stage + 1)

    pre, z, y = pre_ref[...], z_ref[...], y_ref[...]
    ext[0:8, :] = jnp.where(i == 0, 0.0, halo_ref[...])
    ext[8 : 8 + n, :] = pre
    blk = Block(i, pre, ext, z, taps_ref, rows_ref, lengths_ref, count, state, C)
    three = three_ref[:, :depth]
    pg = mm(three, out_w_ref[...], NT)
    cross = jnp.sum(three_ref[:, depth:].astype(F32), axis=1, keepdims=True)
    act_z = silu(z)
    gated = y * act_z
    gout_ref[...] += mm((gated * blk.gain).astype(B16), three, TN)
    grad_gated = pg * blk.gain - gated * cross
    gy = grad_gated * act_z
    gz = grad_gated * y * silu_grad(z)
    st = st_ref[0]
    st_low, grad = st.astype(B16), held[...]
    grad_low = grad.astype(B16)
    gy_low = gy.astype(B16)
    y_all = blk.inner() + blk.carry * mm(blk.c, st_low)
    back = sum(mm(blk.mats[j], gy_low * blk.low[j], TN) for j in range(2))
    gate = (blk.carry * gy_low.astype(F32)).astype(B16)
    tail_back = blk.tail * mm(blk.b, grad_low)
    pull = sum(mm(gy_low, blk.xts[j], NT) * blk.decays[j] for j in range(2)).astype(B16)
    g_c = mm(pull, blk.b) + mm(gate, st_low, NT)
    g_b = mm(pull, blk.c, TN) + mm(blk.tail_xt, grad_low, NT)
    held[...] = blk.keep * grad + mm(blk.c, gate, TN)
    g_xt = back + tail_back
    xt = blk.xt.astype(F32)
    cols = cols_ref[...]
    after = exact(gy_low.astype(F32) * y_all - xt * back, cols)
    used = exact(xt * tail_back, cols)
    through = exact(jnp.broadcast_to(blk.keep * jnp.sum(grad * st, axis=0, keepdims=True), (8, cp)), cols)[0:1, :]
    g_rate = (
        exact((blk.row <= blk.col).astype(F32), after) + exact((blk.row > blk.col).astype(F32), used) + through
    )
    g_dt = exact(g_xt * blk.x, cols) - g_rate * blk.decay
    g_dtr = g_dt / (1.0 + jnp.exp(-blk.dtr))
    g_x = g_xt * blk.dtc + blk.skip * gy
    for r, v in enumerate((pg * gated, g_dtr, g_rate * blk.rate, gy * blk.x)):
        gvec_ref[r : r + 1, :] += jnp.sum(v, axis=0, keepdims=True)
    gconv = jnp.concatenate([g_x, g_b, g_c], axis=1) * silu_grad(blk.conv)
    gext[0:n, :] = gconv
    gpre = taps_ref[3:4, :] * gconv
    gtaps_ref[3:4, :] += jnp.sum(gconv * pre, axis=0, keepdims=True)
    for k in (1, 2, 3):
        gpre = gpre + taps_ref[3 - k : 4 - k, :] * gext[k : n + k, :] * blk.later[k]
        gtaps_ref[3 - k : 4 - k, :] += jnp.sum(gconv * ext[8 - k : 8 - k + n, :] * blk.joined[k], axis=0, keepdims=True)
    gext[n : n + 8, :] = gconv[0:8, :]
    made = jnp.concatenate([gz + g_dtr, gpre], axis=1).astype(B16)
    one = one_ref[:, :depth]
    part = mm(made, w_ref[...], NT)
    part_low = part.astype(B16)
    for xx in range(X):
        for cc in range(2):
            at = slice((xx * 2 + cc) * R, (xx * 2 + cc + 1) * R)
            parts[i // Y, i % Y, xx, cc] = part_low[at]
    gnorm_ref[...] += jnp.sum(part * one.astype(F32), axis=0, keepdims=True)
    gw_ref[...] += mm(made, one, TN)

    @pl.when(i == 0)
    def _():
        acts.run(0, 1)
        line = 0
        for ref in (gnorm_ref, norm2_ref):
            for j in range(depth // LANES):
                small[seq, line : line + 1, :] = ref[0:1, j * LANES : (j + 1) * LANES]
                line += 1
        for r in range(4):
            for j in range(2 * state // LANES):
                small[seq, line : line + 1, :] = gtaps_ref[r : r + 1, cp + j * LANES : cp + (j + 1) * LANES]
                line += 1
        small[seq, line : line + 4, :] = gtaps_ref[0:4, :cp]
        small[seq, line + 4 : line + 7, :] = gvec_ref[0:3, :]
        small[seq, line + 7 : line + 8, :] = exact(gvec_ref[...], cols)[3:4, :]
        for copy in column:
            copy.start()
        wide = depth // S
        cut = zx_ref.shape[1]
        for t in range(S):
            at = slice(t * wide, (t + 1) * wide)
            zx_ref[t, :, :wide] = gw_ref[:cut, at].astype(B16)
            zx_ref[t, :, wide:] = gw_ref[cp : cp + cut, at].astype(B16)
            wo_ref[t] = gout_ref[: wo_ref.shape[1], at].astype(B16)
        for copy in keep_here + group:
            copy.start()
        for script, stage in final_acts[1:5]:
            script.run(stage, stage + 1)
        per = depth // N
        bc = gw_ref[2 * cp :, :].T
        router = router_ref[...].astype(F32)
        for t in range(N):
            at = slice(t * per, (t + 1) * per)
            where = (t // (Y * X * 2), t // (X * 2) % Y, t // 2 % X, t % 2)
            extra[(*where, slice(0, per), slice(0, 2 * state))] = bc[at].astype(B16)
            extra[(*where, slice(0, per), slice(2 * state, 2 * state + LANES))] = router[at].astype(B16)
        sides.run(0, 1)
        for script, stage in final_acts[5:7]:
            script.run(stage, stage + 1)
        sides.run(1, 2)
        for copy in column:
            copy.wait_recv()
        joint[0:line, :] = functools.reduce(jnp.add, [small[t, 0:line, :] for t in range(S)])
        for t in range(S):
            joint[line + 8 * t : line + 8 * t + 8, :] = small[t, line : line + 8, :]
        keep_joint.start()
        for copy in row:
            copy.start()
        for script, stage in final_acts[7:]:
            script.run(stage, stage + 1)
        sides.run(2, 3)
        sums.run(8)
        output_ref[...] = res_ref[...] + total[...] if beside else res_ref[...]
        sides.run(3)
        acts.run(4 * Z)
        values, gone = in_ref[...], total[...]
        gin_ref[...] = gres_ref[...] + rms_back(values, inverse_rms(values), gain_ref[...].reshape(1, depth), gone)
        for copy in row:
            copy.wait()
        for copy in column:
            copy.wait_send()
        keep_joint.wait()
        for copy in keep_here + group:
            copy.wait()
        mail.finish(scatter_count(S, H) if beside else 0)
        mail2.finish(scatter_count(S, H) - 3 + scatter_count(S, H, (False,)))


def mixer_backward(
    lengths, three, one, pre, z, y, states, in_w, taps, rows, cols, out_w, out_part, residual, grad_res, hidden_in, gain,
    norm2, router_part, state, C, S, H,
):
    T, depth = three.shape[0], in_w.shape[0]
    cp, nb = out_w.shape[0], T // BLOCK
    conv_width = cp + 2 * state
    R, N = residual.shape[0], S * H
    X, Y, Z = sizes(S, H)
    line = 2 * (depth // LANES) + 4 * (2 * state // LANES)
    tall = -(-(depth // N) // 16) * 16
    zx_rows = -(-(C + 2) // 16) * 16
    beside = Y == 2
    wo_rows = -(-C // 16) * 16
    assert line % 8 == 0 and cp == LANES and R * H == BLOCK
    sent = scatter_count(S, H) - 3 + scatter_count(S, H, (False,))

    def block(width, kept=2):
        return pl.BlockSpec((BLOCK, width), lambda k: (nb - 1 - k, 0), pipeline_mode=pl.Buffered(kept))

    kept = 2 if beside else 1

    def halo(k):
        return (jnp.maximum((nb - 1 - k) * (BLOCK // 8) - 1, 0), 0)

    return pl.pallas_call(
        functools.partial(mixer_backward_kernel, S, H, beside, lengths.shape[0], state, C),
        grid=(nb,),
        in_specs=[
            pl.BlockSpec(memory_space=pltpu.SMEM), block(three.shape[1]), block(one.shape[1], kept), block(conv_width, kept),
            pl.BlockSpec((8, conv_width), halo), block(cp), block(cp),
            pl.BlockSpec((1, state, cp), lambda k: (nb - 1 - k, 0, 0)),
            VMEM, VMEM, VMEM, VMEM, VMEM, ANY, VMEM, VMEM, VMEM, VMEM, VMEM, VMEM,
        ],
        out_specs=[VMEM, VMEM, VMEM, ANY, ANY, ANY],
        out_shape=[
            jax.ShapeDtypeStruct((R, depth), F32),
            jax.ShapeDtypeStruct((R, depth), F32),
            jax.ShapeDtypeStruct((tall, 2 * state + LANES), F32),
            jax.ShapeDtypeStruct((H, line + 8 * S, LANES), F32),
            jax.ShapeDtypeStruct((S, zx_rows, 2 * (depth // S)), B16),
            jax.ShapeDtypeStruct((S, wo_rows, depth // S), B16),
        ],
        scratch_shapes=[
            pltpu.VMEM((state, cp), F32),
            pltpu.VMEM((BLOCK + 8, conv_width), F32),
            pltpu.VMEM((BLOCK + 8, conv_width), F32),
            pltpu.VMEM((in_w.shape[1], depth), F32),
            pltpu.VMEM(out_w.shape, F32),
            pltpu.VMEM((8, conv_width), F32),
            pltpu.VMEM((8, cp), F32),
            pltpu.VMEM((1, depth), F32),
            pltpu.VMEM((R, depth), F32),
            pltpu.VMEM((Z, Y, X, 2, R, depth), B16),
            pltpu.VMEM((Z, Y, X, 2, tall, 2 * state + LANES), B16),
            pltpu.VMEM((S, zx_rows, 2 * (depth // S)), B16),
            pltpu.VMEM((S, wo_rows, depth // S), B16),
            pltpu.VMEM((S, line + 8, LANES), F32),
            pltpu.VMEM((line + 8 * S, LANES), F32),
            *(scatter_scratch(S, H, R, depth) if beside else []),
            *sum_scratch(S, H, R, depth),
            *sum_scratch(S, H, tall, 2 * state + LANES, False),
            *sems(scatter_count(S, H)),
            *sems(sent),
            pltpu.SemaphoreType.DMA((4,)), pltpu.SemaphoreType.DMA((3,)),
            pltpu.SemaphoreType.DMA((4, S)), pltpu.SemaphoreType.DMA((4, S)),
            pltpu.SemaphoreType.DMA((3,)),
        ],
        compiler_params=talking(6),
    )(
        lengths, three, one, pre, pre, z, y, states, in_w, taps, rows, cols, out_w, blocks(out_part, S, H), residual,
        grad_res, hidden_in, gain, norm2, router_part,
    )


def expert_block(F, two, grad, named, mine, up_ref, down_ref, gup_ref, gdown_ref, gs_ref):
    mid = mm(two, up_ref[...])
    back = mm(grad, down_ref[...], NT)
    gate, lin = mid[:, :F], mid[:, F : 2 * F]
    s_gate, s_lin = mid[:, 2 * F : 2 * F + LANES], mid[:, 2 * F + LANES :]
    named = named.astype(F32) > 0
    logits = jnp.where(named, s_gate, -1e30)
    odds = jnp.where(named, jnp.exp(logits - jnp.max(logits, axis=1, keepdims=True)), 0.0)
    probs = odds / jnp.sum(odds, axis=1, keepdims=True)
    weight = jnp.sum(probs * mine, axis=1, keepdims=True)
    s_back, back = back[:, F:], back[:, :F]
    act_gate, act_s = silu(gate), silu(s_gate)
    acting = act_gate * lin
    gp = jnp.sum(acting * back, axis=1, keepdims=True)
    back = weight * back
    down_in = jnp.concatenate([weight * acting, act_s * s_lin], axis=1).astype(B16)
    mid_grad = jnp.concatenate(
        [back * lin * silu_grad(gate), back * act_gate, s_back * s_lin * silu_grad(s_gate), s_back * act_s], axis=1
    ).astype(B16)
    gup_ref[...] += mm(two, mid_grad[:, : 2 * F], TN)
    gdown_ref[...] += mm(down_in[:, :F], grad, TN)
    gs_ref[: 2 * LANES, :] += mm(mid_grad[:, 2 * F :], two, TN)
    gs_ref[2 * LANES :, :] += mm(down_in[:, F:], grad, TN)
    out = mm(down_in, down_ref[...]).astype(B16)
    part = mm(mid_grad, up_ref[...], NT).astype(B16)
    return out, part, (gp * mine).astype(B16), probs


def expert_kernel(
    S, H, F, width, total_ref, in_ref, gain_ref, grad_ref, named_ref, up_ref, down_ref, mine_ref, ograd_ref,
    three_ref, res_ref, gres_ref, gnorm_ref, grouter_ref, out_ref, gup_out, gdown_ref, sh_out,
    gup_ref, total, rows, two, grads, names, parts, stage_out, probs, gs_ref, *rest,
):
    buffers, (rows3, pieces, send2, recv2, sh_send, sh_recv, own_sem, own3_sem, sh_sem, name_sem, grad_sem, out_sem) = (
        rest[:-12], rest[-12:]
    )
    pc = Place(S, H)
    X, Y, Z = pc.X, pc.Y, pc.Z
    R, D = in_ref.shape
    n = BLOCK
    N, me = S * H, pc.slot()
    mail2 = Mail(send2, recv2)

    def hello(m, carry):
        to = (me + m) % N
        hail([(to // H, to % H)])
        return carry

    lax.fori_loop(1, N, hello, 0)
    stay = pltpu.make_async_copy(pieces.at[me], sh_out.at[me], sh_sem)

    def to_all(function):
        def body(m, carry):
            to = (me + m) % N
            function(
                pltpu.make_async_remote_copy(
                    src_ref=pieces.at[to], dst_ref=sh_out.at[me], send_sem=sh_send.at[m], recv_sem=sh_recv.at[m],
                    device_id=(to // H, to % H), device_id_type=MESH,
                )
            )
            return carry

        lax.fori_loop(1, N, body, 0)

    def cell(dz, yy, xx, rows):
        return parts.at[dz, yy, xx, pc.c, rows]

    moves = gather(pc, mail2, rows, two, own_sem, planes=True)
    onward = gather(pc, mail2, rows3, three_ref, own3_sem)
    acts = Script()
    second = Sum(pc, mail2, acts, cell, lambda dz: parts.at[dz, :, :, 1 - pc.c], buffers, R, direct=True)
    for dz in range(Z):
        acts.stage()
        second.across(dz)
        acts.stage()
        second.cores(dz)
        acts.stage()
        second.firsts(dz)
        acts.stage()
        second.seconds(dz)
    acts.stage()
    second.last(total)

    def seq_of(k):
        return pc.partner(k // Y) * Y + k % Y

    def loads(k, slot):
        at = pl.ds(pl.multiple_of(seq_of(k) * n, n), n)
        return [
            pltpu.make_async_copy(grad_ref.at[at], grads.at[slot], grad_sem.at[slot]),
            pltpu.make_async_copy(named_ref.at[at, pl.ds(D, LANES)], names.at[slot], name_sem.at[slot]),
        ]

    def store(k, slot):
        at = pl.ds(pl.multiple_of(seq_of(k) * n, n), n)
        return pltpu.make_async_copy(stage_out.at[slot], out_ref.at[at], out_sem.at[slot])

    for copy in loads(0, 0):
        copy.start()
    gain = gain_ref[...].reshape(1, D)
    mixed = total_ref[:, :D]
    square = jnp.sum(total_ref[:, D:], axis=1, keepdims=True)
    inv = lax.rsqrt(square / width + EPS)
    residual = in_ref[...] + inv * mixed
    res_ref[...] = residual
    rows[...] = (residual * inverse_rms(residual) * gain).astype(B16)
    cube = inv * inv * inv / width
    settle(N - 1)
    moves.run(0, 1)
    gup_ref[...] = jnp.zeros_like(gup_ref)
    gdown_ref[...] = jnp.zeros_like(gdown_ref)
    gs_ref[...] = jnp.zeros_like(gs_ref)
    moves.run(1, 5)
    moves.run(12, 13)

    count = Y * Z
    before = {k: [] for k in range(count)}
    after = []
    for dz in range(Z):
        for late, stage in ((0, 0), (1, 1), (3, 2), (4, 3)):
            k = (dz + 1) * Y + late
            before.get(k, after).append((acts, 4 * dz + stage))
    after = [(acts, 4 * dz + stage) for dz, stage in ((3, 0), (1, 2), (1, 3), (2, 2), (3, 1), (2, 3), (3, 2), (3, 3))]
    after = [entry for entry in after if all(entry not in before[k] for k in before)]
    for k, stage in (
        (0, 5), (1, 6), (1, 7), (Y, 8), (Y, 13), (Y + 1, 9), (Y + 1, 10), (2 * Y, 11), (2 * Y, 14), (3 * Y, 15),
    ):
        before[k].append((moves, stage))
    mine = mine_ref[...]

    def step(k, carry):
        for at in range(count):
            if before[at]:

                @pl.when(k == at)
                def _():
                    for script, stage in before[at]:
                        script.run(stage, stage + 1)

        slot = k % 2

        @pl.when(k + 1 < count)
        def _():
            for copy in loads(k + 1, 1 - slot):
                copy.start()

        for copy in loads(k, slot):
            copy.wait()
        block = two[pl.ds(pl.multiple_of(seq_of(k) * n, n), n), :]
        out, part, gp, chance = expert_block(
            F, block, grads[slot], names[slot], mine, up_ref, down_ref, gup_ref, gdown_ref, gs_ref
        )
        for xx in range(X):
            for cc in range(2):
                at = slice((xx * 2 + cc) * R, (xx * 2 + cc + 1) * R)
                parts[k // Y, k % Y, xx, cc, :, :D] = part[at]
                parts[k // Y, k % Y, xx, cc, :, D:] = gp[at]

        @pl.when(k == pc.y)
        def _():
            probs[...] = chance

        @pl.when(k >= 2)
        def _():
            store(k - 2, slot).wait()

        stage_out[slot] = out
        store(k, slot).start()
        return carry

    lax.fori_loop(0, count, step, 0)
    for script, stage in after[:1]:
        script.run(stage, stage + 1)
    for k in range(2):
        gup_out[0, :, k, :] = gup_ref[:, k * F : (k + 1) * F]
    per, FS = D // N, pieces.shape[2] // 3
    turned = jnp.concatenate([gs_ref[k * LANES : k * LANES + FS, :] for k in range(3)], axis=0).T
    for k in range(N):
        pieces[k, :per, :] = turned[k * per : (k + 1) * per, :].astype(B16)
        if per < pieces.shape[1]:
            pieces[k, per:, :] = jnp.zeros((pieces.shape[1] - per, 3 * FS), B16)
    for script, stage in after[1:]:
        script.run(stage, stage + 1)
    head = lax.axis_index("head")
    p = probs[pl.ds(pl.multiple_of(head * R, R), R), :]
    acts.run(4 * Z)
    gp = total[:, D:]
    glogits = (p * (gp - jnp.sum(p * gp, axis=1, keepdims=True))).astype(B16)
    gtwo = total[:, :D] + mm(glogits, up_ref[:, 2 * F : 2 * F + LANES], NT)
    residual = res_ref[...]
    inv_two = inverse_rms(residual)
    gres = ograd_ref[...] + rms_back(residual, inv_two, gain, gtwo)
    cross = jnp.sum(gres * mixed, axis=1, keepdims=True) * cube
    high, low = hi_lo(cross)
    lane = lax.broadcasted_iota(jnp.int32, (R, LANES), 1)
    rows3[:, :D] = (inv * gres).astype(B16)
    rows3[:, D:] = jnp.where(lane == 0, high.astype(F32), jnp.where(lane == 1, low.astype(F32), 0.0)).astype(B16)
    onward.run(0, 1)
    stay.start()
    to_all(lambda copy: copy.start())
    gres_ref[...] = gres
    gnorm_ref[...] = jnp.sum(gtwo * residual * inv_two, axis=0, keepdims=True)
    grouter_ref[...] = mm((residual * inv_two * gain).astype(B16), glogits, TN).astype(B16)
    for k in (count - 2, count - 1):
        store(k, k % 2).wait()
    onward.run(1)
    to_all(lambda copy: copy.wait())
    stay.wait()
    mail2.finish(2 * gather_count(S, H) + scatter_count(S, H))


def experts(total, hidden_in, gain, all_grad, gathered, up_w, down_w, mine, out_grad, F, FS, width, S, H):
    R, D = hidden_in.shape
    X, Y, Z = sizes(S, H)
    T, W = S * H * R, D + LANES
    tall = -(-(D // (S * H)) // 16) * 16
    assert R * H == BLOCK
    return pl.pallas_call(
        functools.partial(expert_kernel, S, H, F, width),
        out_shape=[
            jax.ShapeDtypeStruct((T, W), B16),
            jax.ShapeDtypeStruct((R, D), F32),
            jax.ShapeDtypeStruct((R, D), F32),
            jax.ShapeDtypeStruct((1, D), F32),
            jax.ShapeDtypeStruct((D, LANES), B16),
            jax.ShapeDtypeStruct((T, D), B16),
            jax.ShapeDtypeStruct((1, D, 2, F), F32),
            jax.ShapeDtypeStruct((F, D), F32),
            jax.ShapeDtypeStruct((S * H, tall, 3 * FS), B16),
        ],
        in_specs=[VMEM, VMEM, VMEM, ANY, ANY] + [VMEM] * 4,
        out_specs=[ANY] + [VMEM] * 4 + [ANY] + [VMEM] * 2 + [ANY],
        scratch_shapes=[
            pltpu.VMEM((D, 2 * F), F32), pltpu.VMEM((R, W), F32), pltpu.VMEM((R, D), B16), pltpu.VMEM((T, D), B16),
            pltpu.VMEM((2, BLOCK, D), B16), pltpu.VMEM((2, BLOCK, LANES), B16),
            pltpu.VMEM((Z, Y, X, 2, R, W), B16), pltpu.VMEM((2, BLOCK, D), B16), pltpu.VMEM((BLOCK, LANES), F32),
            pltpu.VMEM((3 * LANES, D), F32), *sum_scratch(S, H, R, W),
            pltpu.VMEM((R, W), B16), pltpu.VMEM((S * H, tall, 3 * FS), B16),
            *sems(scatter_count(S, H) + 2 * gather_count(S, H)), *sems(S * H),
            pltpu.SemaphoreType.DMA, pltpu.SemaphoreType.DMA, pltpu.SemaphoreType.DMA, pltpu.SemaphoreType.DMA((2,)),
            pltpu.SemaphoreType.DMA((2,)), pltpu.SemaphoreType.DMA((2,)),
        ],
        compiler_params=talking(2),
    )(total, hidden_in, gain, all_grad, gathered, up_w, down_w, mine, out_grad)


def finish_kernel(
    S, H, C, FS, state, zx_ref, wo_ref, sh_ref, small_ref, pick_ref, kcip_ref, gain_ref, a_in, b_in, c_in, d_in,
    zx_out, dt_out, wo_out, up_out, down_out, norm1_out, norm2_out, taps_out, bc_out, gate_out, heads_out,
    a_out, b_out, c_out, d_out, a_way, b_way, c_way, d_way, sem,
):
    ways = ((a_in, a_way, a_out), (b_in, b_way, b_out), (c_in, c_way, c_out), (d_in, d_way, d_out))
    held = [pltpu.make_async_copy(src, way, sem.at[0, k]) for k, (src, way, dst) in enumerate(ways)]
    gone = [pltpu.make_async_copy(way, dst, sem.at[1, k]) for k, (src, way, dst) in enumerate(ways)]
    for copy in held:
        copy.start()
    wide = wo_ref.shape[2]
    heads = dt_out.shape[0]
    dt = jnp.zeros(dt_out.shape, F32)
    for t in range(S):
        piece = zx_ref[t].astype(F32)
        turned = piece.T
        at = slice(t * C, (t + 1) * C)
        zx_out[:, 0, at] = turned[:wide, :C]
        zx_out[:, 1, at] = turned[wide:, :C]
        dt = dt + exact(kcip_ref[t, :, : piece.shape[0]], piece[:, :wide])
        wo_out[:, at] = wo_ref[t].astype(F32).T[:, :C]
    dt_out[...] = dt
    for come, go in zip(held, gone):
        come.wait()
        go.start()
    for t in range(S * H):
        piece = sh_ref[t].astype(F32)[: up_out.shape[0]]
        at = slice(t * FS, (t + 1) * FS)
        for k in range(2):
            up_out[:, k, at] = piece[:, k * FS : (k + 1) * FS]
        down_out[:, at] = piece[:, 2 * FS :]
    gain = gain_ref[...].reshape(1, gain_ref.shape[0])
    lines = gain.shape[1] // LANES
    total = small_ref[0, : 2 * lines + 4 * (2 * state // LANES), :]
    for h in range(1, H):
        total = total + small_ref[h, : total.shape[0], :]
    for j in range(lines):
        at = slice(j * LANES, (j + 1) * LANES)
        norm1_out[:, at] = total[j : j + 1, :] / gain[:, at]
        norm2_out[:, at] = total[lines + j : lines + j + 1, :]
    line = 2 * lines
    for r in range(4):
        for j in range(2 * state // LANES):
            bc_out[r : r + 1, j * LANES : (j + 1) * LANES] = total[line : line + 1, :]
            line += 1
    for h in range(H):
        by_head = jnp.zeros((8, heads), F32)
        for t in range(S):
            ours = small_ref[h, line + 8 * t : line + 8 * t + 8, :]
            at = slice((h * S + t) * C, (h * S + t + 1) * C)
            taps_out[:, at] = ours[0:4, :C]
            gate_out[:, at] = ours[4:5, :C]
            by_head = by_head + exact(ours, pick_ref[t])
        for r in range(3):
            heads_out[r : r + 1, h * heads : (h + 1) * heads] = by_head[5 + r : 6 + r, :]
    for copy in gone:
        copy.wait()


def finish(zx, wo, shared, small, pick, gain, made, C, FS, state, S, H):
    N, wide, heads, D = S * H, wo.shape[2], pick.shape[2], gain.shape[0]
    per = D // N
    shapes = (
        (wide, 2, S * C), (heads, wide), (wide, S * C), (per, 2, N * FS), (per, N * FS), (1, D), (1, D), (4, S * H * C),
        (4, 2 * state), (1, S * H * C), (3, H * heads),
    )
    return pl.pallas_call(
        functools.partial(finish_kernel, S, H, C, FS, state),
        out_shape=[jax.ShapeDtypeStruct(shape, F32) for shape in shapes + tuple(v.shape for v in made)],
        in_specs=[VMEM] * 7 + [ANY] * 4,
        out_specs=[VMEM] * len(shapes) + [ANY] * 4,
        scratch_shapes=[*(pltpu.VMEM(v.shape, F32) for v in made), pltpu.SemaphoreType.DMA((2, 4))],
        compiler_params=pltpu.CompilerParams(vmem_limit_bytes=56 * 1024 * 1024),
    )(zx, wo, shared, small, pick, pick.transpose(0, 2, 1), gain, *made)


def local(
    hidden_in, norm1_gain, w_zx, w_bc, w_dt, conv_x, conv_bc, dt_bias, a_log, d_skip, gate_gain,
    w_out, norm2_gain, router, expert_up, expert_down, shared_up, shared_down, out_grad,
    seq_lengths, routes,
):
    S, H = lax.axis_size("seq"), lax.axis_size("head")
    N = S * H
    s = lax.axis_index("seq")
    g = s * H + lax.axis_index("head")
    R, D = hidden_in.shape
    heads, inner = dt_bias.shape[0], conv_x.shape[1]
    size = inner // heads
    state = w_bc.shape[1] // 2
    width = inner * H
    C = inner // S
    CP = -(-(C + 2) // LANES) * LANES
    E = N // 2
    F = expert_down.shape[1]
    FS = shared_down.shape[0] // N
    per = D // N

    gain1, gain2 = norm1_gain, norm2_gain
    gathered, rows, taps, cols, in_w, up_w = first_rows(
        hidden_in, gain1, routes.T, conv_x, conv_bc, gate_gain, w_zx, w_bc, w_dt.T, expert_up[0], router.T, shared_up,
        dt_bias, a_log, d_skip, C, CP, FS, S, H
    )

    firsts = [min(k * C // size, heads - 2) for k in range(S)]

    def mine(values, axis, offset, length):
        return lax.dynamic_slice_in_dim(values, offset, length, axis)

    def channels(values, axis):
        cut = mine(values, axis, s * C, C)
        pads = [(0, 0)] * values.ndim
        pads[axis] = (0, CP - C)
        return jnp.pad(cut, pads)

    out_w = channels(w_out, 0)

    pre, z, y, states, mixed, all_grad = mixer_forward(
        seq_lengths, gathered, in_w, taps, rows, out_w, out_grad, state, C, S, H
    )

    down_w = jnp.concatenate([expert_down[0], mine(shared_down, 0, g * FS, FS), jnp.zeros((LANES - FS, D), B16)], axis=0)
    is_mine = (jnp.arange(LANES) == FS + g // 2).astype(F32)[None]
    three, residual, grad_res, norm2_part, router_part, out_part, grad_up, grad_down, sh_in = experts(
        mixed, hidden_in, gain2, all_grad, gathered, up_w, down_w, is_mine, out_grad, F, FS, width, S, H
    )

    output, grad_in, extra_sum, small, zx_in, wo_in = mixer_backward(
        seq_lengths, three, gathered, pre, z, y, states, in_w, taps, rows, cols, out_w, out_part, residual,
        grad_res, hidden_in, gain1, norm2_part, router_part, state, C, S, H,
    )
    if H > 4:
        output = output + lax.psum_scatter(out_part, ("seq", "head"), scatter_dimension=0, tiled=True).astype(F32)
    grad_bc, grad_router = extra_sum[:per, : 2 * state], extra_sum[:per, 2 * state :][:, FS : FS + E]
    pick = np.array(
        [[[C <= c < C + 2 and firsts[k] + c - C == h for h in range(heads)] for c in range(LANES)] for k in range(S)], np.float32
    )
    grad_zx, grad_w_dt, grad_w_out, grad_shared_up, grad_shared_down, *found = finish(
        zx_in, wo_in, sh_in, small, pick, gain1, (grad_up, grad_down[None], output, grad_in), C, FS, state, S, H
    )
    grad_norm1, grad_norm2, grad_conv_x, grad_conv_bc, grad_gate_gain, by_head, *made = found
    grad_up, grad_down, output, grad_in = made
    grad_norm1, grad_norm2, grad_gate_gain = (v.reshape(-1) for v in (grad_norm1, grad_norm2, grad_gate_gain))
    grad_dt_bias, grad_a_log, grad_d_skip = by_head[0], by_head[1], by_head[2]
    return (
        output, grad_in, grad_norm1, grad_zx, grad_bc, grad_w_dt.T, grad_conv_x, grad_conv_bc, grad_dt_bias,
        grad_a_log, grad_d_skip, grad_gate_gain, grad_w_out.T, grad_norm2, grad_router, grad_up, grad_down,
        grad_shared_up, grad_shared_down.T,
    )


def solution(mesh):
    return jax.shard_map(
        local,
        mesh=mesh,
        in_specs=(
            P(("seq", "head"), None),
            P(),
            P(None, None, "head"),
            P(),
            P(None, "head"),
            P(None, "head"),
            P(),
            P("head"),
            P("head"),
            P("head"),
            P("head"),
            P("head", None),
            P(),
            P(),
            P(("seq", "head"), None, None, None),
            P(("seq", "head"), None, None),
            P(),
            P(),
            P(("seq", "head"), None),
            P(),
            P(("seq", "head"), None),
        ),
        out_specs=(
            P(("seq", "head"), None),
            P(("seq", "head"), None),
            P(),
            P("seq", None, "head"),
            P(("seq", "head"), None),
            P("seq", "head"),
            P(),
            P(),
            P(),
            P(),
            P(),
            P(),
            P("head", "seq"),
            P(),
            P(("seq", "head"), None),
            P(("seq", "head"), None, None, None),
            P(("seq", "head"), None, None),
            P(("seq", "head"), None, None),
            P(None, ("seq", "head")),
        ),
        check_vma=False,
    )
```
